32 devices in a mesh: tm: 16 (over z, y, x), space: 2 (over core).
Axes of the slice: x: 2, y: 2, z: 4, core: 2. Of those that a mesh axis runs over, the one named last changes fastest.
Arguments:
- feats: bfloat16 [64, 8, 96, 256], P('tm', 'space'), may hold values from -120 to 120
- clip_ids: int32 [16], replicated, may hold values from 0 to 3, never falling along the last dimension, each value on 1 to 8 neighbouring positions
- gain_one: float32 [256], replicated, may hold values from 0.25 to 1.75
- shift_one: float32 [256], replicated, may hold values from -3 to 3
- kernel_one: bfloat16 [3, 3, 3, 256, 256], replicated, may hold values from -0.078125 to 0.078125
- gain_two: float32 [256], replicated, may hold values from 0.25 to 1.75
- shift_two: float32 [256], replicated, may hold values from -3 to 3
- kernel_two: bfloat16 [3, 3, 3, 256, 256], replicated, may hold values from -0.078125 to 0.078125
Outputs:
- block_out: float32 [64, 8, 96, 256], P('tm', 'space')
The draws below stay inside these ranges and needn't reach their ends.
Inputs may be any that keep to these rules, and one draw needn't show every extreme that they name: `clip_ids`: clip numbers of the slabs in order, never falling; every clip covers 1 to 8 consecutive slabs, at least one exactly 8.
All inputs are finite; a program needn't handle non-finite values.
Results may differ from the reference program's by a relative error of at most 0.0015.
Values may be sent and summed in bfloat16 or wider, within the bound.
No kernel may reach another device: no remote copies, remote signals or barrier semaphores. Data moves between devices by JAX's collectives and lax.ppermute only.
A program may use at most 128 MiB of HBM per device.

```python
import math
import jax
import jax.numpy as jnp
import numpy as np
from jax import lax

C = 256
GROUPS = 32
FR = 4
COLS = 96
NFR = 64
NROWS = 8
CLIPS = 4
N_TM = 16


def draw_feats(key, part):
    key_base = jax.random.fold_in(key, 0)
    key_cell = jax.random.fold_in(key, 1)
    key_chan = jax.random.fold_in(key, 2)
    key_slab = jax.random.fold_in(key, 4)
    key_row = jax.random.fold_in(key, 5)
    shape = (NFR, NROWS, COLS, C)
    slab_total = NFR // FR
    slab_pos = jnp.arange(slab_total, dtype=jnp.float32) / max(slab_total - 1, 1)
    slab_amp = jnp.exp(slab_pos * math.log(3.0) + jax.random.uniform(key_slab, (slab_total,), jnp.float32, 0.0, math.log(4.0)))
    frame_amp = jnp.repeat(slab_amp, FR)[:, None, None, None]
    row_pos = jnp.arange(NROWS, dtype=jnp.float32) / max(NROWS - 1, 1)
    row_amp = jnp.exp(row_pos * math.log(3.0) + jax.random.uniform(key_row, (NROWS,), jnp.float32, 0.0, math.log(6.0)))[None, :, None, None]
    chan = jnp.exp(jax.random.uniform(key_chan, (C,), jnp.float32, -math.log(2.0), math.log(2.0)))
    base = jnp.clip(jax.random.normal(key_base, shape, jnp.float32), -6.0, 6.0)
    cell = jnp.exp(jax.random.uniform(key_cell, (NFR, NROWS, COLS, 1), jnp.float32) * math.log(10.0))
    values = 0.05 * frame_amp * row_amp * cell * chan * base
    return jnp.clip(values, -120.0, 120.0).astype(jnp.bfloat16)


def split_up(number_of, total, bound, lean):
    loads = [(1 << 20) // math.isqrt(grade ** lean) + 1 for grade in range(2, number_of + 1)]
    surplus, counts = total - bound - (number_of - 1), [1] * (number_of - 1)
    while surplus > 0:
        free = [i for i in range(number_of - 1) if counts[i] < bound]
        pool, budget = sum([loads[i] for i in free]), surplus
        for i in free:
            more = min(bound - counts[i], max(1, budget * loads[i] // pool), surplus)
            counts[i] = counts[i] + more
            surplus = surplus - more
    return np.array([bound] + counts)


def uneven(key, count, total, reach, lean):
    if count == 2:
        one = jax.random.randint(key, (), max(1, total - reach), min(reach, total - 1) + 1)
        return jnp.stack([one, total - one])
    sizes = jnp.asarray(split_up(count, total, reach, lean), jnp.int32)
    twos = (count - 1) // 2
    source_of, receiver = sizes[1:1 + 2 * twos:2], sizes[2:2 + 2 * twos:2]
    slack = jnp.minimum(source_of - 1, reach - receiver)
    passed = jax.random.randint(jax.random.fold_in(key, 1), (twos,), 0, 1 << 20) % (slack + 1)
    sizes = sizes.at[1:1 + 2 * twos:2].set(source_of - passed).at[2:2 + 2 * twos:2].set(receiver + passed)
    return sizes[jax.random.permutation(jax.random.fold_in(key, 2), count)]


def scatter_about(rng, extent, deviation, limit, held_as=jnp.bfloat16):
    result = jax.random.normal(rng, extent, jnp.float32) * deviation
    return jnp.minimum(jnp.maximum(result, -limit), limit).astype(held_as)


def setup_inputs(seed: int = 0) -> dict:
    splits = jax.random.split(jax.random.key(seed), 9)
    feats = draw_feats(jax.random.fold_in(splits[8], 71), 0)
    clip_ids = jnp.searchsorted(jnp.cumsum(uneven(splits[1], CLIPS, N_TM, 8, 2)), jnp.arange(N_TM), side="right").astype(jnp.int32)
    gain_one = jnp.clip(1.0 + 0.15 * jax.random.normal(splits[2], (C,), jnp.float32), 0.25, 1.75)
    shift_one = scatter_about(splits[3], (C,), 0.5, 3.0, jnp.float32)
    kernel_one = scatter_about(splits[4], (3, 3, 3, C, C), (27 * C) ** -0.5, 0.078125)
    gain_two = jnp.clip(1.0 + 0.15 * jax.random.normal(splits[5], (C,), jnp.float32), 0.25, 1.75)
    shift_two = scatter_about(splits[6], (C,), 0.5, 3.0, jnp.float32)
    kernel_two = scatter_about(splits[7], (3, 3, 3, C, C), (27 * C) ** -0.5, 0.078125)
    return {"feats": feats, "clip_ids": clip_ids, "gain_one": gain_one, "shift_one": shift_one, "kernel_one": kernel_one, "gain_two": gain_two, "shift_two": shift_two, "kernel_two": kernel_two}


def clip_norm(values, clip_frame, gain, shift):
    width = values.shape[3]
    grouped = values.reshape(NFR, -1, GROUPS, width // GROUPS)
    frame_sum = lax.optimization_barrier(jnp.sum(grouped, axis=(1, 3)))
    frame_square = lax.optimization_barrier(jnp.sum(grouped * grouped, axis=(1, 3)))
    member = (clip_frame[:, None] == jnp.arange(CLIPS, dtype=jnp.int32)[None, :]).astype(jnp.float32)
    clip_sum = jnp.dot(member.T, frame_sum, precision=lax.Precision.HIGHEST)
    clip_square = jnp.dot(member.T, frame_square, precision=lax.Precision.HIGHEST)
    per_sum = jnp.dot(member, clip_sum, precision=lax.Precision.HIGHEST)
    per_square = jnp.dot(member, clip_square, precision=lax.Precision.HIGHEST)
    frames_in = jnp.dot(member, lax.optimization_barrier(jnp.sum(member, axis=0)), precision=lax.Precision.HIGHEST)
    count = frames_in * (NROWS * COLS * (width // GROUPS))
    mean = per_sum / count[:, None]
    variance = per_square / count[:, None] - mean * mean
    scale = lax.rsqrt(variance + 1e-06)
    normed = (grouped - mean[:, None, :, None]) * scale[:, None, :, None]
    normed = normed.reshape(values.shape) * gain + shift
    return jax.nn.silu(normed).astype(jnp.bfloat16)

def causal_conv(act, kernel, start_frame):
    width = act.shape[3]
    frame_index = jnp.arange(NFR, dtype=jnp.int32)
    total = jnp.zeros((NFR * NROWS * COLS, kernel.shape[4]), jnp.float32)
    for tap_time in range(3):
        source = jnp.maximum(frame_index - 2 + tap_time, start_frame).astype(jnp.int32)
        taken = jnp.take(act, source, axis=0)
        padded = jnp.pad(taken, ((0, 0), (1, 1), (1, 1), (0, 0)), mode='edge')
        for tap_row in range(3):
            window = padded[:, tap_row:tap_row + NROWS]
            stacked = jnp.concatenate([window[:, :, offset:offset + COLS] for offset in range(3)], axis=3)
            stacked = stacked.reshape(-1, 3 * width)
            total = total + jnp.dot(stacked, kernel[tap_time, tap_row].reshape(3 * width, -1), preferred_element_type=jnp.float32)
    return total.reshape(NFR, NROWS, COLS, -1)

def reference(feats, clip_ids, gain_one, shift_one, kernel_one, gain_two, shift_two, kernel_two):
    slabs = jnp.arange(N_TM, dtype=jnp.int32)
    starts = jnp.concatenate([jnp.ones((1,), bool), clip_ids[1:] != clip_ids[:-1]])
    first_slab = lax.cummax(jnp.where(starts, slabs, 0).astype(jnp.int32), axis=0)
    slab_of = (jnp.arange(NFR, dtype=jnp.int32) // FR).astype(jnp.int32)
    start_frame = (jnp.take(first_slab, slab_of) * FR).astype(jnp.int32)
    clip_frame = jnp.take(clip_ids, slab_of).astype(jnp.int32)
    inputs = feats.astype(jnp.float32)
    first = clip_norm(inputs, clip_frame, gain_one, shift_one)
    hidden = causal_conv(first, kernel_one, start_frame).astype(jnp.bfloat16)
    second = clip_norm(hidden.astype(jnp.float32), clip_frame, gain_two, shift_two)
    return inputs + causal_conv(second, kernel_two, start_frame)
```

```python
import jax
import jax.numpy as jnp
from jax import lax
from jax.sharding import PartitionSpec as P

GROUPS = 32


def padded_2(value, sides, width):
    for axis, dim in sides:
        peers, length = (lax.axis_size(axis), value.shape[dim])
        up = [(i, (i + 1) % peers) for i in range(peers - 1)]
        down = [(j, i) for i, j in up]
        last = lax.slice_in_dim(value, length - width, length, axis=dim)
        leading = lax.slice_in_dim(value, 0, width, axis=dim)
        before = lax.ppermute(last, axis, up)
        after = lax.ppermute(leading, axis, down)
        value = jnp.concatenate([before, value, after], axis=dim)
    return value


def passed_along(block, axis, distance):
    devices = range(lax.axis_size(axis))
    route = [(i - distance, i) for i in devices if i - distance in devices]
    return lax.ppermute(block, axis, route)


def summed_over(table, axes):
    peers = lax.axis_size(axes)
    if peers & (peers - 1):
        return lax.psum(table, axes)
    step = 1
    while step < peers:
        table = table + lax.ppermute(table, axes, [(i, i ^ step) for i in range(peers)])
        step *= 2
    return table


def clip_stats(values, clip_ids):
    width = values.shape[3]
    grouped = values.reshape(-1, GROUPS, width // GROUPS)
    local_sum = jnp.sum(grouped, axis=(0, 2))
    local_square = jnp.sum(grouped * grouped, axis=(0, 2))
    slab_count = lax.axis_size("tm")
    own_slab = lax.axis_index("tm")
    own_clip = lax.dynamic_index_in_dim(clip_ids, own_slab, keepdims=False)
    own_row = (jnp.arange(slab_count, dtype=jnp.int32) == own_clip).astype(jnp.float32)[:, None]
    table = jnp.concatenate([own_row * local_sum[None, :], own_row * local_square[None, :]], axis=1)
    table = summed_over(table, ("tm", "space"))
    table_sum, table_square = (table[:, :GROUPS], table[:, GROUPS:])
    clip_sum = jnp.sum(table_sum * own_row, axis=0)
    clip_square = jnp.sum(table_square * own_row, axis=0)
    slabs_in = jnp.sum((clip_ids == own_clip).astype(jnp.float32))
    count = slabs_in * (
        values.shape[0]
        * values.shape[1]
        * lax.axis_size("space")
        * values.shape[2]
        * (width // GROUPS)
    )
    mean = clip_sum / count
    variance = clip_square / count - mean * mean
    return (mean, lax.rsqrt(variance + 1e-06))


def apply_norm(values, mean, scale, gain, shift):
    width = values.shape[3]
    grouped = values.reshape(values.shape[:3] + (GROUPS, width // GROUPS))
    normed = (grouped - mean[:, None]) * scale[:, None]
    normed = normed.reshape(values.shape) * gain + shift
    return jax.nn.silu(normed).astype(jnp.bfloat16)


def edge_rows(extended, margin):
    place = lax.axis_index("space")
    last = lax.axis_size("space") - 1
    rows = extended.shape[1]
    row_pos = jnp.arange(rows, dtype=jnp.int32)
    top_row = extended[:, margin : margin + 1]
    bottom_row = extended[:, rows - margin - 1 : rows - margin]
    upper = jnp.logical_and(place == 0, row_pos < margin)[None, :, None, None]
    lower = jnp.logical_and(place == last, row_pos >= rows - margin)[None, :, None, None]
    extended = jnp.where(upper, top_row, extended)
    return jnp.where(lower, bottom_row, extended)


def with_rims(frames):
    return edge_rows(padded_2(frames, (("space", 1),), 1), 1)


def causal_conv(extended, kernel):
    frames = extended.shape[0] - 2
    rows = extended.shape[1] - 2
    cols = extended.shape[2]
    width = extended.shape[3]
    padded = jnp.pad(extended, ((0, 0), (0, 0), (1, 1), (0, 0)), mode="edge")
    total = jnp.zeros((frames * rows * cols, kernel.shape[4]), jnp.float32)
    for tap_time in range(3):
        for tap_row in range(3):
            window = padded[tap_time : tap_time + frames, tap_row : tap_row + rows]
            stacked = jnp.concatenate(
                [window[:, :, offset : offset + cols] for offset in range(3)], axis=3
            )
            stacked = stacked.reshape(-1, 3 * width)
            total = total + jnp.dot(
                stacked,
                kernel[tap_time, tap_row].reshape(3 * width, -1),
                preferred_element_type=jnp.float32,
            )
    return total.reshape(frames, rows, cols, -1)


def repeat_first(act, count):
    return jnp.broadcast_to(act[0:1], (count,) + act.shape[1:])


def temporal_front(act, starting):
    earlier = passed_along(act[-2:], "tm", 1)
    front = jnp.where(starting, repeat_first(act, 2), earlier)
    return jnp.concatenate([front, act], axis=0)


def on_device(feats, clip_ids, gain_one, shift_one, kernel_one, gain_two, shift_two, kernel_two):
    own_slab = lax.axis_index("tm")
    own_clip = lax.dynamic_index_in_dim(clip_ids, own_slab, keepdims=False)
    before_clip = lax.dynamic_index_in_dim(clip_ids, jnp.maximum(own_slab - 1, 0), keepdims=False)
    starting = jnp.logical_or(own_slab == 0, own_clip != before_clip)
    inputs = feats.astype(jnp.float32)
    mean_one, scale_one = clip_stats(inputs, clip_ids)
    first = apply_norm(inputs, mean_one, scale_one, gain_one, shift_one)
    front_first = temporal_front(first, starting)
    hidden = causal_conv(with_rims(front_first), kernel_one).astype(jnp.bfloat16)
    hidden_float = hidden.astype(jnp.float32)
    mean_two, scale_two = clip_stats(hidden_float, clip_ids)
    second = apply_norm(hidden_float, mean_two, scale_two, gain_two, shift_two)
    extended = with_rims(temporal_front(second, starting))
    return inputs + causal_conv(extended, kernel_two)


def solution(mesh):
    return jax.shard_map(
        on_device,
        mesh=mesh,
        in_specs=(P("tm", "space", None, None), P(), P(), P(), P(), P(), P(), P()),
        out_specs=P("tm", "space", None, None),
        check_vma=False,
    )
```

```python
import jax
import jax.numpy as jnp
from jax import lax
from jax.sharding import PartitionSpec as P

GROUPS = 32


def padded_2(value, sides, width):
    for axis, dim in sides:
        peers, length = (lax.axis_size(axis), value.shape[dim])
        up = [(i, (i + 1) % peers) for i in range(peers - 1)]
        down = [(j, i) for i, j in up]
        last = lax.slice_in_dim(value, length - width, length, axis=dim)
        leading = lax.slice_in_dim(value, 0, width, axis=dim)
        before = lax.ppermute(last, axis, up)
        after = lax.ppermute(leading, axis, down)
        value = jnp.concatenate([before, value, after], axis=dim)
    return value


def passed_along(block, axis, distance):
    devices = range(lax.axis_size(axis))
    route = [(i - distance, i) for i in devices if i - distance in devices]
    return lax.ppermute(block, axis, route)


def clip_stats(values, clip_ids):
    width = values.shape[3]
    grouped = values.reshape(-1, GROUPS, width // GROUPS)
    local_sum = jnp.sum(grouped, axis=(0, 2))
    local_square = jnp.sum(grouped * grouped, axis=(0, 2))
    slab_count = lax.axis_size("tm")
    own_slab = lax.axis_index("tm")
    own_clip = lax.dynamic_index_in_dim(clip_ids, own_slab, keepdims=False)
    stats = jnp.concatenate([local_sum, local_square])
    parts = lax.all_to_all(jnp.broadcast_to(stats, (slab_count * lax.axis_size("space"), 2 * GROUPS)), ("tm", "space"), 0, 0)
    same_clip = (clip_ids == own_clip).astype(jnp.float32)
    totals = jnp.sum(parts.reshape(slab_count, -1, 2 * GROUPS) * same_clip[:, None, None], axis=(0, 1))
    clip_sum, clip_square = (totals[:GROUPS], totals[GROUPS:])
    slabs_in = jnp.sum((clip_ids == own_clip).astype(jnp.float32))
    count = slabs_in * (
        values.shape[0]
        * values.shape[1]
        * lax.axis_size("space")
        * values.shape[2]
        * (width // GROUPS)
    )
    mean = clip_sum / count
    variance = clip_square / count - mean * mean
    return (mean, lax.rsqrt(variance + 1e-06))


def apply_norm(values, mean, scale, gain, shift):
    width = values.shape[3]
    grouped = values.reshape(values.shape[:3] + (GROUPS, width // GROUPS))
    normed = (grouped - mean[:, None]) * scale[:, None]
    normed = normed.reshape(values.shape) * gain + shift
    return jax.nn.silu(normed).astype(jnp.bfloat16)


def edge_rows(extended, margin):
    place = lax.axis_index("space")
    last = lax.axis_size("space") - 1
    rows = extended.shape[1]
    row_pos = jnp.arange(rows, dtype=jnp.int32)
    top_row = extended[:, margin : margin + 1]
    bottom_row = extended[:, rows - margin - 1 : rows - margin]
    upper = jnp.logical_and(place == 0, row_pos < margin)[None, :, None, None]
    lower = jnp.logical_and(place == last, row_pos >= rows - margin)[None, :, None, None]
    extended = jnp.where(upper, top_row, extended)
    return jnp.where(lower, bottom_row, extended)


def with_rims(frames):
    return edge_rows(padded_2(frames, (("space", 1),), 1), 1)


def causal_conv(extended, kernel):
    frames = extended.shape[0] - 2
    rows = extended.shape[1] - 2
    cols = extended.shape[2]
    width = extended.shape[3]
    padded = jnp.pad(extended, ((0, 0), (0, 0), (1, 1), (0, 0)), mode="edge")
    total = jnp.zeros((frames * rows * cols, kernel.shape[4]), jnp.float32)
    for tap_time in range(3):
        for tap_row in range(3):
            window = padded[tap_time : tap_time + frames, tap_row : tap_row + rows]
            stacked = jnp.concatenate(
                [window[:, :, offset : offset + cols] for offset in range(3)], axis=3
            )
            stacked = stacked.reshape(-1, 3 * width)
            total = total + jnp.dot(
                stacked,
                kernel[tap_time, tap_row].reshape(3 * width, -1),
                preferred_element_type=jnp.float32,
            )
    return total.reshape(frames, rows, cols, -1)


def repeat_first(act, count):
    return jnp.broadcast_to(act[0:1], (count,) + act.shape[1:])


def temporal_front(act, starting):
    earlier = passed_along(act[-2:], "tm", 1)
    front = jnp.where(starting, repeat_first(act, 2), earlier)
    return jnp.concatenate([front, act], axis=0)


def on_device(feats, clip_ids, gain_one, shift_one, kernel_one, gain_two, shift_two, kernel_two):
    own_slab = lax.axis_index("tm")
    own_clip = lax.dynamic_index_in_dim(clip_ids, own_slab, keepdims=False)
    before_clip = lax.dynamic_index_in_dim(clip_ids, jnp.maximum(own_slab - 1, 0), keepdims=False)
    starting = jnp.logical_or(own_slab == 0, own_clip != before_clip)
    inputs = feats.astype(jnp.float32)
    mean_one, scale_one = clip_stats(inputs, clip_ids)
    first = apply_norm(inputs, mean_one, scale_one, gain_one, shift_one)
    front_first = temporal_front(first, starting)
    hidden = causal_conv(with_rims(front_first), kernel_one).astype(jnp.bfloat16)
    hidden_float = hidden.astype(jnp.float32)
    mean_two, scale_two = clip_stats(hidden_float, clip_ids)
    second = apply_norm(hidden_float, mean_two, scale_two, gain_two, shift_two)
    extended = with_rims(temporal_front(second, starting))
    return inputs + causal_conv(extended, kernel_two)


def solution(mesh):
    return jax.shard_map(
        on_device,
        mesh=mesh,
        in_specs=(P("tm", "space", None, None), P(), P(), P(), P(), P(), P(), P()),
        out_specs=P("tm", "space", None, None),
        check_vma=False,
    )
```

```python
import jax
import jax.numpy as jnp
from jax import lax
from jax.sharding import PartitionSpec as P

GROUPS = 32


def padded_2(value, sides, width):
    for axis, dim in sides:
        peers, length = (lax.axis_size(axis), value.shape[dim])
        up = [(i, (i + 1) % peers) for i in range(peers - 1)]
        down = [(j, i) for i, j in up]
        last = lax.slice_in_dim(value, length - width, length, axis=dim)
        leading = lax.slice_in_dim(value, 0, width, axis=dim)
        before = lax.ppermute(last, axis, up)
        after = lax.ppermute(leading, axis, down)
        value = jnp.concatenate([before, value, after], axis=dim)
    return value


def passed_along(block, axis, distance):
    devices = range(lax.axis_size(axis))
    route = [(i - distance, i) for i in devices if i - distance in devices]
    return lax.ppermute(block, axis, route)


def clip_stats(values, clip_ids):
    width = values.shape[3]
    grouped = values.reshape(-1, GROUPS, width // GROUPS)
    local_sum = jnp.sum(grouped, axis=(0, 2))
    local_square = jnp.sum(grouped * grouped, axis=(0, 2))
    slab_count = lax.axis_size("tm")
    own_slab = lax.axis_index("tm")
    own_clip = lax.dynamic_index_in_dim(clip_ids, own_slab, keepdims=False)
    stats = jnp.concatenate([local_sum, local_square])
    parts = lax.all_gather(stats, ("tm", "space"))
    same_clip = (clip_ids == own_clip).astype(jnp.float32)
    totals = jnp.sum(parts.reshape(slab_count, -1, 2 * GROUPS) * same_clip[:, None, None], axis=(0, 1))
    clip_sum, clip_square = (totals[:GROUPS], totals[GROUPS:])
    slabs_in = jnp.sum((clip_ids == own_clip).astype(jnp.float32))
    count = slabs_in * (
        values.shape[0]
        * values.shape[1]
        * lax.axis_size("space")
        * values.shape[2]
        * (width // GROUPS)
    )
    mean = clip_sum / count
    variance = clip_square / count - mean * mean
    return (mean, lax.rsqrt(variance + 1e-06))


def apply_norm(values, mean, scale, gain, shift):
    width = values.shape[3]
    grouped = values.reshape(values.shape[:3] + (GROUPS, width // GROUPS))
    normed = (grouped - mean[:, None]) * scale[:, None]
    normed = normed.reshape(values.shape) * gain + shift
    return jax.nn.silu(normed).astype(jnp.bfloat16)


def edge_rows(extended, margin):
    place = lax.axis_index("space")
    last = lax.axis_size("space") - 1
    rows = extended.shape[1]
    row_pos = jnp.arange(rows, dtype=jnp.int32)
    top_row = extended[:, margin : margin + 1]
    bottom_row = extended[:, rows - margin - 1 : rows - margin]
    upper = jnp.logical_and(place == 0, row_pos < margin)[None, :, None, None]
    lower = jnp.logical_and(place == last, row_pos >= rows - margin)[None, :, None, None]
    extended = jnp.where(upper, top_row, extended)
    return jnp.where(lower, bottom_row, extended)


def with_rims(frames):
    return edge_rows(padded_2(frames, (("space", 1),), 1), 1)


def causal_conv(extended, kernel):
    frames = extended.shape[0] - 2
    rows = extended.shape[1] - 2
    cols = extended.shape[2]
    width = extended.shape[3]
    padded = jnp.pad(extended, ((0, 0), (0, 0), (1, 1), (0, 0)), mode="edge")
    total = jnp.zeros((frames * rows * cols, kernel.shape[4]), jnp.float32)
    for tap_time in range(3):
        for tap_row in range(3):
            window = padded[tap_time : tap_time + frames, tap_row : tap_row + rows]
            stacked = jnp.concatenate(
                [window[:, :, offset : offset + cols] for offset in range(3)], axis=3
            )
            stacked = stacked.reshape(-1, 3 * width)
            total = total + jnp.dot(
                stacked,
                kernel[tap_time, tap_row].reshape(3 * width, -1),
                preferred_element_type=jnp.float32,
            )
    return total.reshape(frames, rows, cols, -1)


def repeat_first(act, count):
    return jnp.broadcast_to(act[0:1], (count,) + act.shape[1:])


def temporal_front(act, starting):
    earlier = passed_along(act[-2:], "tm", 1)
    front = jnp.where(starting, repeat_first(act, 2), earlier)
    return jnp.concatenate([front, act], axis=0)


def on_device(feats, clip_ids, gain_one, shift_one, kernel_one, gain_two, shift_two, kernel_two):
    own_slab = lax.axis_index("tm")
    own_clip = lax.dynamic_index_in_dim(clip_ids, own_slab, keepdims=False)
    before_clip = lax.dynamic_index_in_dim(clip_ids, jnp.maximum(own_slab - 1, 0), keepdims=False)
    starting = jnp.logical_or(own_slab == 0, own_clip != before_clip)
    inputs = feats.astype(jnp.float32)
    mean_one, scale_one = clip_stats(inputs, clip_ids)
    first = apply_norm(inputs, mean_one, scale_one, gain_one, shift_one)
    front_first = temporal_front(first, starting)
    hidden = causal_conv(with_rims(front_first), kernel_one).astype(jnp.bfloat16)
    hidden_float = hidden.astype(jnp.float32)
    mean_two, scale_two = clip_stats(hidden_float, clip_ids)
    second = apply_norm(hidden_float, mean_two, scale_two, gain_two, shift_two)
    extended = with_rims(temporal_front(second, starting))
    return inputs + causal_conv(extended, kernel_two)


def solution(mesh):
    return jax.shard_map(
        on_device,
        mesh=mesh,
        in_specs=(P("tm", "space", None, None), P(), P(), P(), P(), P(), P(), P()),
        out_specs=P("tm", "space", None, None),
        check_vma=False,
    )
```

```python
import functools

import jax
import jax.numpy as jnp
from jax import lax
from jax.experimental import pallas as pl
from jax.experimental.pallas import tpu as pltpu
from jax.sharding import PartitionSpec as P

GROUPS = 32
AXES = ("tm", "space")


def is_power(number):
    return number & (number - 1) == 0


def traded(value, axis, mask):
    return lax.ppermute(value, axis, [(i, i ^ mask) for i in range(lax.axis_size(axis))])


def space_total(stats):
    peers = lax.axis_size("space")
    if not is_power(peers):
        return lax.psum(stats, "space")
    step = 1
    while step < peers:
        stats = stats + traded(stats, "space", step)
        step *= 2
    return stats


def slab_tables(stats):
    peers = lax.axis_size("tm")
    total = space_total(stats)[None]
    if not is_power(peers):
        return [lax.all_gather(total, "tm", tiled=True)]
    held = [total]
    step = 1
    while step < peers:
        ways = min(4, peers // step)
        block = held[0] if len(held) == 1 else jnp.concatenate(held, axis=0)
        held = [block] + [traded(block, "tm", step * way) for way in range(1, ways)]
        step *= ways
    return held


def slab_weights(clip_ids):
    slabs = jnp.arange(lax.axis_size("tm"), dtype=jnp.int32)
    own_slab = lax.axis_index("tm")
    own_clip = lax.dynamic_index_in_dim(clip_ids, own_slab, keepdims=False)
    order = slabs ^ own_slab if is_power(lax.axis_size("tm")) else slabs
    return (jnp.take(clip_ids, order) == own_clip).astype(jnp.float32)


def next_slab(value):
    peers = lax.axis_size("tm")
    return lax.ppermute(value, "tm", [(i, (i + 1) % peers) for i in range(peers)])


def halos(frames, edges):
    slabs, places = lax.axis_size("tm"), lax.axis_size("space")
    top, bottom = edges
    if places == 2:
        outer = jnp.where(lax.axis_index("space") == 0, bottom, top)
        rows = traded(outer, "space", 1)
        before = next_slab(frames[-2:])
        cross = [(t * 2 + s, (t + 1) % slabs * 2 + 1 - s) for t in range(slabs) for s in range(2)]
        corner = lax.ppermute(outer[-2:], AXES, cross)
        return [rows], before, [corner]
    above = lax.ppermute(bottom, "space", [(i, (i + 1) % places) for i in range(places)])
    below = lax.ppermute(top, "space", [(i, (i - 1) % places) for i in range(places)])
    before = next_slab(frames[-2:])
    return [above, below], before, [next_slab(above[-2:]), next_slab(below[-2:])]


def group_total(values):
    width = values.shape[-1]
    lane = lax.broadcasted_iota(jnp.int32, values.shape, 1)
    step = 1
    while step < width // GROUPS:
        upper = pltpu.roll(values, step, 1)
        lower = pltpu.roll(values, width - step, 1)
        values = values + jnp.where((lane & step) != 0, upper, lower)
        step *= 2
    return values


def conv_kernel(n_tables, n_sides, first, *refs):
    flags, weights = refs[:2]
    tables = refs[2 : 2 + n_tables]
    gain, shift, frames = refs[2 + n_tables : 5 + n_tables]
    rest = refs[5 + n_tables :]
    rows_halo, before, corners = rest[:n_sides], rest[n_sides], rest[n_sides + 1 : 2 * n_sides + 1]
    rest = rest[2 * n_sides + 1 :]
    if first:
        kernel_hbm, hidden, stats, act, taps, sems = rest
    else:
        kernel_hbm, feats, out, act, taps, sems = rest
    n_frames, n_rows, cols, width = frames.shape
    copies = [pltpu.make_async_copy(kernel_hbm.at[i], taps.at[i], sems.at[i]) for i in range(3)]
    for copy in copies:
        copy.start()

    total = jnp.zeros((2, width), jnp.float32)
    entry = 0
    slabs_in = 0.0
    for table in tables:
        for i in range(table.shape[0]):
            total = total + table[i] * weights[entry]
            slabs_in = slabs_in + weights[entry]
            entry += 1
    grouped = group_total(total)
    count = slabs_in * weights[entry]
    mean = grouped[0:1] / count
    variance = grouped[1:2] / count - mean * mean
    scale = lax.rsqrt(variance + 1e-06) * gain[...]
    half_scale = 0.5 * scale
    half_shift = 0.5 * (shift[...] - mean * scale)

    starting = flags[0] != 0
    edge = (flags[1] != 0, flags[2] != 0)

    def put(frame, row, raw):
        half = raw.astype(jnp.float32) * half_scale + half_shift
        act[frame, row] = (half * jnp.tanh(half) + half).astype(jnp.bfloat16)

    def normed(frame):
        for row in range(n_rows + 2):
            side = 0 if row == 0 else n_sides - 1
            inner = min(max(row - 1, 0), n_rows - 1)
            outside = row in (0, n_rows + 1)
            if frame < 2:
                raw = before[frame, inner]
                own = frames[0, inner]
                if outside:
                    at_edge = edge[0 if row == 0 else 1]
                    raw = jnp.where(at_edge, raw, corners[side][frame, 0])
                    own = jnp.where(at_edge, own, rows_halo[side][0, 0])
                raw = jnp.where(starting, own, raw)
            else:
                raw = frames[frame - 2, inner]
                if outside:
                    raw = jnp.where(edge[0 if row == 0 else 1], raw, rows_halo[side][frame - 2, 0])
            put(frame, row, raw)

    column = lax.broadcasted_iota(jnp.int32, (cols, width), 0)

    def conv(frame):
        lhs = jnp.concatenate(
            [
                act[frame + i, j : j + n_rows].reshape(n_rows * cols, width)
                for i in range(3)
                for j in range(3)
            ],
            axis=1,
        )
        sums = []
        for l in range(3):
            rhs = jnp.concatenate([taps[i, j, l] for i in range(3) for j in range(3)], axis=0)
            sums.append(jnp.dot(lhs, rhs, preferred_element_type=jnp.float32))
        done = []
        for row in range(n_rows):
            left, mid, right = (s[row * cols : (row + 1) * cols] for s in sums)
            left = jnp.where(column == 0, left, pltpu.roll(left, 1, 0))
            right = jnp.where(column == cols - 1, right, pltpu.roll(right, cols - 1, 0))
            done.append(left + mid + right)
        return done

    for frame in range(3):
        normed(frame)
    for copy in copies:
        copy.wait()
    if first:
        part_sum = jnp.zeros((8, width), jnp.float32)
        part_square = jnp.zeros((8, width), jnp.float32)
    for frame in range(n_frames):
        for row, value in enumerate(conv(frame)):
            if first:
                rounded = value.astype(jnp.bfloat16)
                hidden[frame, row] = rounded
                again = rounded.astype(jnp.float32)
                part_sum = part_sum + jnp.sum(again.reshape(-1, 8, width), axis=0)
                part_square = part_square + jnp.sum((again * again).reshape(-1, 8, width), axis=0)
            else:
                out[frame, row] = feats[frame, row].astype(jnp.float32) + value
        if frame + 3 < n_frames + 2:
            normed(frame + 3)
    if first:
        stats[0:1] = jnp.sum(part_sum, axis=0, keepdims=True)
        stats[1:2] = jnp.sum(part_square, axis=0, keepdims=True)


def conv_call(first, flags, weights, tables, gain, shift, frames, halo, kernel, feats=None):
    rows_halo, before, corners = halo
    n_frames, n_rows, cols, width = frames.shape
    smem, vmem, anywhere = (pl.BlockSpec(memory_space=m) for m in (pltpu.SMEM, pltpu.VMEM, pl.ANY))
    operands = [*tables, gain[None], shift[None], frames, *rows_halo, before, *corners]
    in_specs = [smem, smem] + [vmem] * len(operands) + [anywhere]
    operands = [flags, weights, *operands, kernel]
    if first:
        out_shape = (
            jax.ShapeDtypeStruct(frames.shape, jnp.bfloat16),
            jax.ShapeDtypeStruct((2, width), jnp.float32),
        )
        out_specs = (vmem, vmem)
    else:
        operands.append(feats)
        in_specs.append(vmem)
        out_shape = jax.ShapeDtypeStruct(frames.shape, jnp.float32)
        out_specs = vmem
    return pl.pallas_call(
        functools.partial(conv_kernel, len(tables), len(rows_halo), first),
        out_shape=out_shape,
        in_specs=in_specs,
        out_specs=out_specs,
        scratch_shapes=[
            pltpu.VMEM((n_frames + 2, n_rows + 2, cols, width), jnp.bfloat16),
            pltpu.VMEM(kernel.shape, jnp.bfloat16),
            pltpu.SemaphoreType.DMA((3,)),
        ],
        compiler_params=pltpu.CompilerParams(vmem_limit_bytes=40 << 20),
        cost_estimate=pl.CostEstimate(
            flops=2 * frames.size * width * 27, bytes_accessed=kernel.size * 2 + frames.size * 8, transcendentals=frames.size * 2
        ),
    )(*operands)


def edge_rows(frames):
    return frames[:, :1], frames[:, -1:]


def on_device(feats, clip_ids, gain_one, shift_one, kernel_one, gain_two, shift_two, kernel_two):
    own_slab = lax.axis_index("tm")
    place, places = lax.axis_index("space"), lax.axis_size("space")
    own_clip = lax.dynamic_index_in_dim(clip_ids, own_slab, keepdims=False)
    before_clip = lax.dynamic_index_in_dim(clip_ids, jnp.maximum(own_slab - 1, 0), keepdims=False)
    starting = jnp.logical_or(own_slab == 0, own_clip != before_clip)
    flags = jnp.stack([starting, place == 0, place == places - 1]).astype(jnp.int32)
    per_slab = feats.size // GROUPS * places
    weights = jnp.concatenate([slab_weights(clip_ids), jnp.full((1,), per_slab, jnp.float32)])

    halo = halos(feats, edge_rows(feats))
    inputs = feats.astype(jnp.float32)
    stats = jnp.stack([jnp.sum(inputs, axis=(0, 1, 2)), jnp.sum(inputs * inputs, axis=(0, 1, 2))])
    hidden, stats = conv_call(True, flags, weights, slab_tables(stats), gain_one, shift_one, feats, halo, kernel_one)
    halo = halos(hidden, edge_rows(hidden))
    return conv_call(False, flags, weights, slab_tables(stats), gain_two, shift_two, hidden, halo, kernel_two, feats)


def solution(mesh):
    return jax.shard_map(
        on_device,
        mesh=mesh,
        in_specs=(P("tm", "space", None, None), P(), P(), P(), P(), P(), P(), P()),
        out_specs=P("tm", "space", None, None),
        check_vma=False,
    )
```

```python
import functools

import jax
import jax.numpy as jnp
from jax import lax
from jax.experimental import pallas as pl
from jax.experimental.pallas import tpu as pltpu
from jax.sharding import PartitionSpec as P

GROUPS = 32
AXES = ("tm", "space")


def is_power(number):
    return number & (number - 1) == 0


def traded(value, axis, mask):
    return lax.ppermute(value, axis, [(i, i ^ mask) for i in range(lax.axis_size(axis))])


def space_total(stats):
    peers = lax.axis_size("space")
    if not is_power(peers):
        return lax.psum(stats, "space")
    step = 1
    while step < peers:
        stats = stats + traded(stats, "space", step)
        step *= 2
    return stats


def slab_tables(stats):
    peers = lax.axis_size("tm")
    total = space_total(stats)[None]
    if not is_power(peers):
        return [lax.all_gather(total, "tm", tiled=True)], None
    held, offsets = [total], [0]
    left = peers
    while left > 1:
        ways = min(4, left)
        left //= ways
        block = held[0] if len(held) == 1 else jnp.concatenate(held, axis=0)
        held = [block] + [traded(block, "tm", left * way) for way in range(1, ways)]
        offsets = [(left * way) ^ offset for way in range(ways) for offset in offsets]
    return held, tuple(offsets)


def next_slab(value):
    peers = lax.axis_size("tm")
    return lax.ppermute(value, "tm", [(i, (i + 1) % peers) for i in range(peers)])


def halos(frames, edges):
    slabs, places = lax.axis_size("tm"), lax.axis_size("space")
    if places == 2:
        (outer,) = edges
        before = next_slab(frames[-2:])
        rows = traded(outer, "space", 1)
        cross = [(t * 2 + s, (t + 1) % slabs * 2 + 1 - s) for t in range(slabs) for s in range(2)]
        corner = lax.ppermute(outer[-2:], AXES, cross)
        return [rows], before, [corner]
    top, bottom = edges
    above = lax.ppermute(bottom, "space", [(i, (i + 1) % places) for i in range(places)])
    below = lax.ppermute(top, "space", [(i, (i - 1) % places) for i in range(places)])
    before = next_slab(frames[-2:])
    return [above, below], before, [next_slab(above[-2:]), next_slab(below[-2:])]


def group_total(values):
    width = values.shape[-1]
    lane = lax.broadcasted_iota(jnp.int32, values.shape, 1)
    step = 1
    while step < width // GROUPS:
        upper = pltpu.roll(values, step, 1)
        lower = pltpu.roll(values, width - step, 1)
        values = values + jnp.where((lane & step) != 0, upper, lower)
        step *= 2
    return values


def sent_rows(frames, frame, places, edges):
    n_rows = frames.shape[1]
    if places == 2:
        low = lax.axis_index("space") == 0
        edges[0][frame, 0] = jnp.where(low, frames[frame, n_rows - 1], frames[frame, 0])
    else:
        edges[0][frame, 0] = frames[frame, 0]
        edges[1][frame, 0] = frames[frame, n_rows - 1]


def stats_kernel(places, frames_hbm, stats, *rest):
    edges, (frames, sems) = rest[:-2], rest[-2:]
    n_frames, n_rows, _, width = frames.shape
    copies = [pltpu.make_async_copy(frames_hbm.at[f], frames.at[f], sems.at[f]) for f in range(n_frames)]
    for copy in copies:
        copy.start()
    part_sum = jnp.zeros((8, width), jnp.float32)
    part_square = jnp.zeros((8, width), jnp.float32)
    for frame in range(n_frames):
        copies[frame].wait()
        for row in range(n_rows):
            values = frames[frame, row].astype(jnp.float32)
            part_sum = part_sum + jnp.sum(values.reshape(-1, 8, width), axis=0)
            part_square = part_square + jnp.sum((values * values).reshape(-1, 8, width), axis=0)
        sent_rows(frames, frame, places, edges)
    stats[0:1] = jnp.sum(part_sum, axis=0, keepdims=True)
    stats[1:2] = jnp.sum(part_square, axis=0, keepdims=True)


def edge_shapes(frames, places):
    shape = (frames.shape[0], 1) + frames.shape[2:]
    return (jax.ShapeDtypeStruct(shape, jnp.bfloat16),) * (1 if places == 2 else 2)


def stats_call(frames):
    places = lax.axis_size("space")
    edges = edge_shapes(frames, places)
    vmem = pl.BlockSpec(memory_space=pltpu.VMEM)
    stats, *edges = pl.pallas_call(
        functools.partial(stats_kernel, places),
        out_shape=(jax.ShapeDtypeStruct((2, frames.shape[3]), jnp.float32),) + edges,
        in_specs=[pl.BlockSpec(memory_space=pl.ANY)],
        out_specs=(vmem,) * (1 + len(edges)),
        scratch_shapes=[pltpu.VMEM(frames.shape, jnp.bfloat16), pltpu.SemaphoreType.DMA((frames.shape[0],))],
        compiler_params=pltpu.CompilerParams(vmem_limit_bytes=8 << 20),
        cost_estimate=pl.CostEstimate(flops=4 * frames.size, bytes_accessed=2 * frames.size, transcendentals=0),
    )(frames)
    return stats, edges


def conv_kernel(n_tables, n_sides, offsets, first, *refs):
    clip_ids = refs[0]
    tables = refs[1 : 1 + n_tables]
    gain, shift, frames = refs[1 + n_tables : 4 + n_tables]
    rest = refs[4 + n_tables :]
    rows_halo, before, corners = rest[:n_sides], rest[n_sides], rest[n_sides + 1 : 2 * n_sides + 1]
    rest = rest[2 * n_sides + 1 :]
    if first:
        kernel_hbm, hidden, stats = rest[:3]
        edges, (act, taps, sems) = rest[3:-3], rest[-3:]
    else:
        kernel_hbm, feats, out, act, taps, sems = rest
    n_frames, n_rows, cols, width = frames.shape
    copies = [pltpu.make_async_copy(kernel_hbm.at[i], taps.at[i], sems.at[i]) for i in range(3)]
    for copy in copies:
        copy.start()

    own_slab = lax.axis_index("tm")
    place, places = lax.axis_index("space"), lax.axis_size("space")
    own_clip = clip_ids[own_slab]
    entries = [(table, i) for table in tables for i in range(table.shape[0])]
    total = jnp.zeros((2, width), jnp.float32)
    slabs_in = jnp.int32(0)
    for entry, (table, i) in enumerate(entries):
        slab = entry if offsets is None else own_slab ^ offsets[entry]
        same = clip_ids[slab] == own_clip
        total = jnp.where(same, total + table[i], total)
        slabs_in = slabs_in + same.astype(jnp.int32)
    grouped = group_total(total)
    count = slabs_in.astype(jnp.float32) * float(n_frames * n_rows * cols * width // GROUPS * places)
    mean = grouped[0:1] / count
    variance = grouped[1:2] / count - mean * mean
    scale = lax.rsqrt(variance + 1e-06) * gain[...]
    half_scale = 0.5 * scale
    half_shift = 0.5 * (shift[...] - mean * scale)

    starting = jnp.logical_or(own_slab == 0, clip_ids[jnp.maximum(own_slab - 1, 0)] != own_clip)
    edge = (place == 0, place == places - 1)

    def put(frame, row, raw):
        half = raw.astype(jnp.float32) * half_scale + half_shift
        act[frame, row] = (half * jnp.tanh(half) + half).astype(jnp.bfloat16)

    def normed(frame):
        for row in range(n_rows + 2):
            side = 0 if row == 0 else n_sides - 1
            inner = min(max(row - 1, 0), n_rows - 1)
            outside = row in (0, n_rows + 1)
            if frame < 2:
                raw = before[frame, inner]
                own = frames[0, inner]
                if outside:
                    at_edge = edge[0 if row == 0 else 1]
                    raw = jnp.where(at_edge, raw, corners[side][frame, 0])
                    own = jnp.where(at_edge, own, rows_halo[side][0, 0])
                raw = jnp.where(starting, own, raw)
            else:
                raw = frames[frame - 2, inner]
                if outside:
                    raw = jnp.where(edge[0 if row == 0 else 1], raw, rows_halo[side][frame - 2, 0])
            put(frame, row, raw)

    column = lax.broadcasted_iota(jnp.int32, (cols, width), 0)

    def conv(frame):
        lhs = jnp.concatenate(
            [
                act[frame + i, j : j + n_rows].reshape(n_rows * cols, width)
                for i in range(3)
                for j in range(3)
            ],
            axis=1,
        )
        sums = []
        for l in range(3):
            rhs = jnp.concatenate([taps[i, j, l] for i in range(3) for j in range(3)], axis=0)
            sums.append(jnp.dot(lhs, rhs, preferred_element_type=jnp.float32))
        done = []
        for row in range(n_rows):
            left, mid, right = (s[row * cols : (row + 1) * cols] for s in sums)
            left = jnp.where(column == 0, left, pltpu.roll(left, 1, 0))
            right = jnp.where(column == cols - 1, right, pltpu.roll(right, cols - 1, 0))
            done.append(left + mid + right)
        return done

    for frame in range(3):
        normed(frame)
    for copy in copies:
        copy.wait()
    if first:
        part_sum = jnp.zeros((8, width), jnp.float32)
        part_square = jnp.zeros((8, width), jnp.float32)
    for frame in range(n_frames):
        for row, value in enumerate(conv(frame)):
            if first:
                rounded = value.astype(jnp.bfloat16)
                hidden[frame, row] = rounded
                again = rounded.astype(jnp.float32)
                part_sum = part_sum + jnp.sum(again.reshape(-1, 8, width), axis=0)
                part_square = part_square + jnp.sum((again * again).reshape(-1, 8, width), axis=0)
            else:
                out[frame, row] = feats[frame, row].astype(jnp.float32) + value
        if first:
            sent_rows(hidden, frame, places, edges)
        if frame + 3 < n_frames + 2:
            normed(frame + 3)
    if first:
        stats[0:1] = jnp.sum(part_sum, axis=0, keepdims=True)
        stats[1:2] = jnp.sum(part_square, axis=0, keepdims=True)


def conv_call(first, clip_ids, tables, gain, shift, frames, halo, kernel, feats=None):
    tables, offsets = tables
    rows_halo, before, corners = halo
    n_frames, n_rows, cols, width = frames.shape
    smem, vmem, hbm = (pl.BlockSpec(memory_space=m) for m in (pltpu.SMEM, pltpu.VMEM, pltpu.HBM))
    operands = [*tables, gain[None], shift[None], frames, *rows_halo, before, *corners]
    in_specs = [smem] + [vmem] * len(operands) + [hbm]
    operands = [clip_ids, *operands, kernel]
    if first:
        edges = edge_shapes(frames, lax.axis_size("space"))
        out_shape = (
            jax.ShapeDtypeStruct(frames.shape, jnp.bfloat16),
            jax.ShapeDtypeStruct((2, width), jnp.float32),
        ) + edges
        out_specs = (vmem,) * len(out_shape)
    else:
        operands.append(feats)
        in_specs.append(vmem)
        out_shape = jax.ShapeDtypeStruct(frames.shape, jnp.float32)
        out_specs = vmem
    return pl.pallas_call(
        functools.partial(conv_kernel, len(tables), len(rows_halo), offsets, first),
        out_shape=out_shape,
        in_specs=in_specs,
        out_specs=out_specs,
        scratch_shapes=[
            pltpu.VMEM((n_frames + 2, n_rows + 2, cols, width), jnp.bfloat16),
            pltpu.VMEM(kernel.shape, jnp.bfloat16),
            pltpu.SemaphoreType.DMA((3,)),
        ],
        compiler_params=pltpu.CompilerParams(vmem_limit_bytes=40 << 20),
        cost_estimate=pl.CostEstimate(
            flops=2 * frames.size * width * 27, bytes_accessed=kernel.size * 2 + frames.size * 8, transcendentals=frames.size * 2
        ),
    )(*operands)


def on_device(feats, clip_ids, gain_one, shift_one, kernel_one, gain_two, shift_two, kernel_two):
    stats, edges = stats_call(feats)
    halo = halos(feats, edges)
    hidden, stats, *edges = conv_call(True, clip_ids, slab_tables(stats), gain_one, shift_one, feats, halo, kernel_one)
    halo = halos(hidden, edges)
    return conv_call(False, clip_ids, slab_tables(stats), gain_two, shift_two, hidden, halo, kernel_two, feats)


def solution(mesh):
    return jax.shard_map(
        on_device,
        mesh=mesh,
        in_specs=(P("tm", "space", None, None), P(), P(), P(), P(), P(), P(), P()),
        out_specs=P("tm", "space", None, None),
        check_vma=False,
    )
```

```python
import functools

import jax
import jax.numpy as jnp
from jax import lax
from jax.experimental import pallas as pl
from jax.experimental.pallas import tpu as pltpu
from jax.sharding import PartitionSpec as P

GROUPS = 32
TAIL = 2
F32, BF16 = jnp.float32, jnp.bfloat16


def vmem_params():
    return pltpu.CompilerParams(vmem_limit_bytes=32 << 20)


def shaped(shape, dtype=BF16):
    return jax.ShapeDtypeStruct(tuple(shape), dtype)


def in_hbm(value):
    return pltpu.with_memory_space_constraint(value, pltpu.HBM)


VMEM = pl.BlockSpec(memory_space=pltpu.VMEM)
ANYWHERE = pl.BlockSpec(memory_space=pl.ANY)


def traded(value, axis, mask):
    return lax.ppermute(value, axis, [(i, i ^ mask) for i in range(lax.axis_size(axis))])


def shifted(value, axis, step):
    peers = lax.axis_size(axis)
    return lax.ppermute(value, axis, [(i, (i + step) % peers) for i in range(peers)])


def slab_table(stats):
    slabs, places = lax.axis_size("tm"), lax.axis_size("space")
    total = stats + traded(stats, "space", 1) if places == 2 else lax.psum(stats, "space")
    copies = jnp.broadcast_to(total, (slabs, total.shape[1]))
    return total, lax.all_to_all(copies, "tm", 0, 0, tiled=True)


def row_halo(edges):
    if lax.axis_size("space") == 2:
        return [traded(edges[0], "space", 1)]
    top, bottom = edges
    return [shifted(bottom, "space", 1), shifted(top, "space", -1)]


def edges_of(frames):
    rows = frames.shape[1]
    if lax.axis_size("space") == 2:
        return [lax.dynamic_slice_in_dim(frames, (rows - 1) * (1 - lax.axis_index("space")), 1, axis=1)]
    return [frames[:, :1], frames[:, rows - 1 :]]


def slab_halo(tail, after=None):
    before = shifted(tail, "tm", 1)
    if after is not None:
        before, after = lax.optimization_barrier((before, after))
    return before, row_halo(edges_of(before)), after


def edge_shapes(frames, count):
    shape = (count, 1) + frames.shape[2:]
    return [shaped(shape)] * (1 if lax.axis_size("space") == 2 else 2)


def send_rows(source, frame, edges):
    rows = source.shape[1]
    if len(edges) == 1:
        edges[0][frame, 0] = jnp.where(lax.axis_index("space") == 0, source[frame, rows - 1], source[frame, 0])
    else:
        edges[0][frame, 0] = source[frame, 0]
        edges[1][frame, 0] = source[frame, rows - 1]


def add_stats(sums, values):
    width = values.shape[1]
    return (
        sums[0] + jnp.sum(values.reshape(-1, 8, width), axis=0),
        sums[1] + jnp.sum((values * values).reshape(-1, 8, width), axis=0),
    )


def no_stats(width):
    return jnp.zeros((8, width), F32), jnp.zeros((8, width), F32)


def store_stats(stats, sums, base=None):
    width = sums[0].shape[1]
    for k in range(2):
        part = jnp.sum(sums[k], axis=0, keepdims=True)
        stats[:, k * width : (k + 1) * width] = part if base is None else part + base[:, k * width : (k + 1) * width]


def entry_kernel(slabs, *refs):
    feats_hbm, clips_hbm = refs[:2]
    params_hbm = refs[2:6]
    frames, tail, stats, aux = refs[6:10]
    edges = refs[10:-4]
    params, clips, sems, frame_sems = refs[-4:]
    n_frames, n_rows, cols, width = frames.shape
    loads = [pltpu.make_async_copy(feats_hbm.at[f], frames.at[f], frame_sems.at[f]) for f in range(n_frames)]
    clip_load = pltpu.make_async_copy(clips_hbm, clips, sems.at[0])
    tail_load = pltpu.make_async_copy(feats_hbm.at[pl.ds(n_frames - TAIL, TAIL)], tail, sems.at[1])
    param_loads = [pltpu.make_async_copy(p, params.at[k], sems.at[2 + k]) for k, p in enumerate(params_hbm)]
    for copy in [*loads, clip_load, tail_load, *param_loads]:
        copy.start()
    sums = no_stats(width)
    for frame in range(n_frames):
        loads[frame].wait()
        for row in range(n_rows):
            sums = add_stats(sums, frames[frame, row].astype(F32))
        send_rows(frames, frame, edges)
    store_stats(stats, sums)
    clip_load.wait()
    own = lax.axis_index("tm")
    own_clip = clips[own]
    slabs_in = jnp.int32(0)
    for slab in range(slabs):
        same = (clips[slab] == own_clip).astype(jnp.int32)
        slabs_in = slabs_in + same
        aux[slab : slab + 1] = jnp.full((1, width), same.astype(F32), F32)
    starting = jnp.logical_or(own == 0, clips[jnp.maximum(own - 1, 0)] != own_clip)
    aux[slabs : slabs + 1] = jnp.full((1, width), starting.astype(F32), F32)
    per_slab = n_frames * n_rows * cols * width // GROUPS * lax.axis_size("space")
    aux[slabs + 1 : slabs + 2] = jnp.full((1, width), slabs_in.astype(F32) * float(per_slab), F32)
    for k, copy in enumerate(param_loads):
        copy.wait()
        aux[slabs + 2 + k : slabs + 3 + k] = params[k]
    tail_load.wait()


def entry_call(feats, clip_ids, params):
    slabs = lax.axis_size("tm")
    n_frames, width = feats.shape[0], feats.shape[3]
    outs = [shaped(feats.shape), shaped((TAIL,) + feats.shape[1:]), shaped((1, 2 * width), F32), shaped((slabs + 8, width), F32)]
    outs += edge_shapes(feats, n_frames)
    frames, tail, stats, aux, *edges = pl.pallas_call(
        functools.partial(entry_kernel, slabs),
        out_shape=outs,
        in_specs=[ANYWHERE] * 6,
        out_specs=[VMEM] * len(outs),
        scratch_shapes=[
            pltpu.VMEM((4, 1, width), F32),
            pltpu.SMEM(clip_ids.shape, jnp.int32),
            pltpu.SemaphoreType.DMA((6,)),
            pltpu.SemaphoreType.DMA((n_frames,)),
        ],
        compiler_params=vmem_params(),
        cost_estimate=pl.CostEstimate(flops=4 * feats.size, bytes_accessed=4 * feats.size, transcendentals=0),
    )(*[in_hbm(x) for x in (feats, clip_ids, *[p[None] for p in params])])
    return frames, tail, stats, aux, edges


def load_kernel(kernel_hbm, after, taps, sem):
    copy = pltpu.make_async_copy(kernel_hbm, taps, sem)
    copy.start()
    copy.wait()


def load_call(kernel, after):
    return pl.pallas_call(
        load_kernel,
        out_shape=shaped(kernel.shape),
        in_specs=[ANYWHERE, ANYWHERE],
        out_specs=VMEM,
        scratch_shapes=[pltpu.SemaphoreType.DMA],
        compiler_params=vmem_params(),
        cost_estimate=pl.CostEstimate(flops=0, bytes_accessed=4 * kernel.size, transcendentals=0),
    )(in_hbm(kernel), after)


def group_total(values):
    width = values.shape[-1]
    lane = lax.broadcasted_iota(jnp.int32, values.shape, 1)
    step = 1
    while step < width // GROUPS:
        upper = pltpu.roll(values, step, 1)
        lower = pltpu.roll(values, width - step, 1)
        values = values + jnp.where((lane & step) != 0, upper, lower)
        step *= 2
    return values


def half_affine(table, aux, which):
    slabs = table.shape[0]
    width = aux.shape[1]
    mask = aux[:slabs]
    sums = [jnp.sum(table[:, k * width : (k + 1) * width] * mask, axis=0, keepdims=True) for k in range(2)]
    grouped = group_total(jnp.concatenate(sums, axis=0))
    count = aux[slabs + 1 : slabs + 2]
    gain = aux[slabs + 2 + 2 * which : slabs + 3 + 2 * which]
    shift = aux[slabs + 3 + 2 * which : slabs + 4 + 2 * which]
    mean = grouped[0:1] / count
    variance = grouped[1:2] / count - mean * mean
    scale = lax.rsqrt(variance + 1e-06) * gain
    return 0.5 * scale, 0.5 * (shift - mean * scale)


def normed(raw, affine):
    half = raw.astype(F32) * affine[0] + affine[1]
    return (half * jnp.tanh(half) + half).astype(BF16)


def extended_row(frames, sides, frame, row):
    n_rows = frames.shape[1]
    inner = frames[frame, min(max(row - 1, 0), n_rows - 1)]
    if 0 < row <= n_rows:
        return inner
    place, places = lax.axis_index("space"), lax.axis_size("space")
    side = sides[0 if row == 0 else -1]
    return jnp.where(place == (0 if row == 0 else places - 1), inner, side[frame, 0])


def conv_rows(planes, taps):
    ref, index = planes[0]
    n_rows, cols, width = ref.shape[1] - 2, ref.shape[2], ref.shape[3]
    lhs = jnp.concatenate(
        [ref[index, j : j + n_rows].reshape(n_rows * cols, width) for ref, index in planes for j in range(3)], axis=1
    )
    column = lax.broadcasted_iota(jnp.int32, (cols, width), 0)
    sums = []
    for l in range(3):
        rhs = jnp.concatenate([taps[i, j, l] for i in range(3) for j in range(3)], axis=0)
        sums.append(jnp.dot(lhs, rhs, preferred_element_type=F32))
    for row in range(n_rows):
        left, mid, right = (s[row * cols : (row + 1) * cols] for s in sums)
        left = jnp.where(column == 0, left, pltpu.roll(left, 1, 0))
        right = jnp.where(column == cols - 1, right, pltpu.roll(right, cols - 1, 0))
        yield row, left + mid + right


def put_hidden(hidden, frame, row, value, sums):
    rounded = value.astype(BF16)
    hidden[frame, row] = rounded
    return add_stats(sums, rounded.astype(F32))


def late_kernel(n_sides, aux, table, frames, *refs):
    sides, taps = refs[:n_sides], refs[n_sides]
    hidden, act_low, stats, affine_out, *edges, act_high = refs[n_sides + 1 :]
    n_frames = frames.shape[0]
    low = act_low.shape[0]
    affine = half_affine(table, aux, 0)
    for k in range(2):
        affine_out[k : k + 1] = affine[k]
    planes = [(act_low, f) for f in range(low)] + [(act_high, f) for f in range(n_frames - low)]
    for frame, (act, index) in enumerate(planes):
        for row in range(frames.shape[1] + 2):
            act[index, row] = normed(extended_row(frames, sides, frame, row), affine)
    sums = no_stats(frames.shape[3])
    for frame in range(n_frames - 2):
        for row, value in conv_rows(planes[frame : frame + 3], taps):
            sums = put_hidden(hidden, frame, row, value, sums)
        send_rows(hidden, frame, edges)
    store_stats(stats, sums)


def early_kernel(n_sides, aux, before, *refs):
    corners, (act_low, affine_in, stats_in, taps) = refs[:n_sides], refs[n_sides : n_sides + 4]
    hidden, stats, *edges, act_before = refs[n_sides + 4 :]
    slabs = aux.shape[0] - 8
    starting = aux[slabs : slabs + 1] != 0.0
    affine = affine_in[0:1], affine_in[1:2]
    for frame in range(2):
        for row in range(before.shape[1] + 2):
            value = normed(extended_row(before, corners, frame, row), affine).astype(F32)
            act_before[frame, row] = jnp.where(starting, act_low[0, row].astype(F32), value).astype(BF16)
    planes = [(act_before, 0), (act_before, 1)] + [(act_low, f) for f in range(act_low.shape[0])]
    sums = no_stats(before.shape[3])
    for frame in range(2):
        for row, value in conv_rows(planes[frame : frame + 3], taps):
            sums = put_hidden(hidden, frame, row, value, sums)
        send_rows(hidden, frame, edges)
    store_stats(stats, sums, stats_in)


def last_kernel(n_sides, aux, table, early, late, *refs):
    sides_early, sides_late = refs[:n_sides], refs[n_sides : 2 * n_sides]
    before, *corners = refs[2 * n_sides : 3 * n_sides + 1]
    taps, feats, out, act = refs[3 * n_sides + 1 :]
    slabs = aux.shape[0] - 8
    starting = aux[slabs : slabs + 1] != 0.0
    affine = half_affine(table, aux, 1)
    n_frames, n_rows = out.shape[:2]

    def fill(frame):
        for row in range(n_rows + 2):
            if frame < 2:
                value = normed(extended_row(before, corners, frame, row), affine).astype(F32)
                act[frame, row] = jnp.where(starting, act[2, row].astype(F32), value).astype(BF16)
            elif frame < 4:
                act[frame, row] = normed(extended_row(early, sides_early, frame - 2, row), affine)
            else:
                act[frame, row] = normed(extended_row(late, sides_late, frame - 4, row), affine)

    for frame in range(2, n_frames + 2):
        fill(frame)
    for frame in list(range(2, n_frames)) + [0, 1]:
        if frame < 2:
            fill(frame)
        if frame == 0:
            fill(1)
        for row, value in conv_rows([(act, frame + i) for i in range(3)], taps):
            out[frame, row] = feats[frame, row].astype(F32) + value


def call(kernel, outs, scratch, frames, *operands):
    return pl.pallas_call(
        kernel,
        out_shape=outs,
        in_specs=[VMEM] * len(operands),
        out_specs=[VMEM] * len(outs) if isinstance(outs, list) else VMEM,
        scratch_shapes=scratch,
        compiler_params=vmem_params(),
        cost_estimate=pl.CostEstimate(flops=54 * frames * 384 * 65536, bytes_accessed=1 << 20, transcendentals=1 << 20),
    )(*operands)


def on_device(feats, clip_ids, gain_one, shift_one, kernel_one, gain_two, shift_two, kernel_two):
    n_frames, n_rows, cols, width = feats.shape
    frames, tail, stats, aux, edges = entry_call(feats, clip_ids, (gain_one, shift_one, gain_two, shift_two))
    before, corners, _ = slab_halo(tail)
    total, table = slab_table(stats)
    sides = row_halo(edges)
    taps = load_call(kernel_one, total)
    n_sides = len(sides)
    plane = (n_rows + 2, cols, width)
    late = n_frames - 2
    hidden_late, act_low, stats, affine, *edges = call(
        functools.partial(late_kernel, n_sides),
        [shaped((late, n_rows, cols, width)), shaped((2,) + plane), shaped((1, 2 * width), F32), shaped((2, width), F32)]
        + edge_shapes(feats, late),
        [pltpu.VMEM((late,) + plane, BF16)],
        late, aux, table, frames, *sides, taps,
    )
    sides_late = row_halo(edges)
    hidden_early, stats, *edges = call(
        functools.partial(early_kernel, n_sides),
        [shaped((2, n_rows, cols, width)), shaped((1, 2 * width), F32)] + edge_shapes(feats, 2),
        [pltpu.VMEM((2,) + plane, BF16)],
        2, aux, before, *corners, act_low, affine, stats, taps,
    )
    sides_early = row_halo(edges)
    total, table = slab_table(stats)
    before, corners, table = slab_halo(hidden_late[late - 2 :], table)
    taps = load_call(kernel_two, total)
    return call(
        functools.partial(last_kernel, n_sides),
        shaped(feats.shape, F32),
        [pltpu.VMEM((n_frames + 2,) + plane, BF16)],
        n_frames, aux, table, hidden_early, hidden_late, *sides_early, *sides_late, before, *corners, taps, frames,
    )


def solution(mesh):
    return jax.shard_map(
        on_device,
        mesh=mesh,
        in_specs=(P("tm", "space", None, None), P(), P(), P(), P(), P(), P(), P()),
        out_specs=P("tm", "space", None, None),
        check_vma=False,
    )
```

```python
import functools

import jax
import jax.numpy as jnp
from jax import lax
from jax.experimental import pallas as pl
from jax.experimental.pallas import tpu as pltpu
from jax.sharding import PartitionSpec as P

GROUPS = 32
TAIL = 2
F32, BF16 = jnp.float32, jnp.bfloat16


def vmem_params():
    return pltpu.CompilerParams(vmem_limit_bytes=32 << 20)


def shaped(shape, dtype=BF16):
    return jax.ShapeDtypeStruct(tuple(shape), dtype)


def in_hbm(value):
    return pltpu.with_memory_space_constraint(value, pltpu.HBM)


VMEM = pl.BlockSpec(memory_space=pltpu.VMEM)
ANYWHERE = pl.BlockSpec(memory_space=pl.ANY)


def traded(value, axis, mask):
    return lax.ppermute(value, axis, [(i, i ^ mask) for i in range(lax.axis_size(axis))])


def shifted(value, axis, step):
    peers = lax.axis_size(axis)
    return lax.ppermute(value, axis, [(i, (i + step) % peers) for i in range(peers)])


def group_sizes(peers):
    sizes = []
    while peers > 1:
        sizes.append(min(4, peers))
        peers //= sizes[-1]
    return sizes


def slab_offsets(peers):
    offsets, left = [0], peers
    for ways in group_sizes(peers):
        left //= ways
        offsets = [(left * way) ^ offset for way in range(ways) for offset in offsets]
    return offsets


def slab_tables(stats):
    peers = lax.axis_size("tm")
    total = stats + traded(stats, "space", 1) if lax.axis_size("space") == 2 else lax.psum(stats, "space")
    held, left = [total], peers
    for ways in group_sizes(peers):
        left //= ways
        block = held[0] if len(held) == 1 else jnp.concatenate(held, axis=0)
        held = [block] + [traded(block, "tm", left * way) for way in range(1, ways)]
    return total, held


def row_halo(edges):
    if lax.axis_size("space") == 2:
        return [traded(edges[0], "space", 1)]
    top, bottom = edges
    return [shifted(bottom, "space", 1), shifted(top, "space", -1)]


def edges_of(frames):
    rows = frames.shape[1]
    if lax.axis_size("space") == 2:
        return [lax.dynamic_slice_in_dim(frames, (rows - 1) * (1 - lax.axis_index("space")), 1, axis=1)]
    return [frames[:, :1], frames[:, rows - 1 :]]


def slab_halo(tail, after=None):
    before = shifted(tail, "tm", 1)
    if after is not None:
        before, after = lax.optimization_barrier((before, after))
    return before, row_halo(edges_of(before)), after


def edge_shapes(frames, count):
    shape = (count, 1) + frames.shape[2:]
    return [shaped(shape)] * (1 if lax.axis_size("space") == 2 else 2)


def send_rows(source, frame, edges):
    rows = source.shape[1]
    if len(edges) == 1:
        edges[0][frame, 0] = jnp.where(lax.axis_index("space") == 0, source[frame, rows - 1], source[frame, 0])
    else:
        edges[0][frame, 0] = source[frame, 0]
        edges[1][frame, 0] = source[frame, rows - 1]


def add_stats(sums, values):
    width = values.shape[1]
    return (
        sums[0] + jnp.sum(values.reshape(-1, 8, width), axis=0),
        sums[1] + jnp.sum((values * values).reshape(-1, 8, width), axis=0),
    )


def no_stats(width):
    return jnp.zeros((8, width), F32), jnp.zeros((8, width), F32)


def store_stats(stats, sums, base=None):
    width = sums[0].shape[1]
    for k in range(2):
        part = jnp.sum(sums[k], axis=0, keepdims=True)
        stats[:, k * width : (k + 1) * width] = part if base is None else part + base[:, k * width : (k + 1) * width]


def entry_kernel(feats_hbm, frames, tail, stats, *rest):
    *edges, sems = rest
    n_frames, n_rows, _, width = frames.shape
    loads = [pltpu.make_async_copy(feats_hbm.at[f], frames.at[f], sems.at[f]) for f in range(n_frames)]
    for copy in loads:
        copy.start()
    sums = no_stats(width)
    for frame in range(n_frames):
        loads[frame].wait()
        for row in range(n_rows):
            if frame >= n_frames - TAIL:
                tail[frame - n_frames + TAIL, row] = frames[frame, row]
            sums = add_stats(sums, frames[frame, row].astype(F32))
        send_rows(frames, frame, edges)
    store_stats(stats, sums)


def entry_call(feats):
    n_frames, width = feats.shape[0], feats.shape[3]
    outs = [shaped(feats.shape), shaped((TAIL,) + feats.shape[1:]), shaped((1, 2 * width), F32)]
    outs += edge_shapes(feats, n_frames)
    frames, tail, stats, *edges = pl.pallas_call(
        entry_kernel,
        out_shape=outs,
        in_specs=[ANYWHERE],
        out_specs=[VMEM] * len(outs),
        scratch_shapes=[pltpu.SemaphoreType.DMA((n_frames,))],
        compiler_params=vmem_params(),
        cost_estimate=pl.CostEstimate(flops=4 * feats.size, bytes_accessed=4 * feats.size, transcendentals=0),
    )(in_hbm(feats))
    return frames, tail, stats, edges


def setup_kernel(slabs, per_slab, kernel_hbm, clips_hbm, *refs):
    params_hbm, (_, taps, aux, params, clips, sems) = refs[:4], refs[4:]
    width = aux.shape[1]
    taps_load = pltpu.make_async_copy(kernel_hbm, taps, sems.at[0])
    clip_load = pltpu.make_async_copy(clips_hbm, clips, sems.at[1])
    param_loads = [pltpu.make_async_copy(p, params.at[k], sems.at[2 + k]) for k, p in enumerate(params_hbm)]
    for copy in [clip_load, *param_loads, taps_load]:
        copy.start()
    clip_load.wait()
    own = lax.axis_index("tm")
    own_clip = clips[own]
    slabs_in = jnp.int32(0)
    for entry, offset in enumerate(slab_offsets(slabs)):
        same = (clips[own ^ offset] == own_clip).astype(jnp.int32)
        slabs_in = slabs_in + same
        aux[entry : entry + 1] = jnp.full((1, width), same.astype(F32), F32)
    starting = jnp.logical_or(own == 0, clips[jnp.maximum(own - 1, 0)] != own_clip)
    aux[slabs : slabs + 1] = jnp.full((1, width), starting.astype(F32), F32)
    aux[slabs + 1 : slabs + 2] = jnp.full((1, width), slabs_in.astype(F32) * float(per_slab), F32)
    for k, copy in enumerate(param_loads):
        copy.wait()
        aux[slabs + 2 + k : slabs + 3 + k] = params[k]
    aux[slabs + 6 : slabs + 8] = jnp.zeros((2, width), F32)
    taps_load.wait()


def setup_call(kernel, clip_ids, params, per_slab, after):
    slabs, width = lax.axis_size("tm"), kernel.shape[4]
    return pl.pallas_call(
        functools.partial(setup_kernel, slabs, per_slab),
        out_shape=[shaped(kernel.shape), shaped((slabs + 8, width), F32)],
        in_specs=[ANYWHERE] * 7,
        out_specs=[VMEM, VMEM],
        scratch_shapes=[
            pltpu.VMEM((4, 1, width), F32),
            pltpu.SMEM(clip_ids.shape, jnp.int32),
            pltpu.SemaphoreType.DMA((6,)),
        ],
        compiler_params=vmem_params(),
        cost_estimate=pl.CostEstimate(flops=0, bytes_accessed=4 * kernel.size, transcendentals=0),
    )(*[in_hbm(x) for x in (kernel, clip_ids, *[p[None] for p in params])], after)


def load_kernel(kernel_hbm, after, taps, sem):
    copy = pltpu.make_async_copy(kernel_hbm, taps, sem)
    copy.start()
    copy.wait()


def load_call(kernel, after):
    return pl.pallas_call(
        load_kernel,
        out_shape=shaped(kernel.shape),
        in_specs=[ANYWHERE, ANYWHERE],
        out_specs=VMEM,
        scratch_shapes=[pltpu.SemaphoreType.DMA],
        compiler_params=vmem_params(),
        cost_estimate=pl.CostEstimate(flops=0, bytes_accessed=4 * kernel.size, transcendentals=0),
    )(in_hbm(kernel), after)


def group_total(values):
    width = values.shape[-1]
    lane = lax.broadcasted_iota(jnp.int32, values.shape, 1)
    step = 1
    while step < width // GROUPS:
        upper = pltpu.roll(values, step, 1)
        lower = pltpu.roll(values, width - step, 1)
        values = values + jnp.where((lane & step) != 0, upper, lower)
        step *= 2
    return values


def half_affine(tables, aux, which):
    width = aux.shape[1]
    slabs = aux.shape[0] - 8
    sums = [jnp.zeros((1, width), F32)] * 2
    entry = 0
    for table in tables:
        mask = aux[entry : entry + table.shape[0]]
        entry += table.shape[0]
        sums = [
            total + jnp.sum(table[:, k * width : (k + 1) * width] * mask, axis=0, keepdims=True) for k, total in enumerate(sums)
        ]
    grouped = group_total(jnp.concatenate(sums, axis=0))
    count = aux[slabs + 1 : slabs + 2]
    gain = aux[slabs + 2 + 2 * which : slabs + 3 + 2 * which]
    shift = aux[slabs + 3 + 2 * which : slabs + 4 + 2 * which]
    mean = grouped[0:1] / count
    variance = grouped[1:2] / count - mean * mean
    scale = lax.rsqrt(variance + 1e-06) * gain
    return 0.5 * scale, 0.5 * (shift - mean * scale)


def normed(raw, affine):
    half = raw.astype(F32) * affine[0] + affine[1]
    return (half * jnp.tanh(half) + half).astype(BF16)


def extended_row(frames, sides, frame, row):
    n_rows = frames.shape[1]
    inner = frames[frame, min(max(row - 1, 0), n_rows - 1)]
    if 0 < row <= n_rows:
        return inner
    place, places = lax.axis_index("space"), lax.axis_size("space")
    side = sides[0 if row == 0 else -1]
    return jnp.where(place == (0 if row == 0 else places - 1), inner, side[frame, 0])


def conv_rows(planes, taps):
    ref, index = planes[0]
    n_rows, cols, width = ref.shape[1] - 2, ref.shape[2], ref.shape[3]
    lhs = jnp.concatenate(
        [ref[index, j : j + n_rows].reshape(n_rows * cols, width) for ref, index in planes for j in range(3)], axis=1
    )
    column = lax.broadcasted_iota(jnp.int32, (cols, width), 0)
    sums = []
    for l in range(3):
        rhs = jnp.concatenate([taps[i, j, l] for i in range(3) for j in range(3)], axis=0)
        sums.append(jnp.dot(lhs, rhs, preferred_element_type=F32))
    for row in range(n_rows):
        left, mid, right = (s[row * cols : (row + 1) * cols] for s in sums)
        left = jnp.where(column == 0, left, pltpu.roll(left, 1, 0))
        right = jnp.where(column == cols - 1, right, pltpu.roll(right, cols - 1, 0))
        yield row, left + mid + right


def put_hidden(hidden, frame, row, value, sums):
    rounded = value.astype(BF16)
    hidden[frame, row] = rounded
    return add_stats(sums, rounded.astype(F32))


def late_kernel(n_tables, n_sides, aux, *refs):
    tables, frames, refs = refs[:n_tables], refs[n_tables], refs[n_tables + 1 :]
    sides, taps = refs[:n_sides], refs[n_sides]
    hidden, act_low, stats, affine_out, *edges, act_high = refs[n_sides + 1 :]
    n_frames = frames.shape[0]
    low = act_low.shape[0]
    affine = half_affine(tables, aux, 0)
    for k in range(2):
        affine_out[k : k + 1] = affine[k]
    planes = [(act_low, f) for f in range(low)] + [(act_high, f) for f in range(n_frames - low)]
    for frame, (act, index) in enumerate(planes):
        for row in range(frames.shape[1] + 2):
            act[index, row] = normed(extended_row(frames, sides, frame, row), affine)
    sums = no_stats(frames.shape[3])
    for frame in range(n_frames - 2):
        for row, value in conv_rows(planes[frame : frame + 3], taps):
            sums = put_hidden(hidden, frame, row, value, sums)
        send_rows(hidden, frame, edges)
    store_stats(stats, sums)


def early_kernel(n_sides, aux, before, *refs):
    corners, (act_low, affine_in, stats_in, taps) = refs[:n_sides], refs[n_sides : n_sides + 4]
    hidden, stats, *edges, act_before = refs[n_sides + 4 :]
    slabs = aux.shape[0] - 8
    starting = aux[slabs : slabs + 1] != 0.0
    affine = affine_in[0:1], affine_in[1:2]
    for frame in range(2):
        for row in range(before.shape[1] + 2):
            value = normed(extended_row(before, corners, frame, row), affine).astype(F32)
            act_before[frame, row] = jnp.where(starting, act_low[0, row].astype(F32), value).astype(BF16)
    planes = [(act_before, 0), (act_before, 1)] + [(act_low, f) for f in range(act_low.shape[0])]
    sums = no_stats(before.shape[3])
    for frame in range(2):
        for row, value in conv_rows(planes[frame : frame + 3], taps):
            sums = put_hidden(hidden, frame, row, value, sums)
        send_rows(hidden, frame, edges)
    store_stats(stats, sums, stats_in)


def last_kernel(n_tables, n_sides, aux, *refs):
    tables, early, late, refs = refs[:n_tables], refs[n_tables], refs[n_tables + 1], refs[n_tables + 2 :]
    sides_early, sides_late = refs[:n_sides], refs[n_sides : 2 * n_sides]
    before, *corners = refs[2 * n_sides : 3 * n_sides + 1]
    taps, feats, out, act = refs[3 * n_sides + 1 :]
    slabs = aux.shape[0] - 8
    starting = aux[slabs : slabs + 1] != 0.0
    affine = half_affine(tables, aux, 1)
    n_frames, n_rows = out.shape[:2]

    def fill(frame):
        for row in range(n_rows + 2):
            if frame < 2:
                value = normed(extended_row(before, corners, frame, row), affine).astype(F32)
                act[frame, row] = jnp.where(starting, act[2, row].astype(F32), value).astype(BF16)
            elif frame < 4:
                act[frame, row] = normed(extended_row(early, sides_early, frame - 2, row), affine)
            else:
                act[frame, row] = normed(extended_row(late, sides_late, frame - 4, row), affine)

    for frame in range(2, n_frames + 2):
        fill(frame)
    for frame in list(range(2, n_frames)) + [0, 1]:
        if frame < 2:
            fill(frame)
        if frame == 0:
            fill(1)
        for row, value in conv_rows([(act, frame + i) for i in range(3)], taps):
            out[frame, row] = feats[frame, row].astype(F32) + value


def call(kernel, outs, scratch, frames, *operands):
    return pl.pallas_call(
        kernel,
        out_shape=outs,
        in_specs=[VMEM] * len(operands),
        out_specs=[VMEM] * len(outs) if isinstance(outs, list) else VMEM,
        scratch_shapes=scratch,
        compiler_params=vmem_params(),
        cost_estimate=pl.CostEstimate(flops=54 * frames * 384 * 65536, bytes_accessed=1 << 20, transcendentals=1 << 20),
    )(*operands)


def on_device(feats, clip_ids, gain_one, shift_one, kernel_one, gain_two, shift_two, kernel_two):
    n_frames, n_rows, cols, width = feats.shape
    params = (gain_one, shift_one, gain_two, shift_two)
    frames, tail, stats, edges = entry_call(feats)
    before, corners, _ = slab_halo(tail)
    total, tables = slab_tables(stats)
    sides = row_halo(edges)
    per_slab = feats.size // GROUPS * lax.axis_size("space")
    taps, aux = setup_call(kernel_one, clip_ids, params, per_slab, total)
    n_sides = len(sides)
    plane = (n_rows + 2, cols, width)
    late = n_frames - 2
    hidden_late, act_low, stats, affine, *edges = call(
        functools.partial(late_kernel, len(tables), n_sides),
        [shaped((late, n_rows, cols, width)), shaped((2,) + plane), shaped((1, 2 * width), F32), shaped((2, width), F32)]
        + edge_shapes(feats, late),
        [pltpu.VMEM((late,) + plane, BF16)],
        late, aux, *tables, frames, *sides, taps,
    )
    sides_late = row_halo(edges)
    hidden_early, stats, *edges = call(
        functools.partial(early_kernel, n_sides),
        [shaped((2, n_rows, cols, width)), shaped((1, 2 * width), F32)] + edge_shapes(feats, 2),
        [pltpu.VMEM((2,) + plane, BF16)],
        2, aux, before, *corners, act_low, affine, stats, taps,
    )
    sides_early = row_halo(edges)
    total, tables = slab_tables(stats)
    before, corners, tables[0] = slab_halo(hidden_late[late - 2 :], tables[0])
    taps = load_call(kernel_two, total)
    return call(
        functools.partial(last_kernel, len(tables), n_sides),
        shaped(feats.shape, F32),
        [pltpu.VMEM((n_frames + 2,) + plane, BF16)],
        n_frames, aux, *tables, hidden_early, hidden_late, *sides_early, *sides_late, before, *corners, taps, frames,
    )


def solution(mesh):
    return jax.shard_map(
        on_device,
        mesh=mesh,
        in_specs=(P("tm", "space", None, None), P(), P(), P(), P(), P(), P(), P()),
        out_specs=P("tm", "space", None, None),
        check_vma=False,
    )
```

```python
import functools

import jax
import jax.numpy as jnp
from jax import lax
from jax.experimental import pallas as pl
from jax.experimental.pallas import tpu as pltpu
from jax.sharding import PartitionSpec as P

GROUPS = 32
TAIL = 2
F32, BF16 = jnp.float32, jnp.bfloat16


def vmem_params():
    return pltpu.CompilerParams(vmem_limit_bytes=32 << 20)


def shaped(shape, dtype=BF16):
    return jax.ShapeDtypeStruct(tuple(shape), dtype)


def in_hbm(value):
    return pltpu.with_memory_space_constraint(value, pltpu.HBM)


VMEM = pl.BlockSpec(memory_space=pltpu.VMEM)
ANYWHERE = pl.BlockSpec(memory_space=pl.ANY)


def traded(value, axis, mask):
    return lax.ppermute(value, axis, [(i, i ^ mask) for i in range(lax.axis_size(axis))])


def shifted(value, axis, step):
    peers = lax.axis_size(axis)
    return lax.ppermute(value, axis, [(i, (i + step) % peers) for i in range(peers)])


def group_sizes(peers):
    sizes = []
    while peers > 1:
        sizes.append(min(4, peers))
        peers //= sizes[-1]
    return sizes


def slab_offsets(peers):
    offsets, left = [0], peers
    for ways in group_sizes(peers):
        left //= ways
        offsets = [(left * way) ^ offset for way in range(ways) for offset in offsets]
    return offsets


def slab_tables(stats):
    peers = lax.axis_size("tm")
    total = stats + traded(stats, "space", 1) if lax.axis_size("space") == 2 else lax.psum(stats, "space")
    held, left = [total], peers
    for ways in group_sizes(peers):
        left //= ways
        block = held[0] if len(held) == 1 else jnp.concatenate(held, axis=0)
        held = [block] + [traded(block, "tm", left * way) for way in range(1, ways)]
    return total, held


def row_halo(edges):
    if lax.axis_size("space") == 2:
        return [traded(edges[0], "space", 1)]
    top, bottom = edges
    return [shifted(bottom, "space", 1), shifted(top, "space", -1)]


def edges_of(frames):
    rows = frames.shape[1]
    if lax.axis_size("space") == 2:
        return [lax.dynamic_slice_in_dim(frames, (rows - 1) * (1 - lax.axis_index("space")), 1, axis=1)]
    return [frames[:, :1], frames[:, rows - 1 :]]


def slab_halo(tail, after=None):
    before = shifted(tail, "tm", 1)
    if after is not None:
        before, after = lax.optimization_barrier((before, after))
    return before, row_halo(edges_of(before)), after


def edge_shapes(frames, count):
    shape = (count, 1) + frames.shape[2:]
    return [shaped(shape)] * (1 if lax.axis_size("space") == 2 else 2)


def send_rows(source, frame, edges):
    rows = source.shape[1]
    if len(edges) == 1:
        edges[0][frame, 0] = jnp.where(lax.axis_index("space") == 0, source[frame, rows - 1], source[frame, 0])
    else:
        edges[0][frame, 0] = source[frame, 0]
        edges[1][frame, 0] = source[frame, rows - 1]


def add_stats(sums, values):
    width = values.shape[1]
    return (
        sums[0] + jnp.sum(values.reshape(-1, 8, width), axis=0),
        sums[1] + jnp.sum((values * values).reshape(-1, 8, width), axis=0),
    )


def no_stats(width):
    return jnp.zeros((8, width), F32), jnp.zeros((8, width), F32)


def store_stats(stats, sums, base=None):
    width = sums[0].shape[1]
    for k in range(2):
        part = jnp.sum(sums[k], axis=0, keepdims=True)
        stats[:, k * width : (k + 1) * width] = part if base is None else part + base[:, k * width : (k + 1) * width]


def entry_kernel(feats_hbm, frames, tail, stats, *rest):
    *edges, sems = rest
    n_frames, n_rows, _, width = frames.shape
    loads = [pltpu.make_async_copy(feats_hbm.at[f], frames.at[f], sems.at[f]) for f in range(n_frames)]
    for copy in loads:
        copy.start()
    sums = no_stats(width)
    for frame in range(n_frames):
        loads[frame].wait()
        for row in range(n_rows):
            if frame >= n_frames - TAIL:
                tail[frame - n_frames + TAIL, row] = frames[frame, row]
            sums = add_stats(sums, frames[frame, row].astype(F32))
        send_rows(frames, frame, edges)
    store_stats(stats, sums)


def entry_call(feats):
    n_frames, width = feats.shape[0], feats.shape[3]
    outs = [shaped(feats.shape), shaped((TAIL,) + feats.shape[1:]), shaped((1, 2 * width), F32)]
    outs += edge_shapes(feats, n_frames)
    frames, tail, stats, *edges = pl.pallas_call(
        entry_kernel,
        out_shape=outs,
        in_specs=[ANYWHERE],
        out_specs=[VMEM] * len(outs),
        scratch_shapes=[pltpu.SemaphoreType.DMA((n_frames,))],
        compiler_params=vmem_params(),
        cost_estimate=pl.CostEstimate(flops=1 << 33, bytes_accessed=4 * feats.size, transcendentals=0),
    )(in_hbm(feats))
    return frames, tail, stats, edges


def setup_kernel(slabs, per_slab, clips_hbm, *refs):
    params_hbm, (_, aux, params, clips, sems) = refs[:4], refs[4:]
    width = aux.shape[1]
    clip_load = pltpu.make_async_copy(clips_hbm, clips, sems.at[0])
    param_loads = [pltpu.make_async_copy(p, params.at[k], sems.at[1 + k]) for k, p in enumerate(params_hbm)]
    for copy in [clip_load, *param_loads]:
        copy.start()
    clip_load.wait()
    own = lax.axis_index("tm")
    own_clip = clips[own]
    slabs_in = jnp.int32(0)
    for entry, offset in enumerate(slab_offsets(slabs)):
        same = (clips[own ^ offset] == own_clip).astype(jnp.int32)
        slabs_in = slabs_in + same
        aux[entry : entry + 1] = jnp.full((1, width), same.astype(F32), F32)
    starting = jnp.logical_or(own == 0, clips[jnp.maximum(own - 1, 0)] != own_clip)
    aux[slabs : slabs + 1] = jnp.full((1, width), starting.astype(F32), F32)
    aux[slabs + 1 : slabs + 2] = jnp.full((1, width), slabs_in.astype(F32) * float(per_slab), F32)
    for k, copy in enumerate(param_loads):
        copy.wait()
        aux[slabs + 2 + k : slabs + 3 + k] = params[k]
    aux[slabs + 6 : slabs + 8] = jnp.zeros((2, width), F32)


def setup_call(clip_ids, params, per_slab, after):
    slabs, width = lax.axis_size("tm"), params[0].shape[0]
    return pl.pallas_call(
        functools.partial(setup_kernel, slabs, per_slab),
        out_shape=shaped((slabs + 8, width), F32),
        in_specs=[ANYWHERE] * 6,
        out_specs=VMEM,
        scratch_shapes=[
            pltpu.VMEM((4, 1, width), F32),
            pltpu.SMEM(clip_ids.shape, jnp.int32),
            pltpu.SemaphoreType.DMA((5,)),
        ],
        compiler_params=vmem_params(),
        cost_estimate=pl.CostEstimate(flops=0, bytes_accessed=1 << 16, transcendentals=0),
    )(*[in_hbm(x) for x in (clip_ids, *[p[None] for p in params])], after)


def group_total(values):
    width = values.shape[-1]
    lane = lax.broadcasted_iota(jnp.int32, values.shape, 1)
    step = 1
    while step < width // GROUPS:
        upper = pltpu.roll(values, step, 1)
        lower = pltpu.roll(values, width - step, 1)
        values = values + jnp.where((lane & step) != 0, upper, lower)
        step *= 2
    return values


def half_affine(tables, aux, which):
    width = aux.shape[1]
    slabs = aux.shape[0] - 8
    sums = [jnp.zeros((1, width), F32)] * 2
    entry = 0
    for table in tables:
        mask = aux[entry : entry + table.shape[0]]
        entry += table.shape[0]
        sums = [
            total + jnp.sum(table[:, k * width : (k + 1) * width] * mask, axis=0, keepdims=True) for k, total in enumerate(sums)
        ]
    grouped = group_total(jnp.concatenate(sums, axis=0))
    count = aux[slabs + 1 : slabs + 2]
    gain = aux[slabs + 2 + 2 * which : slabs + 3 + 2 * which]
    shift = aux[slabs + 3 + 2 * which : slabs + 4 + 2 * which]
    mean = grouped[0:1] / count
    variance = grouped[1:2] / count - mean * mean
    scale = lax.rsqrt(variance + 1e-06) * gain
    return 0.5 * scale, 0.5 * (shift - mean * scale)


def normed(raw, affine):
    half = raw.astype(F32) * affine[0] + affine[1]
    return (half * jnp.tanh(half) + half).astype(BF16)


def extended_row(frames, sides, frame, row):
    n_rows = frames.shape[1]
    inner = frames[frame, min(max(row - 1, 0), n_rows - 1)]
    if 0 < row <= n_rows:
        return inner
    place, places = lax.axis_index("space"), lax.axis_size("space")
    side = sides[0 if row == 0 else -1]
    return jnp.where(place == (0 if row == 0 else places - 1), inner, side[frame, 0])


def conv_rows(planes, taps):
    ref, index = planes[0]
    n_rows, cols, width = ref.shape[1] - 2, ref.shape[2], ref.shape[3]
    lhs = jnp.concatenate(
        [ref[index, j : j + n_rows].reshape(n_rows * cols, width) for ref, index in planes for j in range(3)], axis=1
    )
    column = lax.broadcasted_iota(jnp.int32, (cols, width), 0)
    sums = []
    for l in range(3):
        rhs = jnp.concatenate([taps[i, j, l] for i in range(3) for j in range(3)], axis=0)
        sums.append(jnp.dot(lhs, rhs, preferred_element_type=F32))
    for row in range(n_rows):
        left, mid, right = (s[row * cols : (row + 1) * cols] for s in sums)
        left = jnp.where(column == 0, left, pltpu.roll(left, 1, 0))
        right = jnp.where(column == cols - 1, right, pltpu.roll(right, cols - 1, 0))
        yield row, left + mid + right


def put_hidden(hidden, frame, row, value, sums):
    rounded = value.astype(BF16)
    hidden[frame, row] = rounded
    return add_stats(sums, rounded.astype(F32))


def late_kernel(n_tables, n_sides, aux, *refs):
    tables, frames, refs = refs[:n_tables], refs[n_tables], refs[n_tables + 1 :]
    sides, taps = refs[:n_sides], refs[n_sides]
    hidden, act_low, stats, affine_out, *edges, act_high = refs[n_sides + 1 :]
    n_frames = frames.shape[0]
    low = act_low.shape[0]
    affine = half_affine(tables, aux, 0)
    for k in range(2):
        affine_out[k : k + 1] = affine[k]
    planes = [(act_low, f) for f in range(low)] + [(act_high, f) for f in range(n_frames - low)]
    for frame, (act, index) in enumerate(planes):
        for row in range(frames.shape[1] + 2):
            act[index, row] = normed(extended_row(frames, sides, frame, row), affine)
    sums = no_stats(frames.shape[3])
    for frame in range(n_frames - 2):
        for row, value in conv_rows(planes[frame : frame + 3], taps):
            sums = put_hidden(hidden, frame, row, value, sums)
        send_rows(hidden, frame, edges)
    store_stats(stats, sums)


def early_kernel(n_sides, aux, before, *refs):
    corners, (act_low, affine_in, stats_in, taps) = refs[:n_sides], refs[n_sides : n_sides + 4]
    hidden, stats, *edges, act_before = refs[n_sides + 4 :]
    slabs = aux.shape[0] - 8
    starting = aux[slabs : slabs + 1] != 0.0
    affine = affine_in[0:1], affine_in[1:2]
    for frame in range(2):
        for row in range(before.shape[1] + 2):
            value = normed(extended_row(before, corners, frame, row), affine).astype(F32)
            act_before[frame, row] = jnp.where(starting, act_low[0, row].astype(F32), value).astype(BF16)
    planes = [(act_before, 0), (act_before, 1)] + [(act_low, f) for f in range(act_low.shape[0])]
    sums = no_stats(before.shape[3])
    for frame in range(2):
        for row, value in conv_rows(planes[frame : frame + 3], taps):
            sums = put_hidden(hidden, frame, row, value, sums)
        send_rows(hidden, frame, edges)
    store_stats(stats, sums, stats_in)


def last_kernel(n_tables, n_sides, aux, *refs):
    tables, early, late, refs = refs[:n_tables], refs[n_tables], refs[n_tables + 1], refs[n_tables + 2 :]
    sides_early, sides_late = refs[:n_sides], refs[n_sides : 2 * n_sides]
    before, *corners = refs[2 * n_sides : 3 * n_sides + 1]
    taps, feats, out_hbm, act, out, sems = refs[3 * n_sides + 1 :]
    stores = [pltpu.make_async_copy(out.at[f], out_hbm.at[f], sems.at[f]) for f in range(out.shape[0])]
    slabs = aux.shape[0] - 8
    starting = aux[slabs : slabs + 1] != 0.0
    affine = half_affine(tables, aux, 1)
    n_frames, n_rows = out.shape[:2]

    def fill(frame):
        for row in range(n_rows + 2):
            if frame < 2:
                value = normed(extended_row(before, corners, frame, row), affine).astype(F32)
                act[frame, row] = jnp.where(starting, act[2, row].astype(F32), value).astype(BF16)
            elif frame < 4:
                act[frame, row] = normed(extended_row(early, sides_early, frame - 2, row), affine)
            else:
                act[frame, row] = normed(extended_row(late, sides_late, frame - 4, row), affine)

    for frame in range(2, n_frames + 2):
        fill(frame)
    for frame in list(range(2, n_frames)) + [0, 1]:
        if frame == 0:
            fill(0)
            fill(1)
        for row, value in conv_rows([(act, frame + i) for i in range(3)], taps):
            out[frame, row] = feats[frame, row].astype(F32) + value
        stores[frame].start()
    for store in stores:
        store.wait()


def call(kernel, outs, scratch, frames, *operands):
    return pl.pallas_call(
        kernel,
        out_shape=outs,
        in_specs=[VMEM] * len(operands),
        out_specs=[VMEM] * len(outs) if isinstance(outs, list) else ANYWHERE,
        scratch_shapes=scratch,
        compiler_params=vmem_params(),
        cost_estimate=pl.CostEstimate(flops=54 * frames * 384 * 65536, bytes_accessed=1 << 20, transcendentals=1 << 20),
    )(*operands)


def on_device(feats, clip_ids, gain_one, shift_one, kernel_one, gain_two, shift_two, kernel_two):
    n_frames, n_rows, cols, width = feats.shape
    params = (gain_one, shift_one, gain_two, shift_two)
    frames, tail, stats, edges = entry_call(feats)
    before, corners, _ = slab_halo(tail)
    total, tables = slab_tables(stats)
    sides = row_halo(edges)
    per_slab = feats.size // GROUPS * lax.axis_size("space")
    aux = setup_call(clip_ids, params, per_slab, total)
    n_sides = len(sides)
    plane = (n_rows + 2, cols, width)
    late = n_frames - 2
    hidden_late, act_low, stats, affine, *edges = call(
        functools.partial(late_kernel, len(tables), n_sides),
        [shaped((late, n_rows, cols, width)), shaped((2,) + plane), shaped((1, 2 * width), F32), shaped((2, width), F32)]
        + edge_shapes(feats, late),
        [pltpu.VMEM((late,) + plane, BF16)],
        late, aux, *tables, frames, *sides, kernel_one,
    )
    sides_late = row_halo(edges)
    hidden_early, stats, *edges = call(
        functools.partial(early_kernel, n_sides),
        [shaped((2, n_rows, cols, width)), shaped((1, 2 * width), F32)] + edge_shapes(feats, 2),
        [pltpu.VMEM((2,) + plane, BF16)],
        2, aux, before, *corners, act_low, affine, stats, kernel_one,
    )
    sides_early = row_halo(edges)
    total, tables = slab_tables(stats)
    before, corners, tables[0] = slab_halo(hidden_late[late - 2 :], tables[0])
    return call(
        functools.partial(last_kernel, len(tables), n_sides),
        shaped(feats.shape, F32),
        [pltpu.VMEM((n_frames + 2,) + plane, BF16), pltpu.VMEM(feats.shape, F32), pltpu.SemaphoreType.DMA((n_frames,))],
        n_frames, aux, *tables, hidden_early, hidden_late, *sides_early, *sides_late, before, *corners, kernel_two, frames,
    )


def solution(mesh):
    return jax.shard_map(
        on_device,
        mesh=mesh,
        in_specs=(P("tm", "space", None, None), P(), P(), P(), P(), P(), P(), P()),
        out_specs=P("tm", "space", None, None),
        check_vma=False,
    )
```

```python
import functools

import jax
import jax.numpy as jnp
from jax import lax
from jax.experimental import pallas as pl
from jax.experimental.pallas import tpu as pltpu
from jax.sharding import PartitionSpec as P

GROUPS = 32
TAIL = 2
F32, BF16 = jnp.float32, jnp.bfloat16


def vmem_params():
    return pltpu.CompilerParams(vmem_limit_bytes=32 << 20)


def shaped(shape, dtype=BF16):
    return jax.ShapeDtypeStruct(tuple(shape), dtype)


def in_hbm(value):
    return pltpu.with_memory_space_constraint(value, pltpu.HBM)


VMEM = pl.BlockSpec(memory_space=pltpu.VMEM)
ANYWHERE = pl.BlockSpec(memory_space=pl.ANY)


def traded(value, axis, mask):
    return lax.ppermute(value, axis, [(i, i ^ mask) for i in range(lax.axis_size(axis))])


def shifted(value, axis, step):
    peers = lax.axis_size(axis)
    return lax.ppermute(value, axis, [(i, (i + step) % peers) for i in range(peers)])


def group_sizes(peers):
    sizes = []
    while peers > 1:
        sizes.append(min(4, peers))
        peers //= sizes[-1]
    return sizes


def slab_offsets(peers):
    offsets, left = [0], peers
    for ways in group_sizes(peers):
        left //= ways
        offsets = [(left * way) ^ offset for way in range(ways) for offset in offsets]
    return offsets


def slab_tables(stats, beside=None):
    peers = lax.axis_size("tm")
    total = stats + traded(stats, "space", 1) if lax.axis_size("space") == 2 else lax.psum(stats, "space")
    held, left = [total], peers
    for ways in group_sizes(peers):
        left //= ways
        block = held[0] if len(held) == 1 else jnp.concatenate(held, axis=0)
        if left == 1 and beside is not None:
            block, beside = lax.optimization_barrier((block, beside))
        held = [block] + [traded(block, "tm", left * way) for way in range(1, ways)]
    return total, held, beside


def row_halo(edges):
    if lax.axis_size("space") == 2:
        return [traded(edges[0], "space", 1)]
    top, bottom = edges
    return [shifted(bottom, "space", 1), shifted(top, "space", -1)]


def edges_of(frames):
    rows = frames.shape[1]
    if lax.axis_size("space") == 2:
        return [lax.dynamic_slice_in_dim(frames, (rows - 1) * (1 - lax.axis_index("space")), 1, axis=1)]
    return [frames[:, :1], frames[:, rows - 1 :]]


def edge_shapes(frames, count):
    shape = (count, 1) + frames.shape[2:]
    return [shaped(shape)] * (1 if lax.axis_size("space") == 2 else 2)


def send_rows(source, frame, edges):
    rows = source.shape[1]
    if len(edges) == 1:
        edges[0][frame, 0] = jnp.where(lax.axis_index("space") == 0, source[frame, rows - 1], source[frame, 0])
    else:
        edges[0][frame, 0] = source[frame, 0]
        edges[1][frame, 0] = source[frame, rows - 1]


def add_stats(sums, values):
    width = values.shape[1]
    return (
        sums[0] + jnp.sum(values.reshape(-1, 8, width), axis=0),
        sums[1] + jnp.sum((values * values).reshape(-1, 8, width), axis=0),
    )


def no_stats(width):
    return jnp.zeros((8, width), F32), jnp.zeros((8, width), F32)


def store_stats(stats, sums, base=None):
    width = sums[0].shape[1]
    for k in range(2):
        part = jnp.sum(sums[k], axis=0, keepdims=True)
        stats[:, k * width : (k + 1) * width] = part if base is None else part + base[:, k * width : (k + 1) * width]


def entry_kernel(feats_hbm, frames, tail, stats, *rest):
    *edges, sems = rest
    n_frames, n_rows, _, width = frames.shape
    loads = [pltpu.make_async_copy(feats_hbm.at[f], frames.at[f], sems.at[f]) for f in range(n_frames)]
    for copy in loads:
        copy.start()
    sums = no_stats(width)
    for frame in range(n_frames):
        loads[frame].wait()
        for row in range(n_rows):
            if frame >= n_frames - TAIL:
                tail[frame - n_frames + TAIL, row] = frames[frame, row]
            sums = add_stats(sums, frames[frame, row].astype(F32))
        send_rows(frames, frame, edges)
    store_stats(stats, sums)


def entry_call(feats):
    n_frames, width = feats.shape[0], feats.shape[3]
    outs = [shaped(feats.shape), shaped((TAIL,) + feats.shape[1:]), shaped((1, 2 * width), F32)]
    outs += edge_shapes(feats, n_frames)
    frames, tail, stats, *edges = pl.pallas_call(
        entry_kernel,
        out_shape=outs,
        in_specs=[ANYWHERE],
        out_specs=[VMEM] * len(outs),
        scratch_shapes=[pltpu.SemaphoreType.DMA((n_frames,))],
        compiler_params=vmem_params(),
        cost_estimate=pl.CostEstimate(flops=4 * feats.size, bytes_accessed=4 * feats.size, transcendentals=0),
    )(in_hbm(feats))
    return frames, tail, stats, edges


def setup_kernel(slabs, per_slab, kernel_hbm, clips_hbm, *refs):
    params_hbm, (_, taps, aux, params, clips, sems) = refs[:4], refs[4:]
    width = aux.shape[1]
    clip_load = pltpu.make_async_copy(clips_hbm, clips, sems.at[0])
    param_loads = [pltpu.make_async_copy(p, params.at[k], sems.at[1 + k]) for k, p in enumerate(params_hbm)]
    taps_load = pltpu.make_async_copy(kernel_hbm, taps, sems.at[5])
    for copy in [clip_load, *param_loads, taps_load]:
        copy.start()
    clip_load.wait()
    own = lax.axis_index("tm")
    own_clip = clips[own]
    slabs_in = jnp.int32(0)
    for entry, offset in enumerate(slab_offsets(slabs)):
        same = (clips[own ^ offset] == own_clip).astype(jnp.int32)
        slabs_in = slabs_in + same
        aux[entry : entry + 1] = jnp.full((1, width), same.astype(F32), F32)
    starting = jnp.logical_or(own == 0, clips[jnp.maximum(own - 1, 0)] != own_clip)
    aux[slabs : slabs + 1] = jnp.full((1, width), starting.astype(F32), F32)
    aux[slabs + 1 : slabs + 2] = jnp.full((1, width), slabs_in.astype(F32) * float(per_slab), F32)
    for k, copy in enumerate(param_loads):
        copy.wait()
        aux[slabs + 2 + k : slabs + 3 + k] = params[k]
    aux[slabs + 6 : slabs + 8] = jnp.zeros((2, width), F32)
    taps_load.wait()


def setup_call(kernel, clip_ids, params, per_slab, after):
    slabs, width = lax.axis_size("tm"), params[0].shape[0]
    return pl.pallas_call(
        functools.partial(setup_kernel, slabs, per_slab),
        out_shape=[shaped(kernel.shape), shaped((slabs + 8, width), F32)],
        in_specs=[ANYWHERE] * 7,
        out_specs=[VMEM, VMEM],
        scratch_shapes=[
            pltpu.VMEM((4, 1, width), F32),
            pltpu.SMEM(clip_ids.shape, jnp.int32),
            pltpu.SemaphoreType.DMA((6,)),
        ],
        compiler_params=vmem_params(),
        cost_estimate=pl.CostEstimate(flops=0, bytes_accessed=4 * kernel.size, transcendentals=0),
    )(*[in_hbm(x) for x in (kernel, clip_ids, *[p[None] for p in params])], after)


def group_total(values):
    width = values.shape[-1]
    lane = lax.broadcasted_iota(jnp.int32, values.shape, 1)
    step = 1
    while step < width // GROUPS:
        upper = pltpu.roll(values, step, 1)
        lower = pltpu.roll(values, width - step, 1)
        values = values + jnp.where((lane & step) != 0, upper, lower)
        step *= 2
    return values


def half_affine(tables, aux, which):
    width = aux.shape[1]
    slabs = aux.shape[0] - 8
    sums = [jnp.zeros((1, width), F32)] * 2
    entry = 0
    for table in tables:
        mask = aux[entry : entry + table.shape[0]]
        entry += table.shape[0]
        sums = [
            total + jnp.sum(table[:, k * width : (k + 1) * width] * mask, axis=0, keepdims=True) for k, total in enumerate(sums)
        ]
    grouped = group_total(jnp.concatenate(sums, axis=0))
    count = aux[slabs + 1 : slabs + 2]
    gain = aux[slabs + 2 + 2 * which : slabs + 3 + 2 * which]
    shift = aux[slabs + 3 + 2 * which : slabs + 4 + 2 * which]
    mean = grouped[0:1] / count
    variance = grouped[1:2] / count - mean * mean
    scale = lax.rsqrt(variance + 1e-06) * gain
    return 0.5 * scale, 0.5 * (shift - mean * scale)


def normed(raw, affine):
    half = raw.astype(F32) * affine[0] + affine[1]
    return (half * jnp.tanh(half) + half).astype(BF16)


def extended_row(frames, sides, frame, row):
    n_rows = frames.shape[1]
    inner = frames[frame, min(max(row - 1, 0), n_rows - 1)]
    if 0 < row <= n_rows:
        return inner
    place, places = lax.axis_index("space"), lax.axis_size("space")
    side = sides[0 if row == 0 else -1]
    return jnp.where(place == (0 if row == 0 else places - 1), inner, side[frame, 0])


def conv_rows(planes, taps):
    ref, index = planes[0]
    n_rows, cols, width = ref.shape[1] - 2, ref.shape[2], ref.shape[3]
    lhs = jnp.concatenate(
        [ref[index, j : j + n_rows].reshape(n_rows * cols, width) for ref, index in planes for j in range(3)], axis=1
    )
    column = lax.broadcasted_iota(jnp.int32, (cols, width), 0)
    sums = []
    for l in range(3):
        rhs = jnp.concatenate([taps[i, j, l] for i in range(3) for j in range(3)], axis=0)
        sums.append(jnp.dot(lhs, rhs, preferred_element_type=F32))
    for row in range(n_rows):
        left, mid, right = (s[row * cols : (row + 1) * cols] for s in sums)
        left = jnp.where(column == 0, left, pltpu.roll(left, 1, 0))
        right = jnp.where(column == cols - 1, right, pltpu.roll(right, cols - 1, 0))
        yield row, left + mid + right


def put_hidden(hidden, frame, row, value, sums):
    rounded = value.astype(BF16)
    hidden[frame, row] = rounded
    return add_stats(sums, rounded.astype(F32))


def late_kernel(n_tables, n_sides, which, aux, *refs):
    tables, frames, refs = refs[:n_tables], refs[n_tables], refs[n_tables + 1 :]
    early_sides, late_sides, taps = refs[:n_sides], refs[n_sides : 2 * n_sides], refs[2 * n_sides]
    if which == 0:
        act_low, affine_out, hidden, stats, *edges, act_high = refs[2 * n_sides + 1 :]
        early = late = frames
        late_first = 0
    else:
        late, feats, act_low, affine_out, out_hbm, act_high, out, sems = refs[2 * n_sides + 1 :]
        early, late_first = frames, frames.shape[0]
    n_rows, width = frames.shape[1], frames.shape[3]
    low, high = act_low.shape[0], act_high.shape[0]
    affine = half_affine(tables, aux, which)
    for k in range(2):
        affine_out[k : k + 1] = affine[k]
    planes = [(act_low, f) for f in range(low)] + [(act_high, f) for f in range(high)]
    for frame, (act, index) in enumerate(planes):
        for row in range(n_rows + 2):
            if which == 0 or frame < 2:
                value = extended_row(early, early_sides, frame, row)
            else:
                value = extended_row(late, late_sides, frame - late_first, row)
            act[index, row] = normed(value, affine)
    sums = no_stats(width)
    stores = []
    for frame in range(high):
        for row, value in conv_rows(planes[frame : frame + 3], taps):
            if which == 0:
                sums = put_hidden(hidden, frame, row, value, sums)
            else:
                out[frame, row] = feats[low + frame, row].astype(F32) + value
        if which == 0:
            send_rows(hidden, frame, edges)
        else:
            stores.append(pltpu.make_async_copy(out.at[frame], out_hbm.at[low + frame], sems.at[frame]))
            stores[-1].start()
    if which == 0:
        store_stats(stats, sums)
    for store in stores:
        store.wait()


def early_kernel(n_sides, n_before, which, aux, *refs):
    before = [(ref, f) for ref in refs[:n_before] for f in range(ref.shape[0])]
    corners = [refs[n_before + k * n_sides : n_before + (k + 1) * n_sides] for k in range(n_before)]
    corners = [corners[k] for k in range(n_before) for _ in range(refs[k].shape[0])]
    act_low, affine_in, taps, *refs = refs[n_before * (n_sides + 1) :]
    if which == 0:
        stats_in, hidden, stats, *edges, act_before = refs
    else:
        feats, _, out_hbm, act_before, out, sems = refs
    slabs = aux.shape[0] - 8
    starting = aux[slabs : slabs + 1] != 0.0
    affine = affine_in[0:1], affine_in[1:2]
    for frame, (ref, index) in enumerate(before):
        for row in range(ref.shape[1] + 2):
            value = normed(extended_row(ref, corners[frame], index, row), affine).astype(F32)
            act_before[frame, row] = jnp.where(starting, act_low[0, row].astype(F32), value).astype(BF16)
    planes = [(act_before, 0), (act_before, 1)] + [(act_low, f) for f in range(act_low.shape[0])]
    sums = no_stats(act_low.shape[3])
    stores = []
    for frame in range(2):
        for row, value in conv_rows(planes[frame : frame + 3], taps):
            if which == 0:
                sums = put_hidden(hidden, frame, row, value, sums)
            else:
                out[frame, row] = feats[frame, row].astype(F32) + value
        if which == 0:
            send_rows(hidden, frame, edges)
        else:
            stores.append(pltpu.make_async_copy(out.at[frame], out_hbm.at[frame], sems.at[frame]))
            stores[-1].start()
    if which == 0:
        store_stats(stats, sums, stats_in)
    for store in stores:
        store.wait()


def call(kernel, outs, scratch, frames, operands, out_specs=None, aliases=None):
    return pl.pallas_call(
        kernel,
        out_shape=outs,
        in_specs=[VMEM if aliases is None or k not in aliases else ANYWHERE for k in range(len(operands))],
        out_specs=[VMEM] * len(outs) if out_specs is None else out_specs,
        scratch_shapes=scratch,
        input_output_aliases=aliases or {},
        compiler_params=vmem_params(),
        cost_estimate=pl.CostEstimate(flops=54 * frames * 384 * 65536, bytes_accessed=1 << 20, transcendentals=1 << 20),
    )(*operands)


def on_device(feats, clip_ids, gain_one, shift_one, kernel_one, gain_two, shift_two, kernel_two):
    n_frames, n_rows, cols, width = feats.shape
    params = (gain_one, shift_one, gain_two, shift_two)
    per_slab = feats.size // GROUPS * lax.axis_size("space")
    late = n_frames - 2
    plane = (n_rows + 2, cols, width)
    act = pltpu.VMEM((2,) + plane, BF16)
    act_late = pltpu.VMEM((late,) + plane, BF16)
    act_shapes = [shaped((2,) + plane), shaped((2, width), F32)]
    stats_shape = shaped((1, 2 * width), F32)

    frames, tail, stats, edges = entry_call(feats)
    total, tables, first_part = slab_tables(stats, shifted(tail[:1], "tm", 1))
    sides = row_halo(edges)
    second, _ = lax.optimization_barrier((tail[1:], total))
    before = [first_part, shifted(second, "tm", 1)]
    corners = [corner for part in before for corner in row_halo(edges_of(part))]
    taps, aux = setup_call(kernel_one, clip_ids, params, per_slab, total)
    n_sides = len(sides)
    act_low, affine, hidden_late, stats, *edges = call(
        functools.partial(late_kernel, len(tables), n_sides, 0),
        act_shapes + [shaped((late, n_rows, cols, width)), stats_shape] + edge_shapes(feats, late),
        [act_late],
        late,
        [aux, *tables, frames, *sides, *sides, taps],
    )
    tail = hidden_late[late - 2 :]
    before_two = shifted(tail, "tm", 1)
    sides_late = row_halo(edges)
    hidden_early, stats, *edges = call(
        functools.partial(early_kernel, n_sides, len(before), 0),
        [shaped((2, n_rows, cols, width)), stats_shape] + edge_shapes(feats, 2),
        [act],
        2,
        [aux, *before, *corners, act_low, affine, taps, stats],
    )

    sides_early = row_halo(edges)
    _, tables, _ = slab_tables(stats)
    before_two, *tables = lax.optimization_barrier((before_two, *tables))
    corners = row_halo(edges_of(before_two))
    act_low, affine, out = call(
        functools.partial(late_kernel, len(tables), n_sides, 1),
        act_shapes + [shaped(feats.shape, F32)],
        [act_late, pltpu.VMEM((late, n_rows, cols, width), F32), pltpu.SemaphoreType.DMA((late,))],
        late,
        [aux, *tables, hidden_early, *sides_early, *sides_late, kernel_two, hidden_late, frames],
        out_specs=[VMEM, VMEM, ANYWHERE],
    )
    operands = [aux, before_two, *corners, act_low, affine, kernel_two, frames, out]
    return call(
        functools.partial(early_kernel, n_sides, 1, 1),
        shaped(feats.shape, F32),
        [act, pltpu.VMEM((2, n_rows, cols, width), F32), pltpu.SemaphoreType.DMA((2,))],
        2,
        operands,
        out_specs=ANYWHERE,
        aliases={len(operands) - 1: 0},
    )


def solution(mesh):
    return jax.shard_map(
        on_device,
        mesh=mesh,
        in_specs=(P("tm", "space", None, None), P(), P(), P(), P(), P(), P(), P()),
        out_specs=P("tm", "space", None, None),
        check_vma=False,
    )
```

```python
import functools

import jax
import jax.numpy as jnp
from jax import lax
from jax.experimental import pallas as pl
from jax.experimental.pallas import tpu as pltpu
from jax.sharding import PartitionSpec as P

GROUPS = 32
TAIL = 2
F32, BF16 = jnp.float32, jnp.bfloat16


def vmem_params():
    return pltpu.CompilerParams(vmem_limit_bytes=32 << 20)


def shaped(shape, dtype=BF16):
    return jax.ShapeDtypeStruct(tuple(shape), dtype)


def in_hbm(value):
    return pltpu.with_memory_space_constraint(value, pltpu.HBM)


VMEM = pl.BlockSpec(memory_space=pltpu.VMEM)
ANYWHERE = pl.BlockSpec(memory_space=pl.ANY)


def traded(value, axis, mask):
    return lax.ppermute(value, axis, [(i, i ^ mask) for i in range(lax.axis_size(axis))])


def shifted(value, axis, step):
    peers = lax.axis_size(axis)
    return lax.ppermute(value, axis, [(i, (i + step) % peers) for i in range(peers)])


def group_sizes(peers):
    sizes = []
    while peers > 1:
        sizes.append(min(4, peers))
        peers //= sizes[-1]
    return sizes


def slab_offsets(peers):
    offsets, left = [0], peers
    for ways in group_sizes(peers):
        left //= ways
        offsets = [(left * way) ^ offset for way in range(ways) for offset in offsets]
    return offsets


def slab_tables(stats, rows):
    peers = lax.axis_size("tm")
    total = stats + traded(stats, "space", 1) if lax.axis_size("space") == 2 else lax.psum(stats, "space")
    total, *rows = lax.optimization_barrier((total, *rows))
    held, left = [total], peers
    marks = []
    for ways in group_sizes(peers):
        left //= ways
        block = held[0] if len(held) == 1 else jnp.concatenate(held, axis=0)
        held = [block] + [traded(block, "tm", left * way) for way in range(1, ways)]
        marks += [block, held[-1]]
    return held, rows, (total, marks[-2])


def slab_halo(frames, marks):
    parts = []
    for part, mark in enumerate(marks):
        frame, _ = lax.optimization_barrier((frames[part : part + 1], mark))
        parts.append(shifted(frame, "tm", 1))
    return parts


def corner_rows(parts, after):
    *parts, after = lax.optimization_barrier((*parts, after))
    edges = [edges_of(part) for part in parts]
    return parts, row_halo([jnp.concatenate(side, axis=0) for side in zip(*edges)]), after


def row_halo(edges):
    if lax.axis_size("space") == 2:
        return [traded(edges[0], "space", 1)]
    top, bottom = edges
    return [shifted(bottom, "space", 1), shifted(top, "space", -1)]


def edges_of(frames):
    rows = frames.shape[1]
    if lax.axis_size("space") == 2:
        return [lax.dynamic_slice_in_dim(frames, (rows - 1) * (1 - lax.axis_index("space")), 1, axis=1)]
    return [frames[:, :1], frames[:, rows - 1 :]]


def edge_shapes(frames, count):
    shape = (count, 1) + frames.shape[2:]
    return [shaped(shape)] * (1 if lax.axis_size("space") == 2 else 2)


def send_rows(source, frame, edges):
    rows = source.shape[1]
    if len(edges) == 1:
        edges[0][frame, 0] = jnp.where(lax.axis_index("space") == 0, source[frame, rows - 1], source[frame, 0])
    else:
        edges[0][frame, 0] = source[frame, 0]
        edges[1][frame, 0] = source[frame, rows - 1]


def add_stats(sums, values):
    width = values.shape[1]
    return (
        sums[0] + jnp.sum(values.reshape(-1, 8, width), axis=0),
        sums[1] + jnp.sum((values * values).reshape(-1, 8, width), axis=0),
    )


def no_stats(width):
    return jnp.zeros((8, width), F32), jnp.zeros((8, width), F32)


def store_stats(stats, sums, base=None):
    width = sums[0].shape[1]
    for k in range(2):
        part = jnp.sum(sums[k], axis=0, keepdims=True)
        stats[:, k * width : (k + 1) * width] = part if base is None else part + base[:, k * width : (k + 1) * width]


def entry_kernel(slabs, per_slab, feats_hbm, kernel_hbm, clips_hbm, *refs):
    params_hbm, (frames, taps, tail, stats, aux, *edges, params, clips, frame_sems, sems) = refs[:4], refs[4:]
    n_frames, n_rows, _, width = frames.shape
    loads = [pltpu.make_async_copy(feats_hbm.at[f], frames.at[f], frame_sems.at[f]) for f in range(n_frames)]
    clip_load = pltpu.make_async_copy(clips_hbm, clips, sems.at[0])
    param_loads = [pltpu.make_async_copy(p, params.at[k], sems.at[1 + k]) for k, p in enumerate(params_hbm)]
    taps_load = pltpu.make_async_copy(kernel_hbm, taps, sems.at[5])
    for copy in [*loads, clip_load, *param_loads, taps_load]:
        copy.start()
    sums = no_stats(width)
    for frame in range(n_frames):
        loads[frame].wait()
        for row in range(n_rows):
            if frame >= n_frames - TAIL:
                tail[frame - n_frames + TAIL, row] = frames[frame, row]
            sums = add_stats(sums, frames[frame, row].astype(F32))
        send_rows(frames, frame, edges)
    store_stats(stats, sums)
    clip_load.wait()
    own = lax.axis_index("tm")
    own_clip = clips[own]
    slabs_in = jnp.int32(0)
    for entry, offset in enumerate(slab_offsets(slabs)):
        same = (clips[own ^ offset] == own_clip).astype(jnp.int32)
        slabs_in = slabs_in + same
        aux[entry : entry + 1] = jnp.full((1, width), same.astype(F32), F32)
    starting = jnp.logical_or(own == 0, clips[jnp.maximum(own - 1, 0)] != own_clip)
    aux[slabs : slabs + 1] = jnp.full((1, width), starting.astype(F32), F32)
    aux[slabs + 1 : slabs + 2] = jnp.full((1, width), slabs_in.astype(F32) * float(per_slab), F32)
    for k, copy in enumerate(param_loads):
        copy.wait()
        aux[slabs + 2 + k : slabs + 3 + k] = params[k]
    aux[slabs + 6 : slabs + 8] = jnp.zeros((2, width), F32)
    taps_load.wait()


def entry_call(feats, kernel, clip_ids, params, per_slab):
    slabs = lax.axis_size("tm")
    n_frames, width = feats.shape[0], feats.shape[3]
    outs = [shaped(feats.shape), shaped(kernel.shape), shaped((TAIL,) + feats.shape[1:])]
    outs += [shaped((1, 2 * width), F32), shaped((slabs + 8, width), F32)]
    outs += edge_shapes(feats, n_frames)
    frames, taps, tail, stats, aux, *edges = pl.pallas_call(
        functools.partial(entry_kernel, slabs, per_slab),
        out_shape=outs,
        in_specs=[ANYWHERE] * 7,
        out_specs=[VMEM] * len(outs),
        scratch_shapes=[
            pltpu.VMEM((4, 1, width), F32),
            pltpu.SMEM(clip_ids.shape, jnp.int32),
            pltpu.SemaphoreType.DMA((n_frames,)),
            pltpu.SemaphoreType.DMA((6,)),
        ],
        compiler_params=vmem_params(),
        cost_estimate=pl.CostEstimate(flops=4 * feats.size, bytes_accessed=4 * kernel.size, transcendentals=0),
    )(*[in_hbm(x) for x in (feats, kernel, clip_ids, *[p[None] for p in params])])
    return frames, taps, tail, stats, aux, edges


def group_total(values):
    width = values.shape[-1]
    lane = lax.broadcasted_iota(jnp.int32, values.shape, 1)
    step = 1
    while step < width // GROUPS:
        upper = pltpu.roll(values, step, 1)
        lower = pltpu.roll(values, width - step, 1)
        values = values + jnp.where((lane & step) != 0, upper, lower)
        step *= 2
    return values


def half_affine(tables, aux, which):
    width = aux.shape[1]
    slabs = aux.shape[0] - 8
    sums = [jnp.zeros((1, width), F32)] * 2
    entry = 0
    for table in tables:
        mask = aux[entry : entry + table.shape[0]]
        entry += table.shape[0]
        sums = [
            total + jnp.sum(table[:, k * width : (k + 1) * width] * mask, axis=0, keepdims=True) for k, total in enumerate(sums)
        ]
    grouped = group_total(jnp.concatenate(sums, axis=0))
    count = aux[slabs + 1 : slabs + 2]
    gain = aux[slabs + 2 + 2 * which : slabs + 3 + 2 * which]
    shift = aux[slabs + 3 + 2 * which : slabs + 4 + 2 * which]
    mean = grouped[0:1] / count
    variance = grouped[1:2] / count - mean * mean
    scale = lax.rsqrt(variance + 1e-06) * gain
    return 0.5 * scale, 0.5 * (shift - mean * scale)


def normed(raw, affine):
    half = raw.astype(F32) * affine[0] + affine[1]
    return (half * jnp.tanh(half) + half).astype(BF16)


def extended_row(frames, sides, frame, row, side_frame=None):
    n_rows = frames.shape[1]
    inner = frames[frame, min(max(row - 1, 0), n_rows - 1)]
    if 0 < row <= n_rows:
        return inner
    place, places = lax.axis_index("space"), lax.axis_size("space")
    side = sides[0 if row == 0 else -1]
    return jnp.where(place == (0 if row == 0 else places - 1), inner, side[frame if side_frame is None else side_frame, 0])


def conv_rows(planes, taps):
    ref, index = planes[0]
    n_rows, cols, width = ref.shape[1] - 2, ref.shape[2], ref.shape[3]
    lhs = jnp.concatenate(
        [ref[index, j : j + n_rows].reshape(n_rows * cols, width) for ref, index in planes for j in range(3)], axis=1
    )
    column = lax.broadcasted_iota(jnp.int32, (cols, width), 0)
    sums = []
    for l in range(3):
        rhs = jnp.concatenate([taps[i, j, l] for i in range(3) for j in range(3)], axis=0)
        sums.append(jnp.dot(lhs, rhs, preferred_element_type=F32))
    for row in range(n_rows):
        left, mid, right = (s[row * cols : (row + 1) * cols] for s in sums)
        left = jnp.where(column == 0, left, pltpu.roll(left, 1, 0))
        right = jnp.where(column == cols - 1, right, pltpu.roll(right, cols - 1, 0))
        yield row, left + mid + right


def put_hidden(hidden, frame, row, value, sums):
    rounded = value.astype(BF16)
    hidden[frame, row] = rounded
    return add_stats(sums, rounded.astype(F32))


def late_kernel(n_tables, n_sides, which, aux, *refs):
    tables, frames, refs = refs[:n_tables], refs[n_tables], refs[n_tables + 1 :]
    early_sides, late_sides, taps = refs[:n_sides], refs[n_sides : 2 * n_sides], refs[2 * n_sides]
    if which == 0:
        act_low, affine_out, hidden, stats, *edges, act_high = refs[2 * n_sides + 1 :]
        early = late = frames
        late_first = 0
    else:
        late, feats, act_low, affine_out, out_hbm, act_high, out, sems = refs[2 * n_sides + 1 :]
        early, late_first = frames, frames.shape[0]
    n_rows, width = frames.shape[1], frames.shape[3]
    low, high = act_low.shape[0], act_high.shape[0]
    affine = half_affine(tables, aux, which)
    for k in range(2):
        affine_out[k : k + 1] = affine[k]
    planes = [(act_low, f) for f in range(low)] + [(act_high, f) for f in range(high)]
    for frame, (act, index) in enumerate(planes):
        for row in range(n_rows + 2):
            if which == 0 or frame < 2:
                value = extended_row(early, early_sides, frame, row)
            else:
                value = extended_row(late, late_sides, frame - late_first, row)
            act[index, row] = normed(value, affine)
    sums = no_stats(width)
    stores = []
    for frame in range(high):
        for row, value in conv_rows(planes[frame : frame + 3], taps):
            if which == 0:
                sums = put_hidden(hidden, frame, row, value, sums)
            else:
                out[frame, row] = feats[low + frame, row].astype(F32) + value
        if which == 0:
            send_rows(hidden, frame, edges)
        else:
            stores.append(pltpu.make_async_copy(out.at[frame], out_hbm.at[low + frame], sems.at[frame]))
            stores[-1].start()
    if which == 0:
        store_stats(stats, sums)
    for store in stores:
        store.wait()


def early_kernel(n_sides, which, aux, *refs):
    before, corners = refs[:2], refs[2 : 2 + n_sides]
    act_low, affine_in, taps, *refs = refs[2 + n_sides :]
    if which == 0:
        stats_in, hidden, stats, *edges, act_before = refs
    else:
        feats, _, out_hbm, act_before, out, sems = refs
    slabs = aux.shape[0] - 8
    starting = aux[slabs : slabs + 1] != 0.0
    affine = affine_in[0:1], affine_in[1:2]
    for frame in range(2):
        for row in range(act_low.shape[1]):
            value = normed(extended_row(before[frame], corners, 0, row, frame), affine).astype(F32)
            act_before[frame, row] = jnp.where(starting, act_low[0, row].astype(F32), value).astype(BF16)
    planes = [(act_before, 0), (act_before, 1)] + [(act_low, f) for f in range(act_low.shape[0])]
    sums = no_stats(act_low.shape[3])
    stores = []
    for frame in range(2):
        for row, value in conv_rows(planes[frame : frame + 3], taps):
            if which == 0:
                sums = put_hidden(hidden, frame, row, value, sums)
            else:
                out[frame, row] = feats[frame, row].astype(F32) + value
        if which == 0:
            send_rows(hidden, frame, edges)
        else:
            stores.append(pltpu.make_async_copy(out.at[frame], out_hbm.at[frame], sems.at[frame]))
            stores[-1].start()
    if which == 0:
        store_stats(stats, sums, stats_in)
    for store in stores:
        store.wait()


def call(kernel, outs, scratch, frames, operands, out_specs=None, aliases=None):
    return pl.pallas_call(
        kernel,
        out_shape=outs,
        in_specs=[VMEM if aliases is None or k not in aliases else ANYWHERE for k in range(len(operands))],
        out_specs=[VMEM] * len(outs) if out_specs is None else out_specs,
        scratch_shapes=scratch,
        input_output_aliases=aliases or {},
        compiler_params=vmem_params(),
        cost_estimate=pl.CostEstimate(flops=54 * frames * 384 * 65536, bytes_accessed=1 << 20, transcendentals=1 << 20),
    )(*operands)


def on_device(feats, clip_ids, gain_one, shift_one, kernel_one, gain_two, shift_two, kernel_two):
    n_frames, n_rows, cols, width = feats.shape
    params = (gain_one, shift_one, gain_two, shift_two)
    per_slab = feats.size // GROUPS * lax.axis_size("space")
    late = n_frames - 2
    plane = (n_rows + 2, cols, width)
    act = pltpu.VMEM((2,) + plane, BF16)
    act_late = pltpu.VMEM((late,) + plane, BF16)
    act_shapes = [shaped((2,) + plane), shaped((2, width), F32)]
    stats_shape = shaped((1, 2 * width), F32)

    frames, taps, tail, stats, aux, edges = entry_call(feats, kernel_one, clip_ids, params, per_slab)
    tables, sides, marks = slab_tables(stats, row_halo(edges))
    before = slab_halo(tail, marks)
    aux, before[0] = lax.optimization_barrier((aux, before[0]))
    n_sides = len(sides)
    act_low, affine, hidden_late, stats, *edges = call(
        functools.partial(late_kernel, len(tables), n_sides, 0),
        act_shapes + [shaped((late, n_rows, cols, width)), stats_shape] + edge_shapes(feats, late),
        [act_late],
        late,
        [aux, *tables, frames, *sides, *sides, taps],
    )
    sides_late = row_halo(edges)
    before, corners, affine = corner_rows(before, affine)
    hidden_early, stats, *edges = call(
        functools.partial(early_kernel, n_sides, 0),
        [shaped((2, n_rows, cols, width)), stats_shape] + edge_shapes(feats, 2),
        [act],
        2,
        [aux, *before, *corners, act_low, affine, taps, stats],
    )

    tables, sides, marks = slab_tables(stats, [*row_halo(edges), *sides_late])
    before = slab_halo(hidden_late[late - 2 :], marks)
    aux, before[0] = lax.optimization_barrier((aux, before[0]))
    act_low, affine, out = call(
        functools.partial(late_kernel, len(tables), n_sides, 1),
        act_shapes + [shaped(feats.shape, F32)],
        [act_late, pltpu.VMEM((late, n_rows, cols, width), F32), pltpu.SemaphoreType.DMA((late,))],
        late,
        [aux, *tables, hidden_early, *sides, kernel_two, hidden_late, frames],
        out_specs=[VMEM, VMEM, ANYWHERE],
    )
    before, corners, affine = corner_rows(before, affine)
    operands = [aux, *before, *corners, act_low, affine, kernel_two, frames, out]
    return call(
        functools.partial(early_kernel, n_sides, 1),
        shaped(feats.shape, F32),
        [act, pltpu.VMEM((2, n_rows, cols, width), F32), pltpu.SemaphoreType.DMA((2,))],
        2,
        operands,
        out_specs=ANYWHERE,
        aliases={len(operands) - 1: 0},
    )


def solution(mesh):
    return jax.shard_map(
        on_device,
        mesh=mesh,
        in_specs=(P("tm", "space", None, None), P(), P(), P(), P(), P(), P(), P()),
        out_specs=P("tm", "space", None, None),
        check_vma=False,
    )
```

```python
import functools

import jax
import jax.numpy as jnp
from jax import lax
from jax.experimental import pallas as pl
from jax.experimental.pallas import tpu as pltpu
from jax.sharding import PartitionSpec as P

GROUPS = 32
TAIL = 2
F32, BF16 = jnp.float32, jnp.bfloat16


def vmem_params():
    return pltpu.CompilerParams(vmem_limit_bytes=32 << 20)


def shaped(shape, dtype=BF16):
    return jax.ShapeDtypeStruct(tuple(shape), dtype)


def in_hbm(value):
    return pltpu.with_memory_space_constraint(value, pltpu.HBM)


VMEM = pl.BlockSpec(memory_space=pltpu.VMEM)
ANYWHERE = pl.BlockSpec(memory_space=pl.ANY)


def traded(value, axis, mask):
    return lax.ppermute(value, axis, [(i, i ^ mask) for i in range(lax.axis_size(axis))])


def shifted(value, axis, step):
    peers = lax.axis_size(axis)
    return lax.ppermute(value, axis, [(i, (i + step) % peers) for i in range(peers)])


def stats_table(copies):
    return lax.all_to_all(copies, ("tm", "space"), 0, 0, tiled=True)


def corner_rows(before, after):
    before, after = lax.optimization_barrier((before, after))
    return before, row_halo(edges_of(before)), after


def row_halo(edges):
    if lax.axis_size("space") == 2:
        return [traded(edges, "space", 1)]
    return [shifted(edges[:, 1:], "space", 1), shifted(edges[:, :1], "space", -1)]


def edges_of(frames):
    rows = frames.shape[1]
    if lax.axis_size("space") == 2:
        return lax.dynamic_slice_in_dim(frames, (rows - 1) * (1 - lax.axis_index("space")), 1, axis=1)
    return jnp.concatenate([frames[:, :1], frames[:, rows - 1 :]], axis=1)


def edge_shape(frames, count):
    return (count, 1 if lax.axis_size("space") == 2 else 2) + frames.shape[2:]


def send_rows(source, frame, edges, at=0):
    rows = source.shape[1]
    if edges.shape[1] == 1:
        low = lax.axis_index("space") == 0
        edges[at + frame, 0] = jnp.where(low, source[frame, rows - 1], source[frame, 0])
    else:
        edges[at + frame, 0] = source[frame, 0]
        edges[at + frame, 1] = source[frame, rows - 1]


def add_stats(sums, values):
    width = values.shape[1]
    return (
        sums[0] + jnp.sum(values.reshape(-1, 8, width), axis=0),
        sums[1] + jnp.sum((values * values).reshape(-1, 8, width), axis=0),
    )


def no_stats(width):
    return jnp.zeros((8, width), F32), jnp.zeros((8, width), F32)


def store_stats(stats, sums):
    width = sums[0].shape[1]
    for k in range(2):
        stats[:, k * width : (k + 1) * width] = jnp.sum(sums[k], axis=0, keepdims=True)


def store_copies(copies, stats):
    copies[...] = jnp.broadcast_to(stats[...][None], copies.shape)


def stored_in_hbm(shape, dtype=BF16):
    return pltpu.HBM(tuple(shape), dtype)


def device_count():
    return lax.axis_size("tm") * lax.axis_size("space")


def entry_kernel(feats_hbm, copies_hbm, tail_hbm, edges_hbm, frames, edges, copies, stats, sems, out_sems):
    n_frames, n_rows, _, width = frames.shape
    loads = [pltpu.make_async_copy(feats_hbm.at[f], frames.at[f], sems.at[f]) for f in range(n_frames)]
    for copy in loads:
        copy.start()
    tail_copy = pltpu.make_async_copy(feats_hbm.at[pl.ds(n_frames - TAIL, TAIL)], tail_hbm, out_sems.at[0])
    tail_copy.start()
    sums = no_stats(width)
    for frame in range(n_frames):
        loads[frame].wait()
        for row in range(n_rows):
            sums = add_stats(sums, frames[frame, row].astype(F32))
        send_rows(frames, frame, edges)
    store_stats(stats, sums)
    store_copies(copies, stats)
    stores = [
        pltpu.make_async_copy(copies, copies_hbm, out_sems.at[1]),
        pltpu.make_async_copy(edges, edges_hbm, out_sems.at[2]),
    ]
    for copy in stores:
        copy.start()
    for copy in [tail_copy, *stores]:
        copy.wait()


def entry_call(feats):
    n_frames, width = feats.shape[0], feats.shape[3]
    copies = (device_count(), 1, 2 * width)
    return pl.pallas_call(
        entry_kernel,
        out_shape=[
            stored_in_hbm(copies, F32),
            stored_in_hbm((TAIL,) + feats.shape[1:]),
            stored_in_hbm(edge_shape(feats, n_frames)),
        ],
        in_specs=[ANYWHERE],
        out_specs=[ANYWHERE] * 3,
        scratch_shapes=[
            pltpu.VMEM(feats.shape, BF16),
            pltpu.VMEM(edge_shape(feats, n_frames), BF16),
            pltpu.VMEM(copies, F32),
            pltpu.VMEM((1, 2 * width), F32),
            pltpu.SemaphoreType.DMA((n_frames,)),
            pltpu.SemaphoreType.DMA((3,)),
        ],
        compiler_params=vmem_params(),
        cost_estimate=pl.CostEstimate(flops=4 * feats.size, bytes_accessed=4 * feats.size, transcendentals=0),
    )(in_hbm(feats))


def load_kernel(slabs, per_slab, n_big, clips_hbm, *refs):
    params_hbm, bigs_hbm, _ = refs[:4], refs[4 : 4 + n_big], refs[4 + n_big]
    bigs, (aux, params, clips, sems) = refs[5 + n_big : 5 + 2 * n_big], refs[5 + 2 * n_big :]
    width = aux.shape[1]
    clip_load = pltpu.make_async_copy(clips_hbm, clips, sems.at[0])
    param_loads = [pltpu.make_async_copy(p, params.at[k], sems.at[1 + k]) for k, p in enumerate(params_hbm)]
    loads = [pltpu.make_async_copy(src, dst, sems.at[5 + k]) for k, (src, dst) in enumerate(zip(bigs_hbm, bigs))]
    for copy in [clip_load, *param_loads, *loads]:
        copy.start()
    clip_load.wait()
    own = lax.axis_index("tm")
    own_clip = clips[own]
    slabs_in = jnp.int32(0)
    for slab in range(slabs):
        same = (clips[slab] == own_clip).astype(jnp.int32)
        slabs_in = slabs_in + same
        aux[slab : slab + 1] = jnp.full((1, width), same.astype(F32), F32)
    starting = jnp.logical_or(own == 0, clips[jnp.maximum(own - 1, 0)] != own_clip)
    aux[slabs : slabs + 1] = jnp.full((1, width), starting.astype(F32), F32)
    aux[slabs + 1 : slabs + 2] = jnp.full((1, width), slabs_in.astype(F32) * float(per_slab), F32)
    for k, copy in enumerate(param_loads):
        copy.wait()
        aux[slabs + 2 + k : slabs + 3 + k] = params[k]
    aux[slabs + 6 : slabs + 8] = jnp.zeros((2, width), F32)
    for copy in loads:
        copy.wait()


def load_call(bigs, clip_ids, params, per_slab, after):
    slabs, width = lax.axis_size("tm"), params[0].shape[0]
    return pl.pallas_call(
        functools.partial(load_kernel, slabs, per_slab, len(bigs)),
        out_shape=[*[shaped(big.shape) for big in bigs], shaped((slabs + 8, width), F32)],
        in_specs=[ANYWHERE] * (6 + len(bigs)),
        out_specs=[VMEM] * (1 + len(bigs)),
        scratch_shapes=[
            pltpu.VMEM((4, 1, width), F32),
            pltpu.SMEM(clip_ids.shape, jnp.int32),
            pltpu.SemaphoreType.DMA((5 + len(bigs),)),
        ],
        compiler_params=vmem_params(),
        cost_estimate=pl.CostEstimate(flops=0, bytes_accessed=4 * sum(b.size for b in bigs), transcendentals=0),
    )(*[in_hbm(x) for x in (clip_ids, *[p[None] for p in params], *bigs)], after)


def group_total(values):
    width = values.shape[-1]
    lane = lax.broadcasted_iota(jnp.int32, values.shape, 1)
    step = 1
    while step < width // GROUPS:
        upper = pltpu.roll(values, step, 1)
        lower = pltpu.roll(values, width - step, 1)
        values = values + jnp.where((lane & step) != 0, upper, lower)
        step *= 2
    return values


def half_affine(table, aux, which):
    width = aux.shape[1]
    slabs = aux.shape[0] - 8
    places = table.shape[0] // slabs
    sums = []
    for k in range(2):
        parts = [
            aux[slab : slab + 1] * sum(table[slab * places + p, :, k * width : (k + 1) * width] for p in range(places))
            for slab in range(slabs)
        ]
        while len(parts) > 1:
            parts = [sum(parts[i : i + 2]) for i in range(0, len(parts), 2)]
        sums += parts
    grouped = group_total(jnp.concatenate(sums, axis=0))
    count = aux[slabs + 1 : slabs + 2]
    gain = aux[slabs + 2 + 2 * which : slabs + 3 + 2 * which]
    shift = aux[slabs + 3 + 2 * which : slabs + 4 + 2 * which]
    mean = grouped[0:1] / count
    variance = grouped[1:2] / count - mean * mean
    scale = lax.rsqrt(variance + 1e-06) * gain
    return 0.5 * scale, 0.5 * (shift - mean * scale)


def normed(raw, affine):
    half = raw.astype(F32) * affine[0] + affine[1]
    return (half * jnp.tanh(half) + half).astype(BF16)


def extended_row(frames, sides, frame, row):
    n_rows = frames.shape[1]
    inner = frames[frame, min(max(row - 1, 0), n_rows - 1)]
    if 0 < row <= n_rows:
        return inner
    place, places = lax.axis_index("space"), lax.axis_size("space")
    side = sides[0 if row == 0 else -1]
    return jnp.where(place == (0 if row == 0 else places - 1), inner, side[frame, 0])


def conv_rows(planes, taps):
    ref, index = planes[0]
    n_rows, cols, width = ref.shape[1] - 2, ref.shape[2], ref.shape[3]
    lhs = jnp.concatenate(
        [ref[index, j : j + n_rows].reshape(n_rows * cols, width) for ref, index in planes for j in range(3)], axis=1
    )
    column = lax.broadcasted_iota(jnp.int32, (cols, width), 0)
    sums = []
    for l in range(3):
        rhs = jnp.concatenate([taps[i, j, l] for i in range(3) for j in range(3)], axis=0)
        sums.append(jnp.dot(lhs, rhs, preferred_element_type=F32))
    for row in range(n_rows):
        left, mid, right = (s[row * cols : (row + 1) * cols] for s in sums)
        left = jnp.where(column == 0, left, pltpu.roll(left, 1, 0))
        right = jnp.where(column == cols - 1, right, pltpu.roll(right, cols - 1, 0))
        yield row, left + mid + right


def put_hidden(hidden, frame, row, value, sums):
    rounded = value.astype(BF16)
    hidden[frame, row] = rounded
    return add_stats(sums, rounded.astype(F32))


def late_kernel(n_sides, which, aux, table, frames, *refs):
    sides, taps, refs = refs[:n_sides], refs[n_sides], refs[n_sides + 1 :]
    if which == 0:
        act_low, affine_out, hidden, stats, edges, act_high = refs
    else:
        feats, act_low, affine_out, out_hbm, act_high, out, sems = refs
    n_rows, width = frames.shape[1], frames.shape[3]
    low, high = act_low.shape[0], act_high.shape[0]
    affine = half_affine(table, aux, which)
    for k in range(2):
        affine_out[k : k + 1] = affine[k]
    planes = [(act_low, f) for f in range(low)] + [(act_high, f) for f in range(high)]
    for frame, (act, index) in enumerate(planes):
        for row in range(n_rows + 2):
            act[index, row] = normed(extended_row(frames, sides, frame, row), affine)
    sums = no_stats(width)
    stores = []
    for frame in range(high):
        for row, value in conv_rows(planes[frame : frame + 3], taps):
            if which == 0:
                sums = put_hidden(hidden, frame, row, value, sums)
            else:
                out[frame, row] = feats[low + frame, row].astype(F32) + value
        if which == 0:
            send_rows(hidden, frame, edges)
        else:
            stores.append(pltpu.make_async_copy(out.at[frame], out_hbm.at[low + frame], sems.at[frame]))
            stores[-1].start()
    if which == 0:
        for k in range(2):
            stats[k] = sums[k]
    for store in stores:
        store.wait()


def early_act(n_sides, aux, refs):
    before, corners, (act_low, affine_in), act_before = refs[0], refs[1 : 1 + n_sides], refs[1 + n_sides : 3 + n_sides], refs[-1]
    slabs = aux.shape[0] - 8
    starting = aux[slabs : slabs + 1] != 0.0
    affine = affine_in[0:1], affine_in[1:2]
    for frame in range(2):
        for row in range(act_low.shape[1]):
            value = normed(extended_row(before, corners, frame, row), affine).astype(F32)
            act_before[frame, row] = jnp.where(starting, act_low[0, row].astype(F32), value).astype(BF16)
    return [(act_before, 0), (act_before, 1)] + [(act_low, f) for f in range(act_low.shape[0])]


def early_hidden_kernel(n_sides, aux, *refs):
    refs, act_before, (hidden, edges, copies, stats, sems) = refs[:-6], refs[-6], refs[-5:]
    taps, late, late_stats, late_edges, hidden_hbm, tail_hbm, edges_hbm, copies_hbm = refs[3 + n_sides :]
    n_late = late.shape[0]
    stores = [
        pltpu.make_async_copy(late, hidden_hbm.at[pl.ds(2, n_late)], sems.at[0]),
        pltpu.make_async_copy(late.at[pl.ds(n_late - TAIL, TAIL)], tail_hbm, sems.at[1]),
        pltpu.make_async_copy(late_edges, edges_hbm.at[pl.ds(2, n_late)], sems.at[2]),
    ]
    for store in stores:
        store.start()
    planes = early_act(n_sides, aux, (*refs[: 3 + n_sides], act_before))
    sums = late_stats[0], late_stats[1]
    for frame in range(2):
        for row, value in conv_rows(planes[frame : frame + 3], taps):
            sums = put_hidden(hidden, frame, row, value, sums)
        send_rows(hidden, frame, edges)
        if frame == 1:
            store_stats(stats, sums)
            store_copies(copies, stats)
            stores.append(pltpu.make_async_copy(copies, copies_hbm, sems.at[5]))
            stores[-1].start()
            stores.append(pltpu.make_async_copy(edges, edges_hbm.at[pl.ds(0, 2)], sems.at[6]))
            stores[-1].start()
        stores.append(pltpu.make_async_copy(hidden.at[frame], hidden_hbm.at[frame], sems.at[3 + frame]))
        stores[-1].start()
    for store in stores:
        store.wait()


def early_out_kernel(n_sides, aux, *refs):
    refs, act_before, (out, sems) = refs[:-3], refs[-3], refs[-2:]
    taps, feats, _, out_hbm = refs[3 + n_sides :]
    planes = early_act(n_sides, aux, (*refs[: 3 + n_sides], act_before))
    stores = []
    for frame in range(2):
        for row, value in conv_rows(planes[frame : frame + 3], taps):
            out[frame, row] = feats[frame, row].astype(F32) + value
        stores.append(pltpu.make_async_copy(out.at[frame], out_hbm.at[frame], sems.at[frame]))
        stores[-1].start()
    for store in stores:
        store.wait()


def call(kernel, outs, scratch, frames, operands, out_specs=None, aliases=None):
    return pl.pallas_call(
        kernel,
        out_shape=outs,
        in_specs=[VMEM if aliases is None or k not in aliases else ANYWHERE for k in range(len(operands))],
        out_specs=[VMEM] * len(outs) if out_specs is None else out_specs,
        scratch_shapes=scratch,
        input_output_aliases=aliases or {},
        compiler_params=vmem_params(),
        cost_estimate=pl.CostEstimate(flops=54 * frames * 384 * 65536, bytes_accessed=1 << 20, transcendentals=1 << 20),
    )(*operands)


def on_device(feats, clip_ids, gain_one, shift_one, kernel_one, gain_two, shift_two, kernel_two):
    n_frames, n_rows, cols, width = feats.shape
    params = (gain_one, shift_one, gain_two, shift_two)
    per_slab = feats.size // GROUPS * lax.axis_size("space")
    late = n_frames - 2
    plane = (n_rows + 2, cols, width)
    act = pltpu.VMEM((2,) + plane, BF16)
    act_late = pltpu.VMEM((late,) + plane, BF16)
    act_shapes = [shaped((2,) + plane), shaped((2, width), F32)]

    copies, tail, edges = entry_call(feats)
    table = stats_table(copies)
    tail, edges, _ = lax.optimization_barrier((tail, edges, copies))
    before = shifted(tail, "tm", 1)
    sides = row_halo(edges)
    taps, frames, aux = load_call((kernel_one, feats), clip_ids, params, per_slab, copies)
    n_sides = len(sides)
    act_low, affine, hidden_late, stats, edges = call(
        functools.partial(late_kernel, n_sides, 0),
        act_shapes
        + [shaped((late, n_rows, cols, width)), shaped((2, 8, width), F32), shaped(edge_shape(feats, late))],
        [act_late],
        late,
        [aux, table, frames, *sides, taps],
    )
    before, corners, affine = corner_rows(before, affine)
    hidden, tail, edges, copies = call(
        functools.partial(early_hidden_kernel, n_sides),
        [
            stored_in_hbm(feats.shape),
            stored_in_hbm((TAIL,) + feats.shape[1:]),
            stored_in_hbm(edge_shape(feats, n_frames)),
            stored_in_hbm(copies.shape, F32),
        ],
        [
            act,
            pltpu.VMEM((2, n_rows, cols, width), BF16),
            pltpu.VMEM(edge_shape(feats, 2), BF16),
            pltpu.VMEM(copies.shape, F32),
            pltpu.VMEM((1, 2 * width), F32),
            pltpu.SemaphoreType.DMA((7,)),
        ],
        2,
        [aux, before, *corners, act_low, affine, taps, hidden_late, stats, edges],
        out_specs=[ANYWHERE] * 4,
    )

    table = stats_table(copies)
    before = shifted(tail, "tm", 1)
    sides = row_halo(edges)
    taps, frames, hidden, aux = load_call((kernel_two, feats, hidden), clip_ids, params, per_slab, copies)
    act_low, affine, out = call(
        functools.partial(late_kernel, n_sides, 1),
        act_shapes + [shaped(feats.shape, F32)],
        [act_late, pltpu.VMEM((late, n_rows, cols, width), F32), pltpu.SemaphoreType.DMA((late,))],
        late,
        [aux, table, hidden, *sides, taps, frames],
        out_specs=[VMEM, VMEM, ANYWHERE],
    )
    before, corners, affine = corner_rows(before, affine)
    operands = [aux, before, *corners, act_low, affine, taps, frames, out]
    return call(
        functools.partial(early_out_kernel, n_sides),
        shaped(feats.shape, F32),
        [act, pltpu.VMEM((2, n_rows, cols, width), F32), pltpu.SemaphoreType.DMA((2,))],
        2,
        operands,
        out_specs=ANYWHERE,
        aliases={len(operands) - 1: 0},
    )


def solution(mesh):
    return jax.shard_map(
        on_device,
        mesh=mesh,
        in_specs=(P("tm", "space", None, None), P(), P(), P(), P(), P(), P(), P()),
        out_specs=P("tm", "space", None, None),
        check_vma=False,
    )
```

```python
import functools

import jax
import jax.numpy as jnp
from jax import lax
from jax.experimental import pallas as pl
from jax.experimental.pallas import tpu as pltpu
from jax.sharding import PartitionSpec as P

GROUPS = 32
TAIL = 2
F32, BF16 = jnp.float32, jnp.bfloat16


def vmem_params():
    return pltpu.CompilerParams(vmem_limit_bytes=32 << 20)


def shaped(shape, dtype=BF16):
    return jax.ShapeDtypeStruct(tuple(shape), dtype)


def in_hbm(value):
    return pltpu.with_memory_space_constraint(value, pltpu.HBM)


VMEM = pl.BlockSpec(memory_space=pltpu.VMEM)
ANYWHERE = pl.BlockSpec(memory_space=pl.ANY)


def traded(value, axis, mask):
    return lax.ppermute(value, axis, [(i, i ^ mask) for i in range(lax.axis_size(axis))])


def shifted(value, axis, step):
    peers = lax.axis_size(axis)
    return lax.ppermute(value, axis, [(i, (i + step) % peers) for i in range(peers)])


def slab_tables(stats):
    return stats, [lax.all_gather(stats, ("tm", "space"))]


def row_halo(edges):
    if lax.axis_size("space") == 2:
        return [traded(edges[0], "space", 1)]
    top, bottom = edges
    return [shifted(bottom, "space", 1), shifted(top, "space", -1)]


def edges_of(frames):
    rows = frames.shape[1]
    if lax.axis_size("space") == 2:
        return [lax.dynamic_slice_in_dim(frames, (rows - 1) * (1 - lax.axis_index("space")), 1, axis=1)]
    return [frames[:, :1], frames[:, rows - 1 :]]


def slab_halo(tail, after=None):
    before = shifted(tail, "tm", 1)
    if after is not None:
        before, after = lax.optimization_barrier((before, after))
    return before, row_halo(edges_of(before)), after


def edge_shapes(frames, count):
    shape = (count, 1) + frames.shape[2:]
    return [shaped(shape)] * (1 if lax.axis_size("space") == 2 else 2)


def send_rows(source, frame, edges):
    rows = source.shape[1]
    if len(edges) == 1:
        edges[0][frame, 0] = jnp.where(lax.axis_index("space") == 0, source[frame, rows - 1], source[frame, 0])
    else:
        edges[0][frame, 0] = source[frame, 0]
        edges[1][frame, 0] = source[frame, rows - 1]


def add_stats(sums, values):
    width = values.shape[1]
    return (
        sums[0] + jnp.sum(values.reshape(-1, 8, width), axis=0),
        sums[1] + jnp.sum((values * values).reshape(-1, 8, width), axis=0),
    )


def no_stats(width):
    return jnp.zeros((8, width), F32), jnp.zeros((8, width), F32)


def store_stats(stats, sums, base=None):
    width = sums[0].shape[1]
    for k in range(2):
        at = slice(k * width, (k + 1) * width)
        stats[:, at] = sums[k] if base is None else sums[k] + base[:, at]


def entry_kernel(feats_hbm, frames, tail, stats, *rest):
    *edges, sems = rest
    n_frames, n_rows, _, width = frames.shape
    loads = [pltpu.make_async_copy(feats_hbm.at[f], frames.at[f], sems.at[f]) for f in range(n_frames)]
    for copy in loads:
        copy.start()
    sums = no_stats(width)
    for frame in range(n_frames):
        loads[frame].wait()
        for row in range(n_rows):
            if frame >= n_frames - TAIL:
                tail[frame - n_frames + TAIL, row] = frames[frame, row]
            sums = add_stats(sums, frames[frame, row].astype(F32))
        send_rows(frames, frame, edges)
    store_stats(stats, sums)


def entry_call(feats):
    n_frames, width = feats.shape[0], feats.shape[3]
    outs = [shaped(feats.shape), shaped((TAIL,) + feats.shape[1:]), shaped((8, 2 * width), F32)]
    outs += edge_shapes(feats, n_frames)
    frames, tail, stats, *edges = pl.pallas_call(
        entry_kernel,
        out_shape=outs,
        in_specs=[ANYWHERE],
        out_specs=[VMEM] * len(outs),
        scratch_shapes=[pltpu.SemaphoreType.DMA((n_frames,))],
        compiler_params=vmem_params(),
        cost_estimate=pl.CostEstimate(flops=4 * feats.size, bytes_accessed=4 * feats.size, transcendentals=0),
    )(in_hbm(feats))
    return frames, tail, stats, edges


def setup_kernel(slabs, per_slab, kernel_hbm, clips_hbm, *refs):
    params_hbm, (_, taps, aux, params, clips, sems) = refs[:4], refs[4:]
    width = aux.shape[1]
    taps_load = pltpu.make_async_copy(kernel_hbm, taps, sems.at[0])
    clip_load = pltpu.make_async_copy(clips_hbm, clips, sems.at[1])
    param_loads = [pltpu.make_async_copy(p, params.at[k], sems.at[2 + k]) for k, p in enumerate(params_hbm)]
    for copy in [clip_load, *param_loads, taps_load]:
        copy.start()
    clip_load.wait()
    own = lax.axis_index("tm")
    own_clip = clips[own]
    slabs_in = jnp.int32(0)
    for entry in range(slabs):
        same = (clips[entry] == own_clip).astype(jnp.int32)
        slabs_in = slabs_in + same
        aux[entry : entry + 1] = jnp.full((1, width), same.astype(F32), F32)
    starting = jnp.logical_or(own == 0, clips[jnp.maximum(own - 1, 0)] != own_clip)
    aux[slabs : slabs + 1] = jnp.full((1, width), starting.astype(F32), F32)
    aux[slabs + 1 : slabs + 2] = jnp.full((1, width), slabs_in.astype(F32) * float(per_slab), F32)
    for k, copy in enumerate(param_loads):
        copy.wait()
        aux[slabs + 2 + k : slabs + 3 + k] = params[k]
    aux[slabs + 6 : slabs + 8] = jnp.zeros((2, width), F32)
    taps_load.wait()


def setup_call(kernel, clip_ids, params, per_slab, after):
    slabs, width = lax.axis_size("tm"), kernel.shape[4]
    return pl.pallas_call(
        functools.partial(setup_kernel, slabs, per_slab),
        out_shape=[shaped(kernel.shape), shaped((slabs + 8, width), F32)],
        in_specs=[ANYWHERE] * 7,
        out_specs=[VMEM, VMEM],
        scratch_shapes=[
            pltpu.VMEM((4, 1, width), F32),
            pltpu.SMEM(clip_ids.shape, jnp.int32),
            pltpu.SemaphoreType.DMA((6,)),
        ],
        compiler_params=vmem_params(),
        cost_estimate=pl.CostEstimate(flops=0, bytes_accessed=4 * kernel.size, transcendentals=0),
    )(*[in_hbm(x) for x in (kernel, clip_ids, *[p[None] for p in params])], after)


def group_total(values):
    width = values.shape[-1]
    lane = lax.broadcasted_iota(jnp.int32, values.shape, 1)
    step = 1
    while step < width // GROUPS:
        upper = pltpu.roll(values, step, 1)
        lower = pltpu.roll(values, width - step, 1)
        values = values + jnp.where((lane & step) != 0, upper, lower)
        step *= 2
    return values


def half_affine(tables, aux, which):
    width = aux.shape[1]
    slabs = aux.shape[0] - 8
    (table,) = tables
    places = table.shape[0] // slabs
    sums = []
    for k in range(2):
        parts = [
            aux[slab : slab + 1] * sum(table[slab * places + p, :, k * width : (k + 1) * width] for p in range(places))
            for slab in range(slabs)
        ]
        while len(parts) > 1:
            parts = [sum(parts[i : i + 2]) for i in range(0, len(parts), 2)]
        sums.append(jnp.sum(parts[0], axis=0, keepdims=True))
    grouped = group_total(jnp.concatenate(sums, axis=0))
    count = aux[slabs + 1 : slabs + 2]
    gain = aux[slabs + 2 + 2 * which : slabs + 3 + 2 * which]
    shift = aux[slabs + 3 + 2 * which : slabs + 4 + 2 * which]
    mean = grouped[0:1] / count
    variance = grouped[1:2] / count - mean * mean
    scale = lax.rsqrt(variance + 1e-06) * gain
    return 0.5 * scale, 0.5 * (shift - mean * scale)


def normed(raw, affine):
    half = raw.astype(F32) * affine[0] + affine[1]
    return (half * jnp.tanh(half) + half).astype(BF16)


def extended_row(frames, sides, frame, row):
    n_rows = frames.shape[1]
    inner = frames[frame, min(max(row - 1, 0), n_rows - 1)]
    if 0 < row <= n_rows:
        return inner
    place, places = lax.axis_index("space"), lax.axis_size("space")
    side = sides[0 if row == 0 else -1]
    return jnp.where(place == (0 if row == 0 else places - 1), inner, side[frame, 0])


def conv_rows(planes, taps):
    ref, index = planes[0]
    n_rows, cols, width = ref.shape[1] - 2, ref.shape[2], ref.shape[3]
    lhs = jnp.concatenate(
        [ref[index, j : j + n_rows].reshape(n_rows * cols, width) for ref, index in planes for j in range(3)], axis=1
    )
    column = lax.broadcasted_iota(jnp.int32, (cols, width), 0)
    sums = []
    for l in range(3):
        rhs = jnp.concatenate([taps[i, j, l] for i in range(3) for j in range(3)], axis=0)
        sums.append(jnp.dot(lhs, rhs, preferred_element_type=F32))
    for row in range(n_rows):
        left, mid, right = (s[row * cols : (row + 1) * cols] for s in sums)
        left = jnp.where(column == 0, left, pltpu.roll(left, 1, 0))
        right = jnp.where(column == cols - 1, right, pltpu.roll(right, cols - 1, 0))
        yield row, left + mid + right


def put_hidden(hidden, frame, row, value, sums):
    rounded = value.astype(BF16)
    hidden[frame, row] = rounded
    return add_stats(sums, rounded.astype(F32))


def late_kernel(n_tables, n_sides, aux, *refs):
    tables, frames, refs = refs[:n_tables], refs[n_tables], refs[n_tables + 1 :]
    sides, taps = refs[:n_sides], refs[n_sides]
    hidden, act_low, stats, affine_out, *edges, act_high = refs[n_sides + 1 :]
    n_frames = frames.shape[0]
    low = act_low.shape[0]
    affine = half_affine(tables, aux, 0)
    for k in range(2):
        affine_out[k : k + 1] = affine[k]
    planes = [(act_low, f) for f in range(low)] + [(act_high, f) for f in range(n_frames - low)]
    for frame, (act, index) in enumerate(planes):
        for row in range(frames.shape[1] + 2):
            act[index, row] = normed(extended_row(frames, sides, frame, row), affine)
    sums = no_stats(frames.shape[3])
    for frame in range(n_frames - 2):
        for row, value in conv_rows(planes[frame : frame + 3], taps):
            sums = put_hidden(hidden, frame, row, value, sums)
        send_rows(hidden, frame, edges)
    store_stats(stats, sums)


def early_kernel(n_sides, aux, before, *refs):
    corners, (act_low, affine_in, stats_in, taps) = refs[:n_sides], refs[n_sides : n_sides + 4]
    hidden, stats, *edges, act_before = refs[n_sides + 4 :]
    slabs = aux.shape[0] - 8
    starting = aux[slabs : slabs + 1] != 0.0
    affine = affine_in[0:1], affine_in[1:2]
    for frame in range(2):
        for row in range(before.shape[1] + 2):
            value = normed(extended_row(before, corners, frame, row), affine).astype(F32)
            act_before[frame, row] = jnp.where(starting, act_low[0, row].astype(F32), value).astype(BF16)
    planes = [(act_before, 0), (act_before, 1)] + [(act_low, f) for f in range(act_low.shape[0])]
    sums = no_stats(before.shape[3])
    for frame in range(2):
        for row, value in conv_rows(planes[frame : frame + 3], taps):
            sums = put_hidden(hidden, frame, row, value, sums)
        send_rows(hidden, frame, edges)
    store_stats(stats, sums, stats_in)


def last_kernel(n_tables, n_sides, aux, *refs):
    tables, early, late, refs = refs[:n_tables], refs[n_tables], refs[n_tables + 1], refs[n_tables + 2 :]
    sides_early, sides_late = refs[:n_sides], refs[n_sides : 2 * n_sides]
    before, *corners = refs[2 * n_sides : 3 * n_sides + 1]
    taps, feats, out_hbm, act, out, sems = refs[3 * n_sides + 1 :]
    stores = [pltpu.make_async_copy(out.at[f], out_hbm.at[f], sems.at[f]) for f in range(out.shape[0])]
    slabs = aux.shape[0] - 8
    starting = aux[slabs : slabs + 1] != 0.0
    affine = half_affine(tables, aux, 1)
    n_frames, n_rows = out.shape[:2]

    def fill(frame):
        for row in range(n_rows + 2):
            if frame < 2:
                value = normed(extended_row(before, corners, frame, row), affine).astype(F32)
                act[frame, row] = jnp.where(starting, act[2, row].astype(F32), value).astype(BF16)
            elif frame < 4:
                act[frame, row] = normed(extended_row(early, sides_early, frame - 2, row), affine)
            else:
                act[frame, row] = normed(extended_row(late, sides_late, frame - 4, row), affine)

    for frame in range(2, n_frames + 2):
        fill(frame)
    for frame in list(range(2, n_frames)) + [0, 1]:
        if frame == 0:
            fill(0)
            fill(1)
        for row, value in conv_rows([(act, frame + i) for i in range(3)], taps):
            out[frame, row] = feats[frame, row].astype(F32) + value
        stores[frame].start()
    for store in stores:
        store.wait()


def call(kernel, outs, scratch, frames, *operands):
    return pl.pallas_call(
        kernel,
        out_shape=outs,
        in_specs=[VMEM] * len(operands),
        out_specs=[VMEM] * len(outs) if isinstance(outs, list) else ANYWHERE,
        scratch_shapes=scratch,
        compiler_params=vmem_params(),
        cost_estimate=pl.CostEstimate(flops=54 * frames * 384 * 65536, bytes_accessed=1 << 20, transcendentals=1 << 20),
    )(*operands)


def on_device(feats, clip_ids, gain_one, shift_one, kernel_one, gain_two, shift_two, kernel_two):
    n_frames, n_rows, cols, width = feats.shape
    params = (gain_one, shift_one, gain_two, shift_two)
    frames, tail, stats, edges = entry_call(feats)
    before, corners, _ = slab_halo(tail)
    total, tables = slab_tables(stats)
    sides = row_halo(edges)
    per_slab = feats.size // GROUPS * lax.axis_size("space")
    taps, aux = setup_call(kernel_one, clip_ids, params, per_slab, total)
    n_sides = len(sides)
    plane = (n_rows + 2, cols, width)
    late = n_frames - 2
    hidden_late, act_low, stats, affine, *edges = call(
        functools.partial(late_kernel, len(tables), n_sides),
        [shaped((late, n_rows, cols, width)), shaped((2,) + plane), shaped((8, 2 * width), F32), shaped((2, width), F32)]
        + edge_shapes(feats, late),
        [pltpu.VMEM((late,) + plane, BF16)],
        late, aux, *tables, frames, *sides, taps,
    )
    sides_late = row_halo(edges)
    hidden_early, stats, *edges = call(
        functools.partial(early_kernel, n_sides),
        [shaped((2, n_rows, cols, width)), shaped((8, 2 * width), F32)] + edge_shapes(feats, 2),
        [pltpu.VMEM((2,) + plane, BF16)],
        2, aux, before, *corners, act_low, affine, stats, taps,
    )
    sides_early = row_halo(edges)
    total, tables = slab_tables(stats)
    before, corners, tables[0] = slab_halo(hidden_late[late - 2 :], tables[0])
    return call(
        functools.partial(last_kernel, len(tables), n_sides),
        shaped(feats.shape, F32),
        [pltpu.VMEM((n_frames + 2,) + plane, BF16), pltpu.VMEM(feats.shape, F32), pltpu.SemaphoreType.DMA((n_frames,))],
        n_frames, aux, *tables, hidden_early, hidden_late, *sides_early, *sides_late, before, *corners, kernel_two, frames,
    )


def solution(mesh):
    return jax.shard_map(
        on_device,
        mesh=mesh,
        in_specs=(P("tm", "space", None, None), P(), P(), P(), P(), P(), P(), P()),
        out_specs=P("tm", "space", None, None),
        check_vma=False,
    )
```

```python
import functools

import jax
import jax.numpy as jnp
from jax import lax
from jax.experimental import pallas as pl
from jax.experimental.pallas import tpu as pltpu
from jax.sharding import PartitionSpec as P

GROUPS = 32
AXES = ("tm", "space")
TAIL = 2
F32, BF16 = jnp.float32, jnp.bfloat16


def vmem_params():
    return pltpu.CompilerParams(vmem_limit_bytes=32 << 20)


def shaped(shape, dtype=BF16):
    return jax.ShapeDtypeStruct(tuple(shape), dtype)


def in_hbm(value):
    return pltpu.with_memory_space_constraint(value, pltpu.HBM)


VMEM = pl.BlockSpec(memory_space=pltpu.VMEM)
ANYWHERE = pl.BlockSpec(memory_space=pl.ANY)


def traded(value, axis, mask):
    return lax.ppermute(value, axis, [(i, i ^ mask) for i in range(lax.axis_size(axis))])


def shifted(value, axis, step):
    peers = lax.axis_size(axis)
    return lax.ppermute(value, axis, [(i, (i + step) % peers) for i in range(peers)])


def group_sizes(peers):
    sizes = []
    while peers > 1:
        sizes.append(min(4, peers))
        peers //= sizes[-1]
    return sizes


def slab_offsets(peers):
    offsets, left = [0], peers
    for ways in group_sizes(peers):
        left //= ways
        offsets = [(left * way) ^ offset for way in range(ways) for offset in offsets]
    return offsets


def chip_pairs(place, target):
    slabs = lax.axis_size("tm")
    return [(t * 2 + s, (target(t) if s == place else t) * 2 + s) for t in range(slabs) for s in range(2)]


def slab_tables(stats, tail, beside=None):
    peers = lax.axis_size("tm")
    shared = lax.axis_size("space") == 2
    total = stats + traded(stats, "space", 1) if shared else lax.psum(stats, "space")
    first, total = lax.optimization_barrier((tail, total))
    done = () if beside is None else beside(total)
    arrived = [lax.ppermute(first, AXES, chip_pairs(0, lambda t: (t + 1) % peers)) if shared else shifted(first, "tm", 1)]
    held, left = [total], peers
    for ways in group_sizes(peers):
        left //= ways
        block = held[0] if len(held) == 1 else jnp.concatenate(held, axis=0)
        held = [block]
        for way in range(1, ways):
            mask = left * way
            held.append(lax.ppermute(block, AXES, chip_pairs(1, lambda t: t ^ mask)) if shared else traded(block, "tm", mask))
    if shared:
        second, _ = lax.optimization_barrier((tail, held[0]))
        table, arrived[0], *done = lax.optimization_barrier((jnp.concatenate(held, axis=0), arrived[0], *done))
        arrived.append(lax.ppermute(second, AXES, chip_pairs(1, lambda t: (t + 1) % peers)))
        held = [jnp.where(lax.axis_index("space") == 0, traded(table, "space", 1), table)]
    return held, arrived, done


def corner_rows(arrived):
    if len(arrived) == 1:
        return row_halo(edges_of(arrived[0]))
    upper, lower = arrived
    edge = jnp.where(lax.axis_index("space") == 0, upper[:, upper.shape[1] - 1 :], lower[:, :1])
    return [traded(edge, "space", 1)]


def row_halo(edges):
    if lax.axis_size("space") == 2:
        return [traded(edges[0], "space", 1)]
    top, bottom = edges
    return [shifted(bottom, "space", 1), shifted(top, "space", -1)]


def edges_of(frames):
    rows = frames.shape[1]
    if lax.axis_size("space") == 2:
        return [lax.dynamic_slice_in_dim(frames, (rows - 1) * (1 - lax.axis_index("space")), 1, axis=1)]
    return [frames[:, :1], frames[:, rows - 1 :]]


def edge_shapes(frames, count):
    shape = (count, 1) + frames.shape[2:]
    return [shaped(shape)] * (1 if lax.axis_size("space") == 2 else 2)


def send_rows(source, frame, edges):
    rows = source.shape[1]
    if len(edges) == 1:
        edges[0][frame, 0] = jnp.where(lax.axis_index("space") == 0, source[frame, rows - 1], source[frame, 0])
    else:
        edges[0][frame, 0] = source[frame, 0]
        edges[1][frame, 0] = source[frame, rows - 1]


def add_stats(sums, values):
    width = values.shape[1]
    return (
        sums[0] + jnp.sum(values.reshape(-1, 8, width), axis=0),
        sums[1] + jnp.sum((values * values).reshape(-1, 8, width), axis=0),
    )


def no_stats(width):
    return jnp.zeros((8, width), F32), jnp.zeros((8, width), F32)


def store_stats(stats, sums, base=None):
    width = sums[0].shape[1]
    for k in range(2):
        part = jnp.sum(sums[k], axis=0, keepdims=True)
        stats[:, k * width : (k + 1) * width] = part if base is None else part + base[:, k * width : (k + 1) * width]


def entry_kernel(feats_hbm, frames, tail, stats, *rest):
    *edges, sems = rest
    n_frames, n_rows, _, width = frames.shape
    loads = [pltpu.make_async_copy(feats_hbm.at[f], frames.at[f], sems.at[f]) for f in range(n_frames)]
    for copy in loads:
        copy.start()
    sums = no_stats(width)
    for frame in range(n_frames):
        loads[frame].wait()
        for row in range(n_rows):
            if frame >= n_frames - TAIL:
                tail[frame - n_frames + TAIL, row] = frames[frame, row]
            sums = add_stats(sums, frames[frame, row].astype(F32))
        send_rows(frames, frame, edges)
    store_stats(stats, sums)


def entry_call(feats):
    n_frames, width = feats.shape[0], feats.shape[3]
    outs = [shaped(feats.shape), shaped((TAIL,) + feats.shape[1:]), shaped((1, 2 * width), F32)]
    outs += edge_shapes(feats, n_frames)
    frames, tail, stats, *edges = pl.pallas_call(
        entry_kernel,
        out_shape=outs,
        in_specs=[ANYWHERE],
        out_specs=[VMEM] * len(outs),
        scratch_shapes=[pltpu.SemaphoreType.DMA((n_frames,))],
        compiler_params=vmem_params(),
        cost_estimate=pl.CostEstimate(flops=4 * feats.size, bytes_accessed=4 * feats.size, transcendentals=0),
    )(in_hbm(feats))
    return frames, tail, stats, edges


def setup_kernel(slabs, per_slab, kernel_hbm, clips_hbm, *refs):
    params_hbm, (_, taps, aux, params, clips, sems) = refs[:4], refs[4:]
    width = aux.shape[1]
    clip_load = pltpu.make_async_copy(clips_hbm, clips, sems.at[0])
    param_loads = [pltpu.make_async_copy(p, params.at[k], sems.at[1 + k]) for k, p in enumerate(params_hbm)]
    taps_load = pltpu.make_async_copy(kernel_hbm, taps, sems.at[5])
    for copy in [clip_load, *param_loads, taps_load]:
        copy.start()
    clip_load.wait()
    own = lax.axis_index("tm")
    own_clip = clips[own]
    slabs_in = jnp.int32(0)
    for entry, offset in enumerate(slab_offsets(slabs)):
        same = (clips[own ^ offset] == own_clip).astype(jnp.int32)
        slabs_in = slabs_in + same
        aux[entry : entry + 1] = jnp.full((1, width), same.astype(F32), F32)
    starting = jnp.logical_or(own == 0, clips[jnp.maximum(own - 1, 0)] != own_clip)
    aux[slabs : slabs + 1] = jnp.full((1, width), starting.astype(F32), F32)
    aux[slabs + 1 : slabs + 2] = jnp.full((1, width), slabs_in.astype(F32) * float(per_slab), F32)
    for k, copy in enumerate(param_loads):
        copy.wait()
        aux[slabs + 2 + k : slabs + 3 + k] = params[k]
    aux[slabs + 6 : slabs + 8] = jnp.zeros((2, width), F32)
    taps_load.wait()


def setup_call(kernel, clip_ids, params, per_slab, after):
    slabs, width = lax.axis_size("tm"), params[0].shape[0]
    return pl.pallas_call(
        functools.partial(setup_kernel, slabs, per_slab),
        out_shape=[shaped(kernel.shape), shaped((slabs + 8, width), F32)],
        in_specs=[ANYWHERE] * 7,
        out_specs=[VMEM, VMEM],
        scratch_shapes=[
            pltpu.VMEM((4, 1, width), F32),
            pltpu.SMEM(clip_ids.shape, jnp.int32),
            pltpu.SemaphoreType.DMA((6,)),
        ],
        compiler_params=vmem_params(),
        cost_estimate=pl.CostEstimate(flops=0, bytes_accessed=4 * kernel.size, transcendentals=0),
    )(*[in_hbm(x) for x in (kernel, clip_ids, *[p[None] for p in params])], after)


def group_total(values):
    width = values.shape[-1]
    lane = lax.broadcasted_iota(jnp.int32, values.shape, 1)
    step = 1
    while step < width // GROUPS:
        upper = pltpu.roll(values, step, 1)
        lower = pltpu.roll(values, width - step, 1)
        values = values + jnp.where((lane & step) != 0, upper, lower)
        step *= 2
    return values


def half_affine(tables, aux, which):
    width = aux.shape[1]
    slabs = aux.shape[0] - 8
    sums = [jnp.zeros((1, width), F32)] * 2
    entry = 0
    for table in tables:
        mask = aux[entry : entry + table.shape[0]]
        entry += table.shape[0]
        sums = [
            total + jnp.sum(table[:, k * width : (k + 1) * width] * mask, axis=0, keepdims=True) for k, total in enumerate(sums)
        ]
    grouped = group_total(jnp.concatenate(sums, axis=0))
    count = aux[slabs + 1 : slabs + 2]
    gain = aux[slabs + 2 + 2 * which : slabs + 3 + 2 * which]
    shift = aux[slabs + 3 + 2 * which : slabs + 4 + 2 * which]
    mean = grouped[0:1] / count
    variance = grouped[1:2] / count - mean * mean
    scale = lax.rsqrt(variance + 1e-06) * gain
    return 0.5 * scale, 0.5 * (shift - mean * scale)


def normed(raw, affine):
    half = raw.astype(F32) * affine[0] + affine[1]
    return (half * jnp.tanh(half) + half).astype(BF16)


def extended_row(frames, sides, frame, row):
    frames = frames if isinstance(frames, (list, tuple)) else [frames]
    n_rows = frames[0].shape[1]
    place, places = lax.axis_index("space"), lax.axis_size("space")
    inner = [ref[frame, min(max(row - 1, 0), n_rows - 1)] for ref in frames]
    inner = inner[0] if len(inner) == 1 else jnp.where(place == 0, inner[0], inner[1])
    if 0 < row <= n_rows:
        return inner
    side = sides[0 if row == 0 else -1]
    return jnp.where(place == (0 if row == 0 else places - 1), inner, side[frame, 0])


def conv_rows(planes, taps):
    ref, index = planes[0]
    n_rows, cols, width = ref.shape[1] - 2, ref.shape[2], ref.shape[3]
    lhs = jnp.concatenate(
        [ref[index, j : j + n_rows].reshape(n_rows * cols, width) for ref, index in planes for j in range(3)], axis=1
    )
    column = lax.broadcasted_iota(jnp.int32, (cols, width), 0)
    sums = []
    for l in range(3):
        rhs = jnp.concatenate([taps[i, j, l] for i in range(3) for j in range(3)], axis=0)
        sums.append(jnp.dot(lhs, rhs, preferred_element_type=F32))
    for row in range(n_rows):
        left, mid, right = (s[row * cols : (row + 1) * cols] for s in sums)
        left = jnp.where(column == 0, left, pltpu.roll(left, 1, 0))
        right = jnp.where(column == cols - 1, right, pltpu.roll(right, cols - 1, 0))
        yield row, left + mid + right


def put_hidden(hidden, frame, row, value, sums):
    rounded = value.astype(BF16)
    hidden[frame, row] = rounded
    return add_stats(sums, rounded.astype(F32))


def late_kernel(n_tables, n_sides, which, aux, *refs):
    tables, frames, refs = refs[:n_tables], refs[n_tables], refs[n_tables + 1 :]
    early_sides, late_sides, taps = refs[:n_sides], refs[n_sides : 2 * n_sides], refs[2 * n_sides]
    if which == 0:
        act_low, affine_out, hidden, stats, *edges, act_high = refs[2 * n_sides + 1 :]
        early = late = frames
        late_first = 0
    else:
        late, feats, act_low, affine_out, out_hbm, act_high, out, sems = refs[2 * n_sides + 1 :]
        early, late_first = frames, frames.shape[0]
    n_rows, width = frames.shape[1], frames.shape[3]
    low, high = act_low.shape[0], act_high.shape[0]
    affine = half_affine(tables, aux, which)
    for k in range(2):
        affine_out[k : k + 1] = affine[k]
    planes = [(act_low, f) for f in range(low)] + [(act_high, f) for f in range(high)]
    for frame, (act, index) in enumerate(planes):
        for row in range(n_rows + 2):
            if which == 0 or frame < 2:
                value = extended_row(early, early_sides, frame, row)
            else:
                value = extended_row(late, late_sides, frame - late_first, row)
            act[index, row] = normed(value, affine)
    sums = no_stats(width)
    stores = []
    for frame in range(high):
        for row, value in conv_rows(planes[frame : frame + 3], taps):
            if which == 0:
                sums = put_hidden(hidden, frame, row, value, sums)
            else:
                out[frame, row] = feats[low + frame, row].astype(F32) + value
        if which == 0:
            send_rows(hidden, frame, edges)
        else:
            stores.append(pltpu.make_async_copy(out.at[frame], out_hbm.at[low + frame], sems.at[frame]))
            stores[-1].start()
    if which == 0:
        store_stats(stats, sums)
    for store in stores:
        store.wait()


def early_kernel(n_sides, n_before, which, aux, *refs):
    before, corners = refs[:n_before], refs[n_before : n_before + n_sides]
    act_low, affine_in, taps, *refs = refs[n_before + n_sides :]
    if which == 0:
        stats_in, hidden, stats, *edges, act_before = refs
    else:
        feats, _, out_hbm, act_before, out, sems = refs
    slabs = aux.shape[0] - 8
    starting = aux[slabs : slabs + 1] != 0.0
    affine = affine_in[0:1], affine_in[1:2]
    for frame in range(2):
        for row in range(act_low.shape[1]):
            value = normed(extended_row(before, corners, frame, row), affine).astype(F32)
            act_before[frame, row] = jnp.where(starting, act_low[0, row].astype(F32), value).astype(BF16)
    planes = [(act_before, 0), (act_before, 1)] + [(act_low, f) for f in range(act_low.shape[0])]
    sums = no_stats(act_low.shape[3])
    stores = []
    for frame in range(2):
        for row, value in conv_rows(planes[frame : frame + 3], taps):
            if which == 0:
                sums = put_hidden(hidden, frame, row, value, sums)
            else:
                out[frame, row] = feats[frame, row].astype(F32) + value
        if which == 0:
            send_rows(hidden, frame, edges)
        else:
            stores.append(pltpu.make_async_copy(out.at[frame], out_hbm.at[frame], sems.at[frame]))
            stores[-1].start()
    if which == 0:
        store_stats(stats, sums, stats_in)
    for store in stores:
        store.wait()


def call(kernel, outs, scratch, frames, operands, out_specs=None, aliases=None):
    return pl.pallas_call(
        kernel,
        out_shape=outs,
        in_specs=[VMEM if aliases is None or k not in aliases else ANYWHERE for k in range(len(operands))],
        out_specs=[VMEM] * len(outs) if out_specs is None else out_specs,
        scratch_shapes=scratch,
        input_output_aliases=aliases or {},
        compiler_params=vmem_params(),
        cost_estimate=pl.CostEstimate(flops=54 * frames * 384 * 65536, bytes_accessed=1 << 20, transcendentals=1 << 20),
    )(*operands)


def on_device(feats, clip_ids, gain_one, shift_one, kernel_one, gain_two, shift_two, kernel_two):
    n_frames, n_rows, cols, width = feats.shape
    params = (gain_one, shift_one, gain_two, shift_two)
    per_slab = feats.size // GROUPS * lax.axis_size("space")
    late = n_frames - 2
    plane = (n_rows + 2, cols, width)
    act = pltpu.VMEM((2,) + plane, BF16)
    act_late = pltpu.VMEM((late,) + plane, BF16)
    act_shapes = [shaped((2,) + plane), shaped((2, width), F32)]
    stats_shape = shaped((1, 2 * width), F32)

    frames, tail, stats, edges = entry_call(feats)
    setup = functools.partial(setup_call, kernel_one, clip_ids, params, per_slab)
    tables, before, (taps, aux) = slab_tables(stats, tail, setup)
    sides = row_halo(edges)
    n_sides = len(sides)
    act_low, affine, hidden_late, stats, *edges = call(
        functools.partial(late_kernel, len(tables), n_sides, 0),
        act_shapes + [shaped((late, n_rows, cols, width)), stats_shape] + edge_shapes(feats, late),
        [act_late],
        late,
        [aux, *tables, frames, *sides, *sides, taps],
    )
    *before, affine = lax.optimization_barrier((*before, affine))
    corners = corner_rows(before)
    sides_late = row_halo(edges)
    hidden_early, stats, *edges = call(
        functools.partial(early_kernel, n_sides, len(before), 0),
        [shaped((2, n_rows, cols, width)), stats_shape] + edge_shapes(feats, 2),
        [act],
        2,
        [aux, *before, *corners, act_low, affine, taps, stats],
    )

    sides_early = row_halo(edges)
    tables, before, _ = slab_tables(stats, hidden_late[late - 2 :])
    act_low, affine, out = call(
        functools.partial(late_kernel, len(tables), n_sides, 1),
        act_shapes + [shaped(feats.shape, F32)],
        [act_late, pltpu.VMEM((late, n_rows, cols, width), F32), pltpu.SemaphoreType.DMA((late,))],
        late,
        [aux, *tables, hidden_early, *sides_early, *sides_late, kernel_two, hidden_late, frames],
        out_specs=[VMEM, VMEM, ANYWHERE],
    )
    *before, affine = lax.optimization_barrier((*before, affine))
    corners = corner_rows(before)
    operands = [aux, *before, *corners, act_low, affine, kernel_two, frames, out]
    return call(
        functools.partial(early_kernel, n_sides, len(before), 1),
        shaped(feats.shape, F32),
        [act, pltpu.VMEM((2, n_rows, cols, width), F32), pltpu.SemaphoreType.DMA((2,))],
        2,
        operands,
        out_specs=ANYWHERE,
        aliases={len(operands) - 1: 0},
    )


def solution(mesh):
    return jax.shard_map(
        on_device,
        mesh=mesh,
        in_specs=(P("tm", "space", None, None), P(), P(), P(), P(), P(), P(), P()),
        out_specs=P("tm", "space", None, None),
        check_vma=False,
    )
```

```python
import functools

import jax
import jax.numpy as jnp
from jax import lax
from jax.experimental import pallas as pl
from jax.experimental.pallas import tpu as pltpu
from jax.sharding import PartitionSpec as P

GROUPS = 32
TAIL = 2
F32, BF16 = jnp.float32, jnp.bfloat16


def vmem_params():
    return pltpu.CompilerParams(vmem_limit_bytes=32 << 20)


def shaped(shape, dtype=BF16):
    return jax.ShapeDtypeStruct(tuple(shape), dtype)


def in_hbm(value):
    return pltpu.with_memory_space_constraint(value, pltpu.HBM)


VMEM = pl.BlockSpec(memory_space=pltpu.VMEM)
ANYWHERE = pl.BlockSpec(memory_space=pl.ANY)


def traded(value, axis, mask):
    return lax.ppermute(value, axis, [(i, i ^ mask) for i in range(lax.axis_size(axis))])


def shifted(value, axis, step):
    peers = lax.axis_size(axis)
    return lax.ppermute(value, axis, [(i, (i + step) % peers) for i in range(peers)])


def stats_table(copies):
    return lax.all_to_all(copies, ("tm", "space"), 0, 0, tiled=True)


def corner_rows(before, after):
    before, after = lax.optimization_barrier((before, after))
    return before, row_halo(edges_of(before)), after


def row_halo(edges):
    if lax.axis_size("space") == 2:
        return [traded(edges, "space", 1)]
    return [shifted(edges[:, 1:], "space", 1), shifted(edges[:, :1], "space", -1)]


def edges_of(frames):
    rows = frames.shape[1]
    if lax.axis_size("space") == 2:
        return lax.dynamic_slice_in_dim(frames, (rows - 1) * (1 - lax.axis_index("space")), 1, axis=1)
    return jnp.concatenate([frames[:, :1], frames[:, rows - 1 :]], axis=1)


def edge_shape(frames, count):
    return (count, 1 if lax.axis_size("space") == 2 else 2) + frames.shape[2:]


def send_rows(source, frame, edges, at=0):
    rows = source.shape[1]
    if edges.shape[1] == 1:
        low = lax.axis_index("space") == 0
        edges[at + frame, 0] = jnp.where(low, source[frame, rows - 1], source[frame, 0])
    else:
        edges[at + frame, 0] = source[frame, 0]
        edges[at + frame, 1] = source[frame, rows - 1]


def add_stats(sums, values):
    width = values.shape[1]
    return (
        sums[0] + jnp.sum(values.reshape(-1, 8, width), axis=0),
        sums[1] + jnp.sum((values * values).reshape(-1, 8, width), axis=0),
    )


def no_stats(width):
    return jnp.zeros((8, width), F32), jnp.zeros((8, width), F32)


def store_stats(stats, sums):
    width = sums[0].shape[1]
    for k in range(2):
        stats[:, k * width : (k + 1) * width] = jnp.sum(sums[k], axis=0, keepdims=True)


def store_copies(copies, stats):
    copies[...] = jnp.broadcast_to(stats[...][None], copies.shape)


def device_count():
    return lax.axis_size("tm") * lax.axis_size("space")


def entry_kernel(feats_hbm, frames, tail, edges, copies, mark, stats, sems):
    n_frames, n_rows, _, width = frames.shape
    loads = [pltpu.make_async_copy(feats_hbm.at[f], frames.at[f], sems.at[f]) for f in range(n_frames)]
    for copy in loads:
        copy.start()
    mark[...] = jnp.zeros_like(mark)
    sums = no_stats(width)
    for frame in range(n_frames):
        loads[frame].wait()
        for row in range(n_rows):
            if frame >= n_frames - TAIL:
                tail[frame - n_frames + TAIL, row] = frames[frame, row]
            sums = add_stats(sums, frames[frame, row].astype(F32))
        send_rows(frames, frame, edges)
    store_stats(stats, sums)
    store_copies(copies, stats)


def copies_shape(width):
    return shaped((device_count(), 1, 2 * width), F32)


MARK = jax.ShapeDtypeStruct((8, 128), F32)


def entry_call(feats):
    n_frames, width = feats.shape[0], feats.shape[3]
    outs = [
        shaped(feats.shape),
        shaped((TAIL,) + feats.shape[1:]),
        shaped(edge_shape(feats, n_frames)),
        copies_shape(width),
        MARK,
    ]
    return pl.pallas_call(
        entry_kernel,
        out_shape=outs,
        in_specs=[ANYWHERE],
        out_specs=[VMEM] * len(outs),
        scratch_shapes=[pltpu.VMEM((1, 2 * width), F32), pltpu.SemaphoreType.DMA((n_frames,))],
        compiler_params=vmem_params(),
        cost_estimate=pl.CostEstimate(flops=4 * feats.size, bytes_accessed=4 * feats.size, transcendentals=0),
    )(in_hbm(feats))


def passed_kernel(before, after):
    after[...] = before[...]


def passed(mark):
    return pl.pallas_call(
        passed_kernel,
        out_shape=MARK,
        in_specs=[VMEM],
        out_specs=VMEM,
        compiler_params=vmem_params(),
        cost_estimate=pl.CostEstimate(flops=1 << 32, bytes_accessed=8192, transcendentals=0),
    )(mark)


def setup_kernel(slabs, per_slab, clips_hbm, *refs):
    params_hbm, (_, aux, params, clips, sems) = refs[:4], refs[4:]
    width = aux.shape[1]
    clip_load = pltpu.make_async_copy(clips_hbm, clips, sems.at[0])
    param_loads = [pltpu.make_async_copy(p, params.at[k], sems.at[1 + k]) for k, p in enumerate(params_hbm)]
    for copy in [clip_load, *param_loads]:
        copy.start()
    clip_load.wait()
    own = lax.axis_index("tm")
    own_clip = clips[own]
    slabs_in = jnp.int32(0)
    for slab in range(slabs):
        same = (clips[slab] == own_clip).astype(jnp.int32)
        slabs_in = slabs_in + same
        aux[slab : slab + 1] = jnp.full((1, width), same.astype(F32), F32)
    starting = jnp.logical_or(own == 0, clips[jnp.maximum(own - 1, 0)] != own_clip)
    aux[slabs : slabs + 1] = jnp.full((1, width), starting.astype(F32), F32)
    aux[slabs + 1 : slabs + 2] = jnp.full((1, width), slabs_in.astype(F32) * float(per_slab), F32)
    for k, copy in enumerate(param_loads):
        copy.wait()
        aux[slabs + 2 + k : slabs + 3 + k] = params[k]
    aux[slabs + 6 : slabs + 8] = jnp.zeros((2, width), F32)


def setup_call(clip_ids, params, per_slab, mark):
    slabs, width = lax.axis_size("tm"), params[0].shape[0]
    return pl.pallas_call(
        functools.partial(setup_kernel, slabs, per_slab),
        out_shape=shaped((slabs + 8, width), F32),
        in_specs=[ANYWHERE] * 5 + [VMEM],
        out_specs=VMEM,
        scratch_shapes=[
            pltpu.VMEM((4, 1, width), F32),
            pltpu.SMEM(clip_ids.shape, jnp.int32),
            pltpu.SemaphoreType.DMA((5,)),
        ],
        compiler_params=vmem_params(),
        cost_estimate=pl.CostEstimate(flops=1 << 30, bytes_accessed=1 << 16, transcendentals=0),
    )(*[in_hbm(x) for x in (clip_ids, *[p[None] for p in params])], mark)


def group_total(values):
    width = values.shape[-1]
    lane = lax.broadcasted_iota(jnp.int32, values.shape, 1)
    step = 1
    while step < width // GROUPS:
        upper = pltpu.roll(values, step, 1)
        lower = pltpu.roll(values, width - step, 1)
        values = values + jnp.where((lane & step) != 0, upper, lower)
        step *= 2
    return values


def half_affine(table, aux, which):
    width = aux.shape[1]
    slabs = aux.shape[0] - 8
    places = table.shape[0] // slabs
    sums = []
    for k in range(2):
        parts = [
            aux[slab : slab + 1] * sum(table[slab * places + p, :, k * width : (k + 1) * width] for p in range(places))
            for slab in range(slabs)
        ]
        while len(parts) > 1:
            parts = [sum(parts[i : i + 2]) for i in range(0, len(parts), 2)]
        sums += parts
    grouped = group_total(jnp.concatenate(sums, axis=0))
    count = aux[slabs + 1 : slabs + 2]
    gain = aux[slabs + 2 + 2 * which : slabs + 3 + 2 * which]
    shift = aux[slabs + 3 + 2 * which : slabs + 4 + 2 * which]
    mean = grouped[0:1] / count
    variance = grouped[1:2] / count - mean * mean
    scale = lax.rsqrt(variance + 1e-06) * gain
    return 0.5 * scale, 0.5 * (shift - mean * scale)


def normed(raw, affine):
    half = raw.astype(F32) * affine[0] + affine[1]
    return (half * jnp.tanh(half) + half).astype(BF16)


def extended_row(frames, sides, frame, row):
    n_rows = frames.shape[1]
    inner = frames[frame, min(max(row - 1, 0), n_rows - 1)]
    if 0 < row <= n_rows:
        return inner
    place, places = lax.axis_index("space"), lax.axis_size("space")
    side = sides[0 if row == 0 else -1]
    return jnp.where(place == (0 if row == 0 else places - 1), inner, side[frame, 0])


def conv_rows(planes, taps, loads=None):
    ref, index = planes[0]
    n_rows, cols, width = ref.shape[1] - 2, ref.shape[2], ref.shape[3]
    lhs = jnp.concatenate(
        [ref[index, j : j + n_rows].reshape(n_rows * cols, width) for ref, index in planes for j in range(3)], axis=1
    )
    column = lax.broadcasted_iota(jnp.int32, (cols, width), 0)
    sums = []
    for l in range(3):
        if loads is not None:
            loads[l].wait()
        rhs = jnp.concatenate([taps[i, j, l] for i in range(3) for j in range(3)], axis=0)
        sums.append(jnp.dot(lhs, rhs, preferred_element_type=F32))
    for row in range(n_rows):
        left, mid, right = (s[row * cols : (row + 1) * cols] for s in sums)
        left = jnp.where(column == 0, left, pltpu.roll(left, 1, 0))
        right = jnp.where(column == cols - 1, right, pltpu.roll(right, cols - 1, 0))
        yield row, left + mid + right


def put_hidden(hidden, frame, row, value, sums):
    rounded = value.astype(BF16)
    hidden[frame, row] = rounded
    return add_stats(sums, rounded.astype(F32))


def late_kernel(n_sides, which, aux, table, _, frames, *refs):
    early_sides, late_sides, kernel_hbm = refs[:n_sides], refs[n_sides : 2 * n_sides], refs[2 * n_sides]
    if which == 0:
        act_low, affine_out, taps, hidden, stats, edges, act_high, taps_sems = refs[2 * n_sides + 1 :]
        early = late = frames
        late_first = 0
    else:
        late, feats, act_low, affine_out, taps, out_hbm, act_high, taps_sems, out, sems = refs[2 * n_sides + 1 :]
        early, late_first = frames, frames.shape[0]
    loads = [pltpu.make_async_copy(kernel_hbm.at[:, :, l], taps.at[:, :, l], taps_sems.at[l]) for l in range(3)]
    for copy in loads:
        copy.start()
    n_rows, width = frames.shape[1], frames.shape[3]
    low, high = act_low.shape[0], act_high.shape[0]
    affine = half_affine(table, aux, which)
    for k in range(2):
        affine_out[k : k + 1] = affine[k]
    planes = [(act_low, f) for f in range(low)] + [(act_high, f) for f in range(high)]
    for frame, (act, index) in enumerate(planes):
        for row in range(n_rows + 2):
            if which == 0 or frame < 2:
                value = extended_row(early, early_sides, frame, row)
            else:
                value = extended_row(late, late_sides, frame - late_first, row)
            act[index, row] = normed(value, affine)
    sums = no_stats(width)
    stores = []
    for frame in range(high):
        for row, value in conv_rows(planes[frame : frame + 3], taps, loads if frame == 0 else None):
            if which == 0:
                sums = put_hidden(hidden, frame, row, value, sums)
            else:
                out[frame, row] = feats[low + frame, row].astype(F32) + value
        if which == 0:
            send_rows(hidden, frame, edges)
        else:
            stores.append(pltpu.make_async_copy(out.at[frame], out_hbm.at[low + frame], sems.at[frame]))
            stores[-1].start()
    if which == 0:
        for k in range(2):
            stats[k] = sums[k]
    for store in stores:
        store.wait()


def early_kernel(n_sides, which, aux, before, *refs):
    corners, (act_low, affine_in, taps), refs = refs[:n_sides], refs[n_sides : n_sides + 3], refs[n_sides + 3 :]
    if which == 0:
        late_stats, hidden, edges, copies, mark, act_before, stats = refs
        mark[...] = jnp.zeros_like(mark)
        sums = late_stats[0], late_stats[1]
    else:
        feats, _, out_hbm, act_before, out, sems = refs
    slabs = aux.shape[0] - 8
    starting = aux[slabs : slabs + 1] != 0.0
    affine = affine_in[0:1], affine_in[1:2]
    for frame in range(2):
        for row in range(act_low.shape[1]):
            value = normed(extended_row(before, corners, frame, row), affine).astype(F32)
            act_before[frame, row] = jnp.where(starting, act_low[0, row].astype(F32), value).astype(BF16)
    planes = [(act_before, 0), (act_before, 1)] + [(act_low, f) for f in range(act_low.shape[0])]
    stores = []
    for frame in range(2):
        for row, value in conv_rows(planes[frame : frame + 3], taps):
            if which == 0:
                sums = put_hidden(hidden, frame, row, value, sums)
            else:
                out[frame, row] = feats[frame, row].astype(F32) + value
        if which == 0:
            send_rows(hidden, frame, edges)
        else:
            stores.append(pltpu.make_async_copy(out.at[frame], out_hbm.at[frame], sems.at[frame]))
            stores[-1].start()
    if which == 0:
        store_stats(stats, sums)
        store_copies(copies, stats)
    for store in stores:
        store.wait()


def call(kernel, outs, scratch, frames, operands, out_specs=None, aliases=None, outside=()):
    return pl.pallas_call(
        kernel,
        out_shape=outs,
        in_specs=[ANYWHERE if k in (aliases or {}) or k in outside else VMEM for k in range(len(operands))],
        out_specs=[VMEM] * len(outs) if out_specs is None else out_specs,
        scratch_shapes=scratch,
        input_output_aliases=aliases or {},
        compiler_params=vmem_params(),
        cost_estimate=pl.CostEstimate(flops=54 * frames * 384 * 65536, bytes_accessed=1 << 20, transcendentals=1 << 20),
    )(*operands)


def on_device(feats, clip_ids, gain_one, shift_one, kernel_one, gain_two, shift_two, kernel_two):
    n_frames, n_rows, cols, width = feats.shape
    params = (gain_one, shift_one, gain_two, shift_two)
    per_slab = feats.size // GROUPS * lax.axis_size("space")
    late = n_frames - 2
    plane = (n_rows + 2, cols, width)
    act = pltpu.VMEM((2,) + plane, BF16)
    act_late = pltpu.VMEM((late,) + plane, BF16)
    late_shapes = [shaped((2,) + plane), shaped((2, width), F32), shaped(kernel_one.shape)]
    hidden_shapes = [shaped((late, n_rows, cols, width)), shaped((2, 8, width), F32), shaped(edge_shape(feats, late))]
    taps_sems = pltpu.SemaphoreType.DMA((3,))

    frames, tail, edges, copies, mark = entry_call(feats)
    table = stats_table(copies)
    tail, edges, mark = lax.optimization_barrier((tail, edges, passed(mark)))
    before = shifted(tail, "tm", 1)
    sides = row_halo(edges)
    n_sides = len(sides)
    aux = setup_call(clip_ids, params, per_slab, mark)
    operands = [aux, table, mark, frames, *sides, *sides, in_hbm(kernel_one)]
    act_low, affine, taps, hidden_late, stats, edges_late = call(
        functools.partial(late_kernel, n_sides, 0),
        late_shapes + hidden_shapes,
        [act_late, taps_sems],
        late,
        operands,
        outside=(len(operands) - 1,),
    )
    before, corners, affine = corner_rows(before, affine)
    hidden_early, edges, copies, mark = call(
        functools.partial(early_kernel, n_sides, 0),
        [shaped((2, n_rows, cols, width)), shaped(edge_shape(feats, 2)), copies_shape(width), MARK],
        [act, pltpu.VMEM((1, 2 * width), F32)],
        2,
        [aux, before, *corners, act_low, affine, taps, stats],
    )

    table = stats_table(copies)
    tail, edges, edges_late, mark = lax.optimization_barrier((hidden_late[late - 2 :], edges, edges_late, passed(mark)))
    before = shifted(tail, "tm", 1)
    operands = [aux, table, mark, hidden_early, *row_halo(edges), *row_halo(edges_late), in_hbm(kernel_two), hidden_late, frames]
    act_low, affine, taps, out = call(
        functools.partial(late_kernel, n_sides, 1),
        late_shapes + [shaped(feats.shape, F32)],
        [act_late, taps_sems, pltpu.VMEM((late, n_rows, cols, width), F32), pltpu.SemaphoreType.DMA((late,))],
        late,
        operands,
        out_specs=[VMEM, VMEM, VMEM, ANYWHERE],
        outside=(len(operands) - 3,),
    )
    before, corners, affine = corner_rows(before, affine)
    operands = [aux, before, *corners, act_low, affine, taps, frames, out]
    return call(
        functools.partial(early_kernel, n_sides, 1),
        shaped(feats.shape, F32),
        [act, pltpu.VMEM((2, n_rows, cols, width), F32), pltpu.SemaphoreType.DMA((2,))],
        2,
        operands,
        out_specs=ANYWHERE,
        aliases={len(operands) - 1: 0},
    )


def solution(mesh):
    return jax.shard_map(
        on_device,
        mesh=mesh,
        in_specs=(P("tm", "space", None, None), P(), P(), P(), P(), P(), P(), P()),
        out_specs=P("tm", "space", None, None),
        check_vma=False,
    )
```

```python
import functools

import jax
import jax.numpy as jnp
from jax import lax
from jax.experimental import pallas as pl
from jax.experimental.pallas import tpu as pltpu
from jax.sharding import PartitionSpec as P

GROUPS = 32
TAIL = 2
F32, BF16 = jnp.float32, jnp.bfloat16


def vmem_params():
    return pltpu.CompilerParams(vmem_limit_bytes=32 << 20)


def shaped(shape, dtype=BF16):
    return jax.ShapeDtypeStruct(tuple(shape), dtype)


def in_hbm(value):
    return pltpu.with_memory_space_constraint(value, pltpu.HBM)


VMEM = pl.BlockSpec(memory_space=pltpu.VMEM)
ANYWHERE = pl.BlockSpec(memory_space=pl.ANY)


def traded(value, axis, mask):
    return lax.ppermute(value, axis, [(i, i ^ mask) for i in range(lax.axis_size(axis))])


def shifted(value, axis, step):
    peers = lax.axis_size(axis)
    return lax.ppermute(value, axis, [(i, (i + step) % peers) for i in range(peers)])


def stats_table(copies):
    return lax.all_to_all(copies, ("tm", "space"), 0, 0, tiled=True)


def corner_rows(before, after):
    before, after = lax.optimization_barrier((before, after))
    return before, row_halo(edges_of(before)), after


def row_halo(edges):
    if lax.axis_size("space") == 2:
        return [traded(edges, "space", 1)]
    return [shifted(edges[:, 1:], "space", 1), shifted(edges[:, :1], "space", -1)]


def edges_of(frames):
    rows = frames.shape[1]
    if lax.axis_size("space") == 2:
        return lax.dynamic_slice_in_dim(frames, (rows - 1) * (1 - lax.axis_index("space")), 1, axis=1)
    return jnp.concatenate([frames[:, :1], frames[:, rows - 1 :]], axis=1)


def edge_shape(frames, count):
    return (count, 1 if lax.axis_size("space") == 2 else 2) + frames.shape[2:]


def send_rows(source, frame, edges, at=0):
    rows = source.shape[1]
    if edges.shape[1] == 1:
        low = lax.axis_index("space") == 0
        edges[at + frame, 0] = jnp.where(low, source[frame, rows - 1], source[frame, 0])
    else:
        edges[at + frame, 0] = source[frame, 0]
        edges[at + frame, 1] = source[frame, rows - 1]


def add_stats(sums, values):
    width = values.shape[1]
    return (
        sums[0] + jnp.sum(values.reshape(-1, 8, width), axis=0),
        sums[1] + jnp.sum((values * values).reshape(-1, 8, width), axis=0),
    )


def no_stats(width):
    return jnp.zeros((8, width), F32), jnp.zeros((8, width), F32)


def store_stats(stats, sums):
    width = sums[0].shape[1]
    for k in range(2):
        stats[:, k * width : (k + 1) * width] = jnp.sum(sums[k], axis=0, keepdims=True)


def store_copies(copies, stats):
    copies[...] = jnp.broadcast_to(stats[...][None], copies.shape)


def device_count():
    return lax.axis_size("tm") * lax.axis_size("space")


def entry_kernel(feats_hbm, frames, tail, edges, copies, mark, stats, sems):
    n_frames, n_rows, _, width = frames.shape
    loads = [pltpu.make_async_copy(feats_hbm.at[f], frames.at[f], sems.at[f]) for f in range(n_frames)]
    for copy in loads:
        copy.start()
    mark[...] = jnp.zeros_like(mark)
    sums = no_stats(width)
    for frame in range(n_frames):
        loads[frame].wait()
        for row in range(n_rows):
            if frame >= n_frames - TAIL:
                tail[frame - n_frames + TAIL, row] = frames[frame, row]
            sums = add_stats(sums, frames[frame, row].astype(F32))
        send_rows(frames, frame, edges)
    store_stats(stats, sums)
    store_copies(copies, stats)


def copies_shape(width):
    return shaped((device_count(), 1, 2 * width), F32)


MARK = jax.ShapeDtypeStruct((8, 128), F32)


def entry_call(feats):
    n_frames, width = feats.shape[0], feats.shape[3]
    outs = [
        shaped(feats.shape),
        shaped((TAIL,) + feats.shape[1:]),
        shaped(edge_shape(feats, n_frames)),
        copies_shape(width),
        MARK,
    ]
    return pl.pallas_call(
        entry_kernel,
        out_shape=outs,
        in_specs=[ANYWHERE],
        out_specs=[VMEM] * len(outs),
        scratch_shapes=[pltpu.VMEM((1, 2 * width), F32), pltpu.SemaphoreType.DMA((n_frames,))],
        compiler_params=vmem_params(),
        cost_estimate=pl.CostEstimate(flops=4 * feats.size, bytes_accessed=4 * feats.size, transcendentals=0),
    )(in_hbm(feats))


def setup_kernel(slabs, per_slab, clips_hbm, *refs):
    params_hbm, (_, aux, params, clips, sems) = refs[:4], refs[4:]
    width = aux.shape[1]
    clip_load = pltpu.make_async_copy(clips_hbm, clips, sems.at[0])
    param_loads = [pltpu.make_async_copy(p, params.at[k], sems.at[1 + k]) for k, p in enumerate(params_hbm)]
    for copy in [clip_load, *param_loads]:
        copy.start()
    clip_load.wait()
    own = lax.axis_index("tm")
    own_clip = clips[own]
    slabs_in = jnp.int32(0)
    for slab in range(slabs):
        same = (clips[slab] == own_clip).astype(jnp.int32)
        slabs_in = slabs_in + same
        aux[slab : slab + 1] = jnp.full((1, width), same.astype(F32), F32)
    starting = jnp.logical_or(own == 0, clips[jnp.maximum(own - 1, 0)] != own_clip)
    aux[slabs : slabs + 1] = jnp.full((1, width), starting.astype(F32), F32)
    aux[slabs + 1 : slabs + 2] = jnp.full((1, width), slabs_in.astype(F32) * float(per_slab), F32)
    for k, copy in enumerate(param_loads):
        copy.wait()
        aux[slabs + 2 + k : slabs + 3 + k] = params[k]
    aux[slabs + 6 : slabs + 8] = jnp.zeros((2, width), F32)


def setup_call(clip_ids, params, per_slab, mark):
    slabs, width = lax.axis_size("tm"), params[0].shape[0]
    return pl.pallas_call(
        functools.partial(setup_kernel, slabs, per_slab),
        out_shape=shaped((slabs + 8, width), F32),
        in_specs=[ANYWHERE] * 5 + [VMEM],
        out_specs=VMEM,
        scratch_shapes=[
            pltpu.VMEM((4, 1, width), F32),
            pltpu.SMEM(clip_ids.shape, jnp.int32),
            pltpu.SemaphoreType.DMA((5,)),
        ],
        compiler_params=vmem_params(),
        cost_estimate=pl.CostEstimate(flops=1 << 30, bytes_accessed=1 << 16, transcendentals=0),
    )(*[in_hbm(x) for x in (clip_ids, *[p[None] for p in params])], mark)


def group_total(values):
    width = values.shape[-1]
    lane = lax.broadcasted_iota(jnp.int32, values.shape, 1)
    step = 1
    while step < width // GROUPS:
        upper = pltpu.roll(values, step, 1)
        lower = pltpu.roll(values, width - step, 1)
        values = values + jnp.where((lane & step) != 0, upper, lower)
        step *= 2
    return values


def half_affine(table, aux, which):
    width = aux.shape[1]
    slabs = aux.shape[0] - 8
    places = table.shape[0] // slabs
    sums = []
    for k in range(2):
        parts = [
            aux[slab : slab + 1] * sum(table[slab * places + p, :, k * width : (k + 1) * width] for p in range(places))
            for slab in range(slabs)
        ]
        while len(parts) > 1:
            parts = [sum(parts[i : i + 2]) for i in range(0, len(parts), 2)]
        sums += parts
    grouped = group_total(jnp.concatenate(sums, axis=0))
    count = aux[slabs + 1 : slabs + 2]
    gain = aux[slabs + 2 + 2 * which : slabs + 3 + 2 * which]
    shift = aux[slabs + 3 + 2 * which : slabs + 4 + 2 * which]
    mean = grouped[0:1] / count
    variance = grouped[1:2] / count - mean * mean
    scale = lax.rsqrt(variance + 1e-06) * gain
    return 0.5 * scale, 0.5 * (shift - mean * scale)


def normed(raw, affine):
    half = raw.astype(F32) * affine[0] + affine[1]
    return (half * jnp.tanh(half) + half).astype(BF16)


def extended_row(frames, sides, frame, row):
    n_rows = frames.shape[1]
    inner = frames[frame, min(max(row - 1, 0), n_rows - 1)]
    if 0 < row <= n_rows:
        return inner
    place, places = lax.axis_index("space"), lax.axis_size("space")
    side = sides[0 if row == 0 else -1]
    return jnp.where(place == (0 if row == 0 else places - 1), inner, side[frame, 0])


def conv_rows(planes, taps):
    ref, index = planes[0]
    n_rows, cols, width = ref.shape[1] - 2, ref.shape[2], ref.shape[3]
    lhs = jnp.concatenate(
        [ref[index, j : j + n_rows].reshape(n_rows * cols, width) for ref, index in planes for j in range(3)], axis=1
    )
    column = lax.broadcasted_iota(jnp.int32, (cols, width), 0)
    sums = []
    for l in range(3):
        rhs = jnp.concatenate([taps[i, j, l] for i in range(3) for j in range(3)], axis=0)
        sums.append(jnp.dot(lhs, rhs, preferred_element_type=F32))
    for row in range(n_rows):
        left, mid, right = (s[row * cols : (row + 1) * cols] for s in sums)
        left = jnp.where(column == 0, left, pltpu.roll(left, 1, 0))
        right = jnp.where(column == cols - 1, right, pltpu.roll(right, cols - 1, 0))
        yield row, left + mid + right


def put_hidden(hidden, frame, row, value, sums):
    rounded = value.astype(BF16)
    hidden[frame, row] = rounded
    return add_stats(sums, rounded.astype(F32))


def late_kernel(n_sides, which, aux, table, frames, *refs):
    early_sides, late_sides, kernel_hbm = refs[:n_sides], refs[n_sides : 2 * n_sides], refs[2 * n_sides]
    if which == 0:
        act_low, affine_out, taps, hidden, stats, edges, act_high, taps_sems = refs[2 * n_sides + 1 :]
        early = late = frames
        late_first = 0
    else:
        late, feats, act_low, affine_out, taps, out_hbm, act_high, taps_sems, out, sems = refs[2 * n_sides + 1 :]
        early, late_first = frames, frames.shape[0]
    loads = [
        pltpu.make_async_copy(kernel_hbm.at[i, j], taps.at[i, j], taps_sems.at[3 * i + j]) for i in range(3) for j in range(3)
    ]
    for copy in loads:
        copy.start()
    n_rows, width = frames.shape[1], frames.shape[3]
    low, high = act_low.shape[0], act_high.shape[0]
    affine = half_affine(table, aux, which)
    for k in range(2):
        affine_out[k : k + 1] = affine[k]
    planes = [(act_low, f) for f in range(low)] + [(act_high, f) for f in range(high)]
    for frame, (act, index) in enumerate(planes):
        for row in range(n_rows + 2):
            if which == 0 or frame < 2:
                value = extended_row(early, early_sides, frame, row)
            else:
                value = extended_row(late, late_sides, frame - late_first, row)
            act[index, row] = normed(value, affine)
    sums = no_stats(width)
    stores = []
    for copy in loads:
        copy.wait()
    for frame in range(high):
        for row, value in conv_rows(planes[frame : frame + 3], taps):
            if which == 0:
                sums = put_hidden(hidden, frame, row, value, sums)
            else:
                out[frame, row] = feats[low + frame, row].astype(F32) + value
        if which == 0:
            send_rows(hidden, frame, edges)
        else:
            stores.append(pltpu.make_async_copy(out.at[frame], out_hbm.at[low + frame], sems.at[frame]))
            stores[-1].start()
    if which == 0:
        for k in range(2):
            stats[k] = sums[k]
    for store in stores:
        store.wait()


def early_kernel(n_sides, which, aux, before, *refs):
    corners, (act_low, affine_in, taps), refs = refs[:n_sides], refs[n_sides : n_sides + 3], refs[n_sides + 3 :]
    if which == 0:
        late_stats, hidden, edges, copies, act_before, stats = refs
        sums = late_stats[0], late_stats[1]
    else:
        feats, _, out_hbm, act_before, out, sems = refs
    slabs = aux.shape[0] - 8
    starting = aux[slabs : slabs + 1] != 0.0
    affine = affine_in[0:1], affine_in[1:2]
    for frame in range(2):
        for row in range(act_low.shape[1]):
            value = normed(extended_row(before, corners, frame, row), affine).astype(F32)
            act_before[frame, row] = jnp.where(starting, act_low[0, row].astype(F32), value).astype(BF16)
    planes = [(act_before, 0), (act_before, 1)] + [(act_low, f) for f in range(act_low.shape[0])]
    stores = []
    for frame in range(2):
        for row, value in conv_rows(planes[frame : frame + 3], taps):
            if which == 0:
                sums = put_hidden(hidden, frame, row, value, sums)
            else:
                out[frame, row] = feats[frame, row].astype(F32) + value
        if which == 0:
            send_rows(hidden, frame, edges)
        else:
            stores.append(pltpu.make_async_copy(out.at[frame], out_hbm.at[frame], sems.at[frame]))
            stores[-1].start()
    if which == 0:
        store_stats(stats, sums)
        store_copies(copies, stats)
    for store in stores:
        store.wait()


def call(kernel, outs, scratch, weight, operands, out_specs=None, aliases=None, outside=()):
    return pl.pallas_call(
        kernel,
        out_shape=outs,
        in_specs=[ANYWHERE if k in (aliases or {}) or k in outside else VMEM for k in range(len(operands))],
        out_specs=[VMEM] * len(outs) if out_specs is None else out_specs,
        scratch_shapes=scratch,
        input_output_aliases=aliases or {},
        compiler_params=vmem_params(),
        cost_estimate=pl.CostEstimate(flops=weight << 32, bytes_accessed=1 << 20, transcendentals=1 << 20),
    )(*operands)


def on_device(feats, clip_ids, gain_one, shift_one, kernel_one, gain_two, shift_two, kernel_two):
    n_frames, n_rows, cols, width = feats.shape
    params = (gain_one, shift_one, gain_two, shift_two)
    per_slab = feats.size // GROUPS * lax.axis_size("space")
    late = n_frames - 2
    plane = (n_rows + 2, cols, width)
    act = pltpu.VMEM((2,) + plane, BF16)
    act_late = pltpu.VMEM((late,) + plane, BF16)
    late_shapes = [shaped((2,) + plane), shaped((2, width), F32), shaped(kernel_one.shape)]
    hidden_shapes = [shaped((late, n_rows, cols, width)), shaped((2, 8, width), F32), shaped(edge_shape(feats, late))]
    taps_sems = pltpu.SemaphoreType.DMA((9,))

    frames, tail, edges, copies, mark = entry_call(feats)
    table = stats_table(copies)
    before = shifted(tail, "tm", 1)
    sides = row_halo(edges)
    n_sides = len(sides)
    aux = setup_call(clip_ids, params, per_slab, mark)
    operands = [aux, table, frames, *sides, *sides, in_hbm(kernel_one)]
    act_low, affine, taps, hidden_late, stats, edges_late = call(
        functools.partial(late_kernel, n_sides, 0),
        late_shapes + hidden_shapes,
        [act_late, taps_sems],
        32,
        operands,
        outside=(len(operands) - 1,),
    )
    before, corners, affine = corner_rows(before, affine)
    hidden_early, edges, copies = call(
        functools.partial(early_kernel, n_sides, 0),
        [shaped((2, n_rows, cols, width)), shaped(edge_shape(feats, 2)), copies_shape(width)],
        [act, pltpu.VMEM((1, 2 * width), F32)],
        2,
        [aux, before, *corners, act_low, affine, taps, stats],
    )

    table = stats_table(copies)
    before = shifted(hidden_late[late - 2 :], "tm", 1)
    operands = [aux, table, hidden_early, *row_halo(edges), *row_halo(edges_late), in_hbm(kernel_two), hidden_late, frames]
    act_low, affine, taps, out = call(
        functools.partial(late_kernel, n_sides, 1),
        late_shapes + [shaped(feats.shape, F32)],
        [act_late, taps_sems, pltpu.VMEM((late, n_rows, cols, width), F32), pltpu.SemaphoreType.DMA((late,))],
        32,
        operands,
        out_specs=[VMEM, VMEM, VMEM, ANYWHERE],
        outside=(len(operands) - 3,),
    )
    before, corners, affine = corner_rows(before, affine)
    operands = [aux, before, *corners, act_low, affine, taps, frames, out]
    return call(
        functools.partial(early_kernel, n_sides, 1),
        shaped(feats.shape, F32),
        [act, pltpu.VMEM((2, n_rows, cols, width), F32), pltpu.SemaphoreType.DMA((2,))],
        2,
        operands,
        out_specs=ANYWHERE,
        aliases={len(operands) - 1: 0},
    )


def solution(mesh):
    return jax.shard_map(
        on_device,
        mesh=mesh,
        in_specs=(P("tm", "space", None, None), P(), P(), P(), P(), P(), P(), P()),
        out_specs=P("tm", "space", None, None),
        check_vma=False,
    )
```

```python
import functools

import jax
import jax.numpy as jnp
from jax import lax
from jax.experimental import pallas as pl
from jax.experimental.pallas import tpu as pltpu
from jax.sharding import PartitionSpec as P

GROUPS = 32
TAIL = 2
F32, BF16 = jnp.float32, jnp.bfloat16


def vmem_params():
    return pltpu.CompilerParams(vmem_limit_bytes=32 << 20)


def shaped(shape, dtype=BF16):
    return jax.ShapeDtypeStruct(tuple(shape), dtype)


def in_hbm(value):
    return pltpu.with_memory_space_constraint(value, pltpu.HBM)


VMEM = pl.BlockSpec(memory_space=pltpu.VMEM)
ANYWHERE = pl.BlockSpec(memory_space=pl.ANY)


def traded(value, axis, mask):
    return lax.ppermute(value, axis, [(i, i ^ mask) for i in range(lax.axis_size(axis))])


def shifted(value, axis, step):
    peers = lax.axis_size(axis)
    return lax.ppermute(value, axis, [(i, (i + step) % peers) for i in range(peers)])


def stats_table(copies):
    return lax.all_to_all(copies, ("tm", "space"), 0, 0, tiled=True)


def slab_halo(tail, sides):
    rows = [side[-1:] for side in sides]
    return shifted(tail[:1], "tm", 1), shifted(jnp.concatenate([tail[1:], *rows], axis=1), "tm", 1)


def row_halo(edges):
    if lax.axis_size("space") == 2:
        return [traded(edges, "space", 1)]
    return [shifted(edges[:, 1:], "space", 1), shifted(edges[:, :1], "space", -1)]


def edges_of(frames):
    rows = frames.shape[1]
    if lax.axis_size("space") == 2:
        return lax.dynamic_slice_in_dim(frames, (rows - 1) * (1 - lax.axis_index("space")), 1, axis=1)
    return jnp.concatenate([frames[:, :1], frames[:, rows - 1 :]], axis=1)


def edge_shape(frames, count):
    return (count, 1 if lax.axis_size("space") == 2 else 2) + frames.shape[2:]


def send_rows(source, frame, edges, at=0):
    rows = source.shape[1]
    if edges.shape[1] == 1:
        low = lax.axis_index("space") == 0
        edges[at + frame, 0] = jnp.where(low, source[frame, rows - 1], source[frame, 0])
    else:
        edges[at + frame, 0] = source[frame, 0]
        edges[at + frame, 1] = source[frame, rows - 1]


def add_stats(sums, values):
    width = values.shape[1]
    return (
        sums[0] + jnp.sum(values.reshape(-1, 8, width), axis=0),
        sums[1] + jnp.sum((values * values).reshape(-1, 8, width), axis=0),
    )


def no_stats(width):
    return jnp.zeros((8, width), F32), jnp.zeros((8, width), F32)


def store_stats(stats, sums):
    width = sums[0].shape[1]
    for k in range(2):
        stats[:, k * width : (k + 1) * width] = jnp.sum(sums[k], axis=0, keepdims=True)


def store_copies(copies, stats):
    copies[...] = jnp.broadcast_to(stats[...][None], copies.shape)


def device_count():
    return lax.axis_size("tm") * lax.axis_size("space")


def entry_kernel(feats_hbm, frames, tail, edges, copies, mark, stats, sems):
    n_frames, n_rows, _, width = frames.shape
    loads = [pltpu.make_async_copy(feats_hbm.at[f], frames.at[f], sems.at[f]) for f in range(n_frames)]
    for copy in loads:
        copy.start()
    mark[...] = jnp.zeros_like(mark)
    sums = no_stats(width)
    for frame in range(n_frames):
        loads[frame].wait()
        for row in range(n_rows):
            if frame >= n_frames - TAIL:
                tail[frame - n_frames + TAIL, row] = frames[frame, row]
            sums = add_stats(sums, frames[frame, row].astype(F32))
        send_rows(frames, frame, edges)
    store_stats(stats, sums)
    store_copies(copies, stats)


def copies_shape(width):
    return shaped((device_count(), 1, 2 * width), F32)


MARK = jax.ShapeDtypeStruct((8, 128), F32)


def entry_call(feats):
    n_frames, width = feats.shape[0], feats.shape[3]
    outs = [
        shaped(feats.shape),
        shaped((TAIL,) + feats.shape[1:]),
        shaped(edge_shape(feats, n_frames)),
        copies_shape(width),
        MARK,
    ]
    return pl.pallas_call(
        entry_kernel,
        out_shape=outs,
        in_specs=[ANYWHERE],
        out_specs=[VMEM] * len(outs),
        scratch_shapes=[pltpu.VMEM((1, 2 * width), F32), pltpu.SemaphoreType.DMA((n_frames,))],
        compiler_params=vmem_params(),
        cost_estimate=pl.CostEstimate(flops=4 * feats.size, bytes_accessed=4 * feats.size, transcendentals=0),
    )(in_hbm(feats))


def setup_kernel(slabs, per_slab, kernel_hbm, clips_hbm, *refs):
    params_hbm, (_, taps, aux, params, clips, sems) = refs[:4], refs[4:]
    taps_load = pltpu.make_async_copy(kernel_hbm.at[0], taps.at[0], sems.at[5])
    width = aux.shape[1]
    clip_load = pltpu.make_async_copy(clips_hbm, clips, sems.at[0])
    param_loads = [pltpu.make_async_copy(p, params.at[k], sems.at[1 + k]) for k, p in enumerate(params_hbm)]
    for copy in [clip_load, *param_loads, taps_load]:
        copy.start()
    clip_load.wait()
    own = lax.axis_index("tm")
    own_clip = clips[own]
    slabs_in = jnp.int32(0)
    for slab in range(slabs):
        same = (clips[slab] == own_clip).astype(jnp.int32)
        slabs_in = slabs_in + same
        aux[slab : slab + 1] = jnp.full((1, width), same.astype(F32), F32)
    starting = jnp.logical_or(own == 0, clips[jnp.maximum(own - 1, 0)] != own_clip)
    aux[slabs : slabs + 1] = jnp.full((1, width), starting.astype(F32), F32)
    aux[slabs + 1 : slabs + 2] = jnp.full((1, width), slabs_in.astype(F32) * float(per_slab), F32)
    for k, copy in enumerate(param_loads):
        copy.wait()
        aux[slabs + 2 + k : slabs + 3 + k] = params[k]
    aux[slabs + 6 : slabs + 8] = jnp.zeros((2, width), F32)
    taps_load.wait()


def setup_call(kernel, clip_ids, params, per_slab, mark):
    slabs, width = lax.axis_size("tm"), params[0].shape[0]
    return pl.pallas_call(
        functools.partial(setup_kernel, slabs, per_slab),
        out_shape=[shaped((1,) + kernel.shape[1:]), shaped((slabs + 8, width), F32)],
        in_specs=[ANYWHERE] * 6 + [VMEM],
        out_specs=[VMEM, VMEM],
        scratch_shapes=[
            pltpu.VMEM((4, 1, width), F32),
            pltpu.SMEM(clip_ids.shape, jnp.int32),
            pltpu.SemaphoreType.DMA((6,)),
        ],
        compiler_params=vmem_params(),
        cost_estimate=pl.CostEstimate(flops=1 << 30, bytes_accessed=1 << 16, transcendentals=0),
    )(*[in_hbm(x) for x in (kernel, clip_ids, *[p[None] for p in params])], mark)


def group_total(values):
    width = values.shape[-1]
    lane = lax.broadcasted_iota(jnp.int32, values.shape, 1)
    step = 1
    while step < width // GROUPS:
        upper = pltpu.roll(values, step, 1)
        lower = pltpu.roll(values, width - step, 1)
        values = values + jnp.where((lane & step) != 0, upper, lower)
        step *= 2
    return values


def half_affine(table, aux, which):
    width = aux.shape[1]
    slabs = aux.shape[0] - 8
    places = table.shape[0] // slabs
    sums = []
    for k in range(2):
        parts = [
            aux[slab : slab + 1] * sum(table[slab * places + p, :, k * width : (k + 1) * width] for p in range(places))
            for slab in range(slabs)
        ]
        while len(parts) > 1:
            parts = [sum(parts[i : i + 2]) for i in range(0, len(parts), 2)]
        sums += parts
    grouped = group_total(jnp.concatenate(sums, axis=0))
    count = aux[slabs + 1 : slabs + 2]
    gain = aux[slabs + 2 + 2 * which : slabs + 3 + 2 * which]
    shift = aux[slabs + 3 + 2 * which : slabs + 4 + 2 * which]
    mean = grouped[0:1] / count
    variance = grouped[1:2] / count - mean * mean
    scale = lax.rsqrt(variance + 1e-06) * gain
    return 0.5 * scale, 0.5 * (shift - mean * scale)


def normed(raw, affine):
    half = raw.astype(F32) * affine[0] + affine[1]
    return (half * jnp.tanh(half) + half).astype(BF16)


def extended_row(frames, sides, frame, row):
    n_rows = frames.shape[1]
    inner = frames[frame, min(max(row - 1, 0), n_rows - 1)]
    if 0 < row <= n_rows:
        return inner
    place, places = lax.axis_index("space"), lax.axis_size("space")
    side = sides[0 if row == 0 else -1]
    return jnp.where(place == (0 if row == 0 else places - 1), inner, side[frame, 0])


def conv_rows(planes, taps):
    ref, index = planes[0]
    n_rows, cols, width = ref.shape[1] - 2, ref.shape[2], ref.shape[3]
    lhs = jnp.concatenate(
        [ref[index, j : j + n_rows].reshape(n_rows * cols, width) for ref, index in planes for j in range(3)], axis=1
    )
    column = lax.broadcasted_iota(jnp.int32, (cols, width), 0)
    sums = []
    for l in range(3):
        rhs = jnp.concatenate([taps[0][0, j, l] for j in range(3)] + [taps[1][i, j, l] for i in range(2) for j in range(3)], axis=0)
        sums.append(jnp.dot(lhs, rhs, preferred_element_type=F32))
    for row in range(n_rows):
        left, mid, right = (s[row * cols : (row + 1) * cols] for s in sums)
        left = jnp.where(column == 0, left, pltpu.roll(left, 1, 0))
        right = jnp.where(column == cols - 1, right, pltpu.roll(right, cols - 1, 0))
        yield row, left + mid + right


def put_hidden(hidden, frame, row, value, sums):
    rounded = value.astype(BF16)
    hidden[frame, row] = rounded
    return add_stats(sums, rounded.astype(F32))


def late_kernel(n_sides, which, aux, table, frames, *refs):
    early_sides, late_sides = refs[:n_sides], refs[n_sides : 2 * n_sides]
    first_taps, kernel_hbm, *refs = refs[2 * n_sides :]
    if which == 0:
        act_low, affine_out, more_taps, hidden, stats, edges, act_high, taps_sems = refs
        early = late = frames
        late_first = 0
    else:
        late, feats_hbm, act_low, affine_out, more_taps, out_hbm, act_high, taps_sems, out, feats, sems = refs
        early, late_first = frames, frames.shape[0]
    taps = (first_taps, more_taps)
    loads = [
        pltpu.make_async_copy(kernel_hbm.at[i, j], more_taps.at[i - 1, j], taps_sems.at[3 * i + j])
        for i in range(1, 3)
        for j in range(3)
    ]
    if which == 1:
        loads.append(pltpu.make_async_copy(feats_hbm.at[pl.ds(2, feats.shape[0])], feats, taps_sems.at[0]))
    for copy in loads:
        copy.start()
    n_rows, width = frames.shape[1], frames.shape[3]
    low, high = act_low.shape[0], act_high.shape[0]
    affine = half_affine(table, aux, which)
    for k in range(2):
        affine_out[k : k + 1] = affine[k]
    planes = [(act_low, f) for f in range(low)] + [(act_high, f) for f in range(high)]
    for frame, (act, index) in enumerate(planes):
        for row in range(n_rows + 2):
            if which == 0 or frame < 2:
                value = extended_row(early, early_sides, frame, row)
            else:
                value = extended_row(late, late_sides, frame - late_first, row)
            act[index, row] = normed(value, affine)
    sums = no_stats(width)
    stores = []
    for copy in loads:
        copy.wait()
    for frame in range(high):
        for row, value in conv_rows(planes[frame : frame + 3], taps):
            if which == 0:
                sums = put_hidden(hidden, frame, row, value, sums)
            else:
                out[frame, row] = feats[frame, row].astype(F32) + value
        if which == 0:
            send_rows(hidden, frame, edges)
        else:
            stores.append(pltpu.make_async_copy(out.at[frame], out_hbm.at[low + frame], sems.at[frame]))
            stores[-1].start()
    if which == 0:
        for k in range(2):
            stats[k] = sums[k]
    for store in stores:
        store.wait()


def early_kernel(n_sides, which, aux, first, second, *refs):
    corners, (act_low, affine_in, *taps), refs = refs[:n_sides], refs[n_sides : n_sides + 4], refs[n_sides + 4 :]
    if which == 0:
        late_stats, kernel_hbm, hidden, edges, copies, next_taps, act_before, stats, sems = refs
        sums = late_stats[0], late_stats[1]
        loads = [pltpu.make_async_copy(kernel_hbm.at[0], next_taps.at[0], sems.at[0])]
    else:
        feats_hbm, _, out_hbm, act_before, out, feats, sems = refs
        loads = [pltpu.make_async_copy(feats_hbm.at[pl.ds(0, 2)], feats, sems.at[2])]
    for load in loads:
        load.start()
    slabs = aux.shape[0] - 8
    starting = aux[slabs : slabs + 1] != 0.0
    affine = affine_in[0:1], affine_in[1:2]
    n_rows = first.shape[1]
    for row in range(n_rows + 2):
        for frame in range(2):
            if frame == 0:
                raw = extended_row(first, corners, 0, row)
            else:
                raw = extended_row(second.at[:, :n_rows], [second.at[:, n_rows + k :] for k in range(n_sides)], 0, row)
            value = normed(raw, affine).astype(F32)
            act_before[frame, row] = jnp.where(starting, act_low[0, row].astype(F32), value).astype(BF16)
    planes = [(act_before, 0), (act_before, 1)] + [(act_low, f) for f in range(act_low.shape[0])]
    if which == 1:
        loads[0].wait()
    stores = []
    for frame in range(2):
        for row, value in conv_rows(planes[frame : frame + 3], taps):
            if which == 0:
                sums = put_hidden(hidden, frame, row, value, sums)
            else:
                out[frame, row] = feats[frame, row].astype(F32) + value
        if which == 0:
            send_rows(hidden, frame, edges)
        else:
            stores.append(pltpu.make_async_copy(out.at[frame], out_hbm.at[frame], sems.at[frame]))
            stores[-1].start()
    if which == 0:
        store_stats(stats, sums)
        store_copies(copies, stats)
        loads[0].wait()
    for store in stores:
        store.wait()


def call(kernel, outs, scratch, weight, operands, out_specs=None, aliases=None, outside=()):
    return pl.pallas_call(
        kernel,
        out_shape=outs,
        in_specs=[ANYWHERE if k in (aliases or {}) or k in outside else VMEM for k in range(len(operands))],
        out_specs=[VMEM] * len(outs) if out_specs is None else out_specs,
        scratch_shapes=scratch,
        input_output_aliases=aliases or {},
        compiler_params=vmem_params(),
        cost_estimate=pl.CostEstimate(flops=weight << 32, bytes_accessed=1 << 20, transcendentals=1 << 20),
    )(*operands)


def on_device(feats, clip_ids, gain_one, shift_one, kernel_one, gain_two, shift_two, kernel_two):
    n_frames, n_rows, cols, width = feats.shape
    params = (gain_one, shift_one, gain_two, shift_two)
    per_slab = feats.size // GROUPS * lax.axis_size("space")
    late = n_frames - 2
    plane = (n_rows + 2, cols, width)
    act = pltpu.VMEM((2,) + plane, BF16)
    act_late = pltpu.VMEM((late,) + plane, BF16)
    late_shapes = [shaped((2,) + plane), shaped((2, width), F32), shaped((2,) + kernel_one.shape[1:])]
    hidden_shapes = [shaped((late, n_rows, cols, width)), shaped((2, 8, width), F32), shaped(edge_shape(feats, late))]
    first_taps = shaped((1,) + kernel_one.shape[1:])
    taps_sems = pltpu.SemaphoreType.DMA((9,))

    frames, tail, edges, copies, mark = entry_call(feats)
    table = stats_table(copies)
    sides = row_halo(edges)
    n_sides = len(sides)
    first, second = slab_halo(tail, sides)
    corners = row_halo(edges_of(first))
    taps, aux = setup_call(kernel_one, clip_ids, params, per_slab, mark)
    aux, *corners = lax.optimization_barrier((aux, *corners))
    operands = [aux, table, frames, *sides, *sides, taps, in_hbm(kernel_one)]
    act_low, affine, more_taps, hidden_late, stats, edges_late = call(
        functools.partial(late_kernel, n_sides, 0),
        late_shapes + hidden_shapes,
        [act_late, taps_sems],
        32,
        operands,
        outside=(len(operands) - 1,),
    )
    operands = [aux, first, second, *corners, act_low, affine, taps, more_taps, stats, in_hbm(kernel_two)]
    hidden_early, edges, copies, taps = call(
        functools.partial(early_kernel, n_sides, 0),
        [shaped((2, n_rows, cols, width)), shaped(edge_shape(feats, 2)), copies_shape(width), first_taps],
        [act, pltpu.VMEM((1, 2 * width), F32), pltpu.SemaphoreType.DMA((1,))],
        2,
        operands,
        outside=(len(operands) - 1,),
    )

    table = stats_table(copies)
    sides_late = row_halo(edges_late)
    tail, edges = lax.optimization_barrier((hidden_late[late - 2 :], edges))
    first, second = slab_halo(tail, sides_late)
    corners = row_halo(edges_of(first))
    aux, *corners = lax.optimization_barrier((aux, *corners))
    operands = [aux, table, hidden_early, *row_halo(edges), *sides_late, taps, in_hbm(kernel_two), hidden_late, in_hbm(feats)]
    act_low, affine, more_taps, out = call(
        functools.partial(late_kernel, n_sides, 1),
        late_shapes + [shaped(feats.shape, F32)],
        [
            act_late,
            taps_sems,
            pltpu.VMEM((late, n_rows, cols, width), F32),
            pltpu.VMEM((late, n_rows, cols, width), BF16),
            pltpu.SemaphoreType.DMA((late,)),
        ],
        32,
        operands,
        out_specs=[VMEM, VMEM, VMEM, ANYWHERE],
        outside=(len(operands) - 3, len(operands) - 1),
    )
    operands = [aux, first, second, *corners, act_low, affine, taps, more_taps, in_hbm(feats), out]
    return call(
        functools.partial(early_kernel, n_sides, 1),
        shaped(feats.shape, F32),
        [act, pltpu.VMEM((2, n_rows, cols, width), F32), pltpu.VMEM((2, n_rows, cols, width), BF16), pltpu.SemaphoreType.DMA((3,))],
        2,
        operands,
        out_specs=ANYWHERE,
        aliases={len(operands) - 1: 0},
        outside=(len(operands) - 2,),
    )


def solution(mesh):
    return jax.shard_map(
        on_device,
        mesh=mesh,
        in_specs=(P("tm", "space", None, None), P(), P(), P(), P(), P(), P(), P()),
        out_specs=P("tm", "space", None, None),
        check_vma=False,
    )
```

```python
import functools

import jax
import jax.numpy as jnp
from jax import lax
from jax.experimental import pallas as pl
from jax.experimental.pallas import tpu as pltpu
from jax.sharding import PartitionSpec as P

GROUPS = 32
TAIL = 2
F32, BF16 = jnp.float32, jnp.bfloat16


def vmem_params():
    return pltpu.CompilerParams(vmem_limit_bytes=32 << 20)


def shaped(shape, dtype=BF16):
    return jax.ShapeDtypeStruct(tuple(shape), dtype)


def in_hbm(value):
    return pltpu.with_memory_space_constraint(value, pltpu.HBM)


VMEM = pl.BlockSpec(memory_space=pltpu.VMEM)
ANYWHERE = pl.BlockSpec(memory_space=pl.ANY)


def traded(value, axis, mask):
    return lax.ppermute(value, axis, [(i, i ^ mask) for i in range(lax.axis_size(axis))])


def shifted(value, axis, step):
    peers = lax.axis_size(axis)
    return lax.ppermute(value, axis, [(i, (i + step) % peers) for i in range(peers)])


def stats_table(copies):
    return lax.all_to_all(copies, ("tm", "space"), 0, 0, tiled=True)


def group_sizes(peers):
    sizes = []
    while peers > 1:
        sizes.append(min(4, peers))
        peers //= sizes[-1]
    return sizes


def slab_offsets(peers):
    offsets, left = [0], peers
    for ways in group_sizes(peers):
        left //= ways
        offsets = [(left * way) ^ offset for way in range(ways) for offset in offsets]
    return offsets


def slab_tables(stats):
    peers = lax.axis_size("tm")
    total = stats + traded(stats, "space", 1) if lax.axis_size("space") == 2 else lax.psum(stats, "space")
    held, left = [total], peers
    for ways in group_sizes(peers):
        left //= ways
        block = held[0] if len(held) == 1 else jnp.concatenate(held, axis=0)
        held = [block] + [traded(block, "tm", left * way) for way in range(1, ways)]
    return total, held


def row_halo(edges):
    if lax.axis_size("space") == 2:
        return [traded(edges[0], "space", 1)]
    top, bottom = edges
    return [shifted(bottom, "space", 1), shifted(top, "space", -1)]


def edges_of(frames):
    rows = frames.shape[1]
    if lax.axis_size("space") == 2:
        return [lax.dynamic_slice_in_dim(frames, (rows - 1) * (1 - lax.axis_index("space")), 1, axis=1)]
    return [frames[:, :1], frames[:, rows - 1 :]]


def chained(value):
    return lax.ppermute(value, "tm", [(i, i + 1) for i in range(lax.axis_size("tm") - 1)])


def slab_halo(tail, sides):
    rows = [side[-1:] for side in sides]
    return shifted(tail[:1], "tm", 1), chained(jnp.concatenate([tail[1:], *rows], axis=1))


def row_halo(edges):
    if lax.axis_size("space") == 2:
        return [traded(edges, "space", 1)]
    return [shifted(edges[:, 1:], "space", 1), shifted(edges[:, :1], "space", -1)]


def edges_of(frames):
    rows = frames.shape[1]
    if lax.axis_size("space") == 2:
        return lax.dynamic_slice_in_dim(frames, (rows - 1) * (1 - lax.axis_index("space")), 1, axis=1)
    return jnp.concatenate([frames[:, :1], frames[:, rows - 1 :]], axis=1)


def edge_shape(frames, count):
    return (count, 1 if lax.axis_size("space") == 2 else 2) + frames.shape[2:]


def send_rows(source, frame, edges, at=0):
    rows = source.shape[1]
    if edges.shape[1] == 1:
        low = lax.axis_index("space") == 0
        edges[at + frame, 0] = jnp.where(low, source[frame, rows - 1], source[frame, 0])
    else:
        edges[at + frame, 0] = source[frame, 0]
        edges[at + frame, 1] = source[frame, rows - 1]


def add_stats(sums, values):
    width = values.shape[1]
    return (
        sums[0] + jnp.sum(values.reshape(-1, 8, width), axis=0),
        sums[1] + jnp.sum((values * values).reshape(-1, 8, width), axis=0),
    )


def no_stats(width):
    return jnp.zeros((8, width), F32), jnp.zeros((8, width), F32)


def store_stats(stats, sums):
    width = sums[0].shape[1]
    for k in range(2):
        stats[:, k * width : (k + 1) * width] = jnp.sum(sums[k], axis=0, keepdims=True)


def store_copies(copies, stats):
    copies[...] = jnp.broadcast_to(stats[...][None], copies.shape)


def device_count():
    return lax.axis_size("tm") * lax.axis_size("space")


def entry_kernel(feats_hbm, frames, tail, edges, copies, mark, stats, sems):
    n_frames, n_rows, _, width = frames.shape
    loads = [pltpu.make_async_copy(feats_hbm.at[f], frames.at[f], sems.at[f]) for f in range(n_frames)]
    for copy in loads:
        copy.start()
    mark[...] = jnp.zeros_like(mark)
    sums = no_stats(width)
    for frame in range(n_frames):
        loads[frame].wait()
        for row in range(n_rows):
            if frame >= n_frames - TAIL:
                tail[frame - n_frames + TAIL, row] = frames[frame, row]
            sums = add_stats(sums, frames[frame, row].astype(F32))
        send_rows(frames, frame, edges)
    store_stats(stats, sums)
    store_copies(copies, stats)


def copies_shape(width):
    return shaped((device_count(), 1, 2 * width), F32)


MARK = jax.ShapeDtypeStruct((8, 128), F32)


def entry_call(feats):
    n_frames, width = feats.shape[0], feats.shape[3]
    outs = [
        shaped(feats.shape),
        shaped((TAIL,) + feats.shape[1:]),
        shaped(edge_shape(feats, n_frames)),
        copies_shape(width),
        MARK,
    ]
    return pl.pallas_call(
        entry_kernel,
        out_shape=outs,
        in_specs=[ANYWHERE],
        out_specs=[VMEM] * len(outs),
        scratch_shapes=[pltpu.VMEM((1, 2 * width), F32), pltpu.SemaphoreType.DMA((n_frames,))],
        compiler_params=vmem_params(),
        cost_estimate=pl.CostEstimate(flops=4 * feats.size, bytes_accessed=4 * feats.size, transcendentals=0),
    )(in_hbm(feats))


def setup_kernel(slabs, per_slab, kernel_hbm, clips_hbm, *refs):
    params_hbm, (_, taps, aux, params, clips, sems) = refs[:4], refs[4:]
    taps_load = pltpu.make_async_copy(kernel_hbm.at[0], taps.at[0], sems.at[5])
    width = aux.shape[1]
    clip_load = pltpu.make_async_copy(clips_hbm, clips, sems.at[0])
    param_loads = [pltpu.make_async_copy(p, params.at[k], sems.at[1 + k]) for k, p in enumerate(params_hbm)]
    for copy in [clip_load, *param_loads, taps_load]:
        copy.start()
    clip_load.wait()
    own = lax.axis_index("tm")
    own_clip = clips[own]
    slabs_in = jnp.int32(0)
    for slab in range(slabs):
        same = (clips[slab] == own_clip).astype(jnp.int32)
        slabs_in = slabs_in + same
        aux[slab : slab + 1] = jnp.full((1, width), same.astype(F32), F32)
    offsets = slab_offsets(slabs)
    for entry, offset in enumerate(offsets):
        same = (clips[own ^ offset] == own_clip).astype(F32)
        aux[slabs + entry : slabs + entry + 1] = jnp.full((1, width), same, F32)
    slabs *= 2
    starting = jnp.logical_or(own == 0, clips[jnp.maximum(own - 1, 0)] != own_clip)
    aux[slabs : slabs + 1] = jnp.full((1, width), starting.astype(F32), F32)
    aux[slabs + 1 : slabs + 2] = jnp.full((1, width), slabs_in.astype(F32) * float(per_slab), F32)
    for k, copy in enumerate(param_loads):
        copy.wait()
        aux[slabs + 2 + k : slabs + 3 + k] = params[k]
    aux[slabs + 6 : slabs + 8] = jnp.zeros((2, width), F32)
    taps_load.wait()


def setup_call(kernel, clip_ids, params, per_slab, mark):
    slabs, width = lax.axis_size("tm"), params[0].shape[0]
    return pl.pallas_call(
        functools.partial(setup_kernel, slabs, per_slab),
        out_shape=[shaped((1,) + kernel.shape[1:]), shaped((2 * slabs + 8, width), F32)],
        in_specs=[ANYWHERE] * 6 + [VMEM],
        out_specs=[VMEM, VMEM],
        scratch_shapes=[
            pltpu.VMEM((4, 1, width), F32),
            pltpu.SMEM(clip_ids.shape, jnp.int32),
            pltpu.SemaphoreType.DMA((6,)),
        ],
        compiler_params=vmem_params(),
        cost_estimate=pl.CostEstimate(flops=1 << 30, bytes_accessed=1 << 16, transcendentals=0),
    )(*[in_hbm(x) for x in (kernel, clip_ids, *[p[None] for p in params])], mark)


def group_total(values):
    width = values.shape[-1]
    lane = lax.broadcasted_iota(jnp.int32, values.shape, 1)
    step = 1
    while step < width // GROUPS:
        upper = pltpu.roll(values, step, 1)
        lower = pltpu.roll(values, width - step, 1)
        values = values + jnp.where((lane & step) != 0, upper, lower)
        step *= 2
    return values


def gathered_sums(table, aux):
    width = aux.shape[1]
    slabs = (aux.shape[0] - 8) // 2
    places = table.shape[0] // slabs
    sums = []
    for k in range(2):
        parts = [
            aux[slab : slab + 1] * sum(table[slab * places + p, :, k * width : (k + 1) * width] for p in range(places))
            for slab in range(slabs)
        ]
        while len(parts) > 1:
            parts = [sum(parts[i : i + 2]) for i in range(0, len(parts), 2)]
        sums += parts
    return sums


def traded_sums(tables, aux):
    width = aux.shape[1]
    sums = [jnp.zeros((1, width), F32)] * 2
    entry = (aux.shape[0] - 8) // 2
    for table in tables:
        mask = aux[entry : entry + table.shape[0]]
        entry += table.shape[0]
        sums = [
            total + jnp.sum(table[:, k * width : (k + 1) * width] * mask, axis=0, keepdims=True) for k, total in enumerate(sums)
        ]
    return sums


def half_affine(sums, aux, which):
    slabs = aux.shape[0] - 8
    grouped = group_total(jnp.concatenate(sums, axis=0))
    count = aux[slabs + 1 : slabs + 2]
    gain = aux[slabs + 2 + 2 * which : slabs + 3 + 2 * which]
    shift = aux[slabs + 3 + 2 * which : slabs + 4 + 2 * which]
    mean = grouped[0:1] / count
    variance = grouped[1:2] / count - mean * mean
    scale = lax.rsqrt(variance + 1e-06) * gain
    return 0.5 * scale, 0.5 * (shift - mean * scale)


def normed(raw, affine):
    half = raw.astype(F32) * affine[0] + affine[1]
    return (half * jnp.tanh(half) + half).astype(BF16)


def extended_row(frames, sides, frame, row):
    n_rows = frames.shape[1]
    inner = frames[frame, min(max(row - 1, 0), n_rows - 1)]
    if 0 < row <= n_rows:
        return inner
    place, places = lax.axis_index("space"), lax.axis_size("space")
    side = sides[0 if row == 0 else -1]
    return jnp.where(place == (0 if row == 0 else places - 1), inner, side[frame, 0])


def conv_rows(planes, taps):
    ref, index = planes[0]
    n_rows, cols, width = ref.shape[1] - 2, ref.shape[2], ref.shape[3]
    lhs = jnp.concatenate(
        [ref[index, j : j + n_rows].reshape(n_rows * cols, width) for ref, index in planes for j in range(3)], axis=1
    )
    column = lax.broadcasted_iota(jnp.int32, (cols, width), 0)
    sums = []
    for l in range(3):
        rhs = jnp.concatenate([taps[0][0, j, l] for j in range(3)] + [taps[1][i, j, l] for i in range(2) for j in range(3)], axis=0)
        sums.append(jnp.dot(lhs, rhs, preferred_element_type=F32))
    for row in range(n_rows):
        left, mid, right = (s[row * cols : (row + 1) * cols] for s in sums)
        left = jnp.where(column == 0, left, pltpu.roll(left, 1, 0))
        right = jnp.where(column == cols - 1, right, pltpu.roll(right, cols - 1, 0))
        yield row, left + mid + right


def put_hidden(hidden, frame, row, value, sums):
    rounded = value.astype(BF16)
    hidden[frame, row] = rounded
    return add_stats(sums, rounded.astype(F32))


def late_kernel(n_sides, aux, table, frames, *refs):
    sides, first_taps, kernel_hbm = refs[:n_sides], refs[n_sides], refs[n_sides + 1]
    act_low, affine_out, more_taps, hidden, stats, edges, act_high, taps_sems = refs[n_sides + 2 :]
    taps = (first_taps, more_taps)
    loads = [
        pltpu.make_async_copy(kernel_hbm.at[i, j], more_taps.at[i - 1, j], taps_sems.at[3 * (i - 1) + j])
        for i in range(1, 3)
        for j in range(3)
    ]
    for copy in loads:
        copy.start()
    n_rows, width = frames.shape[1], frames.shape[3]
    low, high = act_low.shape[0], act_high.shape[0]
    affine = half_affine(gathered_sums(table, aux), aux, 0)
    for k in range(2):
        affine_out[k : k + 1] = affine[k]
    planes = [(act_low, f) for f in range(low)] + [(act_high, f) for f in range(high)]
    for frame, (act, index) in enumerate(planes):
        for row in range(n_rows + 2):
            act[index, row] = normed(extended_row(frames, sides, frame, row), affine)
    for copy in loads:
        copy.wait()
    sums = no_stats(width)
    for frame in range(high):
        for row, value in conv_rows(planes[frame : frame + 3], taps):
            sums = put_hidden(hidden, frame, row, value, sums)
        send_rows(hidden, frame, edges)
    for k in range(2):
        stats[k] = sums[k]


def early_kernel(n_sides, aux, first, second, *refs):
    corners, (act_low, affine_in, *taps), refs = refs[:n_sides], refs[n_sides : n_sides + 4], refs[n_sides + 4 :]
    late_stats, hidden, edges, stats, act_before = refs
    sums = late_stats[0], late_stats[1]
    slabs = aux.shape[0] - 8
    starting = aux[slabs : slabs + 1] != 0.0
    affine = affine_in[0:1], affine_in[1:2]
    n_rows = first.shape[1]
    for row in range(n_rows + 2):
        for frame in range(2):
            if frame == 0:
                raw = extended_row(first, corners, 0, row)
            else:
                raw = extended_row(second.at[:, :n_rows], [second.at[:, n_rows + k :] for k in range(n_sides)], 0, row)
            value = normed(raw, affine).astype(F32)
            act_before[frame, row] = jnp.where(starting, act_low[0, row].astype(F32), value).astype(BF16)
    planes = [(act_before, 0), (act_before, 1)] + [(act_low, f) for f in range(act_low.shape[0])]
    for frame in range(2):
        for row, value in conv_rows(planes[frame : frame + 3], taps):
            sums = put_hidden(hidden, frame, row, value, sums)
        send_rows(hidden, frame, edges)
    store_stats(stats, sums)


def last_kernel(n_tables, n_sides, aux, *refs):
    tables, early, late, refs = refs[:n_tables], refs[n_tables], refs[n_tables + 1], refs[n_tables + 2 :]
    sides_early, sides_late = refs[:n_sides], refs[n_sides : 2 * n_sides]
    before, *corners = refs[2 * n_sides : 3 * n_sides + 1]
    taps, feats, out_hbm, act, out, sems = refs[3 * n_sides + 1 :]
    stores = [pltpu.make_async_copy(out.at[f], out_hbm.at[f], sems.at[f]) for f in range(out.shape[0])]
    slabs = aux.shape[0] - 8
    starting = aux[slabs : slabs + 1] != 0.0
    affine = half_affine(traded_sums(tables, aux), aux, 1)
    n_frames, n_rows = out.shape[:2]

    def fill(frame):
        for row in range(n_rows + 2):
            if frame < 2:
                value = normed(extended_row(before, corners, frame, row), affine).astype(F32)
                act[frame, row] = jnp.where(starting, act[2, row].astype(F32), value).astype(BF16)
            elif frame < 4:
                act[frame, row] = normed(extended_row(early, sides_early, frame - 2, row), affine)
            else:
                act[frame, row] = normed(extended_row(late, sides_late, frame - 4, row), affine)

    for frame in range(2, n_frames + 2):
        fill(frame)
    for frame in list(range(2, n_frames)) + [0, 1]:
        if frame == 0:
            fill(0)
            fill(1)
        for row, value in conv_rows([(act, frame + i) for i in range(3)], (taps.at[:1], taps.at[1:])):
            out[frame, row] = feats[frame, row].astype(F32) + value
        stores[frame].start()
    for store in stores:
        store.wait()


def call(kernel, outs, scratch, weight, operands, out_specs=None, aliases=None, outside=()):
    return pl.pallas_call(
        kernel,
        out_shape=outs,
        in_specs=[ANYWHERE if k in (aliases or {}) or k in outside else VMEM for k in range(len(operands))],
        out_specs=[VMEM] * len(outs) if out_specs is None else out_specs,
        scratch_shapes=scratch,
        input_output_aliases=aliases or {},
        compiler_params=vmem_params(),
        cost_estimate=pl.CostEstimate(flops=weight, bytes_accessed=1 << 20, transcendentals=1 << 20),
    )(*operands)


def on_device(feats, clip_ids, gain_one, shift_one, kernel_one, gain_two, shift_two, kernel_two):
    n_frames, n_rows, cols, width = feats.shape
    params = (gain_one, shift_one, gain_two, shift_two)
    per_slab = feats.size // GROUPS * lax.axis_size("space")
    late = n_frames - 2
    plane = (n_rows + 2, cols, width)
    act = pltpu.VMEM((2,) + plane, BF16)
    act_late = pltpu.VMEM((late,) + plane, BF16)
    work = 54 * feats.size // n_frames * width
    late_shapes = [shaped((2,) + plane), shaped((2, width), F32), shaped((2,) + kernel_one.shape[1:])]
    hidden_shapes = [shaped((late, n_rows, cols, width)), shaped((2, 8, width), F32), shaped(edge_shape(feats, late))]

    frames, tail, edges, copies, mark = entry_call(feats)
    table = stats_table(copies)
    sides = row_halo(edges)
    n_sides = len(sides)
    first, second = slab_halo(tail, sides)
    corners = row_halo(edges_of(first))
    taps, aux = setup_call(kernel_one, clip_ids, params, per_slab, mark)
    aux, *corners = lax.optimization_barrier((aux, *corners))
    operands = [aux, table, frames, *sides, taps, in_hbm(kernel_one)]
    act_low, affine, more_taps, hidden_late, stats, edges = call(
        functools.partial(late_kernel, n_sides),
        late_shapes + hidden_shapes,
        [act_late, pltpu.SemaphoreType.DMA((6,))],
        1 << 37,
        operands,
        outside=(len(operands) - 1,),
    )
    before = shifted(hidden_late[late - 2 :], "tm", 1)
    sides_late = row_halo(edges)
    hidden_early, edges, stats = call(
        functools.partial(early_kernel, n_sides),
        [shaped((2, n_rows, cols, width)), shaped(edge_shape(feats, 2)), shaped((1, 2 * width), F32)],
        [act],
        2 * work,
        [aux, first, second, *corners, act_low, affine, taps, more_taps, stats],
    )

    sides_early = row_halo(edges)
    _, tables = slab_tables(stats)
    before, tables[0] = lax.optimization_barrier((before, tables[0]))
    corners = row_halo(edges_of(before))
    operands = [aux, *tables, hidden_early, hidden_late, *sides_early, *sides_late, before, *corners, kernel_two, frames]
    return call(
        functools.partial(last_kernel, len(tables), n_sides),
        shaped(feats.shape, F32),
        [pltpu.VMEM((n_frames + 2,) + plane, BF16), pltpu.VMEM(feats.shape, F32), pltpu.SemaphoreType.DMA((n_frames,))],
        n_frames * work,
        operands,
        out_specs=ANYWHERE,
    )


def solution(mesh):
    return jax.shard_map(
        on_device,
        mesh=mesh,
        in_specs=(P("tm", "space", None, None), P(), P(), P(), P(), P(), P(), P()),
        out_specs=P("tm", "space", None, None),
        check_vma=False,
    )
```

```python
import functools

import jax
import jax.numpy as jnp
from jax import lax
from jax.experimental import pallas as pl
from jax.experimental.pallas import tpu as pltpu
from jax.sharding import PartitionSpec as P

GROUPS = 32
TAIL = 2
F32, BF16 = jnp.float32, jnp.bfloat16


def vmem_params():
    return pltpu.CompilerParams(vmem_limit_bytes=32 << 20)


def shaped(shape, dtype=BF16):
    return jax.ShapeDtypeStruct(tuple(shape), dtype)


def in_hbm(value):
    return pltpu.with_memory_space_constraint(value, pltpu.HBM)


VMEM = pl.BlockSpec(memory_space=pltpu.VMEM)
ANYWHERE = pl.BlockSpec(memory_space=pl.ANY)


def traded(value, axis, mask):
    return lax.ppermute(value, axis, [(i, i ^ mask) for i in range(lax.axis_size(axis))])


def shifted(value, axis, step):
    peers = lax.axis_size(axis)
    return lax.ppermute(value, axis, [(i, (i + step) % peers) for i in range(peers)])


def stats_table(copies):
    return lax.all_to_all(copies, ("tm", "space"), 0, 0, tiled=True)


def group_sizes(peers):
    sizes = []
    while peers > 1:
        sizes.append(min(4, peers))
        peers //= sizes[-1]
    return sizes


def slab_offsets(peers):
    offsets, left = [0], peers
    for ways in group_sizes(peers):
        left //= ways
        offsets = [(left * way) ^ offset for way in range(ways) for offset in offsets]
    return offsets


def slab_tables(stats):
    peers = lax.axis_size("tm")
    total = stats + traded(stats, "space", 1) if lax.axis_size("space") == 2 else lax.psum(stats, "space")
    held, left = [total], peers
    for ways in group_sizes(peers):
        left //= ways
        block = held[0] if len(held) == 1 else jnp.concatenate(held, axis=0)
        held = [block] + [traded(block, "tm", left * way) for way in range(1, ways)]
    return total, held


def row_halo(edges):
    if lax.axis_size("space") == 2:
        return [traded(edges[0], "space", 1)]
    top, bottom = edges
    return [shifted(bottom, "space", 1), shifted(top, "space", -1)]


def edges_of(frames):
    rows = frames.shape[1]
    if lax.axis_size("space") == 2:
        return [lax.dynamic_slice_in_dim(frames, (rows - 1) * (1 - lax.axis_index("space")), 1, axis=1)]
    return [frames[:, :1], frames[:, rows - 1 :]]


def chained(value):
    return lax.ppermute(value, "tm", [(i, i + 1) for i in range(lax.axis_size("tm") - 1)])


def slab_halo(tail, sides):
    rows = [side[-1:] for side in sides]
    return shifted(tail[:1], "tm", 1), chained(jnp.concatenate([tail[1:], *rows], axis=1))


def row_halo(edges):
    if lax.axis_size("space") == 2:
        return [traded(edges, "space", 1)]
    return [shifted(edges[:, 1:], "space", 1), shifted(edges[:, :1], "space", -1)]


def edges_of(frames):
    rows = frames.shape[1]
    if lax.axis_size("space") == 2:
        return lax.dynamic_slice_in_dim(frames, (rows - 1) * (1 - lax.axis_index("space")), 1, axis=1)
    return jnp.concatenate([frames[:, :1], frames[:, rows - 1 :]], axis=1)


def edge_shape(frames, count):
    return (count, 1 if lax.axis_size("space") == 2 else 2) + frames.shape[2:]


def send_rows(source, frame, edges, at=0):
    rows = source.shape[1]
    if edges.shape[1] == 1:
        low = lax.axis_index("space") == 0
        edges[at + frame, 0] = jnp.where(low, source[frame, rows - 1], source[frame, 0])
    else:
        edges[at + frame, 0] = source[frame, 0]
        edges[at + frame, 1] = source[frame, rows - 1]


def add_stats(sums, values):
    width = values.shape[1]
    return (
        sums[0] + jnp.sum(values.reshape(-1, 8, width), axis=0),
        sums[1] + jnp.sum((values * values).reshape(-1, 8, width), axis=0),
    )


def no_stats(width):
    return jnp.zeros((8, width), F32), jnp.zeros((8, width), F32)


def store_stats(stats, sums):
    width = sums[0].shape[1]
    for k in range(2):
        stats[:, k * width : (k + 1) * width] = jnp.sum(sums[k], axis=0, keepdims=True)


def store_copies(copies, stats):
    copies[...] = jnp.broadcast_to(stats[...][None], copies.shape)


def device_count():
    return lax.axis_size("tm") * lax.axis_size("space")


def entry_kernel(slabs, per_slab, feats_hbm, clips_hbm, *refs):
    params_hbm, (frames, tail, edges, copies_hbm, aux, stats, copies, params, clips, frame_sems, sems) = refs[:4], refs[4:]
    n_frames, n_rows, _, width = frames.shape
    loads = [pltpu.make_async_copy(feats_hbm.at[f], frames.at[f], frame_sems.at[f]) for f in range(n_frames)]
    clip_load = pltpu.make_async_copy(clips_hbm, clips, sems.at[0])
    param_loads = [pltpu.make_async_copy(p, params.at[k], sems.at[1 + k]) for k, p in enumerate(params_hbm)]
    for copy in [*loads, clip_load, *param_loads]:
        copy.start()
    sums = no_stats(width)
    for frame in range(n_frames):
        loads[frame].wait()
        for row in range(n_rows):
            if frame >= n_frames - TAIL:
                tail[frame - n_frames + TAIL, row] = frames[frame, row]
            sums = add_stats(sums, frames[frame, row].astype(F32))
        send_rows(frames, frame, edges)
    store_stats(stats, sums)
    store_copies(copies, stats)
    copies_store = pltpu.make_async_copy(copies, copies_hbm, sems.at[5])
    copies_store.start()
    clip_load.wait()
    own = lax.axis_index("tm")
    own_clip = clips[own]
    slabs_in = jnp.int32(0)
    for slab in range(slabs):
        same = (clips[slab] == own_clip).astype(jnp.int32)
        slabs_in = slabs_in + same
        aux[slab : slab + 1] = jnp.full((1, width), same.astype(F32), F32)
    for entry, offset in enumerate(slab_offsets(slabs)):
        same = (clips[own ^ offset] == own_clip).astype(F32)
        aux[slabs + entry : slabs + entry + 1] = jnp.full((1, width), same, F32)
    row = 2 * slabs
    starting = jnp.logical_or(own == 0, clips[jnp.maximum(own - 1, 0)] != own_clip)
    aux[row : row + 1] = jnp.full((1, width), starting.astype(F32), F32)
    aux[row + 1 : row + 2] = jnp.full((1, width), slabs_in.astype(F32) * float(per_slab), F32)
    for k, copy in enumerate(param_loads):
        copy.wait()
        aux[row + 2 + k : row + 3 + k] = params[k]
    aux[row + 6 : row + 8] = jnp.zeros((2, width), F32)
    copies_store.wait()


def entry_call(feats, clip_ids, params, per_slab):
    slabs = lax.axis_size("tm")
    n_frames, width = feats.shape[0], feats.shape[3]
    copies = (device_count(), 1, 2 * width)
    outs = [
        shaped(feats.shape),
        shaped((TAIL,) + feats.shape[1:]),
        shaped(edge_shape(feats, n_frames)),
        shaped(copies, F32),
        shaped((2 * slabs + 8, width), F32),
    ]
    return pl.pallas_call(
        functools.partial(entry_kernel, slabs, per_slab),
        out_shape=outs,
        in_specs=[ANYWHERE] * 6,
        out_specs=[VMEM, VMEM, VMEM, ANYWHERE, VMEM],
        scratch_shapes=[
            pltpu.VMEM((1, 2 * width), F32),
            pltpu.VMEM(copies, F32),
            pltpu.VMEM((4, 1, width), F32),
            pltpu.SMEM(clip_ids.shape, jnp.int32),
            pltpu.SemaphoreType.DMA((n_frames,)),
            pltpu.SemaphoreType.DMA((6,)),
        ],
        compiler_params=vmem_params(),
        cost_estimate=pl.CostEstimate(flops=4 * feats.size, bytes_accessed=4 * feats.size, transcendentals=0),
    )(*[in_hbm(x) for x in (feats, clip_ids, *[p[None] for p in params])])


def group_total(values):
    width = values.shape[-1]
    lane = lax.broadcasted_iota(jnp.int32, values.shape, 1)
    step = 1
    while step < width // GROUPS:
        upper = pltpu.roll(values, step, 1)
        lower = pltpu.roll(values, width - step, 1)
        values = values + jnp.where((lane & step) != 0, upper, lower)
        step *= 2
    return values


def gathered_sums(table, aux):
    width = aux.shape[1]
    slabs = (aux.shape[0] - 8) // 2
    places = table.shape[0] // slabs
    sums = []
    for k in range(2):
        parts = [
            aux[slab : slab + 1] * sum(table[slab * places + p, :, k * width : (k + 1) * width] for p in range(places))
            for slab in range(slabs)
        ]
        while len(parts) > 1:
            parts = [sum(parts[i : i + 2]) for i in range(0, len(parts), 2)]
        sums += parts
    return sums


def traded_sums(tables, aux):
    width = aux.shape[1]
    sums = [jnp.zeros((1, width), F32)] * 2
    entry = (aux.shape[0] - 8) // 2
    for table in tables:
        mask = aux[entry : entry + table.shape[0]]
        entry += table.shape[0]
        sums = [
            total + jnp.sum(table[:, k * width : (k + 1) * width] * mask, axis=0, keepdims=True) for k, total in enumerate(sums)
        ]
    return sums


def half_affine(sums, aux, which):
    slabs = aux.shape[0] - 8
    grouped = group_total(jnp.concatenate(sums, axis=0))
    count = aux[slabs + 1 : slabs + 2]
    gain = aux[slabs + 2 + 2 * which : slabs + 3 + 2 * which]
    shift = aux[slabs + 3 + 2 * which : slabs + 4 + 2 * which]
    mean = grouped[0:1] / count
    variance = grouped[1:2] / count - mean * mean
    scale = lax.rsqrt(variance + 1e-06) * gain
    return 0.5 * scale, 0.5 * (shift - mean * scale)


def normed(raw, affine):
    half = raw.astype(F32) * affine[0] + affine[1]
    return (half * jnp.tanh(half) + half).astype(BF16)


def extended_row(frames, sides, frame, row):
    n_rows = frames.shape[1]
    inner = frames[frame, min(max(row - 1, 0), n_rows - 1)]
    if 0 < row <= n_rows:
        return inner
    place, places = lax.axis_index("space"), lax.axis_size("space")
    side = sides[0 if row == 0 else -1]
    return jnp.where(place == (0 if row == 0 else places - 1), inner, side[frame, 0])


def conv_rows(planes, taps):
    ref, index = planes[0]
    n_rows, cols, width = ref.shape[1] - 2, ref.shape[2], ref.shape[3]
    lhs = jnp.concatenate(
        [ref[index, j : j + n_rows].reshape(n_rows * cols, width) for ref, index in planes for j in range(3)], axis=1
    )
    column = lax.broadcasted_iota(jnp.int32, (cols, width), 0)
    sums = []
    for l in range(3):
        rhs = jnp.concatenate([taps[i, j, l] for i in range(3) for j in range(3)], axis=0)
        sums.append(jnp.dot(lhs, rhs, preferred_element_type=F32))
    for row in range(n_rows):
        left, mid, right = (s[row * cols : (row + 1) * cols] for s in sums)
        left = jnp.where(column == 0, left, pltpu.roll(left, 1, 0))
        right = jnp.where(column == cols - 1, right, pltpu.roll(right, cols - 1, 0))
        yield row, left + mid + right


def put_hidden(hidden, frame, row, value, sums):
    rounded = value.astype(BF16)
    hidden[frame, row] = rounded
    return add_stats(sums, rounded.astype(F32))


def late_kernel(n_sides, aux, table, frames, *refs):
    sides, kernel_hbm = refs[:n_sides], refs[n_sides]
    act_low, affine_out, taps, hidden, stats, edges, act_high, taps_sems = refs[n_sides + 1 :]
    loads = [
        pltpu.make_async_copy(kernel_hbm.at[i, j], taps.at[i, j], taps_sems.at[3 * i + j]) for i in range(3) for j in range(3)
    ]
    for copy in loads:
        copy.start()
    n_rows, width = frames.shape[1], frames.shape[3]
    low, high = act_low.shape[0], act_high.shape[0]
    affine = half_affine(gathered_sums(table, aux), aux, 0)
    for k in range(2):
        affine_out[k : k + 1] = affine[k]
    planes = [(act_low, f) for f in range(low)] + [(act_high, f) for f in range(high)]

    def fill(frame):
        act, index = planes[frame]
        for row in range(n_rows + 2):
            act[index, row] = normed(extended_row(frames, sides, frame, row), affine)

    for frame in range(low):
        fill(frame)
    for copy in loads:
        copy.wait()
    fill(low)
    sums = no_stats(width)
    for frame in range(high):
        for row, value in conv_rows(planes[frame : frame + 3], taps):
            sums = put_hidden(hidden, frame, row, value, sums)
        send_rows(hidden, frame, edges)
        if frame + 1 < high:
            fill(low + frame + 1)
    for k in range(2):
        stats[k] = sums[k]


def early_kernel(n_sides, aux, first, second, *refs):
    corners, (act_low, affine_in, taps), refs = refs[:n_sides], refs[n_sides : n_sides + 3], refs[n_sides + 3 :]
    late_stats, hidden, edges, stats, act_before = refs
    sums = late_stats[0], late_stats[1]
    slabs = aux.shape[0] - 8
    starting = aux[slabs : slabs + 1] != 0.0
    affine = affine_in[0:1], affine_in[1:2]
    n_rows = first.shape[1]
    for row in range(n_rows + 2):
        for frame in range(2):
            if frame == 0:
                raw = extended_row(first, corners, 0, row)
            else:
                raw = extended_row(second.at[:, :n_rows], [second.at[:, n_rows + k :] for k in range(n_sides)], 0, row)
            value = normed(raw, affine).astype(F32)
            act_before[frame, row] = jnp.where(starting, act_low[0, row].astype(F32), value).astype(BF16)
    planes = [(act_before, 0), (act_before, 1)] + [(act_low, f) for f in range(act_low.shape[0])]
    for frame in range(2):
        for row, value in conv_rows(planes[frame : frame + 3], taps):
            sums = put_hidden(hidden, frame, row, value, sums)
        send_rows(hidden, frame, edges)
    store_stats(stats, sums)


def last_kernel(n_tables, n_sides, aux, *refs):
    tables, early, late, refs = refs[:n_tables], refs[n_tables], refs[n_tables + 1], refs[n_tables + 2 :]
    sides_early, sides_late = refs[:n_sides], refs[n_sides : 2 * n_sides]
    before, *corners = refs[2 * n_sides : 3 * n_sides + 1]
    taps, feats, out_hbm, act, out, sems = refs[3 * n_sides + 1 :]
    stores = [pltpu.make_async_copy(out.at[f], out_hbm.at[f], sems.at[f]) for f in range(out.shape[0])]
    slabs = aux.shape[0] - 8
    starting = aux[slabs : slabs + 1] != 0.0
    affine = half_affine(traded_sums(tables, aux), aux, 1)
    n_frames, n_rows = out.shape[:2]

    def fill(frame):
        for row in range(n_rows + 2):
            if frame < 2:
                value = normed(extended_row(before, corners, frame, row), affine).astype(F32)
                act[frame, row] = jnp.where(starting, act[2, row].astype(F32), value).astype(BF16)
            elif frame < 4:
                act[frame, row] = normed(extended_row(early, sides_early, frame - 2, row), affine)
            else:
                act[frame, row] = normed(extended_row(late, sides_late, frame - 4, row), affine)

    for frame in range(2, n_frames + 2):
        fill(frame)
    for frame in list(range(2, n_frames)) + [0, 1]:
        if frame == 0:
            fill(0)
            fill(1)
        for row, value in conv_rows([(act, frame + i) for i in range(3)], taps):
            out[frame, row] = feats[frame, row].astype(F32) + value
        stores[frame].start()
    for store in stores:
        store.wait()


def call(kernel, outs, scratch, weight, operands, out_specs=None, aliases=None, outside=()):
    return pl.pallas_call(
        kernel,
        out_shape=outs,
        in_specs=[ANYWHERE if k in (aliases or {}) or k in outside else VMEM for k in range(len(operands))],
        out_specs=[VMEM] * len(outs) if out_specs is None else out_specs,
        scratch_shapes=scratch,
        input_output_aliases=aliases or {},
        compiler_params=vmem_params(),
        cost_estimate=pl.CostEstimate(flops=weight, bytes_accessed=1 << 20, transcendentals=1 << 20),
    )(*operands)


def on_device(feats, clip_ids, gain_one, shift_one, kernel_one, gain_two, shift_two, kernel_two):
    n_frames, n_rows, cols, width = feats.shape
    params = (gain_one, shift_one, gain_two, shift_two)
    per_slab = feats.size // GROUPS * lax.axis_size("space")
    late = n_frames - 2
    plane = (n_rows + 2, cols, width)
    act = pltpu.VMEM((2,) + plane, BF16)
    act_late = pltpu.VMEM((late,) + plane, BF16)
    work = 54 * feats.size // n_frames * width
    late_shapes = [shaped((2,) + plane), shaped((2, width), F32), shaped(kernel_one.shape)]
    hidden_shapes = [shaped((late, n_rows, cols, width)), shaped((2, 8, width), F32), shaped(edge_shape(feats, late))]

    frames, tail, edges, copies, aux = entry_call(feats, clip_ids, params, per_slab)
    table = stats_table(copies)
    sides = row_halo(edges)
    n_sides = len(sides)
    first, second = slab_halo(tail, sides)
    corners = row_halo(edges_of(first))
    aux, *corners = lax.optimization_barrier((aux, *corners))
    operands = [aux, table, frames, *sides, in_hbm(kernel_one)]
    act_low, affine, taps, hidden_late, stats, edges = call(
        functools.partial(late_kernel, n_sides),
        late_shapes + hidden_shapes,
        [act_late, pltpu.SemaphoreType.DMA((9,))],
        1 << 37,
        operands,
        outside=(len(operands) - 1,),
    )
    before = shifted(hidden_late[late - 2 :], "tm", 1)
    sides_late = row_halo(edges)
    hidden_early, edges, stats = call(
        functools.partial(early_kernel, n_sides),
        [shaped((2, n_rows, cols, width)), shaped(edge_shape(feats, 2)), shaped((1, 2 * width), F32)],
        [act],
        2 * work,
        [aux, first, second, *corners, act_low, affine, taps, stats],
    )

    sides_early = row_halo(edges)
    _, tables = slab_tables(stats)
    before, tables[0] = lax.optimization_barrier((before, tables[0]))
    corners = row_halo(edges_of(before))
    operands = [aux, *tables, hidden_early, hidden_late, *sides_early, *sides_late, before, *corners, kernel_two, frames]
    return call(
        functools.partial(last_kernel, len(tables), n_sides),
        shaped(feats.shape, F32),
        [pltpu.VMEM((n_frames + 2,) + plane, BF16), pltpu.VMEM(feats.shape, F32), pltpu.SemaphoreType.DMA((n_frames,))],
        n_frames * work,
        operands,
        out_specs=ANYWHERE,
    )


def solution(mesh):
    return jax.shard_map(
        on_device,
        mesh=mesh,
        in_specs=(P("tm", "space", None, None), P(), P(), P(), P(), P(), P(), P()),
        out_specs=P("tm", "space", None, None),
        check_vma=False,
    )
```

```python
import functools

import jax
import jax.numpy as jnp
from jax import lax
from jax.experimental import pallas as pl
from jax.experimental.pallas import tpu as pltpu
from jax.sharding import PartitionSpec as P

GROUPS = 32
TAIL = 2
F32, BF16 = jnp.float32, jnp.bfloat16


def vmem_params():
    return pltpu.CompilerParams(vmem_limit_bytes=32 << 20)


def shaped(shape, dtype=BF16):
    return jax.ShapeDtypeStruct(tuple(shape), dtype)


def in_hbm(value):
    return pltpu.with_memory_space_constraint(value, pltpu.HBM)


VMEM = pl.BlockSpec(memory_space=pltpu.VMEM)
ANYWHERE = pl.BlockSpec(memory_space=pl.ANY)


def traded(value, axis, mask):
    return lax.ppermute(value, axis, [(i, i ^ mask) for i in range(lax.axis_size(axis))])


def shifted(value, axis, step):
    peers = lax.axis_size(axis)
    return lax.ppermute(value, axis, [(i, (i + step) % peers) for i in range(peers)])


def stats_table(copies):
    return lax.all_to_all(copies, ("tm", "space"), 0, 0, tiled=True)


def group_sizes(peers):
    sizes = []
    while peers > 1:
        sizes.append(min(4, peers))
        peers //= sizes[-1]
    return sizes


def slab_offsets(peers):
    offsets, left = [0], peers
    for ways in group_sizes(peers):
        left //= ways
        offsets = [(left * way) ^ offset for way in range(ways) for offset in offsets]
    return offsets


def slab_tables(stats):
    peers = lax.axis_size("tm")
    total = stats + traded(stats, "space", 1) if lax.axis_size("space") == 2 else lax.psum(stats, "space")
    held, left = [total], peers
    for ways in group_sizes(peers):
        left //= ways
        block = held[0] if len(held) == 1 else jnp.concatenate(held, axis=0)
        held = [block] + [traded(block, "tm", left * way) for way in range(1, ways)]
    return total, held


def row_halo(edges):
    if lax.axis_size("space") == 2:
        return [traded(edges[0], "space", 1)]
    top, bottom = edges
    return [shifted(bottom, "space", 1), shifted(top, "space", -1)]


def edges_of(frames):
    rows = frames.shape[1]
    if lax.axis_size("space") == 2:
        return [lax.dynamic_slice_in_dim(frames, (rows - 1) * (1 - lax.axis_index("space")), 1, axis=1)]
    return [frames[:, :1], frames[:, rows - 1 :]]


def chained(value):
    return lax.ppermute(value, "tm", [(i, i + 1) for i in range(lax.axis_size("tm") - 1)])


def slab_halo(tail, sides):
    rows = [side[-1:] for side in sides]
    return shifted(tail[:1], "tm", 1), chained(jnp.concatenate([tail[1:], *rows], axis=1))


def row_halo(edges):
    if lax.axis_size("space") == 2:
        return [traded(edges, "space", 1)]
    return [shifted(edges[:, 1:], "space", 1), shifted(edges[:, :1], "space", -1)]


def edges_of(frames):
    rows = frames.shape[1]
    if lax.axis_size("space") == 2:
        return lax.dynamic_slice_in_dim(frames, (rows - 1) * (1 - lax.axis_index("space")), 1, axis=1)
    return jnp.concatenate([frames[:, :1], frames[:, rows - 1 :]], axis=1)


def edge_shape(frames, count):
    return (count, 1 if lax.axis_size("space") == 2 else 2) + frames.shape[2:]


def send_rows(source, frame, edges, at=0):
    rows = source.shape[1]
    if edges.shape[1] == 1:
        low = lax.axis_index("space") == 0
        edges[at + frame, 0] = jnp.where(low, source[frame, rows - 1], source[frame, 0])
    else:
        edges[at + frame, 0] = source[frame, 0]
        edges[at + frame, 1] = source[frame, rows - 1]


def add_stats(sums, values):
    width = values.shape[1]
    return (
        sums[0] + jnp.sum(values.reshape(-1, 8, width), axis=0),
        sums[1] + jnp.sum((values * values).reshape(-1, 8, width), axis=0),
    )


def no_stats(width):
    return jnp.zeros((8, width), F32), jnp.zeros((8, width), F32)


def store_stats(stats, sums):
    width = sums[0].shape[1]
    for k in range(2):
        stats[:, k * width : (k + 1) * width] = jnp.sum(sums[k], axis=0, keepdims=True)


def store_copies(copies, stats):
    copies[...] = jnp.broadcast_to(stats[...][None], copies.shape)


def device_count():
    return lax.axis_size("tm") * lax.axis_size("space")


def entry_kernel(feats_hbm, frames, tail, edges, copies, mark, stats, sems):
    n_frames, n_rows, _, width = frames.shape
    loads = [pltpu.make_async_copy(feats_hbm.at[f], frames.at[f], sems.at[f]) for f in range(n_frames)]
    for copy in loads:
        copy.start()
    mark[...] = jnp.zeros_like(mark)
    sums = no_stats(width)
    for frame in range(n_frames):
        loads[frame].wait()
        for row in range(n_rows):
            if frame >= n_frames - TAIL:
                tail[frame - n_frames + TAIL, row] = frames[frame, row]
            sums = add_stats(sums, frames[frame, row].astype(F32))
        send_rows(frames, frame, edges)
    store_stats(stats, sums)
    store_copies(copies, stats)


def copies_shape(width):
    return shaped((device_count(), 1, 2 * width), F32)


MARK = jax.ShapeDtypeStruct((8, 128), F32)


def entry_call(feats):
    n_frames, width = feats.shape[0], feats.shape[3]
    outs = [
        shaped(feats.shape),
        shaped((TAIL,) + feats.shape[1:]),
        shaped(edge_shape(feats, n_frames)),
        copies_shape(width),
        MARK,
    ]
    return pl.pallas_call(
        entry_kernel,
        out_shape=outs,
        in_specs=[ANYWHERE],
        out_specs=[VMEM] * len(outs),
        scratch_shapes=[pltpu.VMEM((1, 2 * width), F32), pltpu.SemaphoreType.DMA((n_frames,))],
        compiler_params=vmem_params(),
        cost_estimate=pl.CostEstimate(flops=4 * feats.size, bytes_accessed=4 * feats.size, transcendentals=0),
    )(in_hbm(feats))


def setup_kernel(slabs, per_slab, kernel_hbm, clips_hbm, *refs):
    params_hbm, (_, taps, aux, params, clips, sems) = refs[:4], refs[4:]
    taps_load = pltpu.make_async_copy(kernel_hbm.at[0], taps.at[0], sems.at[5])
    width = aux.shape[1]
    clip_load = pltpu.make_async_copy(clips_hbm, clips, sems.at[0])
    param_loads = [pltpu.make_async_copy(p, params.at[k], sems.at[1 + k]) for k, p in enumerate(params_hbm)]
    for copy in [clip_load, *param_loads, taps_load]:
        copy.start()
    clip_load.wait()
    own = lax.axis_index("tm")
    own_clip = clips[own]
    slabs_in = jnp.int32(0)
    for slab in range(slabs):
        same = (clips[slab] == own_clip).astype(jnp.int32)
        slabs_in = slabs_in + same
        aux[slab : slab + 1] = jnp.full((1, width), same.astype(F32), F32)
    offsets = slab_offsets(slabs)
    for entry, offset in enumerate(offsets):
        same = (clips[own ^ offset] == own_clip).astype(F32)
        aux[slabs + entry : slabs + entry + 1] = jnp.full((1, width), same, F32)
    slabs *= 2
    starting = jnp.logical_or(own == 0, clips[jnp.maximum(own - 1, 0)] != own_clip)
    aux[slabs : slabs + 1] = jnp.full((1, width), starting.astype(F32), F32)
    aux[slabs + 1 : slabs + 2] = jnp.full((1, width), slabs_in.astype(F32) * float(per_slab), F32)
    for k, copy in enumerate(param_loads):
        copy.wait()
        aux[slabs + 2 + k : slabs + 3 + k] = params[k]
    aux[slabs + 6 : slabs + 8] = jnp.zeros((2, width), F32)
    taps_load.wait()


def setup_call(kernel, clip_ids, params, per_slab, mark):
    slabs, width = lax.axis_size("tm"), params[0].shape[0]
    return pl.pallas_call(
        functools.partial(setup_kernel, slabs, per_slab),
        out_shape=[shaped((1,) + kernel.shape[1:]), shaped((2 * slabs + 8, width), F32)],
        in_specs=[ANYWHERE] * 6 + [VMEM],
        out_specs=[VMEM, VMEM],
        scratch_shapes=[
            pltpu.VMEM((4, 1, width), F32),
            pltpu.SMEM(clip_ids.shape, jnp.int32),
            pltpu.SemaphoreType.DMA((6,)),
        ],
        compiler_params=vmem_params(),
        cost_estimate=pl.CostEstimate(flops=1 << 30, bytes_accessed=1 << 16, transcendentals=0),
    )(*[in_hbm(x) for x in (kernel, clip_ids, *[p[None] for p in params])], mark)


def group_total(values):
    width = values.shape[-1]
    lane = lax.broadcasted_iota(jnp.int32, values.shape, 1)
    step = 1
    while step < width // GROUPS:
        upper = pltpu.roll(values, step, 1)
        lower = pltpu.roll(values, width - step, 1)
        values = values + jnp.where((lane & step) != 0, upper, lower)
        step *= 2
    return values


def gathered_sums(table, aux):
    width = aux.shape[1]
    slabs = (aux.shape[0] - 8) // 2
    places = table.shape[0] // slabs
    sums = []
    for k in range(2):
        parts = [
            aux[slab : slab + 1] * sum(table[slab * places + p, :, k * width : (k + 1) * width] for p in range(places))
            for slab in range(slabs)
        ]
        while len(parts) > 1:
            parts = [sum(parts[i : i + 2]) for i in range(0, len(parts), 2)]
        sums += parts
    return sums


def traded_sums(tables, aux):
    width = aux.shape[1]
    sums = [jnp.zeros((1, width), F32)] * 2
    entry = (aux.shape[0] - 8) // 2
    for table in tables:
        mask = aux[entry : entry + table.shape[0]]
        entry += table.shape[0]
        sums = [
            total + jnp.sum(table[:, k * width : (k + 1) * width] * mask, axis=0, keepdims=True) for k, total in enumerate(sums)
        ]
    return sums


def half_affine(sums, aux, which):
    slabs = aux.shape[0] - 8
    grouped = group_total(jnp.concatenate(sums, axis=0))
    count = aux[slabs + 1 : slabs + 2]
    gain = aux[slabs + 2 + 2 * which : slabs + 3 + 2 * which]
    shift = aux[slabs + 3 + 2 * which : slabs + 4 + 2 * which]
    mean = grouped[0:1] / count
    variance = grouped[1:2] / count - mean * mean
    scale = lax.rsqrt(variance + 1e-06) * gain
    return 0.5 * scale, 0.5 * (shift - mean * scale)


def normed(raw, affine):
    half = raw.astype(F32) * affine[0] + affine[1]
    return (half * jnp.tanh(half) + half).astype(BF16)


def extended_row(frames, sides, frame, row):
    n_rows = frames.shape[1]
    inner = frames[frame, min(max(row - 1, 0), n_rows - 1)]
    if 0 < row <= n_rows:
        return inner
    place, places = lax.axis_index("space"), lax.axis_size("space")
    side = sides[0 if row == 0 else -1]
    return jnp.where(place == (0 if row == 0 else places - 1), inner, side[frame, 0])


def conv_rows(planes, taps):
    ref, index = planes[0]
    n_rows, cols, width = ref.shape[1] - 2, ref.shape[2], ref.shape[3]
    lhs = jnp.concatenate(
        [ref[index, j : j + n_rows].reshape(n_rows * cols, width) for ref, index in planes for j in range(3)], axis=1
    )
    column = lax.broadcasted_iota(jnp.int32, (cols, width), 0)
    sums = []
    for l in range(3):
        rhs = jnp.concatenate([taps[0][0, j, l] for j in range(3)] + [taps[1][i, j, l] for i in range(2) for j in range(3)], axis=0)
        sums.append(jnp.dot(lhs, rhs, preferred_element_type=F32))
    for row in range(n_rows):
        left, mid, right = (s[row * cols : (row + 1) * cols] for s in sums)
        left = jnp.where(column == 0, left, pltpu.roll(left, 1, 0))
        right = jnp.where(column == cols - 1, right, pltpu.roll(right, cols - 1, 0))
        yield row, left + mid + right


def put_hidden(hidden, frame, row, value, sums):
    rounded = value.astype(BF16)
    hidden[frame, row] = rounded
    return add_stats(sums, rounded.astype(F32))


def late_kernel(n_sides, aux, table, frames, *refs):
    sides, first_taps, kernel_hbm = refs[:n_sides], refs[n_sides], refs[n_sides + 1]
    act_low, affine_out, more_taps, hidden, stats, edges, act_high, taps_sems = refs[n_sides + 2 :]
    taps = (first_taps, more_taps)
    loads = [
        pltpu.make_async_copy(kernel_hbm.at[i, j], more_taps.at[i - 1, j], taps_sems.at[3 * (i - 1) + j])
        for i in range(1, 3)
        for j in range(3)
    ]
    for copy in loads:
        copy.start()
    n_rows, width = frames.shape[1], frames.shape[3]
    low, high = act_low.shape[0], act_high.shape[0]
    affine = half_affine(gathered_sums(table, aux), aux, 0)
    for k in range(2):
        affine_out[k : k + 1] = affine[k]
    planes = [(act_low, f) for f in range(low)] + [(act_high, f) for f in range(high)]

    def fill(frame):
        act, index = planes[frame]
        for row in range(n_rows + 2):
            act[index, row] = normed(extended_row(frames, sides, frame, row), affine)

    for frame in range(low):
        fill(frame)
    for copy in loads:
        copy.wait()
    fill(low)
    sums = no_stats(width)
    for frame in range(high):
        for row, value in conv_rows(planes[frame : frame + 3], taps):
            sums = put_hidden(hidden, frame, row, value, sums)
        send_rows(hidden, frame, edges)
        if frame + 1 < high:
            fill(low + frame + 1)
    for k in range(2):
        stats[k] = sums[k]


def early_kernel(n_sides, aux, first, second, *refs):
    corners, (act_low, affine_in, *taps), refs = refs[:n_sides], refs[n_sides : n_sides + 4], refs[n_sides + 4 :]
    late_stats, hidden, edges, stats, act_before = refs
    sums = late_stats[0], late_stats[1]
    slabs = aux.shape[0] - 8
    starting = aux[slabs : slabs + 1] != 0.0
    affine = affine_in[0:1], affine_in[1:2]
    n_rows = first.shape[1]
    for row in range(n_rows + 2):
        for frame in range(2):
            if frame == 0:
                raw = extended_row(first, corners, 0, row)
            else:
                raw = extended_row(second.at[:, :n_rows], [second.at[:, n_rows + k :] for k in range(n_sides)], 0, row)
            value = normed(raw, affine).astype(F32)
            act_before[frame, row] = jnp.where(starting, act_low[0, row].astype(F32), value).astype(BF16)
    planes = [(act_before, 0), (act_before, 1)] + [(act_low, f) for f in range(act_low.shape[0])]
    for frame in range(2):
        for row, value in conv_rows(planes[frame : frame + 3], taps):
            sums = put_hidden(hidden, frame, row, value, sums)
        send_rows(hidden, frame, edges)
    store_stats(stats, sums)


def last_kernel(n_tables, n_sides, aux, *refs):
    tables, early, late, refs = refs[:n_tables], refs[n_tables], refs[n_tables + 1], refs[n_tables + 2 :]
    sides_early, sides_late = refs[:n_sides], refs[n_sides : 2 * n_sides]
    before, *corners = refs[2 * n_sides : 3 * n_sides + 1]
    taps, feats, out_hbm, act, out, sems = refs[3 * n_sides + 1 :]
    stores = [pltpu.make_async_copy(out.at[f], out_hbm.at[f], sems.at[f]) for f in range(out.shape[0])]
    slabs = aux.shape[0] - 8
    starting = aux[slabs : slabs + 1] != 0.0
    affine = half_affine(traded_sums(tables, aux), aux, 1)
    n_frames, n_rows = out.shape[:2]

    def fill(frame):
        for row in range(n_rows + 2):
            if frame < 2:
                value = normed(extended_row(before, corners, frame, row), affine).astype(F32)
                act[frame, row] = jnp.where(starting, act[2, row].astype(F32), value).astype(BF16)
            elif frame < 4:
                act[frame, row] = normed(extended_row(early, sides_early, frame - 2, row), affine)
            else:
                act[frame, row] = normed(extended_row(late, sides_late, frame - 4, row), affine)

    for frame in range(2, 5):
        fill(frame)
    for frame in list(range(2, n_frames)) + [0, 1]:
        if frame == 0:
            fill(0)
            fill(1)
        elif 2 < frame:
            fill(frame + 2)
        for row, value in conv_rows([(act, frame + i) for i in range(3)], (taps.at[:1], taps.at[1:])):
            out[frame, row] = feats[frame, row].astype(F32) + value
        stores[frame].start()
    for store in stores:
        store.wait()


def call(kernel, outs, scratch, weight, operands, out_specs=None, aliases=None, outside=()):
    return pl.pallas_call(
        kernel,
        out_shape=outs,
        in_specs=[ANYWHERE if k in (aliases or {}) or k in outside else VMEM for k in range(len(operands))],
        out_specs=[VMEM] * len(outs) if out_specs is None else out_specs,
        scratch_shapes=scratch,
        input_output_aliases=aliases or {},
        compiler_params=vmem_params(),
        cost_estimate=pl.CostEstimate(flops=weight, bytes_accessed=1 << 20, transcendentals=1 << 20),
    )(*operands)


def on_device(feats, clip_ids, gain_one, shift_one, kernel_one, gain_two, shift_two, kernel_two):
    n_frames, n_rows, cols, width = feats.shape
    params = (gain_one, shift_one, gain_two, shift_two)
    per_slab = feats.size // GROUPS * lax.axis_size("space")
    late = n_frames - 2
    plane = (n_rows + 2, cols, width)
    act = pltpu.VMEM((2,) + plane, BF16)
    act_late = pltpu.VMEM((late,) + plane, BF16)
    work = 54 * feats.size // n_frames * width
    late_shapes = [shaped((2,) + plane), shaped((2, width), F32), shaped((2,) + kernel_one.shape[1:])]
    hidden_shapes = [shaped((late, n_rows, cols, width)), shaped((2, 8, width), F32), shaped(edge_shape(feats, late))]

    frames, tail, edges, copies, mark = entry_call(feats)
    table = stats_table(copies)
    sides = row_halo(edges)
    n_sides = len(sides)
    first, second = slab_halo(tail, sides)
    corners = row_halo(edges_of(first))
    taps, aux = setup_call(kernel_one, clip_ids, params, per_slab, mark)
    aux, *corners = lax.optimization_barrier((aux, *corners))
    operands = [aux, table, frames, *sides, taps, in_hbm(kernel_one)]
    act_low, affine, more_taps, hidden_late, stats, edges = call(
        functools.partial(late_kernel, n_sides),
        late_shapes + hidden_shapes,
        [act_late, pltpu.SemaphoreType.DMA((6,))],
        2 * work,
        operands,
        outside=(len(operands) - 1,),
    )
    before = shifted(hidden_late[late - 2 :], "tm", 1)
    sides_late = row_halo(edges)
    hidden_early, edges, stats = call(
        functools.partial(early_kernel, n_sides),
        [shaped((2, n_rows, cols, width)), shaped(edge_shape(feats, 2)), shaped((1, 2 * width), F32)],
        [act],
        2 * work,
        [aux, first, second, *corners, act_low, affine, taps, more_taps, stats],
    )

    sides_early = row_halo(edges)
    _, tables = slab_tables(stats)
    before, tables[0] = lax.optimization_barrier((before, tables[0]))
    corners = row_halo(edges_of(before))
    operands = [aux, *tables, hidden_early, hidden_late, *sides_early, *sides_late, before, *corners, kernel_two, frames]
    return call(
        functools.partial(last_kernel, len(tables), n_sides),
        shaped(feats.shape, F32),
        [pltpu.VMEM((n_frames + 2,) + plane, BF16), pltpu.VMEM(feats.shape, F32), pltpu.SemaphoreType.DMA((n_frames,))],
        n_frames * work,
        operands,
        out_specs=ANYWHERE,
    )


def solution(mesh):
    return jax.shard_map(
        on_device,
        mesh=mesh,
        in_specs=(P("tm", "space", None, None), P(), P(), P(), P(), P(), P(), P()),
        out_specs=P("tm", "space", None, None),
        check_vma=False,
    )
```

```python
import functools

import jax
import jax.numpy as jnp
from jax import lax
from jax.experimental import pallas as pl
from jax.experimental.pallas import tpu as pltpu
from jax.sharding import PartitionSpec as P

GROUPS = 32
TAIL = 2
F32, BF16 = jnp.float32, jnp.bfloat16


def vmem_params():
    return pltpu.CompilerParams(vmem_limit_bytes=32 << 20)


def shaped(shape, dtype=BF16):
    return jax.ShapeDtypeStruct(tuple(shape), dtype)


def in_hbm(value):
    return pltpu.with_memory_space_constraint(value, pltpu.HBM)


VMEM = pl.BlockSpec(memory_space=pltpu.VMEM)
ANYWHERE = pl.BlockSpec(memory_space=pl.ANY)


def traded(value, axis, mask):
    return lax.ppermute(value, axis, [(i, i ^ mask) for i in range(lax.axis_size(axis))])


def shifted(value, axis, step):
    peers = lax.axis_size(axis)
    return lax.ppermute(value, axis, [(i, (i + step) % peers) for i in range(peers)])


def stats_table(copies):
    return lax.all_to_all(copies, ("tm", "space"), 0, 0, tiled=True)


def group_sizes(peers):
    sizes = []
    while peers > 1:
        sizes.append(min(4, peers))
        peers //= sizes[-1]
    return sizes


def slab_offsets(peers):
    offsets, left = [0], peers
    for ways in group_sizes(peers):
        left //= ways
        offsets = [(left * way) ^ offset for way in range(ways) for offset in offsets]
    return offsets


def slab_tables(stats):
    peers = lax.axis_size("tm")
    total = stats + traded(stats, "space", 1) if lax.axis_size("space") == 2 else lax.psum(stats, "space")
    held, left = [total], peers
    for ways in group_sizes(peers):
        left //= ways
        block = held[0] if len(held) == 1 else jnp.concatenate(held, axis=0)
        held = [block] + [traded(block, "tm", left * way) for way in range(1, ways)]
    return total, held


def row_halo(edges):
    if lax.axis_size("space") == 2:
        return [traded(edges[0], "space", 1)]
    top, bottom = edges
    return [shifted(bottom, "space", 1), shifted(top, "space", -1)]


def edges_of(frames):
    rows = frames.shape[1]
    if lax.axis_size("space") == 2:
        return [lax.dynamic_slice_in_dim(frames, (rows - 1) * (1 - lax.axis_index("space")), 1, axis=1)]
    return [frames[:, :1], frames[:, rows - 1 :]]


def chained(value):
    return lax.ppermute(value, "tm", [(i, i + 1) for i in range(lax.axis_size("tm") - 1)])


def slab_halo(tail, sides):
    rows = [side[-1:] for side in sides]
    return shifted(tail[:1], "tm", 1), chained(jnp.concatenate([tail[1:], *rows], axis=1))


def row_halo(edges):
    if lax.axis_size("space") == 2:
        return [traded(edges, "space", 1)]
    return [shifted(edges[:, 1:], "space", 1), shifted(edges[:, :1], "space", -1)]


def edges_of(frames):
    rows = frames.shape[1]
    if lax.axis_size("space") == 2:
        return lax.dynamic_slice_in_dim(frames, (rows - 1) * (1 - lax.axis_index("space")), 1, axis=1)
    return jnp.concatenate([frames[:, :1], frames[:, rows - 1 :]], axis=1)


def edge_shape(frames, count):
    return (count, 1 if lax.axis_size("space") == 2 else 2) + frames.shape[2:]


def send_rows(source, frame, edges, at=0):
    rows = source.shape[1]
    if edges.shape[1] == 1:
        low = lax.axis_index("space") == 0
        edges[at + frame, 0] = jnp.where(low, source[frame, rows - 1], source[frame, 0])
    else:
        edges[at + frame, 0] = source[frame, 0]
        edges[at + frame, 1] = source[frame, rows - 1]


def add_stats(sums, values):
    width = values.shape[1]
    return (
        sums[0] + jnp.sum(values.reshape(-1, 8, width), axis=0),
        sums[1] + jnp.sum((values * values).reshape(-1, 8, width), axis=0),
    )


def no_stats(width):
    return jnp.zeros((8, width), F32), jnp.zeros((8, width), F32)


def store_stats(stats, sums):
    width = sums[0].shape[1]
    for k in range(2):
        stats[:, k * width : (k + 1) * width] = jnp.sum(sums[k], axis=0, keepdims=True)


def store_copies(copies, stats):
    copies[...] = jnp.broadcast_to(stats[...][None], copies.shape)


def device_count():
    return lax.axis_size("tm") * lax.axis_size("space")


def entry_kernel(feats_hbm, frames, tail, edges, copies, mark, stats, sems):
    n_frames, n_rows, _, width = frames.shape
    loads = [pltpu.make_async_copy(feats_hbm.at[f], frames.at[f], sems.at[f]) for f in range(n_frames)]
    for copy in loads:
        copy.start()
    mark[...] = jnp.zeros_like(mark)
    sums = no_stats(width)
    for frame in range(n_frames):
        loads[frame].wait()
        for row in range(n_rows):
            if frame >= n_frames - TAIL:
                tail[frame - n_frames + TAIL, row] = frames[frame, row]
            sums = add_stats(sums, frames[frame, row].astype(F32))
        send_rows(frames, frame, edges)
    store_stats(stats, sums)
    store_copies(copies, stats)


def copies_shape(width):
    return shaped((device_count(), 1, 2 * width), F32)


MARK = jax.ShapeDtypeStruct((8, 128), F32)


def entry_call(feats):
    n_frames, width = feats.shape[0], feats.shape[3]
    outs = [
        shaped(feats.shape),
        shaped((TAIL,) + feats.shape[1:]),
        shaped(edge_shape(feats, n_frames)),
        copies_shape(width),
        MARK,
    ]
    return pl.pallas_call(
        entry_kernel,
        out_shape=outs,
        in_specs=[ANYWHERE],
        out_specs=[VMEM] * len(outs),
        scratch_shapes=[pltpu.VMEM((1, 2 * width), F32), pltpu.SemaphoreType.DMA((n_frames,))],
        compiler_params=vmem_params(),
        cost_estimate=pl.CostEstimate(flops=4 * feats.size, bytes_accessed=4 * feats.size, transcendentals=0),
    )(in_hbm(feats))


def setup_kernel(slabs, per_slab, kernel_hbm, clips_hbm, *refs):
    params_hbm, (_, taps, aux, params, clips, sems) = refs[:4], refs[4:]
    taps_load = pltpu.make_async_copy(kernel_hbm.at[0], taps.at[0], sems.at[5])
    width = aux.shape[1]
    clip_load = pltpu.make_async_copy(clips_hbm, clips, sems.at[0])
    param_loads = [pltpu.make_async_copy(p, params.at[k], sems.at[1 + k]) for k, p in enumerate(params_hbm)]
    for copy in [clip_load, *param_loads, taps_load]:
        copy.start()
    clip_load.wait()
    own = lax.axis_index("tm")
    own_clip = clips[own]
    slabs_in = jnp.int32(0)
    for slab in range(slabs):
        same = (clips[slab] == own_clip).astype(jnp.int32)
        slabs_in = slabs_in + same
        aux[slab : slab + 1] = jnp.full((1, width), same.astype(F32), F32)
    offsets = slab_offsets(slabs)
    for entry, offset in enumerate(offsets):
        same = (clips[own ^ offset] == own_clip).astype(F32)
        aux[slabs + entry : slabs + entry + 1] = jnp.full((1, width), same, F32)
    slabs *= 2
    starting = jnp.logical_or(own == 0, clips[jnp.maximum(own - 1, 0)] != own_clip)
    aux[slabs : slabs + 1] = jnp.full((1, width), starting.astype(F32), F32)
    aux[slabs + 1 : slabs + 2] = jnp.full((1, width), slabs_in.astype(F32) * float(per_slab), F32)
    for k, copy in enumerate(param_loads):
        copy.wait()
        aux[slabs + 2 + k : slabs + 3 + k] = params[k]
    aux[slabs + 6 : slabs + 8] = jnp.zeros((2, width), F32)
    taps_load.wait()


def setup_call(kernel, clip_ids, params, per_slab, mark):
    slabs, width = lax.axis_size("tm"), params[0].shape[0]
    return pl.pallas_call(
        functools.partial(setup_kernel, slabs, per_slab),
        out_shape=[shaped((1,) + kernel.shape[1:]), shaped((2 * slabs + 8, width), F32)],
        in_specs=[ANYWHERE] * 6 + [VMEM],
        out_specs=[VMEM, VMEM],
        scratch_shapes=[
            pltpu.VMEM((4, 1, width), F32),
            pltpu.SMEM(clip_ids.shape, jnp.int32),
            pltpu.SemaphoreType.DMA((6,)),
        ],
        compiler_params=vmem_params(),
        cost_estimate=pl.CostEstimate(flops=1 << 30, bytes_accessed=1 << 16, transcendentals=0),
    )(*[in_hbm(x) for x in (kernel, clip_ids, *[p[None] for p in params])], mark)


def group_total(values):
    width = values.shape[-1]
    lane = lax.broadcasted_iota(jnp.int32, values.shape, 1)
    step = 1
    while step < width // GROUPS:
        upper = pltpu.roll(values, step, 1)
        lower = pltpu.roll(values, width - step, 1)
        values = values + jnp.where((lane & step) != 0, upper, lower)
        step *= 2
    return values


def gathered_sums(table, aux):
    width = aux.shape[1]
    slabs = (aux.shape[0] - 8) // 2
    places = table.shape[0] // slabs
    sums = []
    for k in range(2):
        parts = [
            aux[slab : slab + 1] * sum(table[slab * places + p, :, k * width : (k + 1) * width] for p in range(places))
            for slab in range(slabs)
        ]
        while len(parts) > 1:
            parts = [sum(parts[i : i + 2]) for i in range(0, len(parts), 2)]
        sums += parts
    return sums


def traded_sums(tables, aux):
    width = aux.shape[1]
    sums = [jnp.zeros((1, width), F32)] * 2
    entry = (aux.shape[0] - 8) // 2
    for table in tables:
        mask = aux[entry : entry + table.shape[0]]
        entry += table.shape[0]
        sums = [
            total + jnp.sum(table[:, k * width : (k + 1) * width] * mask, axis=0, keepdims=True) for k, total in enumerate(sums)
        ]
    return sums


def half_affine(sums, aux, which):
    slabs = aux.shape[0] - 8
    grouped = group_total(jnp.concatenate(sums, axis=0))
    count = aux[slabs + 1 : slabs + 2]
    gain = aux[slabs + 2 + 2 * which : slabs + 3 + 2 * which]
    shift = aux[slabs + 3 + 2 * which : slabs + 4 + 2 * which]
    mean = grouped[0:1] / count
    variance = grouped[1:2] / count - mean * mean
    scale = lax.rsqrt(variance + 1e-06) * gain
    return 0.5 * scale, 0.5 * (shift - mean * scale)


def normed(raw, affine):
    half = raw.astype(F32) * affine[0] + affine[1]
    return (half * jnp.tanh(half) + half).astype(BF16)


def extended_row(frames, sides, frame, row):
    n_rows = frames.shape[1]
    inner = frames[frame, min(max(row - 1, 0), n_rows - 1)]
    if 0 < row <= n_rows:
        return inner
    place, places = lax.axis_index("space"), lax.axis_size("space")
    side = sides[0 if row == 0 else -1]
    return jnp.where(place == (0 if row == 0 else places - 1), inner, side[frame, 0])


def conv_rows(planes, taps):
    ref, index = planes[0]
    n_rows, cols, width = ref.shape[1] - 2, ref.shape[2], ref.shape[3]
    lhs = jnp.concatenate(
        [ref[index, j : j + n_rows].reshape(n_rows * cols, width) for ref, index in planes for j in range(3)], axis=1
    )
    column = lax.broadcasted_iota(jnp.int32, (cols, width), 0)
    sums = []
    for l in range(3):
        rhs = jnp.concatenate([taps[0][0, j, l] for j in range(3)] + [taps[1][i, j, l] for i in range(2) for j in range(3)], axis=0)
        sums.append(jnp.dot(lhs, rhs, preferred_element_type=F32))
    for row in range(n_rows):
        left, mid, right = (s[row * cols : (row + 1) * cols] for s in sums)
        left = jnp.where(column == 0, left, pltpu.roll(left, 1, 0))
        right = jnp.where(column == cols - 1, right, pltpu.roll(right, cols - 1, 0))
        yield row, left + mid + right


def put_hidden(hidden, frame, row, value, sums):
    rounded = value.astype(BF16)
    hidden[frame, row] = rounded
    return add_stats(sums, rounded.astype(F32))


def late_kernel(n_sides, aux, table, frames, *refs):
    sides, first_taps, kernel_hbm = refs[:n_sides], refs[n_sides], refs[n_sides + 1]
    act_low, affine_out, more_taps, hidden, stats, edges, act_high, taps_sems = refs[n_sides + 2 :]
    taps = (first_taps, more_taps)
    loads = [
        pltpu.make_async_copy(kernel_hbm.at[i, j], more_taps.at[i - 1, j], taps_sems.at[3 * (i - 1) + j])
        for i in range(1, 3)
        for j in range(3)
    ]
    for copy in loads:
        copy.start()
    n_rows, width = frames.shape[1], frames.shape[3]
    low, high = act_low.shape[0], act_high.shape[0]
    affine = half_affine(gathered_sums(table, aux), aux, 0)
    for k in range(2):
        affine_out[k : k + 1] = affine[k]
    planes = [(act_low, f) for f in range(low)] + [(act_high, f) for f in range(high)]

    def fill(frame):
        act, index = planes[frame]
        for row in range(n_rows + 2):
            act[index, row] = normed(extended_row(frames, sides, frame, row), affine)

    for frame in range(low):
        fill(frame)
    for copy in loads:
        copy.wait()
    fill(low)
    sums = no_stats(width)
    for frame in range(high):
        for row, value in conv_rows(planes[frame : frame + 3], taps):
            sums = put_hidden(hidden, frame, row, value, sums)
        send_rows(hidden, frame, edges)
        if frame + 1 < high:
            fill(low + frame + 1)
    for k in range(2):
        stats[k] = sums[k]


def early_kernel(n_sides, aux, first, second, *refs):
    corners, (act_low, affine_in, *taps), refs = refs[:n_sides], refs[n_sides : n_sides + 4], refs[n_sides + 4 :]
    late_stats, hidden, edges, stats, act_before = refs
    sums = late_stats[0], late_stats[1]
    slabs = aux.shape[0] - 8
    starting = aux[slabs : slabs + 1] != 0.0
    affine = affine_in[0:1], affine_in[1:2]
    n_rows = first.shape[1]
    for row in range(n_rows + 2):
        for frame in range(2):
            if frame == 0:
                raw = extended_row(first, corners, 0, row)
            else:
                raw = extended_row(second.at[:, :n_rows], [second.at[:, n_rows + k :] for k in range(n_sides)], 0, row)
            value = normed(raw, affine).astype(F32)
            act_before[frame, row] = jnp.where(starting, act_low[0, row].astype(F32), value).astype(BF16)
    planes = [(act_before, 0), (act_before, 1)] + [(act_low, f) for f in range(act_low.shape[0])]
    for frame in range(2):
        for row, value in conv_rows(planes[frame : frame + 3], taps):
            sums = put_hidden(hidden, frame, row, value, sums)
        send_rows(hidden, frame, edges)
    store_stats(stats, sums)


def last_kernel(n_tables, n_sides, aux, *refs):
    tables, early, late, refs = refs[:n_tables], refs[n_tables], refs[n_tables + 1], refs[n_tables + 2 :]
    sides_early, sides_late = refs[:n_sides], refs[n_sides : 2 * n_sides]
    before, *corners = refs[2 * n_sides : 3 * n_sides + 1]
    taps, feats, out_hbm, act, out, sems = refs[3 * n_sides + 1 :]
    stores = [pltpu.make_async_copy(out.at[f], out_hbm.at[f], sems.at[f]) for f in range(out.shape[0])]
    slabs = aux.shape[0] - 8
    starting = aux[slabs : slabs + 1] != 0.0
    affine = half_affine(traded_sums(tables, aux), aux, 1)
    n_frames, n_rows = out.shape[:2]

    def fill(frame):
        for row in range(n_rows + 2):
            if frame < 2:
                value = normed(extended_row(before, corners, frame, row), affine).astype(F32)
                act[frame, row] = jnp.where(starting, act[2, row].astype(F32), value).astype(BF16)
            elif frame < 4:
                act[frame, row] = normed(extended_row(early, sides_early, frame - 2, row), affine)
            else:
                act[frame, row] = normed(extended_row(late, sides_late, frame - 4, row), affine)

    for frame in range(2, 5):
        fill(frame)
    for frame in list(range(2, n_frames)) + [0, 1]:
        if frame == 0:
            fill(0)
            fill(1)
        elif 2 < frame:
            fill(frame + 2)
        for row, value in conv_rows([(act, frame + i) for i in range(3)], (taps.at[:1], taps.at[1:])):
            out[frame, row] = feats[frame, row].astype(F32) + value
        stores[frame].start()
    for store in stores:
        store.wait()


def call(kernel, outs, scratch, weight, operands, out_specs=None, aliases=None, outside=()):
    return pl.pallas_call(
        kernel,
        out_shape=outs,
        in_specs=[ANYWHERE if k in (aliases or {}) or k in outside else VMEM for k in range(len(operands))],
        out_specs=[VMEM] * len(outs) if out_specs is None else out_specs,
        scratch_shapes=scratch,
        input_output_aliases=aliases or {},
        compiler_params=vmem_params(),
        cost_estimate=pl.CostEstimate(flops=weight, bytes_accessed=1 << 20, transcendentals=1 << 20),
    )(*operands)


def on_device(feats, clip_ids, gain_one, shift_one, kernel_one, gain_two, shift_two, kernel_two):
    n_frames, n_rows, cols, width = feats.shape
    params = (gain_one, shift_one, gain_two, shift_two)
    per_slab = feats.size // GROUPS * lax.axis_size("space")
    late = n_frames - 2
    plane = (n_rows + 2, cols, width)
    act = pltpu.VMEM((2,) + plane, BF16)
    act_late = pltpu.VMEM((late,) + plane, BF16)
    work = 54 * feats.size // n_frames * width
    late_shapes = [shaped((2,) + plane), shaped((2, width), F32), shaped((2,) + kernel_one.shape[1:])]
    hidden_shapes = [shaped((late, n_rows, cols, width)), shaped((2, 8, width), F32), shaped(edge_shape(feats, late))]

    frames, tail, edges, copies, mark = entry_call(feats)
    table = stats_table(copies)
    sides = row_halo(edges)
    n_sides = len(sides)
    first, second = slab_halo(tail, sides)
    corners = row_halo(edges_of(first))
    taps, aux = setup_call(kernel_one, clip_ids, params, per_slab, mark)
    aux, *corners = lax.optimization_barrier((aux, *corners))
    operands = [aux, table, frames, *sides, taps, in_hbm(kernel_one)]
    act_low, affine, more_taps, hidden_late, stats, edges = call(
        functools.partial(late_kernel, n_sides),
        late_shapes + hidden_shapes,
        [act_late, pltpu.SemaphoreType.DMA((6,))],
        work * 3 // 4,
        operands,
        outside=(len(operands) - 1,),
    )
    before = shifted(hidden_late[late - 2 :], "tm", 1)
    sides_late = row_halo(edges)
    hidden_early, edges, stats = call(
        functools.partial(early_kernel, n_sides),
        [shaped((2, n_rows, cols, width)), shaped(edge_shape(feats, 2)), shaped((1, 2 * width), F32)],
        [act],
        2 * work,
        [aux, first, second, *corners, act_low, affine, taps, more_taps, stats],
    )

    sides_early = row_halo(edges)
    _, tables = slab_tables(stats)
    before, tables[0] = lax.optimization_barrier((before, tables[0]))
    corners = row_halo(edges_of(before))
    operands = [aux, *tables, hidden_early, hidden_late, *sides_early, *sides_late, before, *corners, kernel_two, frames]
    return call(
        functools.partial(last_kernel, len(tables), n_sides),
        shaped(feats.shape, F32),
        [pltpu.VMEM((n_frames + 2,) + plane, BF16), pltpu.VMEM(feats.shape, F32), pltpu.SemaphoreType.DMA((n_frames,))],
        n_frames * work,
        operands,
        out_specs=ANYWHERE,
    )


def solution(mesh):
    return jax.shard_map(
        on_device,
        mesh=mesh,
        in_specs=(P("tm", "space", None, None), P(), P(), P(), P(), P(), P(), P()),
        out_specs=P("tm", "space", None, None),
        check_vma=False,
    )
```

```python
import functools

import jax
import jax.numpy as jnp
from jax import lax
from jax.experimental import pallas as pl
from jax.experimental.pallas import tpu as pltpu
from jax.sharding import PartitionSpec as P

GROUPS = 32
TAIL = 2
F32, BF16 = jnp.float32, jnp.bfloat16


def vmem_params():
    return pltpu.CompilerParams(vmem_limit_bytes=32 << 20)


def shaped(shape, dtype=BF16):
    return jax.ShapeDtypeStruct(tuple(shape), dtype)


def in_hbm(value):
    return pltpu.with_memory_space_constraint(value, pltpu.HBM)


VMEM = pl.BlockSpec(memory_space=pltpu.VMEM)
ANYWHERE = pl.BlockSpec(memory_space=pl.ANY)


def traded(value, axis, mask):
    return lax.ppermute(value, axis, [(i, i ^ mask) for i in range(lax.axis_size(axis))])


def shifted(value, axis, step):
    peers = lax.axis_size(axis)
    return lax.ppermute(value, axis, [(i, (i + step) % peers) for i in range(peers)])


def stats_table(copies):
    return lax.all_to_all(copies, ("tm", "space"), 0, 0, tiled=True)


def group_sizes(peers):
    sizes = []
    while peers > 1:
        sizes.append(min(4, peers))
        peers //= sizes[-1]
    return sizes


def slab_offsets(peers):
    offsets, left = [0], peers
    for ways in group_sizes(peers):
        left //= ways
        offsets = [(left * way) ^ offset for way in range(ways) for offset in offsets]
    return offsets


def slab_tables(stats):
    peers = lax.axis_size("tm")
    total = stats + traded(stats, "space", 1) if lax.axis_size("space") == 2 else lax.psum(stats, "space")
    held, left = [total], peers
    for ways in group_sizes(peers):
        left //= ways
        block = held[0] if len(held) == 1 else jnp.concatenate(held, axis=0)
        held = [block] + [traded(block, "tm", left * way) for way in range(1, ways)]
    return total, held


def row_halo(edges):
    if lax.axis_size("space") == 2:
        return [traded(edges[0], "space", 1)]
    top, bottom = edges
    return [shifted(bottom, "space", 1), shifted(top, "space", -1)]


def edges_of(frames):
    rows = frames.shape[1]
    if lax.axis_size("space") == 2:
        return [lax.dynamic_slice_in_dim(frames, (rows - 1) * (1 - lax.axis_index("space")), 1, axis=1)]
    return [frames[:, :1], frames[:, rows - 1 :]]


def chained(value):
    return lax.ppermute(value, "tm", [(i, i + 1) for i in range(lax.axis_size("tm") - 1)])


def slab_halo(tail, sides):
    rows = [side[-1:] for side in sides]
    return shifted(tail[:1], "tm", 1), chained(jnp.concatenate([tail[1:], *rows], axis=1))


def row_halo(edges):
    if lax.axis_size("space") == 2:
        return [traded(edges, "space", 1)]
    return [shifted(edges[:, 1:], "space", 1), shifted(edges[:, :1], "space", -1)]


def edges_of(frames):
    rows = frames.shape[1]
    if lax.axis_size("space") == 2:
        return lax.dynamic_slice_in_dim(frames, (rows - 1) * (1 - lax.axis_index("space")), 1, axis=1)
    return jnp.concatenate([frames[:, :1], frames[:, rows - 1 :]], axis=1)


def edge_shape(frames, count):
    return (count, 1 if lax.axis_size("space") == 2 else 2) + frames.shape[2:]


def send_rows(source, frame, edges, at=0):
    rows = source.shape[1]
    if edges.shape[1] == 1:
        low = lax.axis_index("space") == 0
        edges[at + frame, 0] = jnp.where(low, source[frame, rows - 1], source[frame, 0])
    else:
        edges[at + frame, 0] = source[frame, 0]
        edges[at + frame, 1] = source[frame, rows - 1]


def add_stats(sums, values):
    width = values.shape[1]
    return (
        sums[0] + jnp.sum(values.reshape(-1, 8, width), axis=0),
        sums[1] + jnp.sum((values * values).reshape(-1, 8, width), axis=0),
    )


def no_stats(width):
    return jnp.zeros((8, width), F32), jnp.zeros((8, width), F32)


def store_stats(stats, sums):
    width = sums[0].shape[1]
    for k in range(2):
        stats[:, k * width : (k + 1) * width] = jnp.sum(sums[k], axis=0, keepdims=True)


def store_copies(copies, stats):
    copies[...] = jnp.broadcast_to(stats[...][None], copies.shape)


def device_count():
    return lax.axis_size("tm") * lax.axis_size("space")


def entry_kernel(feats_hbm, frames, tail, edges, copies, mark, stats, sems):
    n_frames, n_rows, _, width = frames.shape
    loads = [pltpu.make_async_copy(feats_hbm.at[f], frames.at[f], sems.at[f]) for f in range(n_frames)]
    for copy in loads:
        copy.start()
    mark[...] = jnp.zeros_like(mark)
    sums = no_stats(width)
    for frame in range(n_frames):
        loads[frame].wait()
        for row in range(n_rows):
            if frame >= n_frames - TAIL:
                tail[frame - n_frames + TAIL, row] = frames[frame, row]
            sums = add_stats(sums, frames[frame, row].astype(F32))
        send_rows(frames, frame, edges)
    store_stats(stats, sums)
    store_copies(copies, stats)


def copies_shape(width):
    return shaped((device_count(), 1, 2 * width), F32)


MARK = jax.ShapeDtypeStruct((8, 128), F32)


def entry_call(feats):
    n_frames, width = feats.shape[0], feats.shape[3]
    outs = [
        shaped(feats.shape),
        shaped((TAIL,) + feats.shape[1:]),
        shaped(edge_shape(feats, n_frames)),
        copies_shape(width),
        MARK,
    ]
    return pl.pallas_call(
        entry_kernel,
        out_shape=outs,
        in_specs=[ANYWHERE],
        out_specs=[VMEM] * len(outs),
        scratch_shapes=[pltpu.VMEM((1, 2 * width), F32), pltpu.SemaphoreType.DMA((n_frames,))],
        compiler_params=vmem_params(),
        cost_estimate=pl.CostEstimate(flops=4 * feats.size, bytes_accessed=4 * feats.size, transcendentals=0),
    )(in_hbm(feats))


def setup_kernel(slabs, per_slab, kernel_hbm, clips_hbm, *refs):
    params_hbm, (_, taps, aux, params, clips, sems) = refs[:4], refs[4:]
    taps_load = pltpu.make_async_copy(kernel_hbm.at[0], taps.at[0], sems.at[5])
    width = aux.shape[1]
    clip_load = pltpu.make_async_copy(clips_hbm, clips, sems.at[0])
    param_loads = [pltpu.make_async_copy(p, params.at[k], sems.at[1 + k]) for k, p in enumerate(params_hbm)]
    for copy in [clip_load, *param_loads, taps_load]:
        copy.start()
    clip_load.wait()
    own = lax.axis_index("tm")
    own_clip = clips[own]
    slabs_in = jnp.int32(0)
    for slab in range(slabs):
        same = (clips[slab] == own_clip).astype(jnp.int32)
        slabs_in = slabs_in + same
        aux[slab : slab + 1] = jnp.full((1, width), same.astype(F32), F32)
    offsets = slab_offsets(slabs)
    for entry, offset in enumerate(offsets):
        same = (clips[own ^ offset] == own_clip).astype(F32)
        aux[slabs + entry : slabs + entry + 1] = jnp.full((1, width), same, F32)
    slabs *= 2
    starting = jnp.logical_or(own == 0, clips[jnp.maximum(own - 1, 0)] != own_clip)
    aux[slabs : slabs + 1] = jnp.full((1, width), starting.astype(F32), F32)
    aux[slabs + 1 : slabs + 2] = jnp.full((1, width), slabs_in.astype(F32) * float(per_slab), F32)
    for k, copy in enumerate(param_loads):
        copy.wait()
        aux[slabs + 2 + k : slabs + 3 + k] = params[k]
    aux[slabs + 6 : slabs + 8] = jnp.zeros((2, width), F32)
    taps_load.wait()


def setup_call(kernel, clip_ids, params, per_slab, mark):
    slabs, width = lax.axis_size("tm"), params[0].shape[0]
    return pl.pallas_call(
        functools.partial(setup_kernel, slabs, per_slab),
        out_shape=[shaped((1,) + kernel.shape[1:]), shaped((2 * slabs + 8, width), F32)],
        in_specs=[ANYWHERE] * 6 + [VMEM],
        out_specs=[VMEM, VMEM],
        scratch_shapes=[
            pltpu.VMEM((4, 1, width), F32),
            pltpu.SMEM(clip_ids.shape, jnp.int32),
            pltpu.SemaphoreType.DMA((6,)),
        ],
        compiler_params=vmem_params(),
        cost_estimate=pl.CostEstimate(flops=1 << 30, bytes_accessed=1 << 16, transcendentals=0),
    )(*[in_hbm(x) for x in (kernel, clip_ids, *[p[None] for p in params])], mark)


def group_total(values):
    width = values.shape[-1]
    lane = lax.broadcasted_iota(jnp.int32, values.shape, 1)
    step = 1
    while step < width // GROUPS:
        upper = pltpu.roll(values, step, 1)
        lower = pltpu.roll(values, width - step, 1)
        values = values + jnp.where((lane & step) != 0, upper, lower)
        step *= 2
    return values


def gathered_sums(table, aux):
    width = aux.shape[1]
    slabs = (aux.shape[0] - 8) // 2
    places = table.shape[0] // slabs
    sums = []
    for k in range(2):
        parts = [
            aux[slab : slab + 1] * sum(table[slab * places + p, :, k * width : (k + 1) * width] for p in range(places))
            for slab in range(slabs)
        ]
        while len(parts) > 1:
            parts = [sum(parts[i : i + 2]) for i in range(0, len(parts), 2)]
        sums += parts
    return sums


def traded_sums(tables, aux):
    width = aux.shape[1]
    sums = [jnp.zeros((1, width), F32)] * 2
    entry = (aux.shape[0] - 8) // 2
    for table in tables:
        mask = aux[entry : entry + table.shape[0]]
        entry += table.shape[0]
        sums = [
            total + jnp.sum(table[:, k * width : (k + 1) * width] * mask, axis=0, keepdims=True) for k, total in enumerate(sums)
        ]
    return sums


def half_affine(sums, aux, which):
    slabs = aux.shape[0] - 8
    grouped = group_total(jnp.concatenate(sums, axis=0))
    count = aux[slabs + 1 : slabs + 2]
    gain = aux[slabs + 2 + 2 * which : slabs + 3 + 2 * which]
    shift = aux[slabs + 3 + 2 * which : slabs + 4 + 2 * which]
    mean = grouped[0:1] / count
    variance = grouped[1:2] / count - mean * mean
    scale = lax.rsqrt(variance + 1e-06) * gain
    return 0.5 * scale, 0.5 * (shift - mean * scale)


def normed(raw, affine):
    half = raw.astype(F32) * affine[0] + affine[1]
    return (half * jnp.tanh(half) + half).astype(BF16)


def extended_row(frames, sides, frame, row):
    n_rows = frames.shape[1]
    inner = frames[frame, min(max(row - 1, 0), n_rows - 1)]
    if 0 < row <= n_rows:
        return inner
    place, places = lax.axis_index("space"), lax.axis_size("space")
    side = sides[0 if row == 0 else -1]
    return jnp.where(place == (0 if row == 0 else places - 1), inner, side[frame, 0])


def conv_rows(planes, taps):
    ref, index = planes[0]
    n_rows, cols, width = ref.shape[1] - 2, ref.shape[2], ref.shape[3]
    lhs = jnp.concatenate(
        [ref[index, j : j + n_rows].reshape(n_rows * cols, width) for ref, index in planes for j in range(3)], axis=1
    )
    column = lax.broadcasted_iota(jnp.int32, (cols, width), 0)
    sums = []
    for l in range(3):
        rhs = jnp.concatenate([taps[0][0, j, l] for j in range(3)] + [taps[1][i, j, l] for i in range(2) for j in range(3)], axis=0)
        sums.append(jnp.dot(lhs, rhs, preferred_element_type=F32))
    for row in range(n_rows):
        left, mid, right = (s[row * cols : (row + 1) * cols] for s in sums)
        left = jnp.where(column == 0, left, pltpu.roll(left, 1, 0))
        right = jnp.where(column == cols - 1, right, pltpu.roll(right, cols - 1, 0))
        yield row, left + mid + right


def put_hidden(hidden, frame, row, value, sums):
    rounded = value.astype(BF16)
    hidden[frame, row] = rounded
    return add_stats(sums, rounded.astype(F32))


def late_kernel(n_sides, aux, table, frames, *refs):
    sides, first_taps, kernel_hbm = refs[:n_sides], refs[n_sides], refs[n_sides + 1]
    act_low, affine_out, more_taps, hidden, stats, edges, act_high, taps_sems = refs[n_sides + 2 :]
    taps = (first_taps, more_taps)
    loads = [
        pltpu.make_async_copy(kernel_hbm.at[i, j], more_taps.at[i - 1, j], taps_sems.at[3 * (i - 1) + j])
        for i in range(1, 3)
        for j in range(3)
    ]
    for copy in loads:
        copy.start()
    n_rows, width = frames.shape[1], frames.shape[3]
    low, high = act_low.shape[0], act_high.shape[0]
    affine = half_affine(gathered_sums(table, aux), aux, 0)
    for k in range(2):
        affine_out[k : k + 1] = affine[k]
    planes = [(act_low, f) for f in range(low)] + [(act_high, f) for f in range(high)]

    def fill(frame):
        act, index = planes[frame]
        for row in range(n_rows + 2):
            act[index, row] = normed(extended_row(frames, sides, frame, row), affine)

    for frame in range(low):
        fill(frame)
    for copy in loads:
        copy.wait()
    fill(low)
    sums = no_stats(width)
    for frame in range(high):
        for row, value in conv_rows(planes[frame : frame + 3], taps):
            sums = put_hidden(hidden, frame, row, value, sums)
        send_rows(hidden, frame, edges)
        if frame + 1 < high:
            fill(low + frame + 1)
    for k in range(2):
        stats[k] = sums[k]


def early_kernel(n_sides, aux, first, second, *refs):
    corners, (act_low, affine_in, *taps), refs = refs[:n_sides], refs[n_sides : n_sides + 4], refs[n_sides + 4 :]
    late_stats, hidden, edges, stats, act_before = refs
    sums = late_stats[0], late_stats[1]
    slabs = aux.shape[0] - 8
    starting = aux[slabs : slabs + 1] != 0.0
    affine = affine_in[0:1], affine_in[1:2]
    n_rows = first.shape[1]
    for row in range(n_rows + 2):
        for frame in range(2):
            if frame == 0:
                raw = extended_row(first, corners, 0, row)
            else:
                raw = extended_row(second.at[:, :n_rows], [second.at[:, n_rows + k :] for k in range(n_sides)], 0, row)
            value = normed(raw, affine).astype(F32)
            act_before[frame, row] = jnp.where(starting, act_low[0, row].astype(F32), value).astype(BF16)
    planes = [(act_before, 0), (act_before, 1)] + [(act_low, f) for f in range(act_low.shape[0])]
    for frame in range(2):
        for row, value in conv_rows(planes[frame : frame + 3], taps):
            sums = put_hidden(hidden, frame, row, value, sums)
        send_rows(hidden, frame, edges)
    store_stats(stats, sums)


def last_kernel(n_tables, n_sides, aux, *refs):
    tables, early, late, refs = refs[:n_tables], refs[n_tables], refs[n_tables + 1], refs[n_tables + 2 :]
    sides_early, sides_late = refs[:n_sides], refs[n_sides : 2 * n_sides]
    before, *corners = refs[2 * n_sides : 3 * n_sides + 1]
    taps, feats, out_hbm, act, out, sems = refs[3 * n_sides + 1 :]
    stores = [pltpu.make_async_copy(out.at[f], out_hbm.at[f], sems.at[f]) for f in range(out.shape[0])]
    slabs = aux.shape[0] - 8
    starting = aux[slabs : slabs + 1] != 0.0
    affine = half_affine(traded_sums(tables, aux), aux, 1)
    n_frames, n_rows = out.shape[:2]

    def fill(frame):
        for row in range(n_rows + 2):
            if frame < 2:
                value = normed(extended_row(before, corners, frame, row), affine).astype(F32)
                act[frame, row] = jnp.where(starting, act[2, row].astype(F32), value).astype(BF16)
            elif frame < 4:
                act[frame, row] = normed(extended_row(early, sides_early, frame - 2, row), affine)
            else:
                act[frame, row] = normed(extended_row(late, sides_late, frame - 4, row), affine)

    for frame in range(2, 5):
        fill(frame)
    for frame in list(range(2, n_frames)) + [0, 1]:
        if frame == 0:
            fill(0)
            fill(1)
        elif 2 < frame:
            fill(frame + 2)
        for row, value in conv_rows([(act, frame + i) for i in range(3)], (taps.at[:1], taps.at[1:])):
            out[frame, row] = feats[frame, row].astype(F32) + value
        stores[frame].start()
    for store in stores:
        store.wait()


def call(kernel, outs, scratch, weight, operands, out_specs=None, aliases=None, outside=()):
    return pl.pallas_call(
        kernel,
        out_shape=outs,
        in_specs=[ANYWHERE if k in (aliases or {}) or k in outside else VMEM for k in range(len(operands))],
        out_specs=[VMEM] * len(outs) if out_specs is None else out_specs,
        scratch_shapes=scratch,
        input_output_aliases=aliases or {},
        compiler_params=vmem_params(),
        cost_estimate=pl.CostEstimate(flops=weight, bytes_accessed=1 << 20, transcendentals=1 << 20),
    )(*operands)


def on_device(feats, clip_ids, gain_one, shift_one, kernel_one, gain_two, shift_two, kernel_two):
    n_frames, n_rows, cols, width = feats.shape
    params = (gain_one, shift_one, gain_two, shift_two)
    per_slab = feats.size // GROUPS * lax.axis_size("space")
    late = n_frames - 2
    plane = (n_rows + 2, cols, width)
    act = pltpu.VMEM((2,) + plane, BF16)
    act_late = pltpu.VMEM((late,) + plane, BF16)
    work = 54 * feats.size // n_frames * width
    late_shapes = [shaped((2,) + plane), shaped((2, width), F32), shaped((2,) + kernel_one.shape[1:])]
    hidden_shapes = [shaped((late, n_rows, cols, width)), shaped((2, 8, width), F32), shaped(edge_shape(feats, late))]

    frames, tail, edges, copies, mark = entry_call(feats)
    table = stats_table(copies)
    sides = row_halo(edges)
    n_sides = len(sides)
    first, second = slab_halo(tail, sides)
    corners = row_halo(edges_of(first))
    taps, aux = setup_call(kernel_one, clip_ids, params, per_slab, mark)
    aux, *corners = lax.optimization_barrier((aux, *corners))
    operands = [aux, table, frames, *sides, taps, in_hbm(kernel_one)]
    act_low, affine, more_taps, hidden_late, stats, edges = call(
        functools.partial(late_kernel, n_sides),
        late_shapes + hidden_shapes,
        [act_late, pltpu.SemaphoreType.DMA((6,))],
        work * 3 // 4,
        operands,
        outside=(len(operands) - 1,),
    )
    before = chained(hidden_late[late - 2 :])
    sides_late = row_halo(edges)
    hidden_early, edges, stats = call(
        functools.partial(early_kernel, n_sides),
        [shaped((2, n_rows, cols, width)), shaped(edge_shape(feats, 2)), shaped((1, 2 * width), F32)],
        [act],
        2 * work,
        [aux, first, second, *corners, act_low, affine, taps, more_taps, stats],
    )

    sides_early = row_halo(edges)
    _, tables = slab_tables(stats)
    before, tables[0] = lax.optimization_barrier((before, tables[0]))
    corners = row_halo(edges_of(before))
    operands = [aux, *tables, hidden_early, hidden_late, *sides_early, *sides_late, before, *corners, kernel_two, frames]
    return call(
        functools.partial(last_kernel, len(tables), n_sides),
        shaped(feats.shape, F32),
        [pltpu.VMEM((n_frames + 2,) + plane, BF16), pltpu.VMEM(feats.shape, F32), pltpu.SemaphoreType.DMA((n_frames,))],
        n_frames * work,
        operands,
        out_specs=ANYWHERE,
    )


def solution(mesh):
    return jax.shard_map(
        on_device,
        mesh=mesh,
        in_specs=(P("tm", "space", None, None), P(), P(), P(), P(), P(), P(), P()),
        out_specs=P("tm", "space", None, None),
        check_vma=False,
    )
```

```python
import functools

import jax
import jax.numpy as jnp
from jax import lax
from jax.experimental import pallas as pl
from jax.experimental.pallas import tpu as pltpu
from jax.sharding import PartitionSpec as P

GROUPS = 32
TAIL = 2
F32, BF16 = jnp.float32, jnp.bfloat16


def vmem_params():
    return pltpu.CompilerParams(vmem_limit_bytes=32 << 20)


def shaped(shape, dtype=BF16):
    return jax.ShapeDtypeStruct(tuple(shape), dtype)


def in_hbm(value):
    return pltpu.with_memory_space_constraint(value, pltpu.HBM)


VMEM = pl.BlockSpec(memory_space=pltpu.VMEM)
ANYWHERE = pl.BlockSpec(memory_space=pl.ANY)


def traded(value, axis, mask):
    return lax.ppermute(value, axis, [(i, i ^ mask) for i in range(lax.axis_size(axis))])


def shifted(value, axis, step):
    peers = lax.axis_size(axis)
    return lax.ppermute(value, axis, [(i, (i + step) % peers) for i in range(peers)])


def stats_table(copies):
    return lax.all_to_all(copies, ("tm", "space"), 0, 0, tiled=True)


def group_sizes(peers):
    sizes = []
    while peers > 1:
        sizes.append(min(4, peers))
        peers //= sizes[-1]
    return sizes


def slab_offsets(peers):
    offsets, left = [0], peers
    for ways in group_sizes(peers):
        left //= ways
        offsets = [(left * way) ^ offset for way in range(ways) for offset in offsets]
    return offsets


def slab_tables(stats):
    peers = lax.axis_size("tm")
    total = stats + traded(stats, "space", 1) if lax.axis_size("space") == 2 else lax.psum(stats, "space")
    held, left = [total], peers
    for ways in group_sizes(peers):
        left //= ways
        block = held[0] if len(held) == 1 else jnp.concatenate(held, axis=0)
        held = [block] + [traded(block, "tm", left * way) for way in range(1, ways)]
    return total, held


def row_halo(edges):
    if lax.axis_size("space") == 2:
        return [traded(edges[0], "space", 1)]
    top, bottom = edges
    return [shifted(bottom, "space", 1), shifted(top, "space", -1)]


def edges_of(frames):
    rows = frames.shape[1]
    if lax.axis_size("space") == 2:
        return [lax.dynamic_slice_in_dim(frames, (rows - 1) * (1 - lax.axis_index("space")), 1, axis=1)]
    return [frames[:, :1], frames[:, rows - 1 :]]


def chained(value):
    return lax.ppermute(value, "tm", [(i, i + 1) for i in range(lax.axis_size("tm") - 1)])


def slab_halo(tail, sides):
    rows = [side[-1:] for side in sides]
    return shifted(tail[:1], "tm", 1), chained(jnp.concatenate([tail[1:], *rows], axis=1))


def row_halo(edges):
    if lax.axis_size("space") == 2:
        return [traded(edges, "space", 1)]
    return [shifted(edges[:, 1:], "space", 1), shifted(edges[:, :1], "space", -1)]


def edges_of(frames):
    rows = frames.shape[1]
    if lax.axis_size("space") == 2:
        return lax.dynamic_slice_in_dim(frames, (rows - 1) * (1 - lax.axis_index("space")), 1, axis=1)
    return jnp.concatenate([frames[:, :1], frames[:, rows - 1 :]], axis=1)


def edge_shape(frames, count):
    return (count, 1 if lax.axis_size("space") == 2 else 2) + frames.shape[2:]


def send_rows(source, frame, edges, at=0):
    rows = source.shape[1]
    if edges.shape[1] == 1:
        low = lax.axis_index("space") == 0
        edges[at + frame, 0] = jnp.where(low, source[frame, rows - 1], source[frame, 0])
    else:
        edges[at + frame, 0] = source[frame, 0]
        edges[at + frame, 1] = source[frame, rows - 1]


def add_stats(sums, values):
    width = values.shape[1]
    return (
        sums[0] + jnp.sum(values.reshape(-1, 8, width), axis=0),
        sums[1] + jnp.sum((values * values).reshape(-1, 8, width), axis=0),
    )


def no_stats(width):
    return jnp.zeros((8, width), F32), jnp.zeros((8, width), F32)


def store_stats(stats, sums):
    width = sums[0].shape[1]
    for k in range(2):
        stats[:, k * width : (k + 1) * width] = jnp.sum(sums[k], axis=0, keepdims=True)


def store_copies(copies, stats):
    copies[...] = jnp.broadcast_to(stats[...][None], copies.shape)


def device_count():
    return lax.axis_size("tm") * lax.axis_size("space")


def entry_kernel(feats_hbm, frames, tail, edges, copies, mark, stats, sems):
    n_frames, n_rows, _, width = frames.shape
    loads = [pltpu.make_async_copy(feats_hbm.at[f], frames.at[f], sems.at[f]) for f in range(n_frames)]
    for copy in loads:
        copy.start()
    mark[...] = jnp.zeros_like(mark)
    sums = no_stats(width)
    for frame in range(n_frames):
        loads[frame].wait()
        for row in range(n_rows):
            if frame >= n_frames - TAIL:
                tail[frame - n_frames + TAIL, row] = frames[frame, row]
            sums = add_stats(sums, frames[frame, row].astype(F32))
        send_rows(frames, frame, edges)
    store_stats(stats, sums)
    store_copies(copies, stats)


def copies_shape(width):
    return shaped((device_count(), 1, 2 * width), F32)


MARK = jax.ShapeDtypeStruct((8, 128), F32)


def entry_call(feats):
    n_frames, width = feats.shape[0], feats.shape[3]
    outs = [
        shaped(feats.shape),
        shaped((TAIL,) + feats.shape[1:]),
        shaped(edge_shape(feats, n_frames)),
        copies_shape(width),
        MARK,
    ]
    return pl.pallas_call(
        entry_kernel,
        out_shape=outs,
        in_specs=[ANYWHERE],
        out_specs=[VMEM] * len(outs),
        scratch_shapes=[pltpu.VMEM((1, 2 * width), F32), pltpu.SemaphoreType.DMA((n_frames,))],
        compiler_params=vmem_params(),
        cost_estimate=pl.CostEstimate(flops=4 * feats.size, bytes_accessed=4 * feats.size, transcendentals=0),
    )(in_hbm(feats))


def setup_kernel(slabs, per_slab, kernel_hbm, clips_hbm, *refs):
    params_hbm, (_, taps, aux, params, clips, sems) = refs[:4], refs[4:]
    taps_load = pltpu.make_async_copy(kernel_hbm.at[0], taps.at[0], sems.at[5])
    width = aux.shape[1]
    clip_load = pltpu.make_async_copy(clips_hbm, clips, sems.at[0])
    param_loads = [pltpu.make_async_copy(p, params.at[k], sems.at[1 + k]) for k, p in enumerate(params_hbm)]
    for copy in [clip_load, *param_loads, taps_load]:
        copy.start()
    clip_load.wait()
    own = lax.axis_index("tm")
    own_clip = clips[own]
    slabs_in = jnp.int32(0)
    for slab in range(slabs):
        same = (clips[slab] == own_clip).astype(jnp.int32)
        slabs_in = slabs_in + same
        aux[slab : slab + 1] = jnp.full((1, width), same.astype(F32), F32)
    offsets = slab_offsets(slabs)
    for entry, offset in enumerate(offsets):
        same = (clips[own ^ offset] == own_clip).astype(F32)
        aux[slabs + entry : slabs + entry + 1] = jnp.full((1, width), same, F32)
    slabs *= 2
    starting = jnp.logical_or(own == 0, clips[jnp.maximum(own - 1, 0)] != own_clip)
    aux[slabs : slabs + 1] = jnp.full((1, width), starting.astype(F32), F32)
    aux[slabs + 1 : slabs + 2] = jnp.full((1, width), slabs_in.astype(F32) * float(per_slab), F32)
    for k, copy in enumerate(param_loads):
        copy.wait()
        aux[slabs + 2 + k : slabs + 3 + k] = params[k]
    aux[slabs + 6 : slabs + 8] = jnp.zeros((2, width), F32)
    taps_load.wait()


def setup_call(kernel, clip_ids, params, per_slab, mark):
    slabs, width = lax.axis_size("tm"), params[0].shape[0]
    return pl.pallas_call(
        functools.partial(setup_kernel, slabs, per_slab),
        out_shape=[shaped((1,) + kernel.shape[1:]), shaped((2 * slabs + 8, width), F32)],
        in_specs=[ANYWHERE] * 6 + [VMEM],
        out_specs=[VMEM, VMEM],
        scratch_shapes=[
            pltpu.VMEM((4, 1, width), F32),
            pltpu.SMEM(clip_ids.shape, jnp.int32),
            pltpu.SemaphoreType.DMA((6,)),
        ],
        compiler_params=vmem_params(),
        cost_estimate=pl.CostEstimate(flops=1 << 30, bytes_accessed=1 << 16, transcendentals=0),
    )(*[in_hbm(x) for x in (kernel, clip_ids, *[p[None] for p in params])], mark)


def group_total(values):
    width = values.shape[-1]
    lane = lax.broadcasted_iota(jnp.int32, values.shape, 1)
    step = 1
    while step < width // GROUPS:
        upper = pltpu.roll(values, step, 1)
        lower = pltpu.roll(values, width - step, 1)
        values = values + jnp.where((lane & step) != 0, upper, lower)
        step *= 2
    return values


def gathered_sums(table, aux):
    width = aux.shape[1]
    slabs = (aux.shape[0] - 8) // 2
    places = table.shape[0] // slabs
    sums = []
    for k in range(2):
        parts = [
            aux[slab : slab + 1] * sum(table[slab * places + p, :, k * width : (k + 1) * width] for p in range(places))
            for slab in range(slabs)
        ]
        while len(parts) > 1:
            parts = [sum(parts[i : i + 2]) for i in range(0, len(parts), 2)]
        sums += parts
    return sums


def traded_sums(tables, aux):
    width = aux.shape[1]
    sums = [jnp.zeros((1, width), F32)] * 2
    entry = (aux.shape[0] - 8) // 2
    for table in tables:
        mask = aux[entry : entry + table.shape[0]]
        entry += table.shape[0]
        sums = [
            total + jnp.sum(table[:, k * width : (k + 1) * width] * mask, axis=0, keepdims=True) for k, total in enumerate(sums)
        ]
    return sums


def half_affine(sums, aux, which):
    slabs = aux.shape[0] - 8
    grouped = group_total(jnp.concatenate(sums, axis=0))
    count = aux[slabs + 1 : slabs + 2]
    gain = aux[slabs + 2 + 2 * which : slabs + 3 + 2 * which]
    shift = aux[slabs + 3 + 2 * which : slabs + 4 + 2 * which]
    mean = grouped[0:1] / count
    variance = grouped[1:2] / count - mean * mean
    scale = lax.rsqrt(variance + 1e-06) * gain
    return 0.5 * scale, 0.5 * (shift - mean * scale)


def normed(raw, affine):
    half = raw.astype(F32) * affine[0] + affine[1]
    return (half * jnp.tanh(half) + half).astype(BF16)


def extended_row(frames, sides, frame, row):
    n_rows = frames.shape[1]
    inner = frames[frame, min(max(row - 1, 0), n_rows - 1)]
    if 0 < row <= n_rows:
        return inner
    place, places = lax.axis_index("space"), lax.axis_size("space")
    side = sides[0 if row == 0 else -1]
    return jnp.where(place == (0 if row == 0 else places - 1), inner, side[frame, 0])


def conv_rows(planes, taps):
    ref, index = planes[0]
    n_rows, cols, width = ref.shape[1] - 2, ref.shape[2], ref.shape[3]
    lhs = jnp.concatenate(
        [ref[index, j : j + n_rows].reshape(n_rows * cols, width) for ref, index in planes for j in range(3)], axis=1
    )
    column = lax.broadcasted_iota(jnp.int32, (cols, width), 0)
    sums = []
    for l in range(3):
        rhs = jnp.concatenate([taps[0][0, j, l] for j in range(3)] + [taps[1][i, j, l] for i in range(2) for j in range(3)], axis=0)
        sums.append(jnp.dot(lhs, rhs, preferred_element_type=F32))
    for row in range(n_rows):
        left, mid, right = (s[row * cols : (row + 1) * cols] for s in sums)
        left = jnp.where(column == 0, left, pltpu.roll(left, 1, 0))
        right = jnp.where(column == cols - 1, right, pltpu.roll(right, cols - 1, 0))
        yield row, left + mid + right


def put_hidden(hidden, frame, row, value, sums):
    rounded = value.astype(BF16)
    hidden[frame, row] = rounded
    return add_stats(sums, rounded.astype(F32))


def late_kernel(n_sides, aux, table, frames, *refs):
    sides, first_taps, kernel_hbm = refs[:n_sides], refs[n_sides], refs[n_sides + 1]
    act_low, affine_out, more_taps, hidden, stats, edges, act_high, taps_sems = refs[n_sides + 2 :]
    taps = (first_taps, more_taps)
    loads = [
        pltpu.make_async_copy(kernel_hbm.at[i, j], more_taps.at[i - 1, j], taps_sems.at[3 * (i - 1) + j])
        for i in range(1, 3)
        for j in range(3)
    ]
    for copy in loads:
        copy.start()
    n_rows, width = frames.shape[1], frames.shape[3]
    low, high = act_low.shape[0], act_high.shape[0]
    affine = half_affine(gathered_sums(table, aux), aux, 0)
    for k in range(2):
        affine_out[k : k + 1] = affine[k]
    planes = [(act_low, f) for f in range(low)] + [(act_high, f) for f in range(high)]

    def fill(frame):
        act, index = planes[frame]
        for row in range(n_rows + 2):
            act[index, row] = normed(extended_row(frames, sides, frame, row), affine)

    for frame in range(low):
        fill(frame)
    for copy in loads:
        copy.wait()
    fill(low)
    sums = no_stats(width)
    for frame in range(high):
        for row, value in conv_rows(planes[frame : frame + 3], taps):
            sums = put_hidden(hidden, frame, row, value, sums)
        send_rows(hidden, frame, edges)
        if frame + 1 < high:
            fill(low + frame + 1)
    for k in range(2):
        stats[k] = sums[k]


def early_kernel(n_sides, aux, first, second, *refs):
    corners, (act_low, affine_in, *taps), refs = refs[:n_sides], refs[n_sides : n_sides + 4], refs[n_sides + 4 :]
    late_stats, hidden, edges, stats, act_before = refs
    sums = late_stats[0], late_stats[1]
    slabs = aux.shape[0] - 8
    starting = aux[slabs : slabs + 1] != 0.0
    affine = affine_in[0:1], affine_in[1:2]
    n_rows = first.shape[1]
    for row in range(n_rows + 2):
        for frame in range(2):
            if frame == 0:
                raw = extended_row(first, corners, 0, row)
            else:
                raw = extended_row(second.at[:, :n_rows], [second.at[:, n_rows + k :] for k in range(n_sides)], 0, row)
            value = normed(raw, affine).astype(F32)
            act_before[frame, row] = jnp.where(starting, act_low[0, row].astype(F32), value).astype(BF16)
    planes = [(act_before, 0), (act_before, 1)] + [(act_low, f) for f in range(act_low.shape[0])]
    for frame in range(2):
        for row, value in conv_rows(planes[frame : frame + 3], taps):
            sums = put_hidden(hidden, frame, row, value, sums)
        send_rows(hidden, frame, edges)
    store_stats(stats, sums)


def last_kernel(n_tables, n_sides, aux, *refs):
    tables, early, late, refs = refs[:n_tables], refs[n_tables], refs[n_tables + 1], refs[n_tables + 2 :]
    sides_early, sides_late = refs[:n_sides], refs[n_sides : 2 * n_sides]
    before, *corners = refs[2 * n_sides : 3 * n_sides + 1]
    taps, feats, out_hbm, act, out, sems = refs[3 * n_sides + 1 :]
    stores = [pltpu.make_async_copy(out.at[f], out_hbm.at[f], sems.at[f]) for f in range(out.shape[0])]
    slabs = aux.shape[0] - 8
    starting = aux[slabs : slabs + 1] != 0.0
    affine = half_affine(traded_sums(tables, aux), aux, 1)
    n_frames, n_rows = out.shape[:2]

    def fill(frame):
        for row in range(n_rows + 2):
            if frame < 2:
                value = normed(extended_row(before, corners, frame, row), affine).astype(F32)
                act[frame, row] = jnp.where(starting, act[2, row].astype(F32), value).astype(BF16)
            elif frame < 4:
                act[frame, row] = normed(extended_row(early, sides_early, frame - 2, row), affine)
            else:
                act[frame, row] = normed(extended_row(late, sides_late, frame - 4, row), affine)

    for frame in range(2, 5):
        fill(frame)
    for frame in list(range(2, n_frames)) + [0, 1]:
        if 2 <= frame < n_frames - 1:
            fill(frame + 3)
        elif frame == n_frames - 1:
            fill(0)
            fill(1)
        for row, value in conv_rows([(act, frame + i) for i in range(3)], (taps.at[:1], taps.at[1:])):
            out[frame, row] = feats[frame, row].astype(F32) + value
        stores[frame].start()
    for store in stores:
        store.wait()


def call(kernel, outs, scratch, weight, operands, out_specs=None, aliases=None, outside=()):
    return pl.pallas_call(
        kernel,
        out_shape=outs,
        in_specs=[ANYWHERE if k in (aliases or {}) or k in outside else VMEM for k in range(len(operands))],
        out_specs=[VMEM] * len(outs) if out_specs is None else out_specs,
        scratch_shapes=scratch,
        input_output_aliases=aliases or {},
        compiler_params=vmem_params(),
        cost_estimate=pl.CostEstimate(flops=weight, bytes_accessed=1 << 20, transcendentals=1 << 20),
    )(*operands)


def on_device(feats, clip_ids, gain_one, shift_one, kernel_one, gain_two, shift_two, kernel_two):
    n_frames, n_rows, cols, width = feats.shape
    params = (gain_one, shift_one, gain_two, shift_two)
    per_slab = feats.size // GROUPS * lax.axis_size("space")
    late = n_frames - 2
    plane = (n_rows + 2, cols, width)
    act = pltpu.VMEM((2,) + plane, BF16)
    act_late = pltpu.VMEM((late,) + plane, BF16)
    work = 54 * feats.size // n_frames * width
    late_shapes = [shaped((2,) + plane), shaped((2, width), F32), shaped((2,) + kernel_one.shape[1:])]
    hidden_shapes = [shaped((late, n_rows, cols, width)), shaped((2, 8, width), F32), shaped(edge_shape(feats, late))]

    frames, tail, edges, copies, mark = entry_call(feats)
    table = stats_table(copies)
    sides = row_halo(edges)
    n_sides = len(sides)
    first, second = slab_halo(tail, sides)
    corners = row_halo(edges_of(first))
    taps, aux = setup_call(kernel_one, clip_ids, params, per_slab, mark)
    aux, *corners = lax.optimization_barrier((aux, *corners))
    operands = [aux, table, frames, *sides, taps, in_hbm(kernel_one)]
    act_low, affine, more_taps, hidden_late, stats, edges = call(
        functools.partial(late_kernel, n_sides),
        late_shapes + hidden_shapes,
        [act_late, pltpu.SemaphoreType.DMA((6,))],
        work * 3 // 4,
        operands,
        outside=(len(operands) - 1,),
    )
    before = shifted(hidden_late[late - 2 :], "tm", 1)
    sides_late = row_halo(edges)
    affine, *sides_late = lax.optimization_barrier((affine, *sides_late))
    hidden_early, edges, stats = call(
        functools.partial(early_kernel, n_sides),
        [shaped((2, n_rows, cols, width)), shaped(edge_shape(feats, 2)), shaped((1, 2 * width), F32)],
        [act],
        2 * work,
        [aux, first, second, *corners, act_low, affine, taps, more_taps, stats],
    )

    sides_early = row_halo(edges)
    _, tables = slab_tables(stats)
    before, tables[0] = lax.optimization_barrier((before, tables[0]))
    corners = row_halo(edges_of(before))
    operands = [aux, *tables, hidden_early, hidden_late, *sides_early, *sides_late, before, *corners, kernel_two, frames]
    return call(
        functools.partial(last_kernel, len(tables), n_sides),
        shaped(feats.shape, F32),
        [pltpu.VMEM((n_frames + 2,) + plane, BF16), pltpu.VMEM(feats.shape, F32), pltpu.SemaphoreType.DMA((n_frames,))],
        n_frames * work,
        operands,
        out_specs=ANYWHERE,
    )


def solution(mesh):
    return jax.shard_map(
        on_device,
        mesh=mesh,
        in_specs=(P("tm", "space", None, None), P(), P(), P(), P(), P(), P(), P()),
        out_specs=P("tm", "space", None, None),
        check_vma=False,
    )
```

```python
import functools

import jax
import jax.numpy as jnp
from jax import lax
from jax.experimental import pallas as pl
from jax.experimental.pallas import tpu as pltpu
from jax.sharding import PartitionSpec as P

GROUPS = 32
TAIL = 2
F32, BF16 = jnp.float32, jnp.bfloat16


def vmem_params():
    return pltpu.CompilerParams(vmem_limit_bytes=32 << 20)


def shaped(shape, dtype=BF16):
    return jax.ShapeDtypeStruct(tuple(shape), dtype)


def in_hbm(value):
    return pltpu.with_memory_space_constraint(value, pltpu.HBM)


VMEM = pl.BlockSpec(memory_space=pltpu.VMEM)
ANYWHERE = pl.BlockSpec(memory_space=pl.ANY)


def traded(value, axis, mask):
    return lax.ppermute(value, axis, [(i, i ^ mask) for i in range(lax.axis_size(axis))])


def shifted(value, axis, step):
    peers = lax.axis_size(axis)
    return lax.ppermute(value, axis, [(i, (i + step) % peers) for i in range(peers)])


def stats_table(copies):
    return lax.all_to_all(copies, ("tm", "space"), 0, 0, tiled=True)


def group_sizes(peers):
    sizes = []
    while peers > 1:
        sizes.append(min(4, peers))
        peers //= sizes[-1]
    return sizes


def slab_offsets(peers):
    offsets, left = [0], peers
    for ways in group_sizes(peers):
        left //= ways
        offsets = [(left * way) ^ offset for way in range(ways) for offset in offsets]
    return offsets


def slab_tables(stats):
    peers = lax.axis_size("tm")
    total = stats + traded(stats, "space", 1) if lax.axis_size("space") == 2 else lax.psum(stats, "space")
    held, left = [total], peers
    for ways in group_sizes(peers):
        left //= ways
        block = held[0] if len(held) == 1 else jnp.concatenate(held, axis=0)
        held = [block] + [traded(block, "tm", left * way) for way in range(1, ways)]
    return total, held


def row_halo(edges):
    if lax.axis_size("space") == 2:
        return [traded(edges[0], "space", 1)]
    top, bottom = edges
    return [shifted(bottom, "space", 1), shifted(top, "space", -1)]


def edges_of(frames):
    rows = frames.shape[1]
    if lax.axis_size("space") == 2:
        return [lax.dynamic_slice_in_dim(frames, (rows - 1) * (1 - lax.axis_index("space")), 1, axis=1)]
    return [frames[:, :1], frames[:, rows - 1 :]]


def slab_halo(tail, sides):
    rows = [side[-1:] for side in sides]
    return shifted(tail[:1], "tm", 1), shifted(jnp.concatenate([tail[1:], *rows], axis=1), "tm", 1)


def row_halo(edges):
    if lax.axis_size("space") == 2:
        return [traded(edges, "space", 1)]
    return [shifted(edges[:, 1:], "space", 1), shifted(edges[:, :1], "space", -1)]


def edges_of(frames):
    rows = frames.shape[1]
    if lax.axis_size("space") == 2:
        return lax.dynamic_slice_in_dim(frames, (rows - 1) * (1 - lax.axis_index("space")), 1, axis=1)
    return jnp.concatenate([frames[:, :1], frames[:, rows - 1 :]], axis=1)


def edge_shape(frames, count):
    return (count, 1 if lax.axis_size("space") == 2 else 2) + frames.shape[2:]


def send_rows(source, frame, edges, at=0):
    rows = source.shape[1]
    if edges.shape[1] == 1:
        low = lax.axis_index("space") == 0
        edges[at + frame, 0] = jnp.where(low, source[frame, rows - 1], source[frame, 0])
    else:
        edges[at + frame, 0] = source[frame, 0]
        edges[at + frame, 1] = source[frame, rows - 1]


def add_stats(sums, values):
    width = values.shape[1]
    return (
        sums[0] + jnp.sum(values.reshape(-1, 8, width), axis=0),
        sums[1] + jnp.sum((values * values).reshape(-1, 8, width), axis=0),
    )


def no_stats(width):
    return jnp.zeros((8, width), F32), jnp.zeros((8, width), F32)


def store_stats(stats, sums):
    width = sums[0].shape[1]
    for k in range(2):
        stats[:, k * width : (k + 1) * width] = jnp.sum(sums[k], axis=0, keepdims=True)


def store_copies(copies, stats):
    copies[...] = jnp.broadcast_to(stats[...][None], copies.shape)


def device_count():
    return lax.axis_size("tm") * lax.axis_size("space")


def entry_kernel(feats_hbm, frames, tail, edges, copies, mark, stats, sems):
    n_frames, n_rows, _, width = frames.shape
    loads = [pltpu.make_async_copy(feats_hbm.at[f], frames.at[f], sems.at[f]) for f in range(n_frames)]
    for copy in loads:
        copy.start()
    mark[...] = jnp.zeros_like(mark)
    sums = no_stats(width)
    for frame in range(n_frames):
        loads[frame].wait()
        for row in range(n_rows):
            if frame >= n_frames - TAIL:
                tail[frame - n_frames + TAIL, row] = frames[frame, row]
            sums = add_stats(sums, frames[frame, row].astype(F32))
        send_rows(frames, frame, edges)
    store_stats(stats, sums)
    store_copies(copies, stats)


def copies_shape(width):
    return shaped((device_count(), 1, 2 * width), F32)


MARK = jax.ShapeDtypeStruct((8, 128), F32)


def entry_call(feats):
    n_frames, width = feats.shape[0], feats.shape[3]
    outs = [
        shaped(feats.shape),
        shaped((TAIL,) + feats.shape[1:]),
        shaped(edge_shape(feats, n_frames)),
        copies_shape(width),
        MARK,
    ]
    return pl.pallas_call(
        entry_kernel,
        out_shape=outs,
        in_specs=[ANYWHERE],
        out_specs=[VMEM] * len(outs),
        scratch_shapes=[pltpu.VMEM((1, 2 * width), F32), pltpu.SemaphoreType.DMA((n_frames,))],
        compiler_params=vmem_params(),
        cost_estimate=pl.CostEstimate(flops=4 * feats.size, bytes_accessed=4 * feats.size, transcendentals=0),
    )(in_hbm(feats))


def setup_kernel(slabs, per_slab, kernel_hbm, clips_hbm, *refs):
    params_hbm, (_, taps, aux, params, clips, sems) = refs[:4], refs[4:]
    taps_load = pltpu.make_async_copy(kernel_hbm.at[0], taps.at[0], sems.at[5])
    width = aux.shape[1]
    clip_load = pltpu.make_async_copy(clips_hbm, clips, sems.at[0])
    param_loads = [pltpu.make_async_copy(p, params.at[k], sems.at[1 + k]) for k, p in enumerate(params_hbm)]
    for copy in [clip_load, *param_loads, taps_load]:
        copy.start()
    clip_load.wait()
    own = lax.axis_index("tm")
    own_clip = clips[own]
    slabs_in = jnp.int32(0)
    for slab in range(slabs):
        same = (clips[slab] == own_clip).astype(jnp.int32)
        slabs_in = slabs_in + same
        aux[slab : slab + 1] = jnp.full((1, width), same.astype(F32), F32)
    offsets = slab_offsets(slabs)
    for entry, offset in enumerate(offsets):
        same = (clips[own ^ offset] == own_clip).astype(F32)
        aux[slabs + entry : slabs + entry + 1] = jnp.full((1, width), same, F32)
    slabs *= 2
    starting = jnp.logical_or(own == 0, clips[jnp.maximum(own - 1, 0)] != own_clip)
    aux[slabs : slabs + 1] = jnp.full((1, width), starting.astype(F32), F32)
    aux[slabs + 1 : slabs + 2] = jnp.full((1, width), slabs_in.astype(F32) * float(per_slab), F32)
    for k, copy in enumerate(param_loads):
        copy.wait()
        aux[slabs + 2 + k : slabs + 3 + k] = params[k]
    aux[slabs + 6 : slabs + 8] = jnp.zeros((2, width), F32)
    taps_load.wait()


def setup_call(kernel, clip_ids, params, per_slab, mark):
    slabs, width = lax.axis_size("tm"), params[0].shape[0]
    return pl.pallas_call(
        functools.partial(setup_kernel, slabs, per_slab),
        out_shape=[shaped((1,) + kernel.shape[1:]), shaped((2 * slabs + 8, width), F32)],
        in_specs=[ANYWHERE] * 6 + [VMEM],
        out_specs=[VMEM, VMEM],
        scratch_shapes=[
            pltpu.VMEM((4, 1, width), F32),
            pltpu.SMEM(clip_ids.shape, jnp.int32),
            pltpu.SemaphoreType.DMA((6,)),
        ],
        compiler_params=vmem_params(),
        cost_estimate=pl.CostEstimate(flops=1 << 30, bytes_accessed=1 << 16, transcendentals=0),
    )(*[in_hbm(x) for x in (kernel, clip_ids, *[p[None] for p in params])], mark)


def group_total(values):
    width = values.shape[-1]
    lane = lax.broadcasted_iota(jnp.int32, values.shape, 1)
    step = 1
    while step < width // GROUPS:
        upper = pltpu.roll(values, step, 1)
        lower = pltpu.roll(values, width - step, 1)
        values = values + jnp.where((lane & step) != 0, upper, lower)
        step *= 2
    return values


def gathered_sums(table, aux):
    width = aux.shape[1]
    slabs = (aux.shape[0] - 8) // 2
    places = table.shape[0] // slabs
    sums = []
    for k in range(2):
        parts = [
            aux[slab : slab + 1] * sum(table[slab * places + p, :, k * width : (k + 1) * width] for p in range(places))
            for slab in range(slabs)
        ]
        while len(parts) > 1:
            parts = [sum(parts[i : i + 2]) for i in range(0, len(parts), 2)]
        sums += parts
    return sums


def traded_sums(tables, aux):
    width = aux.shape[1]
    sums = [jnp.zeros((1, width), F32)] * 2
    entry = (aux.shape[0] - 8) // 2
    for table in tables:
        mask = aux[entry : entry + table.shape[0]]
        entry += table.shape[0]
        sums = [
            total + jnp.sum(table[:, k * width : (k + 1) * width] * mask, axis=0, keepdims=True) for k, total in enumerate(sums)
        ]
    return sums


def half_affine(sums, aux, which):
    slabs = aux.shape[0] - 8
    grouped = group_total(jnp.concatenate(sums, axis=0))
    count = aux[slabs + 1 : slabs + 2]
    gain = aux[slabs + 2 + 2 * which : slabs + 3 + 2 * which]
    shift = aux[slabs + 3 + 2 * which : slabs + 4 + 2 * which]
    mean = grouped[0:1] / count
    variance = grouped[1:2] / count - mean * mean
    scale = lax.rsqrt(variance + 1e-06) * gain
    return 0.5 * scale, 0.5 * (shift - mean * scale)


def normed(raw, affine):
    half = raw.astype(F32) * affine[0] + affine[1]
    return (half * jnp.tanh(half) + half).astype(BF16)


def extended_row(frames, sides, frame, row):
    n_rows = frames.shape[1]
    inner = frames[frame, min(max(row - 1, 0), n_rows - 1)]
    if 0 < row <= n_rows:
        return inner
    place, places = lax.axis_index("space"), lax.axis_size("space")
    side = sides[0 if row == 0 else -1]
    return jnp.where(place == (0 if row == 0 else places - 1), inner, side[frame, 0])


def conv_rows(planes, taps):
    ref, index = planes[0]
    n_rows, cols, width = ref.shape[1] - 2, ref.shape[2], ref.shape[3]
    lhs = jnp.concatenate(
        [ref[index, j : j + n_rows].reshape(n_rows * cols, width) for ref, index in planes for j in range(3)], axis=1
    )
    column = lax.broadcasted_iota(jnp.int32, (cols, width), 0)
    sums = []
    for l in range(3):
        rhs = jnp.concatenate([taps[0][0, j, l] for j in range(3)] + [taps[1][i, j, l] for i in range(2) for j in range(3)], axis=0)
        sums.append(jnp.dot(lhs, rhs, preferred_element_type=F32))
    for row in range(n_rows):
        left, mid, right = (s[row * cols : (row + 1) * cols] for s in sums)
        left = jnp.where(column == 0, left, pltpu.roll(left, 1, 0))
        right = jnp.where(column == cols - 1, right, pltpu.roll(right, cols - 1, 0))
        yield row, left + mid + right


def put_hidden(hidden, frame, row, value, sums):
    rounded = value.astype(BF16)
    hidden[frame, row] = rounded
    return add_stats(sums, rounded.astype(F32))


def late_kernel(n_sides, aux, table, frames, *refs):
    sides, first_taps, kernel_hbm = refs[:n_sides], refs[n_sides], refs[n_sides + 1]
    act_low, affine_out, more_taps, hidden, stats, edges, act_high, taps_sems = refs[n_sides + 2 :]
    taps = (first_taps, more_taps)
    loads = [
        pltpu.make_async_copy(kernel_hbm.at[i, j], more_taps.at[i - 1, j], taps_sems.at[3 * (i - 1) + j])
        for i in range(1, 3)
        for j in range(3)
    ]
    for copy in loads:
        copy.start()
    n_rows, width = frames.shape[1], frames.shape[3]
    low, high = act_low.shape[0], act_high.shape[0]
    affine = half_affine(gathered_sums(table, aux), aux, 0)
    for k in range(2):
        affine_out[k : k + 1] = affine[k]
    planes = [(act_low, f) for f in range(low)] + [(act_high, f) for f in range(high)]

    def fill(frame):
        act, index = planes[frame]
        for row in range(n_rows + 2):
            act[index, row] = normed(extended_row(frames, sides, frame, row), affine)

    for frame in range(low):
        fill(frame)
    for copy in loads:
        copy.wait()
    fill(low)
    sums = no_stats(width)
    for frame in range(high):
        for row, value in conv_rows(planes[frame : frame + 3], taps):
            sums = put_hidden(hidden, frame, row, value, sums)
        send_rows(hidden, frame, edges)
        if frame + 1 < high:
            fill(low + frame + 1)
    for k in range(2):
        stats[k] = sums[k]


def early_kernel(n_sides, aux, first, second, *refs):
    corners, (act_low, affine_in, *taps), refs = refs[:n_sides], refs[n_sides : n_sides + 4], refs[n_sides + 4 :]
    late_stats, hidden, edges, stats, act_before = refs
    sums = late_stats[0], late_stats[1]
    slabs = aux.shape[0] - 8
    starting = aux[slabs : slabs + 1] != 0.0
    affine = affine_in[0:1], affine_in[1:2]
    n_rows = first.shape[1]
    for row in range(n_rows + 2):
        for frame in range(2):
            if frame == 0:
                raw = extended_row(first, corners, 0, row)
            else:
                raw = extended_row(second.at[:, :n_rows], [second.at[:, n_rows + k :] for k in range(n_sides)], 0, row)
            value = normed(raw, affine).astype(F32)
            act_before[frame, row] = jnp.where(starting, act_low[0, row].astype(F32), value).astype(BF16)
    planes = [(act_before, 0), (act_before, 1)] + [(act_low, f) for f in range(act_low.shape[0])]
    for frame in range(2):
        for row, value in conv_rows(planes[frame : frame + 3], taps):
            sums = put_hidden(hidden, frame, row, value, sums)
        send_rows(hidden, frame, edges)
    store_stats(stats, sums)


def last_kernel(n_tables, n_sides, aux, *refs):
    tables, early, late, refs = refs[:n_tables], refs[n_tables], refs[n_tables + 1], refs[n_tables + 2 :]
    sides_early, sides_late = refs[:n_sides], refs[n_sides : 2 * n_sides]
    before, *corners = refs[2 * n_sides : 3 * n_sides + 1]
    taps, feats, out_hbm, act, out, sems = refs[3 * n_sides + 1 :]
    stores = [pltpu.make_async_copy(out.at[f], out_hbm.at[f], sems.at[f]) for f in range(out.shape[0])]
    slabs = aux.shape[0] - 8
    starting = aux[slabs : slabs + 1] != 0.0
    affine = half_affine(traded_sums(tables, aux), aux, 1)
    n_frames, n_rows = out.shape[:2]

    def fill(frame):
        for row in range(n_rows + 2):
            if frame < 2:
                value = normed(extended_row(before, corners, frame, row), affine).astype(F32)
                act[frame, row] = jnp.where(starting, act[2, row].astype(F32), value).astype(BF16)
            elif frame < 4:
                act[frame, row] = normed(extended_row(early, sides_early, frame - 2, row), affine)
            else:
                act[frame, row] = normed(extended_row(late, sides_late, frame - 4, row), affine)

    for frame in range(2, 5):
        fill(frame)
    for frame in list(range(2, n_frames)) + [0, 1]:
        if frame == 0:
            fill(0)
            fill(1)
        elif 2 < frame:
            fill(frame + 2)
        for row, value in conv_rows([(act, frame + i) for i in range(3)], (taps.at[:1], taps.at[1:])):
            out[frame, row] = feats[frame, row].astype(F32) + value
        stores[frame].start()
    for store in stores:
        store.wait()


def call(kernel, outs, scratch, weight, operands, out_specs=None, aliases=None, outside=()):
    return pl.pallas_call(
        kernel,
        out_shape=outs,
        in_specs=[ANYWHERE if k in (aliases or {}) or k in outside else VMEM for k in range(len(operands))],
        out_specs=[VMEM] * len(outs) if out_specs is None else out_specs,
        scratch_shapes=scratch,
        input_output_aliases=aliases or {},
        compiler_params=vmem_params(),
        cost_estimate=pl.CostEstimate(flops=weight, bytes_accessed=1 << 20, transcendentals=1 << 20),
    )(*operands)


def on_device(feats, clip_ids, gain_one, shift_one, kernel_one, gain_two, shift_two, kernel_two):
    n_frames, n_rows, cols, width = feats.shape
    params = (gain_one, shift_one, gain_two, shift_two)
    per_slab = feats.size // GROUPS * lax.axis_size("space")
    late = n_frames - 2
    plane = (n_rows + 2, cols, width)
    act = pltpu.VMEM((2,) + plane, BF16)
    act_late = pltpu.VMEM((late,) + plane, BF16)
    work = 54 * feats.size // n_frames * width
    late_shapes = [shaped((2,) + plane), shaped((2, width), F32), shaped((2,) + kernel_one.shape[1:])]
    hidden_shapes = [shaped((late, n_rows, cols, width)), shaped((2, 8, width), F32), shaped(edge_shape(feats, late))]

    frames, tail, edges, copies, mark = entry_call(feats)
    table = stats_table(copies)
    sides = row_halo(edges)
    n_sides = len(sides)
    first, second = slab_halo(tail, sides)
    corners = row_halo(edges_of(first))
    taps, aux = setup_call(kernel_one, clip_ids, params, per_slab, mark)
    aux, *corners = lax.optimization_barrier((aux, *corners))
    operands = [aux, table, frames, *sides, taps, in_hbm(kernel_one)]
    act_low, affine, more_taps, hidden_late, stats, edges = call(
        functools.partial(late_kernel, n_sides),
        late_shapes + hidden_shapes,
        [act_late, pltpu.SemaphoreType.DMA((6,))],
        work * 3 // 4,
        operands,
        outside=(len(operands) - 1,),
    )
    before = shifted(hidden_late[late - 2 :], "tm", 1)
    sides_late = row_halo(edges)
    hidden_early, edges, stats = call(
        functools.partial(early_kernel, n_sides),
        [shaped((2, n_rows, cols, width)), shaped(edge_shape(feats, 2)), shaped((1, 2 * width), F32)],
        [act],
        2 * work,
        [aux, first, second, *corners, act_low, affine, taps, more_taps, stats],
    )

    sides_early = row_halo(edges)
    _, tables = slab_tables(stats)
    before, tables[0] = lax.optimization_barrier((before, tables[0]))
    corners = row_halo(edges_of(before))
    operands = [aux, *tables, hidden_early, hidden_late, *sides_early, *sides_late, before, *corners, kernel_two, frames]
    return call(
        functools.partial(last_kernel, len(tables), n_sides),
        shaped(feats.shape, F32),
        [pltpu.VMEM((n_frames + 2,) + plane, BF16), pltpu.VMEM(feats.shape, F32), pltpu.SemaphoreType.DMA((n_frames,))],
        n_frames * work,
        operands,
        out_specs=ANYWHERE,
    )


def solution(mesh):
    return jax.shard_map(
        on_device,
        mesh=mesh,
        in_specs=(P("tm", "space", None, None), P(), P(), P(), P(), P(), P(), P()),
        out_specs=P("tm", "space", None, None),
        check_vma=False,
    )
```

```python
import functools

import jax
import jax.numpy as jnp
from jax import lax
from jax.experimental import pallas as pl
from jax.experimental.pallas import tpu as pltpu
from jax.sharding import PartitionSpec as P

GROUPS = 32
TAIL = 2
F32, BF16 = jnp.float32, jnp.bfloat16


def vmem_params():
    return pltpu.CompilerParams(vmem_limit_bytes=32 << 20)


def shaped(shape, dtype=BF16):
    return jax.ShapeDtypeStruct(tuple(shape), dtype)


def in_hbm(value):
    return pltpu.with_memory_space_constraint(value, pltpu.HBM)


VMEM = pl.BlockSpec(memory_space=pltpu.VMEM)
ANYWHERE = pl.BlockSpec(memory_space=pl.ANY)


def traded(value, axis, mask):
    return lax.ppermute(value, axis, [(i, i ^ mask) for i in range(lax.axis_size(axis))])


def shifted(value, axis, step):
    peers = lax.axis_size(axis)
    return lax.ppermute(value, axis, [(i, (i + step) % peers) for i in range(peers)])


def stats_table(copies):
    return lax.all_to_all(copies, ("tm", "space"), 0, 0, tiled=True)


def group_sizes(peers):
    sizes = []
    while peers > 1:
        sizes.append(min(4, peers))
        peers //= sizes[-1]
    return sizes


def slab_offsets(peers):
    offsets, left = [0], peers
    for ways in group_sizes(peers):
        left //= ways
        offsets = [(left * way) ^ offset for way in range(ways) for offset in offsets]
    return offsets


def slab_tables(stats):
    peers = lax.axis_size("tm")
    total = stats + traded(stats, "space", 1) if lax.axis_size("space") == 2 else lax.psum(stats, "space")
    held, left = [total], peers
    for ways in group_sizes(peers):
        left //= ways
        block = held[0] if len(held) == 1 else jnp.concatenate(held, axis=0)
        held = [block] + [traded(block, "tm", left * way) for way in range(1, ways)]
    return total, held


def row_halo(edges):
    if lax.axis_size("space") == 2:
        return [traded(edges[0], "space", 1)]
    top, bottom = edges
    return [shifted(bottom, "space", 1), shifted(top, "space", -1)]


def edges_of(frames):
    rows = frames.shape[1]
    if lax.axis_size("space") == 2:
        return [lax.dynamic_slice_in_dim(frames, (rows - 1) * (1 - lax.axis_index("space")), 1, axis=1)]
    return [frames[:, :1], frames[:, rows - 1 :]]


def chained(value):
    return lax.ppermute(value, "tm", [(i, i + 1) for i in range(lax.axis_size("tm") - 1)])


def slab_halo(tail, sides):
    rows = [side[-1:] for side in sides]
    return shifted(tail[:1], "tm", 1), shifted(jnp.concatenate([tail[1:], *rows], axis=1), "tm", 1)


def row_halo(edges):
    if lax.axis_size("space") == 2:
        return [traded(edges, "space", 1)]
    return [shifted(edges[:, 1:], "space", 1), shifted(edges[:, :1], "space", -1)]


def edges_of(frames):
    rows = frames.shape[1]
    if lax.axis_size("space") == 2:
        return lax.dynamic_slice_in_dim(frames, (rows - 1) * (1 - lax.axis_index("space")), 1, axis=1)
    return jnp.concatenate([frames[:, :1], frames[:, rows - 1 :]], axis=1)


def edge_shape(frames, count):
    return (count, 1 if lax.axis_size("space") == 2 else 2) + frames.shape[2:]


def send_rows(source, frame, edges, at=0):
    rows = source.shape[1]
    if edges.shape[1] == 1:
        low = lax.axis_index("space") == 0
        edges[at + frame, 0] = jnp.where(low, source[frame, rows - 1], source[frame, 0])
    else:
        edges[at + frame, 0] = source[frame, 0]
        edges[at + frame, 1] = source[frame, rows - 1]


def add_stats(sums, values):
    width = values.shape[1]
    return (
        sums[0] + jnp.sum(values.reshape(-1, 8, width), axis=0),
        sums[1] + jnp.sum((values * values).reshape(-1, 8, width), axis=0),
    )


def no_stats(width):
    return jnp.zeros((8, width), F32), jnp.zeros((8, width), F32)


def store_stats(stats, sums):
    width = sums[0].shape[1]
    for k in range(2):
        stats[:, k * width : (k + 1) * width] = jnp.sum(sums[k], axis=0, keepdims=True)


def store_copies(copies, stats):
    copies[...] = jnp.broadcast_to(stats[...][None], copies.shape)


def device_count():
    return lax.axis_size("tm") * lax.axis_size("space")


def entry_kernel(feats_hbm, frames, tail, edges, copies, mark, stats, sems):
    n_frames, n_rows, _, width = frames.shape
    loads = [pltpu.make_async_copy(feats_hbm.at[f], frames.at[f], sems.at[f]) for f in range(n_frames)]
    for copy in loads:
        copy.start()
    mark[...] = jnp.zeros_like(mark)
    sums = no_stats(width)
    for frame in range(n_frames):
        loads[frame].wait()
        for row in range(n_rows):
            if frame >= n_frames - TAIL:
                tail[frame - n_frames + TAIL, row] = frames[frame, row]
            sums = add_stats(sums, frames[frame, row].astype(F32))
        send_rows(frames, frame, edges)
    store_stats(stats, sums)
    store_copies(copies, stats)


def copies_shape(width):
    return shaped((device_count(), 1, 2 * width), F32)


MARK = jax.ShapeDtypeStruct((8, 128), F32)


def entry_call(feats):
    n_frames, width = feats.shape[0], feats.shape[3]
    outs = [
        shaped(feats.shape),
        shaped((TAIL,) + feats.shape[1:]),
        shaped(edge_shape(feats, n_frames)),
        copies_shape(width),
        MARK,
    ]
    return pl.pallas_call(
        entry_kernel,
        out_shape=outs,
        in_specs=[ANYWHERE],
        out_specs=[VMEM] * len(outs),
        scratch_shapes=[pltpu.VMEM((1, 2 * width), F32), pltpu.SemaphoreType.DMA((n_frames,))],
        compiler_params=vmem_params(),
        cost_estimate=pl.CostEstimate(flops=4 * feats.size, bytes_accessed=4 * feats.size, transcendentals=0),
    )(in_hbm(feats))


def setup_kernel(slabs, per_slab, kernel_hbm, clips_hbm, *refs):
    params_hbm, (_, taps, aux, params, clips, sems) = refs[:4], refs[4:]
    taps_load = pltpu.make_async_copy(kernel_hbm.at[0], taps.at[0], sems.at[5])
    width = aux.shape[1]
    clip_load = pltpu.make_async_copy(clips_hbm, clips, sems.at[0])
    param_loads = [pltpu.make_async_copy(p, params.at[k], sems.at[1 + k]) for k, p in enumerate(params_hbm)]
    for copy in [clip_load, *param_loads, taps_load]:
        copy.start()
    clip_load.wait()
    own = lax.axis_index("tm")
    own_clip = clips[own]
    slabs_in = jnp.int32(0)
    for slab in range(slabs):
        same = (clips[slab] == own_clip).astype(jnp.int32)
        slabs_in = slabs_in + same
        aux[slab : slab + 1] = jnp.full((1, width), same.astype(F32), F32)
    offsets = slab_offsets(slabs)
    for entry, offset in enumerate(offsets):
        same = (clips[own ^ offset] == own_clip).astype(F32)
        aux[slabs + entry : slabs + entry + 1] = jnp.full((1, width), same, F32)
    slabs *= 2
    starting = jnp.logical_or(own == 0, clips[jnp.maximum(own - 1, 0)] != own_clip)
    aux[slabs : slabs + 1] = jnp.full((1, width), starting.astype(F32), F32)
    aux[slabs + 1 : slabs + 2] = jnp.full((1, width), slabs_in.astype(F32) * float(per_slab), F32)
    for k, copy in enumerate(param_loads):
        copy.wait()
        aux[slabs + 2 + k : slabs + 3 + k] = params[k]
    aux[slabs + 6 : slabs + 8] = jnp.zeros((2, width), F32)
    taps_load.wait()


def setup_call(kernel, clip_ids, params, per_slab, mark):
    slabs, width = lax.axis_size("tm"), params[0].shape[0]
    return pl.pallas_call(
        functools.partial(setup_kernel, slabs, per_slab),
        out_shape=[shaped((1,) + kernel.shape[1:]), shaped((2 * slabs + 8, width), F32)],
        in_specs=[ANYWHERE] * 6 + [VMEM],
        out_specs=[VMEM, VMEM],
        scratch_shapes=[
            pltpu.VMEM((4, 1, width), F32),
            pltpu.SMEM(clip_ids.shape, jnp.int32),
            pltpu.SemaphoreType.DMA((6,)),
        ],
        compiler_params=vmem_params(),
        cost_estimate=pl.CostEstimate(flops=1 << 30, bytes_accessed=1 << 16, transcendentals=0),
    )(*[in_hbm(x) for x in (kernel, clip_ids, *[p[None] for p in params])], mark)


def group_total(values):
    width = values.shape[-1]
    lane = lax.broadcasted_iota(jnp.int32, values.shape, 1)
    step = 1
    while step < width // GROUPS:
        upper = pltpu.roll(values, step, 1)
        lower = pltpu.roll(values, width - step, 1)
        values = values + jnp.where((lane & step) != 0, upper, lower)
        step *= 2
    return values


def gathered_sums(table, aux):
    width = aux.shape[1]
    slabs = (aux.shape[0] - 8) // 2
    places = table.shape[0] // slabs
    sums = []
    for k in range(2):
        parts = [
            aux[slab : slab + 1] * sum(table[slab * places + p, :, k * width : (k + 1) * width] for p in range(places))
            for slab in range(slabs)
        ]
        while len(parts) > 1:
            parts = [sum(parts[i : i + 2]) for i in range(0, len(parts), 2)]
        sums += parts
    return sums


def traded_sums(tables, aux):
    width = aux.shape[1]
    sums = [jnp.zeros((1, width), F32)] * 2
    entry = (aux.shape[0] - 8) // 2
    for table in tables:
        mask = aux[entry : entry + table.shape[0]]
        entry += table.shape[0]
        sums = [
            total + jnp.sum(table[:, k * width : (k + 1) * width] * mask, axis=0, keepdims=True) for k, total in enumerate(sums)
        ]
    return sums


def half_affine(sums, aux, which):
    slabs = aux.shape[0] - 8
    grouped = group_total(jnp.concatenate(sums, axis=0))
    count = aux[slabs + 1 : slabs + 2]
    gain = aux[slabs + 2 + 2 * which : slabs + 3 + 2 * which]
    shift = aux[slabs + 3 + 2 * which : slabs + 4 + 2 * which]
    mean = grouped[0:1] / count
    variance = grouped[1:2] / count - mean * mean
    scale = lax.rsqrt(variance + 1e-06) * gain
    return 0.5 * scale, 0.5 * (shift - mean * scale)


def normed(raw, affine):
    half = raw.astype(F32) * affine[0] + affine[1]
    return (half * jnp.tanh(half) + half).astype(BF16)


def extended_row(frames, sides, frame, row):
    n_rows = frames.shape[1]
    inner = frames[frame, min(max(row - 1, 0), n_rows - 1)]
    if 0 < row <= n_rows:
        return inner
    place, places = lax.axis_index("space"), lax.axis_size("space")
    side = sides[0 if row == 0 else -1]
    return jnp.where(place == (0 if row == 0 else places - 1), inner, side[frame, 0])


def conv_rows(planes, taps):
    ref, index = planes[0]
    n_rows, cols, width = ref.shape[1] - 2, ref.shape[2], ref.shape[3]
    lhs = jnp.concatenate(
        [ref[index, j : j + n_rows].reshape(n_rows * cols, width) for ref, index in planes for j in range(3)], axis=1
    )
    column = lax.broadcasted_iota(jnp.int32, (cols, width), 0)
    sums = []
    for l in range(3):
        rhs = jnp.concatenate([taps[0][0, j, l] for j in range(3)] + [taps[1][i, j, l] for i in range(2) for j in range(3)], axis=0)
        sums.append(jnp.dot(lhs, rhs, preferred_element_type=F32))
    for row in range(n_rows):
        left, mid, right = (s[row * cols : (row + 1) * cols] for s in sums)
        left = jnp.where(column == 0, left, pltpu.roll(left, 1, 0))
        right = jnp.where(column == cols - 1, right, pltpu.roll(right, cols - 1, 0))
        yield row, left + mid + right


def put_hidden(hidden, frame, row, value, sums):
    rounded = value.astype(BF16)
    hidden[frame, row] = rounded
    return add_stats(sums, rounded.astype(F32))


def late_kernel(n_sides, aux, table, frames, *refs):
    sides, first_taps, kernel_hbm = refs[:n_sides], refs[n_sides], refs[n_sides + 1]
    act_low, affine_out, more_taps, hidden, stats, edges, act_high, taps_sems = refs[n_sides + 2 :]
    taps = (first_taps, more_taps)
    loads = [
        pltpu.make_async_copy(kernel_hbm.at[i, j], more_taps.at[i - 1, j], taps_sems.at[3 * (i - 1) + j])
        for i in range(1, 3)
        for j in range(3)
    ]
    for copy in loads:
        copy.start()
    n_rows, width = frames.shape[1], frames.shape[3]
    low, high = act_low.shape[0], act_high.shape[0]
    affine = half_affine(gathered_sums(table, aux), aux, 0)
    for k in range(2):
        affine_out[k : k + 1] = affine[k]
    planes = [(act_low, f) for f in range(low)] + [(act_high, f) for f in range(high)]

    def fill(frame):
        act, index = planes[frame]
        for row in range(n_rows + 2):
            act[index, row] = normed(extended_row(frames, sides, frame, row), affine)

    for frame in range(low):
        fill(frame)
    for copy in loads:
        copy.wait()
    fill(low)
    sums = no_stats(width)
    for frame in range(high):
        for row, value in conv_rows(planes[frame : frame + 3], taps):
            sums = put_hidden(hidden, frame, row, value, sums)
        send_rows(hidden, frame, edges)
        if frame + 1 < high:
            fill(low + frame + 1)
    for k in range(2):
        stats[k] = sums[k]


def early_kernel(n_sides, aux, first, second, *refs):
    corners, (act_low, affine_in, *taps), refs = refs[:n_sides], refs[n_sides : n_sides + 4], refs[n_sides + 4 :]
    late_stats, hidden, edges, stats, act_before = refs
    sums = late_stats[0], late_stats[1]
    slabs = aux.shape[0] - 8
    starting = aux[slabs : slabs + 1] != 0.0
    affine = affine_in[0:1], affine_in[1:2]
    n_rows = first.shape[1]
    for row in range(n_rows + 2):
        for frame in range(2):
            if frame == 0:
                raw = extended_row(first, corners, 0, row)
            else:
                raw = extended_row(second.at[:, :n_rows], [second.at[:, n_rows + k :] for k in range(n_sides)], 0, row)
            value = normed(raw, affine).astype(F32)
            act_before[frame, row] = jnp.where(starting, act_low[0, row].astype(F32), value).astype(BF16)
    planes = [(act_before, 0), (act_before, 1)] + [(act_low, f) for f in range(act_low.shape[0])]
    for frame in range(2):
        for row, value in conv_rows(planes[frame : frame + 3], taps):
            sums = put_hidden(hidden, frame, row, value, sums)
        send_rows(hidden, frame, edges)
    store_stats(stats, sums)


def last_kernel(n_tables, n_sides, aux, *refs):
    tables, early, late, refs = refs[:n_tables], refs[n_tables], refs[n_tables + 1], refs[n_tables + 2 :]
    sides_early, sides_late = refs[:n_sides], refs[n_sides : 2 * n_sides]
    before, *corners = refs[2 * n_sides : 3 * n_sides + 1]
    taps, feats, out_hbm, act, out, sems = refs[3 * n_sides + 1 :]
    stores = [pltpu.make_async_copy(out.at[f], out_hbm.at[f], sems.at[f]) for f in range(out.shape[0])]
    slabs = aux.shape[0] - 8
    starting = aux[slabs : slabs + 1] != 0.0
    affine = half_affine(traded_sums(tables, aux), aux, 1)
    n_frames, n_rows = out.shape[:2]

    def fill(frame):
        for row in range(n_rows + 2):
            if frame < 2:
                value = normed(extended_row(before, corners, frame, row), affine).astype(F32)
                act[frame, row] = jnp.where(starting, act[2, row].astype(F32), value).astype(BF16)
            elif frame < 4:
                act[frame, row] = normed(extended_row(early, sides_early, frame - 2, row), affine)
            else:
                act[frame, row] = normed(extended_row(late, sides_late, frame - 4, row), affine)

    for frame in range(2, 5):
        fill(frame)
    for frame in list(range(2, n_frames)) + [0, 1]:
        if frame == 0:
            fill(0)
            fill(1)
        elif 2 < frame:
            fill(frame + 2)
        for row, value in conv_rows([(act, frame + i) for i in range(3)], (taps.at[:1], taps.at[1:])):
            out[frame, row] = feats[frame, row].astype(F32) + value
        stores[frame].start()
    for store in stores:
        store.wait()


def call(kernel, outs, scratch, weight, operands, out_specs=None, aliases=None, outside=()):
    return pl.pallas_call(
        kernel,
        out_shape=outs,
        in_specs=[ANYWHERE if k in (aliases or {}) or k in outside else VMEM for k in range(len(operands))],
        out_specs=[VMEM] * len(outs) if out_specs is None else out_specs,
        scratch_shapes=scratch,
        input_output_aliases=aliases or {},
        compiler_params=vmem_params(),
        cost_estimate=pl.CostEstimate(flops=weight, bytes_accessed=1 << 20, transcendentals=1 << 20),
    )(*operands)


def on_device(feats, clip_ids, gain_one, shift_one, kernel_one, gain_two, shift_two, kernel_two):
    n_frames, n_rows, cols, width = feats.shape
    params = (gain_one, shift_one, gain_two, shift_two)
    per_slab = feats.size // GROUPS * lax.axis_size("space")
    late = n_frames - 2
    plane = (n_rows + 2, cols, width)
    act = pltpu.VMEM((2,) + plane, BF16)
    act_late = pltpu.VMEM((late,) + plane, BF16)
    work = 54 * feats.size // n_frames * width
    late_shapes = [shaped((2,) + plane), shaped((2, width), F32), shaped((2,) + kernel_one.shape[1:])]
    hidden_shapes = [shaped((late, n_rows, cols, width)), shaped((2, 8, width), F32), shaped(edge_shape(feats, late))]

    frames, tail, edges, copies, mark = entry_call(feats)
    table = stats_table(copies)
    sides = row_halo(edges)
    n_sides = len(sides)
    first, second = slab_halo(tail, sides)
    corners = row_halo(edges_of(first))
    taps, aux = setup_call(kernel_one, clip_ids, params, per_slab, mark)
    aux, *corners = lax.optimization_barrier((aux, *corners))
    operands = [aux, table, frames, *sides, taps, in_hbm(kernel_one)]
    act_low, affine, more_taps, hidden_late, stats, edges = call(
        functools.partial(late_kernel, n_sides),
        late_shapes + hidden_shapes,
        [act_late, pltpu.SemaphoreType.DMA((6,))],
        work * 3 // 4,
        operands,
        outside=(len(operands) - 1,),
    )
    before = chained(hidden_late[late - 2 :])
    sides_late = row_halo(edges)
    hidden_early, edges, stats = call(
        functools.partial(early_kernel, n_sides),
        [shaped((2, n_rows, cols, width)), shaped(edge_shape(feats, 2)), shaped((1, 2 * width), F32)],
        [act],
        2 * work,
        [aux, first, second, *corners, act_low, affine, taps, more_taps, stats],
    )

    sides_early = row_halo(edges)
    _, tables = slab_tables(stats)
    before, tables[0] = lax.optimization_barrier((before, tables[0]))
    corners = row_halo(edges_of(before))
    operands = [aux, *tables, hidden_early, hidden_late, *sides_early, *sides_late, before, *corners, kernel_two, frames]
    return call(
        functools.partial(last_kernel, len(tables), n_sides),
        shaped(feats.shape, F32),
        [pltpu.VMEM((n_frames + 2,) + plane, BF16), pltpu.VMEM(feats.shape, F32), pltpu.SemaphoreType.DMA((n_frames,))],
        n_frames * work,
        operands,
        out_specs=ANYWHERE,
    )


def solution(mesh):
    return jax.shard_map(
        on_device,
        mesh=mesh,
        in_specs=(P("tm", "space", None, None), P(), P(), P(), P(), P(), P(), P()),
        out_specs=P("tm", "space", None, None),
        check_vma=False,
    )
```
